128 devices in a mesh: clus: 4 (over x), split: 32 (over z, y, core).
Axes of the slice: x: 4, y: 4, z: 4, core: 2. Of those that a mesh axis runs over, the one named last changes fastest.
Arguments:
- embeddings: float32 [16384, 4096], P(('clus', 'split'))
- cluster_ids: int32 [16384], P(('clus', 'split')), may hold values from 0 to 63, as said below
Outputs:
- best_similarity: float32 [16384], P(('clus', 'split'))
The draws below stay inside these ranges and needn't reach their ends.
Inputs may be any that keep to these rules, and one draw needn't show every extreme that they name: `cluster_ids`: the documents of one device's shard hold at most 64 cluster ids with any one residue modulo 4, and every shard has a residue reached exactly 64 times. Some clusters hold a single document.
All inputs are finite; a program needn't handle non-finite values.
Results may differ from the reference program's by a relative error of at most 0.0003.
Values may be sent and summed in bfloat16 or wider, within the bound.
No kernel may reach another device: no remote copies, remote signals or barrier semaphores. Data moves between devices by JAX's collectives and lax.ppermute only.
A program may use at most 192 MiB of HBM per device.

```python
import math
import jax
import jax.numpy as jnp
from jax import lax

D = 4096
DOC_DEV = 128
CLU_PER = 16
CAP = 64
CLUSTERS = 64
DOCS = 16384
N_CLUS = 4
N_SPLIT = 32
DEVICES = 128


def cluster_draw(key):
    keys = jax.random.split(key, DEVICES)

    def one_shard(shard_key, shard):
        first, second, third, fourth, fifth = jax.random.split(shard_key, 5)
        group = shard // N_SPLIT
        marked = shard % N_SPLIT == group % N_SPLIT
        hot = jnp.where(marked, group, jax.random.randint(first, (), 0, N_CLUS))
        slots = jax.random.permutation(second, N_CLUS * CAP)
        owners = slots // CAP
        order_key = jnp.where(owners == hot, 0, 1) * (N_CLUS * CAP) + jnp.arange(N_CLUS * CAP)
        chosen = owners[jnp.argsort(order_key)][:DOC_DEV]
        pick_a = jax.random.randint(fourth, (DOC_DEV,), 0, CLU_PER - 1)
        pick_b = jax.random.randint(fifth, (DOC_DEV,), 0, CLU_PER - 1)
        within = jnp.minimum(pick_a, pick_b)
        lone = marked & (jnp.arange(DOC_DEV) == 0)
        within = jnp.where(lone, CLU_PER - 1, within)
        labels = chosen + N_CLUS * within
        return labels[jax.random.permutation(third, DOC_DEV)].astype(jnp.int32)
    return jax.vmap(one_shard)(keys, jnp.arange(DEVICES, dtype=jnp.int32)).reshape(DOCS)


def draw_cluster_ids(key, part):
    return cluster_draw(key)


def draw_embeddings(key, part):
    labels = cluster_draw(key)
    key = jax.random.fold_in(key, 7)
    center_key = jax.random.fold_in(key, 0)
    noise_key = jax.random.fold_in(key, 1)
    mix_key = jax.random.fold_in(key, 2)
    scale_key = jax.random.fold_in(key, 3)
    sub_key = jax.random.fold_in(key, 5)
    pick_key = jax.random.fold_in(key, 6)
    subs = max(1, DOCS // (3 * CLUSTERS))
    sub_of = jax.random.randint(pick_key, (DOCS,), 0, subs)
    centers = jax.vmap(lambda label: jax.random.normal(jax.random.fold_in(center_key, label), (D,), jnp.float32))(labels)
    offsets = jax.vmap(lambda label, sub: jax.random.normal(jax.random.fold_in(jax.random.fold_in(sub_key, label), sub), (D,), jnp.float32))(labels, sub_of)
    mix = jnp.exp(jax.random.uniform(mix_key, (DOCS, 1), jnp.float32, math.log(0.05), math.log(1.5)))
    scale = jnp.exp(jax.random.uniform(scale_key, (DOCS, 1), jnp.float32, 0.0, 2.302585))
    noise = jax.random.normal(noise_key, (DOCS, D), jnp.float32)
    return (scale * (centers + offsets + mix * noise)).astype(jnp.float32)


def setup_inputs(seed: int = 0) -> dict:
    seeds = jax.random.split(jax.random.key(seed), 3)
    embeddings = draw_embeddings(jax.random.fold_in(seeds[2], 71), 0)
    cluster_ids = draw_cluster_ids(jax.random.fold_in(seeds[2], 71), 0)
    return dict(embeddings=embeddings, cluster_ids=cluster_ids)


def reference(embeddings, cluster_ids):
    squares = lax.optimization_barrier(jnp.sum(embeddings * embeddings, axis=1, keepdims=True))
    unit = (embeddings * lax.rsqrt(squares + 1e-06)).astype(jnp.bfloat16)
    owner_of = (cluster_ids % N_CLUS).astype(jnp.int32)
    onehot = (owner_of[:, None] == jnp.arange(N_CLUS, dtype=jnp.int32)[None, :]).astype(jnp.int32)
    before = jnp.cumsum(onehot, axis=0) - onehot
    rank = lax.optimization_barrier(jnp.sum(before * onehot, axis=1)).astype(jnp.int32)
    capacity = DEVICES * CAP
    block = math.gcd(512, capacity)
    places = jnp.arange(capacity, dtype=jnp.int32)

    def per_owner(owner):
        slot = jnp.where(owner_of == owner, rank, capacity).astype(jnp.int32)
        buffer = jnp.zeros((capacity + 1, D), jnp.bfloat16).at[slot].set(unit)[:capacity]
        labels = jnp.full((capacity + 1,), -1, jnp.int32).at[slot].set(cluster_ids)[:capacity]

        def per_block(index):
            start = (index * block).astype(jnp.int32)
            left = lax.dynamic_slice_in_dim(buffer, start, block, 0)
            left_ids = lax.dynamic_slice_in_dim(labels, start, block, 0)
            scores = lax.dot_general(left, buffer, (((1,), (1,)), ((), ())), preferred_element_type=jnp.float32)
            rows_at = start + jnp.arange(block, dtype=jnp.int32)
            mask = (left_ids[:, None] == labels[None, :]) & (left_ids[:, None] >= 0) & (rows_at[:, None] != places[None, :])
            return lax.optimization_barrier(jnp.max(jnp.where(mask, scores, -1.0), axis=1))
        return lax.map(per_block, jnp.arange(capacity // block, dtype=jnp.int32)).reshape(capacity)
    table = lax.map(per_owner, jnp.arange(N_CLUS, dtype=jnp.int32))
    return table[owner_of, rank]
```

```python
import functools

import jax
import jax.numpy as jnp
from jax import lax
from jax.experimental import pallas as pl
from jax.experimental.pallas import tpu as pltpu
from jax.sharding import Mesh, PartitionSpec as P

ROWS = 128
SLICES = 8
WIDTH = 512
LABEL_ROWS = 16
BINS = 16
BLOCK = 128
SLOTS = BLOCK - 1
CAPS = (704, 512, 320, 256)
STARTS = (0, 704, 1216, 1536)
SORTED = 1792
HALF = 64
CHUNK = 9 * HALF
PARTIAL = 4 * CHUNK
VMEM_LIMIT = 56 * 1024 * 1024
f32, bf16, i32 = jnp.float32, jnp.bfloat16, jnp.int32
WHOLE = pl.BlockSpec(memory_space=pltpu.VMEM)
SCALARS = pl.BlockSpec(memory_space=pltpu.SMEM)


def params():
    return pltpu.CompilerParams(vmem_limit_bytes=VMEM_LIMIT)


def iota(shape, dim):
    return lax.broadcasted_iota(i32, shape, dim)


def dot_last(a, b):
    return lax.dot_general(a, b, (((1,), (1,)), ((), ())), preferred_element_type=f32)


def dot(a, b):
    return lax.dot_general(a, b, (((1,), (0,)), ((), ())), preferred_element_type=f32)


def as_bf16(mask):
    return jnp.where(mask, 1.0, 0.0).astype(bf16)


def bin_of(labels):
    return ((labels >> 2) + 4 * (labels & 3)) & (BINS - 1)


def unit_kernel(x_ref, ids_ref, out_ref):
    x = x_ref[...]
    squares = jnp.sum(x * x, axis=1, keepdims=True)
    unit = (x * lax.rsqrt(squares + 1e-06)).astype(bf16)
    ids = jnp.concatenate([ids_ref[...].astype(f32), jnp.zeros((1, WIDTH - ROWS), f32)], axis=1)
    ids = jnp.broadcast_to(ids, (LABEL_ROWS, WIDTH)).astype(bf16)
    for j in range(SLICES):
        out_ref[j, :ROWS, :] = unit[:, j * WIDTH:(j + 1) * WIDTH]
        out_ref[j, ROWS:, :] = ids


def pack_kernel(x_ref, out_ref, code_ref):
    labels = jnp.max(x_ref[:, ROWS:, :ROWS].astype(f32), axis=1).astype(i32)
    bins = bin_of(labels)
    member = jnp.concatenate([jnp.where(bins == b, 1.0, 0.0) for b in range(BINS)], axis=0)
    member16 = member.astype(bf16)
    row, col = iota((BLOCK, BLOCK), 0), iota((BLOCK, BLOCK), 1)
    along = dot(member16, as_bf16(row < col))
    earlier = dot(as_bf16(((row >> 3) == (col >> 3)) & (col < row)), member16)
    ranks = member * (along + jnp.sum(earlier, axis=1, keepdims=True))
    rank = sum(ranks[8 * b:8 * b + 8] for b in range(BINS)).astype(i32)
    code = jnp.where(rank < SLOTS, bins * BLOCK + rank, -1)
    code_ref[...] = code
    docs = SLICES * ROWS
    flat = lambda v: jnp.concatenate([v[i:i + 1] for i in range(SLICES)], axis=1)
    code_row, label_row = flat(code), flat(labels)
    x = x_ref[:, :ROWS, :].reshape(docs, WIDTH)
    counts = dot_last(jnp.ones((8, docs), bf16), as_bf16(iota((BLOCK, docs), 0) == label_row))[:1]
    high = jnp.floor(counts * (1.0 / 32.0))
    low = counts - 32.0 * high
    plus_one = jnp.broadcast_to((label_row + 1).astype(f32), (8, docs)).astype(bf16)
    is_last = iota((BLOCK, WIDTH), 0) == SLOTS
    group = 4
    for start in range(0, BINS, group):
        onehot = as_bf16(iota((group * BLOCK, docs), 0) + start * BLOCK == code_row)
        packed = dot(onehot, x)
        names = dot_last(plus_one, onehot)[:1]
        for b in range(group):
            extra = jnp.concatenate(
                [names[:, b * BLOCK:(b + 1) * BLOCK], low, high, jnp.zeros((1, BLOCK), f32)], axis=1
            )
            out_ref[start + b] = jnp.where(is_last, extra, packed[b * BLOCK:(b + 1) * BLOCK]).astype(bf16)


def sort_kernel(where_ref, x_ref, out_ref, pos_ref, meta_ref):
    mine = where_ref[0] * 4 + where_ref[1]
    tail = x_ref[:, BLOCK - 16:, :3 * BLOCK].astype(f32)
    tail = jnp.max(jnp.where(iota(tail.shape, 1) == 15, tail, 0.0), axis=1)
    labels = tail[:, :BLOCK].astype(i32) - 1
    low, high = tail[:, BLOCK:2 * BLOCK].astype(bf16), tail[:, 2 * BLOCK:].astype(bf16)
    row, col = iota((BLOCK, BLOCK), 0), iota((BLOCK, BLOCK), 1)
    in_bin = (bin_of(row) == col) & (row < 4 * BINS)
    sizes, total = [], 0.0
    for r in range(4):
        pick = as_bf16(in_bin & ((row & 3) == r))
        counts = dot(low, pick) + 32.0 * dot(high, pick)
        total = total + counts
        sizes.append(jnp.sum(counts, axis=0, keepdims=True))
    a, b = jnp.maximum(sizes[0], sizes[1]), jnp.minimum(sizes[0], sizes[1])
    c, d = jnp.maximum(sizes[2], sizes[3]), jnp.minimum(sizes[2], sizes[3])
    first, e = jnp.maximum(a, c), jnp.minimum(a, c)
    g, fourth = jnp.maximum(b, d), jnp.minimum(b, d)
    ordered = (first, jnp.maximum(e, g), jnp.minimum(e, g), fourth)
    over = jnp.max(jnp.where(total > SLOTS, 1.0, 0.0), axis=0, keepdims=True)
    for size, cap in zip(ordered, CAPS):
        over = jnp.maximum(over, jnp.where(size > cap, 1.0, 0.0))
    over = jnp.max(over, axis=1, keepdims=True)
    here = iota((1, BLOCK), 1) == mine
    own = lambda v: jnp.sum(jnp.where(here, v, 0.0), axis=1, keepdims=True)
    wide = lambda v: jnp.broadcast_to(v, (1, BLOCK))
    meta_ref[...] = jnp.concatenate([wide(own(v)) for v in ordered] + [wide(over)] * 4, axis=0)

    n = [own(v) for v in sizes]
    valid = (labels >= 0) & (iota(labels.shape, 1) < SLOTS)
    upper = as_bf16(row < col)
    lower = as_bf16(iota((BINS, BINS), 1) < iota((BINS, BINS), 0))
    pos = jnp.full(labels.shape, -1.0, f32)
    for r in range(4):
        place = sum(
            jnp.where((n[q] > n[r]) | ((n[q] == n[r]) & (q < r)), 1.0, 0.0) for q in range(4) if q != r
        )
        start = jnp.where(
            place < 0.5, float(STARTS[0]),
            jnp.where(place < 1.5, float(STARTS[1]), jnp.where(place < 2.5, float(STARTS[2]), float(STARTS[3]))),
        )
        member = valid & ((labels & 3) == r)
        member16 = as_bf16(member)
        rank = dot(member16, upper) + jnp.sum(dot(lower, member16), axis=1, keepdims=True)
        pos = jnp.where(member, start + rank, pos)
    pos = pos.astype(i32)
    pos_ref[...] = pos
    x = x_ref[...].reshape(BINS * BLOCK, WIDTH)
    pos_row = jnp.concatenate([pos[i:i + 1] for i in range(BINS)], axis=1)
    step = SORTED // 4
    for i in range(4):
        onehot = as_bf16(iota((step, BINS * BLOCK), 0) + i * step == pos_row)
        out_ref[i * step:(i + 1) * step, :] = dot(onehot, x).astype(bf16)


def column_blocks(core):
    for q in ((0,) if core == 0 else (1, 2, 3)):
        for first in range(0, CAPS[q], BLOCK):
            yield q, first


def gram_kernel(where_ref, a_ref, b_ref, meta_ref, out0, out1, out2, out3, part_ref):
    y, c = where_ref[2], where_ref[3]
    for core in range(2):
        @pl.when(c == core)
        def _():
            at = 0
            for q, first in column_blocks(core):
                rows = CAPS[q] - first
                left = pl.ds(STARTS[q] + first, rows)
                right = pl.ds(STARTS[q] + first, BLOCK)
                score = dot_last(a_ref[left, :], a_ref[right, :]) + dot_last(b_ref[left, :], b_ref[right, :])
                size = meta_ref[q:q + 1, :].astype(i32)
                i, j = iota(score.shape, 0), iota(score.shape, 1)
                keep = (i + first < size) & (j + first < size) & (i != j)
                score = jnp.where(keep, score, -4.0)
                done = 0
                while done < rows:
                    chunk, offset = divmod(at + done, CHUNK)
                    take = min(rows - done, CHUNK - offset)
                    part_ref[chunk, offset:offset + take, :] = score[done:done + take]
                    done += take
                at += rows
            while at < PARTIAL:
                chunk, offset = divmod(at, CHUNK)
                part_ref[chunk, offset:offset + HALF, :] = jnp.full((HALF, BLOCK), -4.0, f32)
                at += HALF
    for shift, out in enumerate((out0, out1, out2, out3)):
        out[...] = part_ref[lax.rem(y + shift, 4)]


def tables():
    rows, cols = [], []
    for core in range(2):
        have = []
        for q, first in column_blocks(core):
            for r in range(first, CAPS[q], HALF):
                have.append((STARTS[q] + r, STARTS[q] + first))
        have += [(SORTED, SORTED)] * (36 - len(have))
        rows += [h[0] for h in have]
        cols += [h[1] for h in have]
    return rows, cols


def max_kernel(where_ref, rows_ref, cols_ref, p0, p1, p2, p3, pos_ref, out_ref, best_ref):
    y, c = where_ref[2], where_ref[3]
    done = p0[...] + p1[...] + p2[...] + p3[...]
    best_ref[...] = jnp.full(best_ref.shape, -1.0, f32)
    eye = iota((BLOCK, BLOCK), 0) == iota((BLOCK, BLOCK), 1)
    for t in range(CHUNK // HALF):
        block = done[t * HALF:(t + 1) * HALF]
        index = c * 36 + y * 9 + t
        at = pl.ds(pl.multiple_of(rows_ref[index], HALF), HALF)
        best_ref[at, :] = jnp.maximum(best_ref[at, :], jnp.max(block, axis=1, keepdims=True))
        column = jnp.max(block, axis=0, keepdims=True)
        column = jnp.max(jnp.where(eye, column, -1.0), axis=1, keepdims=True)
        at = pl.ds(pl.multiple_of(cols_ref[index], HALF), BLOCK)
        best_ref[at, :] = jnp.maximum(best_ref[at, :], column)
    best = best_ref[:SORTED, :]
    index = iota((SORTED, BLOCK), 0)
    for s in range(BINS):
        out_ref[s:s + 1, :] = jnp.max(jnp.where(index == pos_ref[s:s + 1, :], best, -1.0), axis=0, keepdims=True)


def pick_kernel(where_ref, v_ref, code_ref, out_ref):
    line = where_ref[2] * 2 + where_ref[3]
    values = jnp.max(v_ref[...].reshape(BINS, 8, BLOCK), axis=1)
    eye = iota((BLOCK, BLOCK), 0) == iota((BLOCK, BLOCK), 1)
    code = jnp.max(jnp.where(iota((8, ROWS), 0) == line, code_ref[...], -1), axis=0, keepdims=True)
    code = jnp.max(jnp.where(eye, code.astype(f32), -1.0), axis=1, keepdims=True).astype(i32)
    slot = iota((ROWS, BLOCK), 1)
    best = jnp.full((ROWS, BLOCK), -1.0, f32)
    for b in range(BINS):
        best = jnp.maximum(best, jnp.where(slot + b * BLOCK == code, values[b:b + 1], -1.0))
    best = jnp.max(best, axis=1, keepdims=True)
    out_ref[...] = jnp.max(jnp.where(eye, best, -1.0), axis=0, keepdims=True)


def masked_scores(left, left_ids, right, right_ids, left_start):
    scores = dot_last(left, right)
    left_at = left_start + jnp.arange(left.shape[0], dtype=i32)
    right_at = jnp.arange(right.shape[0], dtype=i32)
    mask = (
        (left_ids[:, None] == right_ids[None, :])
        & (left_ids[:, None] >= 0)
        & (left_at[:, None] != right_at[None, :])
    )
    return jnp.where(mask, scores, -1.0)


def gather_groups(embeddings, cluster_ids):
    split = ("z", "y", "c")
    rows = embeddings.shape[0]
    groups = lax.axis_size("x")
    cap = 2 * rows // groups
    slots = groups * cap
    owner_of = cluster_ids % groups
    onehot = (owner_of[:, None] == jnp.arange(groups, dtype=i32)[None, :]).astype(i32)
    before = jnp.cumsum(onehot, axis=0) - onehot
    rank = jnp.sum(before * onehot, axis=1)
    place = owner_of * cap + rank
    picked = place[None, :] == jnp.arange(slots, dtype=i32)[:, None]
    filled = jnp.any(picked, axis=1)
    source = jnp.sum(jnp.where(picked, jnp.arange(rows, dtype=i32)[None, :], 0), axis=1)
    out_labels = jnp.where(filled, cluster_ids[source], -1)
    squares = jnp.sum(embeddings * embeddings, axis=1, keepdims=True)
    local_unit = (embeddings * lax.rsqrt(squares + 1e-06)).astype(bf16)
    outgoing_unit = jnp.where(filled[:, None], local_unit[source], jnp.zeros((), bf16))
    unit = lax.all_to_all(outgoing_unit, "x", split_axis=0, concat_axis=0, tiled=True)
    labels = lax.all_to_all(out_labels, "x", split_axis=0, concat_axis=0, tiled=True)
    scores = masked_scores(
        unit,
        labels,
        lax.all_gather(unit, split, axis=0, tiled=True),
        lax.all_gather(labels, split, axis=0, tiled=True),
        lax.axis_index(split) * slots,
    )
    best = jnp.maximum(-1.0, jnp.max(scores, axis=1))
    returned = lax.all_to_all(best, "x", split_axis=0, concat_axis=0, tiled=True)
    return returned[place]


def on_device(embeddings, cluster_ids):
    where = jnp.stack([lax.axis_index(a) for a in ("x", "z", "y", "c")]).astype(i32)
    shape = jax.ShapeDtypeStruct
    cut = pl.pallas_call(
        unit_kernel,
        out_shape=shape((SLICES, ROWS + LABEL_ROWS, WIDTH), bf16),
        in_specs=[WHOLE, WHOLE], out_specs=WHOLE, compiler_params=params(), name="unit",
    )(embeddings, cluster_ids.reshape(1, ROWS))
    cut = lax.all_to_all(cut, ("y", "c"), 0, 0, tiled=True)
    packed, code = pl.pallas_call(
        pack_kernel,
        out_shape=(shape((BINS, BLOCK, WIDTH), bf16), shape((SLICES, ROWS), i32)),
        in_specs=[WHOLE], out_specs=(WHOLE, WHOLE), compiler_params=params(), name="pack",
    )(cut)
    packed = lax.all_to_all(packed, ("x", "z"), 0, 0, tiled=True)
    ordered, pos, meta = pl.pallas_call(
        sort_kernel,
        out_shape=(shape((SORTED, WIDTH), bf16), shape((BINS, BLOCK), i32), shape((8, BLOCK), f32)),
        in_specs=[SCALARS, WHOLE], out_specs=(WHOLE, WHOLE, WHOLE), compiler_params=params(), name="sort",
    )(where, packed)

    def within_bins(embeddings, cluster_ids):
        other = lax.ppermute(ordered, "c", [(0, 1), (1, 0)])
        partial = pl.pallas_call(
            gram_kernel,
            out_shape=[shape((CHUNK, BLOCK), f32)] * 4,
            in_specs=[SCALARS, WHOLE, WHOLE, WHOLE], out_specs=[WHOLE] * 4,
            scratch_shapes=[pltpu.VMEM((4, CHUNK, BLOCK), f32)],
            compiler_params=params(), name="gram",
        )(where, ordered, other, meta)
        arrived = [partial[0]] + [
            lax.ppermute(partial[s], "y", [(i, (i + s) % 4) for i in range(4)]) for s in (1, 2, 3)
        ]
        rows, cols = tables()
        best = pl.pallas_call(
            max_kernel,
            out_shape=shape((BINS, BLOCK), f32),
            in_specs=[SCALARS] * 3 + [WHOLE] * 5, out_specs=WHOLE,
            scratch_shapes=[pltpu.VMEM((SORTED + BLOCK, 1), f32)],
            compiler_params=params(), name="maxima",
        )(where, jnp.asarray(rows, i32), jnp.asarray(cols, i32), *arrived, pos)
        sent = jnp.broadcast_to(best[:, None, :], (BINS, 8, BLOCK)).reshape(BINS * 8, 1, BLOCK)
        back = lax.all_to_all(sent, ("x", "z", "y", "c"), 0, 0, tiled=True)
        return pl.pallas_call(
            pick_kernel,
            out_shape=shape((1, ROWS), f32),
            in_specs=[SCALARS, WHOLE, WHOLE], out_specs=WHOLE, compiler_params=params(), name="pick",
        )(where, back.reshape(BINS * 8, BLOCK), code).reshape(ROWS)

    return lax.cond(meta[4, 0] < 0.5, within_bins, gather_groups, embeddings, cluster_ids)


def solution(mesh):
    axes = ("x", "z", "y", "c")
    grid = Mesh(mesh.devices.reshape(4, 4, 4, 2), axes)
    return jax.shard_map(
        on_device, mesh=grid, in_specs=(P(axes, None), P(axes)), out_specs=P(axes), check_vma=False
    )
```

```python
import functools

import jax
import jax.numpy as jnp
from jax import lax
from jax.experimental import pallas as pl
from jax.experimental.pallas import tpu as pltpu
from jax.sharding import Mesh, PartitionSpec as P

ROWS = 128
SLICES = 8
WIDTH = 512
LABEL_ROWS = 16
BINS = 16
BLOCK = 128
SLOTS = BLOCK - 1
CAPS = (704, 512, 320, 256)
STARTS = (0, 704, 1216, 1536)
SORTED = 1792
HALF = 64
CHUNK = 9 * HALF
PARTIAL = 4 * CHUNK
f32, bf16, i32 = jnp.float32, jnp.bfloat16, jnp.int32
WHOLE = pl.BlockSpec(memory_space=pltpu.VMEM)
SCALARS = pl.BlockSpec(memory_space=pltpu.SMEM)


def params(mib):
    return pltpu.CompilerParams(vmem_limit_bytes=mib * 1024 * 1024)


def iota(shape, dim):
    return lax.broadcasted_iota(i32, shape, dim)


def dot_last(a, b):
    return lax.dot_general(a, b, (((1,), (1,)), ((), ())), preferred_element_type=f32)


def dot(a, b):
    return lax.dot_general(a, b, (((1,), (0,)), ((), ())), preferred_element_type=f32)


def as_bf16(mask):
    return jnp.where(mask, 1.0, 0.0).astype(bf16)


def bin_of(labels):
    return ((labels >> 2) + 4 * (labels & 3)) & (BINS - 1)


def unit_kernel(x_ref, ids_ref, out_ref):
    x = x_ref[...]
    squares = jnp.sum(x * x, axis=1, keepdims=True)
    unit = (x * lax.rsqrt(squares + 1e-06)).astype(bf16)
    ids = jnp.concatenate([ids_ref[...].astype(f32), jnp.zeros((1, WIDTH - ROWS), f32)], axis=1)
    ids = jnp.broadcast_to(ids, (LABEL_ROWS, WIDTH)).astype(bf16)
    for j in range(SLICES):
        out_ref[j, :ROWS, :] = unit[:, j * WIDTH:(j + 1) * WIDTH]
        out_ref[j, ROWS:, :] = ids


def pack_kernel(x_ref, out_ref, code_ref):
    labels = jnp.max(x_ref[:, ROWS:, :ROWS].astype(f32), axis=1).astype(i32)
    bins = bin_of(labels)
    member = jnp.concatenate([jnp.where(bins == b, 1.0, 0.0) for b in range(BINS)], axis=0)
    member16 = member.astype(bf16)
    row, col = iota((BLOCK, BLOCK), 0), iota((BLOCK, BLOCK), 1)
    along = dot(member16, as_bf16(row < col))
    earlier = dot(as_bf16(((row >> 3) == (col >> 3)) & (col < row)), member16)
    ranks = member * (along + jnp.sum(earlier, axis=1, keepdims=True))
    rank = sum(ranks[8 * b:8 * b + 8] for b in range(BINS)).astype(i32)
    code = jnp.where(rank < SLOTS, bins * BLOCK + rank, -1)
    code_ref[...] = code
    docs = SLICES * ROWS
    flat = lambda v: jnp.concatenate([v[i:i + 1] for i in range(SLICES)], axis=1)
    code_row, label_row = flat(code), flat(labels)
    x = x_ref[:, :ROWS, :].reshape(docs, WIDTH)
    counts = dot_last(jnp.ones((8, docs), bf16), as_bf16(iota((BLOCK, docs), 0) == label_row))[:1]
    high = jnp.floor(counts * (1.0 / 32.0))
    low = counts - 32.0 * high
    plus_one = jnp.broadcast_to((label_row + 1).astype(f32), (8, docs)).astype(bf16)
    is_last = iota((BLOCK, WIDTH), 0) == SLOTS
    group = 4
    for start in range(0, BINS, group):
        onehot = as_bf16(iota((group * BLOCK, docs), 0) + start * BLOCK == code_row)
        packed = dot(onehot, x)
        names = dot_last(plus_one, onehot)[:1]
        for b in range(group):
            extra = jnp.concatenate(
                [names[:, b * BLOCK:(b + 1) * BLOCK], low, high, jnp.zeros((1, BLOCK), f32)], axis=1
            )
            out_ref[start + b] = jnp.where(is_last, extra, packed[b * BLOCK:(b + 1) * BLOCK]).astype(bf16)


def sort_kernel(where_ref, x_ref, out_ref, pos_ref, meta_ref):
    mine = where_ref[0] * 4 + where_ref[1]
    tail = x_ref[:, BLOCK - 16:, :3 * BLOCK].astype(f32)
    tail = jnp.max(jnp.where(iota(tail.shape, 1) == 15, tail, 0.0), axis=1)
    labels = tail[:, :BLOCK].astype(i32) - 1
    low, high = tail[:, BLOCK:2 * BLOCK].astype(bf16), tail[:, 2 * BLOCK:].astype(bf16)
    row, col = iota((BLOCK, BLOCK), 0), iota((BLOCK, BLOCK), 1)
    in_bin = (bin_of(row) == col) & (row < 4 * BINS)
    sizes, total = [], 0.0
    for r in range(4):
        pick = as_bf16(in_bin & ((row & 3) == r))
        counts = dot(low, pick) + 32.0 * dot(high, pick)
        total = total + counts
        sizes.append(jnp.sum(counts, axis=0, keepdims=True))
    a, b = jnp.maximum(sizes[0], sizes[1]), jnp.minimum(sizes[0], sizes[1])
    c, d = jnp.maximum(sizes[2], sizes[3]), jnp.minimum(sizes[2], sizes[3])
    first, e = jnp.maximum(a, c), jnp.minimum(a, c)
    g, fourth = jnp.maximum(b, d), jnp.minimum(b, d)
    ordered = (first, jnp.maximum(e, g), jnp.minimum(e, g), fourth)
    over = jnp.max(jnp.where(total > SLOTS, 1.0, 0.0), axis=0, keepdims=True)
    for size, cap in zip(ordered, CAPS):
        over = jnp.maximum(over, jnp.where(size > cap, 1.0, 0.0))
    over = jnp.max(over, axis=1, keepdims=True)
    here = iota((1, BLOCK), 1) == mine
    own = lambda v: jnp.sum(jnp.where(here, v, 0.0), axis=1, keepdims=True)
    wide = lambda v: jnp.broadcast_to(v, (1, BLOCK))
    meta_ref[...] = jnp.concatenate([wide(own(v)) for v in ordered] + [wide(over)] * 4, axis=0)

    n = [own(v) for v in sizes]
    valid = (labels >= 0) & (iota(labels.shape, 1) < SLOTS)
    upper = as_bf16(row < col)
    lower = as_bf16(iota((BINS, BINS), 1) < iota((BINS, BINS), 0))
    pos = jnp.full(labels.shape, -1.0, f32)
    for r in range(4):
        place = sum(
            jnp.where((n[q] > n[r]) | ((n[q] == n[r]) & (q < r)), 1.0, 0.0) for q in range(4) if q != r
        )
        start = jnp.where(
            place < 0.5, float(STARTS[0]),
            jnp.where(place < 1.5, float(STARTS[1]), jnp.where(place < 2.5, float(STARTS[2]), float(STARTS[3]))),
        )
        member = valid & ((labels & 3) == r)
        member16 = as_bf16(member)
        rank = dot(member16, upper) + jnp.sum(dot(lower, member16), axis=1, keepdims=True)
        pos = jnp.where(member, start + rank, pos)
    pos = pos.astype(i32)
    pos_ref[...] = pos
    x = x_ref[...].reshape(BINS * BLOCK, WIDTH)
    pos_row = jnp.concatenate([pos[i:i + 1] for i in range(BINS)], axis=1)
    step = SORTED // 4
    for i in range(4):
        onehot = as_bf16(iota((step, BINS * BLOCK), 0) + i * step == pos_row)
        out_ref[i * step:(i + 1) * step, :] = dot(onehot, x).astype(bf16)


def column_blocks(core):
    for q in ((0,) if core == 0 else (1, 2, 3)):
        for first in range(0, CAPS[q], BLOCK):
            yield q, first


def gram_kernel(where_ref, a_ref, b_ref, meta_ref, out0, out1, out2, out3, part_ref):
    y, c = where_ref[2], where_ref[3]
    for core in range(2):
        @pl.when(c == core)
        def _():
            at = 0
            for q, first in column_blocks(core):
                rows = CAPS[q] - first
                left = pl.ds(STARTS[q] + first, rows)
                right = pl.ds(STARTS[q] + first, BLOCK)
                score = dot_last(a_ref[left, :], a_ref[right, :]) + dot_last(b_ref[left, :], b_ref[right, :])
                size = meta_ref[q:q + 1, :].astype(i32)
                i, j = iota(score.shape, 0), iota(score.shape, 1)
                keep = (i + first < size) & (j + first < size) & (i != j)
                score = jnp.where(keep, score, -4.0)
                done = 0
                while done < rows:
                    chunk, offset = divmod(at + done, CHUNK)
                    take = min(rows - done, CHUNK - offset)
                    part_ref[chunk, offset:offset + take, :] = score[done:done + take]
                    done += take
                at += rows
            while at < PARTIAL:
                chunk, offset = divmod(at, CHUNK)
                part_ref[chunk, offset:offset + HALF, :] = jnp.full((HALF, BLOCK), -4.0, f32)
                at += HALF
    for shift, out in enumerate((out0, out1, out2, out3)):
        out[...] = part_ref[lax.rem(y + shift, 4)]


def tables():
    rows, cols = [], []
    for core in range(2):
        have = []
        for q, first in column_blocks(core):
            for r in range(first, CAPS[q], HALF):
                have.append((STARTS[q] + r, STARTS[q] + first))
        have += [(SORTED, SORTED)] * (36 - len(have))
        rows += [h[0] for h in have]
        cols += [h[1] for h in have]
    return rows, cols


def max_kernel(where_ref, rows_ref, cols_ref, p0, p1, p2, p3, pos_ref, out_ref, best_ref):
    y, c = where_ref[2], where_ref[3]
    done = p0[...] + p1[...] + p2[...] + p3[...]
    best_ref[...] = jnp.full(best_ref.shape, -1.0, f32)
    eye = iota((BLOCK, BLOCK), 0) == iota((BLOCK, BLOCK), 1)
    for t in range(CHUNK // HALF):
        block = done[t * HALF:(t + 1) * HALF]
        index = c * 36 + y * 9 + t
        at = pl.ds(pl.multiple_of(rows_ref[index], HALF), HALF)
        best_ref[at, :] = jnp.maximum(best_ref[at, :], jnp.max(block, axis=1, keepdims=True))
        column = jnp.max(block, axis=0, keepdims=True)
        column = jnp.max(jnp.where(eye, column, -1.0), axis=1, keepdims=True)
        at = pl.ds(pl.multiple_of(cols_ref[index], HALF), BLOCK)
        best_ref[at, :] = jnp.maximum(best_ref[at, :], column)
    best = best_ref[:SORTED, :]
    index = iota((SORTED, BLOCK), 0)
    for s in range(BINS):
        out_ref[s:s + 1, :] = jnp.max(jnp.where(index == pos_ref[s:s + 1, :], best, -1.0), axis=0, keepdims=True)


def pick_kernel(where_ref, v_ref, code_ref, out_ref):
    line = where_ref[2] * 2 + where_ref[3]
    values = jnp.max(v_ref[...].reshape(BINS, 8, BLOCK), axis=1)
    eye = iota((BLOCK, BLOCK), 0) == iota((BLOCK, BLOCK), 1)
    code = jnp.max(jnp.where(iota((8, ROWS), 0) == line, code_ref[...], -1), axis=0, keepdims=True)
    code = jnp.max(jnp.where(eye, code.astype(f32), -1.0), axis=1, keepdims=True).astype(i32)
    slot = iota((ROWS, BLOCK), 1)
    best = jnp.full((ROWS, BLOCK), -1.0, f32)
    for b in range(BINS):
        best = jnp.maximum(best, jnp.where(slot + b * BLOCK == code, values[b:b + 1], -1.0))
    best = jnp.max(best, axis=1, keepdims=True)
    out_ref[...] = jnp.max(jnp.where(eye, best, -1.0), axis=0, keepdims=True)


def gather_groups(embeddings, cluster_ids):
    split = ("z", "y", "c")
    rows = embeddings.shape[0]
    groups = lax.axis_size("x")
    cap = 2 * rows // groups
    slots = groups * cap
    owner_of = cluster_ids % groups
    onehot = (owner_of[:, None] == jnp.arange(groups, dtype=i32)[None, :]).astype(i32)
    before = jnp.cumsum(onehot, axis=0) - onehot
    rank = jnp.sum(before * onehot, axis=1)
    place = owner_of * cap + rank
    picked = place[None, :] == jnp.arange(slots, dtype=i32)[:, None]
    filled = jnp.any(picked, axis=1)
    source = jnp.sum(jnp.where(picked, jnp.arange(rows, dtype=i32)[None, :], 0), axis=1)
    out_labels = jnp.where(filled, cluster_ids[source], -1)
    squares = jnp.sum(embeddings * embeddings, axis=1, keepdims=True)
    local_unit = (embeddings * lax.rsqrt(squares + 1e-06)).astype(bf16)
    outgoing_unit = jnp.where(filled[:, None], local_unit[source], jnp.zeros((), bf16))
    unit = lax.all_to_all(outgoing_unit, "x", split_axis=0, concat_axis=0, tiled=True)
    labels = lax.all_to_all(out_labels, "x", split_axis=0, concat_axis=0, tiled=True)
    members = lax.axis_size(split)

    def everywhere(v):
        copies = jnp.broadcast_to(v[None], (members,) + v.shape).reshape((members * slots,) + v.shape[1:])
        return lax.all_to_all(copies, split, split_axis=0, concat_axis=0, tiled=True)

    def add_slice(i, scores):
        part = lax.dynamic_slice_in_dim(unit, i * WIDTH, WIDTH, 1)
        return scores + dot_last(part, everywhere(part))

    scores = lax.fori_loop(0, SLICES, add_slice, jnp.zeros((slots, members * slots), f32))
    all_labels = everywhere(labels)
    own = lax.axis_index(split) * slots + jnp.arange(slots, dtype=i32)
    mask = (
        (labels[:, None] == all_labels[None, :])
        & (labels[:, None] >= 0)
        & (own[:, None] != jnp.arange(members * slots, dtype=i32)[None, :])
    )
    scores = jnp.where(mask, scores, -1.0)
    best = jnp.maximum(-1.0, jnp.max(scores, axis=1))
    returned = lax.all_to_all(best, "x", split_axis=0, concat_axis=0, tiled=True)
    return returned[place]


def on_device(embeddings, cluster_ids):
    where = jnp.stack([lax.axis_index(a) for a in ("x", "z", "y", "c")]).astype(i32)
    shape = jax.ShapeDtypeStruct
    cut = pl.pallas_call(
        unit_kernel,
        out_shape=shape((SLICES, ROWS + LABEL_ROWS, WIDTH), bf16),
        in_specs=[WHOLE, WHOLE], out_specs=WHOLE, compiler_params=params(12), name="unit",
    )(embeddings, cluster_ids.reshape(1, ROWS))
    cut = lax.all_to_all(cut, ("y", "c"), 0, 0, tiled=True)
    packed, code = pl.pallas_call(
        pack_kernel,
        out_shape=(shape((BINS, BLOCK, WIDTH), bf16), shape((SLICES, ROWS), i32)),
        in_specs=[WHOLE], out_specs=(WHOLE, WHOLE), compiler_params=params(24), name="pack",
    )(cut)
    packed = lax.all_to_all(packed, ("x", "z"), 0, 0, tiled=True)
    ordered, pos, meta = pl.pallas_call(
        sort_kernel,
        out_shape=(shape((SORTED, WIDTH), bf16), shape((BINS, BLOCK), i32), shape((8, BLOCK), f32)),
        in_specs=[SCALARS, WHOLE], out_specs=(WHOLE, WHOLE, WHOLE), compiler_params=params(28), name="sort",
    )(where, packed)

    def within_bins(embeddings, cluster_ids):
        other = lax.ppermute(ordered, "c", [(0, 1), (1, 0)])
        partial = pl.pallas_call(
            gram_kernel,
            out_shape=[shape((CHUNK, BLOCK), f32)] * 4,
            in_specs=[SCALARS, WHOLE, WHOLE, WHOLE], out_specs=[WHOLE] * 4,
            scratch_shapes=[pltpu.VMEM((4, CHUNK, BLOCK), f32)],
            compiler_params=params(20), name="gram",
        )(where, ordered, other, meta)
        arrived = [partial[0]] + [
            lax.ppermute(partial[s], "y", [(i, (i + s) % 4) for i in range(4)]) for s in (1, 2, 3)
        ]
        rows, cols = tables()
        best = pl.pallas_call(
            max_kernel,
            out_shape=shape((BINS, BLOCK), f32),
            in_specs=[SCALARS] * 3 + [WHOLE] * 5, out_specs=WHOLE,
            scratch_shapes=[pltpu.VMEM((SORTED + BLOCK, 1), f32)],
            compiler_params=params(12), name="maxima",
        )(where, jnp.asarray(rows, i32), jnp.asarray(cols, i32), *arrived, pos)
        sent = jnp.broadcast_to(best[:, None, :], (BINS, 8, BLOCK)).reshape(BINS * 8, 1, BLOCK)
        back = lax.all_to_all(sent, ("x", "z", "y", "c"), 0, 0, tiled=True)
        return pl.pallas_call(
            pick_kernel,
            out_shape=shape((1, ROWS), f32),
            in_specs=[SCALARS, WHOLE, WHOLE], out_specs=WHOLE, compiler_params=params(8), name="pick",
        )(where, back.reshape(BINS * 8, BLOCK), code).reshape(ROWS)

    return lax.cond(meta[4, 0] < 0.5, within_bins, gather_groups, embeddings, cluster_ids)


def solution(mesh):
    axes = ("x", "z", "y", "c")
    grid = Mesh(mesh.devices.reshape(4, 4, 4, 2), axes)
    return jax.shard_map(
        on_device, mesh=grid, in_specs=(P(axes, None), P(axes)), out_specs=P(axes), check_vma=False
    )
```

```python
import jax
import jax.numpy as jnp
from jax import lax
from jax.experimental import pallas as pl
from jax.experimental.pallas import tpu as pltpu
from jax.sharding import Mesh, PartitionSpec as P

ROWS = 128
HALF_WIDTH = 2048
WIDTH = 512
LABEL_ROWS = 16
BINS = 16
CHIPS = 64
BLOCK = 40
SLOTS = BLOCK - 1
LANES = 128
CAPS = (704, 512, 320, 256)
STARTS = (0, 704, 1216, 1536)
SORTED = 1792
HALF = 64
CHUNK = 9 * HALF
PARTIAL = 4 * CHUNK
f32, bf16, i32 = jnp.float32, jnp.bfloat16, jnp.int32
WHOLE = pl.BlockSpec(memory_space=pltpu.VMEM)
SCALARS = pl.BlockSpec(memory_space=pltpu.SMEM)


def params(mib):
    return pltpu.CompilerParams(vmem_limit_bytes=mib * 1024 * 1024)


def iota(shape, dim):
    return lax.broadcasted_iota(i32, shape, dim)


def dot_last(a, b):
    return lax.dot_general(a, b, (((1,), (1,)), ((), ())), preferred_element_type=f32)


def dot(a, b):
    return lax.dot_general(a, b, (((1,), (0,)), ((), ())), preferred_element_type=f32)


def as_bf16(mask):
    return jnp.where(mask, 1.0, 0.0).astype(bf16)


def bin_of(labels):
    rank, residue = labels >> 2, labels & 3
    row, col = rank >> 2, rank & 3
    col = jnp.where((row & 1) == 1, 3 - col, col)
    return 4 * col + ((row - residue) & 3)


def unit_kernel(where_ref, x_ref, ids_ref, keep_ref, send_ref):
    c = where_ref[3]
    x = x_ref[...]
    scale = lax.rsqrt(jnp.sum(x * x, axis=1, keepdims=True) + 1e-06)
    ids = jnp.concatenate([ids_ref[...].astype(f32), jnp.zeros((1, HALF_WIDTH - ROWS), f32)], axis=1)
    ids = jnp.broadcast_to(ids, (LABEL_ROWS, HALF_WIDTH)).astype(bf16)
    for half, out_ref in ((c, keep_ref), (1 - c, send_ref)):
        columns = pl.ds(pl.multiple_of(half * HALF_WIDTH, HALF_WIDTH), HALF_WIDTH)
        out_ref[:ROWS, :] = (x_ref[:, columns] * scale).astype(bf16)
        out_ref[ROWS:, :] = ids


def pack_kernel(where_ref, keep_ref, got_ref, out_ref, code_ref):
    first = where_ref[3] == 0
    kept = jnp.max(keep_ref[ROWS:, :ROWS].astype(f32), axis=0, keepdims=True)
    got = jnp.max(got_ref[ROWS:, :ROWS].astype(f32), axis=0, keepdims=True)
    labels = jnp.concatenate([jnp.where(first, kept, got), jnp.where(first, got, kept)], axis=0).astype(i32)
    bins = bin_of(labels)
    member = jnp.concatenate([jnp.where(bins == b, 1.0, 0.0) for b in range(BINS)], axis=0)
    member16 = member.astype(bf16)
    along = dot(member16, as_bf16(iota((ROWS, ROWS), 0) < iota((ROWS, ROWS), 1)))
    row, col = iota((2 * BINS, 2 * BINS), 0), iota((2 * BINS, 2 * BINS), 1)
    earlier = dot(as_bf16(((row >> 1) == (col >> 1)) & (col < row)), member16)
    ranks = member * (along + jnp.sum(earlier, axis=1, keepdims=True))
    rank = sum(ranks[2 * b:2 * b + 2] for b in range(BINS)).astype(i32)
    code = jnp.where(rank < SLOTS, bins * BLOCK + rank, -1)
    code_ref[...] = jnp.concatenate([code] * 4, axis=0)
    docs = 2 * ROWS
    flat = lambda v: jnp.concatenate([v[:1], v[1:]], axis=1)
    rank_row, bin_row, label_row = flat(rank), flat(bins), flat(labels)
    counts = dot_last(jnp.ones((8, docs), bf16), as_bf16(iota((LANES, docs), 0) == label_row))[:1]
    named = jnp.where(iota((BINS, docs), 0) == bin_row, (label_row + 1).astype(f32), 0.0).astype(bf16)
    names = dot_last(named, as_bf16((iota((LANES, docs), 0) == rank_row) & (rank_row < SLOTS)))
    own = jnp.where(first, code[:1], code[1:])
    other = jnp.where(first, code[1:], code[:1])
    onehot = as_bf16(iota((BINS * BLOCK, docs), 0) == jnp.concatenate([own, other], axis=1))
    is_last = iota((BLOCK, WIDTH), 0) == SLOTS
    for y in range(4):
        columns = slice(y * WIDTH, (y + 1) * WIDTH)
        x = jnp.concatenate([keep_ref[:ROWS, columns], got_ref[:ROWS, columns]], axis=0)
        packed = dot(onehot, x)
        for b in range(BINS):
            extra = jnp.concatenate([names[b:b + 1], counts, jnp.zeros((1, 2 * LANES), f32)], axis=1)
            out_ref[4 * b + y] = jnp.where(is_last, extra, packed[b * BLOCK:(b + 1) * BLOCK]).astype(bf16)


def sort_kernel(where_ref, x_ref, out_ref, pos_ref, meta_ref):
    mine = where_ref[0] * 4 + where_ref[1]
    tail = x_ref[:, BLOCK - 8:, :2 * LANES].astype(f32)
    tail = jnp.max(jnp.where(iota(tail.shape, 1) == 7, tail, 0.0), axis=1)
    labels, chip_counts = tail[:, :LANES].astype(i32) - 1, tail[:, LANES:].astype(bf16)
    row, col = iota((LANES, LANES), 0), iota((LANES, LANES), 1)
    in_bin = (bin_of(row) == col) & (row < 4 * BINS)
    sizes, total = [], 0.0
    for r in range(4):
        counts = dot(chip_counts, as_bf16(in_bin & ((row & 3) == r)))
        total = total + counts
        sizes.append(jnp.sum(counts, axis=0, keepdims=True))
    a, b = jnp.maximum(sizes[0], sizes[1]), jnp.minimum(sizes[0], sizes[1])
    c, d = jnp.maximum(sizes[2], sizes[3]), jnp.minimum(sizes[2], sizes[3])
    first, e = jnp.maximum(a, c), jnp.minimum(a, c)
    g, fourth = jnp.maximum(b, d), jnp.minimum(b, d)
    ordered = (first, jnp.maximum(e, g), jnp.minimum(e, g), fourth)
    over = jnp.max(jnp.where(total > SLOTS, 1.0, 0.0), axis=0, keepdims=True)
    for size, cap in zip(ordered, CAPS):
        over = jnp.maximum(over, jnp.where(size > cap, 1.0, 0.0))
    over = jnp.max(over, axis=1, keepdims=True)
    here = iota((1, LANES), 1) == mine
    own = lambda v: jnp.sum(jnp.where(here, v, 0.0), axis=1, keepdims=True)
    wide = lambda v: jnp.broadcast_to(v, (1, LANES))
    meta_ref[...] = jnp.concatenate([wide(own(v)) for v in ordered] + [wide(over)] * 4, axis=0)

    n = [own(v) for v in sizes]
    valid = (labels >= 0) & (iota(labels.shape, 1) < SLOTS)
    upper = as_bf16(row < col)
    lower = as_bf16(iota((CHIPS, CHIPS), 1) < iota((CHIPS, CHIPS), 0))
    pos = jnp.full(labels.shape, -1.0, f32)
    for r in range(4):
        place = sum(
            jnp.where((n[q] > n[r]) | ((n[q] == n[r]) & (q < r)), 1.0, 0.0) for q in range(4) if q != r
        )
        start = jnp.where(
            place < 0.5, float(STARTS[0]),
            jnp.where(place < 1.5, float(STARTS[1]), jnp.where(place < 2.5, float(STARTS[2]), float(STARTS[3]))),
        )
        member = valid & ((labels & 3) == r)
        member16 = as_bf16(member)
        rank = dot(member16, upper) + jnp.sum(dot(lower, member16), axis=1, keepdims=True)
        pos = jnp.where(member, start + rank, pos)
    pos_ref[...] = pos.astype(i32)
    per, groups = 16, CHIPS // 16
    plus = jnp.where(iota(pos.shape, 1) < BLOCK, pos + 1.0, 0.0)
    lined = jnp.zeros((8, per * BLOCK), f32)
    for t in range(per):
        rows = jnp.concatenate([plus[per * g + t:per * g + t + 1] for g in range(groups)] * 2, axis=0)
        rows = jnp.concatenate([rows, jnp.zeros((8, per * BLOCK - LANES), f32)], axis=1)
        lined = lined + (pltpu.roll(rows, t * BLOCK, 1) if t else rows)
    pos_row = jnp.concatenate([lined[g:g + 1] for g in range(groups)], axis=1).astype(i32) - 1
    x = x_ref[...].reshape(CHIPS * BLOCK, WIDTH)
    step = SORTED // 4
    for i in range(4):
        onehot = as_bf16(iota((step, CHIPS * BLOCK), 0) + i * step == pos_row)
        out_ref[i * step:(i + 1) * step, :] = dot(onehot, x).astype(bf16)


def column_blocks(core):
    for q in ((0,) if core == 0 else (1, 2, 3)):
        for first in range(0, CAPS[q], LANES):
            yield q, first


def gram_kernel(where_ref, a_ref, b_ref, meta_ref, out0, out1, out2, out3, part_ref):
    y, c = where_ref[2], where_ref[3]
    for core in range(2):
        @pl.when(c == core)
        def _():
            at = 0
            for q, first in column_blocks(core):
                rows = CAPS[q] - first
                left = pl.ds(STARTS[q] + first, rows)
                right = pl.ds(STARTS[q] + first, LANES)
                score = dot_last(a_ref[left, :], a_ref[right, :]) + dot_last(b_ref[left, :], b_ref[right, :])
                size = meta_ref[q:q + 1, :].astype(i32)
                i, j = iota(score.shape, 0), iota(score.shape, 1)
                keep = (i + first < size) & (j + first < size) & (i != j)
                score = jnp.where(keep, score, -4.0)
                done = 0
                while done < rows:
                    chunk, offset = divmod(at + done, CHUNK)
                    take = min(rows - done, CHUNK - offset)
                    part_ref[chunk, offset:offset + take, :] = score[done:done + take]
                    done += take
                at += rows
            while at < PARTIAL:
                chunk, offset = divmod(at, CHUNK)
                part_ref[chunk, offset:offset + HALF, :] = jnp.full((HALF, LANES), -4.0, f32)
                at += HALF
    for shift, out in enumerate((out0, out1, out2, out3)):
        out[...] = part_ref[lax.rem(y + shift, 4)]


FIRST_ROW = (0, 6, 10, 13)


def tables():
    rows, odd, cols = [], [], []
    for core in range(2):
        have = []
        for q, first in column_blocks(core):
            for r in range(first, CAPS[q], HALF):
                have.append((FIRST_ROW[q] + r // LANES, r // HALF % 2, FIRST_ROW[q] + first // LANES))
        have += [(15, 0, 15)] * (36 - len(have))
        for table, column in ((rows, 0), (odd, 1), (cols, 2)):
            table += [h[column] for h in have]
    return jnp.asarray(rows + odd + cols, i32)


def max_kernel(where_ref, table_ref, p0, p1, p2, p3, pos_ref, out_ref, best_ref):
    y, c = where_ref[2], where_ref[3]
    best_ref[...] = jnp.full(best_ref.shape, -1.0, f32)
    sub, lane = iota((HALF, LANES), 0), iota((HALF, LANES), 1)
    for t in range(CHUNK // HALF):
        at = slice(t * HALF, (t + 1) * HALF)
        block = (p0[at, :] + p1[at, :]) + (p2[at, :] + p3[at, :])
        index = c * 36 + y * 9 + t
        row, odd, col = (table_ref[72 * i + index] for i in range(3))
        along = jnp.max(block, axis=1, keepdims=True)
        along = jnp.max(jnp.where(sub + odd * HALF == lane, along, -1.0), axis=0, keepdims=True)
        best_ref[pl.ds(row, 1), :] = jnp.maximum(best_ref[pl.ds(row, 1), :], along)
        down = jnp.max(block, axis=0, keepdims=True)
        best_ref[pl.ds(col, 1), :] = jnp.maximum(best_ref[pl.ds(col, 1), :], down)
    pos = pos_ref[...]
    pos = jnp.where(pos >= STARTS[1], pos + HALF, pos)
    pos = jnp.where(pos >= STARTS[3] + HALF, pos + HALF, pos)
    row, lane = pos >> 7, pos & (LANES - 1)
    out = jnp.full(pos.shape, -1.0, f32)
    for r in range(15):
        value = jnp.broadcast_to(best_ref[r:r + 1, :], pos.shape)
        value = jnp.take_along_axis(value, lane, axis=1, mode="promise_in_bounds")
        out = jnp.where(row == r, value, out)
    out_ref[...] = out


def pick_kernel(where_ref, v_ref, code_ref, out_ref):
    c = where_ref[3]
    values = jnp.max(v_ref[...].reshape(BINS, 8, LANES), axis=1)
    eye = iota((LANES, LANES), 0) == iota((LANES, LANES), 1)
    code = jnp.max(jnp.where(iota((8, ROWS), 0) == c, code_ref[...], -1), axis=0, keepdims=True)
    code = jnp.max(jnp.where(eye, code.astype(f32), -1.0), axis=1, keepdims=True).astype(i32)
    slot = iota((ROWS, LANES), 1)
    best = jnp.full((ROWS, LANES), -1.0, f32)
    for b in range(BINS):
        best = jnp.where((slot + b * BLOCK == code) & (slot < BLOCK), values[b:b + 1], best)
    best = jnp.max(best, axis=1, keepdims=True)
    out_ref[...] = jnp.max(jnp.where(eye, best, -1.0), axis=0, keepdims=True)


def gather_groups(embeddings, cluster_ids):
    split = ("z", "y", "c")
    rows = embeddings.shape[0]
    groups = lax.axis_size("x")
    cap = 2 * rows // groups
    slots = groups * cap
    owner_of = cluster_ids % groups
    onehot = (owner_of[:, None] == jnp.arange(groups, dtype=i32)[None, :]).astype(i32)
    before = jnp.cumsum(onehot, axis=0) - onehot
    rank = jnp.sum(before * onehot, axis=1)
    place = owner_of * cap + rank
    picked = place[None, :] == jnp.arange(slots, dtype=i32)[:, None]
    filled = jnp.any(picked, axis=1)
    source = jnp.sum(jnp.where(picked, jnp.arange(rows, dtype=i32)[None, :], 0), axis=1)
    out_labels = jnp.where(filled, cluster_ids[source], -1)
    squares = jnp.sum(embeddings * embeddings, axis=1, keepdims=True)
    local_unit = (embeddings * lax.rsqrt(squares + 1e-06)).astype(bf16)
    outgoing_unit = jnp.where(filled[:, None], local_unit[source], jnp.zeros((), bf16))
    unit = lax.all_to_all(outgoing_unit, "x", split_axis=0, concat_axis=0, tiled=True)
    labels = lax.all_to_all(out_labels, "x", split_axis=0, concat_axis=0, tiled=True)
    members = lax.axis_size(split)

    def everywhere(v):
        copies = jnp.broadcast_to(v[None], (members,) + v.shape).reshape((members * slots,) + v.shape[1:])
        return lax.all_to_all(copies, split, split_axis=0, concat_axis=0, tiled=True)

    def add_slice(i, scores):
        part = lax.dynamic_slice_in_dim(unit, i * WIDTH, WIDTH, 1)
        return scores + dot_last(part, everywhere(part))

    scores = lax.fori_loop(0, embeddings.shape[1] // WIDTH, add_slice, jnp.zeros((slots, members * slots), f32))
    all_labels = everywhere(labels)
    own = lax.axis_index(split) * slots + jnp.arange(slots, dtype=i32)
    mask = (
        (labels[:, None] == all_labels[None, :])
        & (labels[:, None] >= 0)
        & (own[:, None] != jnp.arange(members * slots, dtype=i32)[None, :])
    )
    scores = jnp.where(mask, scores, -1.0)
    best = jnp.maximum(-1.0, jnp.max(scores, axis=1))
    returned = lax.all_to_all(best, "x", split_axis=0, concat_axis=0, tiled=True)
    return returned[place]


def on_device(embeddings, cluster_ids):
    where = jnp.stack([lax.axis_index(a) for a in ("x", "z", "y", "c")]).astype(i32)
    shape = jax.ShapeDtypeStruct
    half = shape((ROWS + LABEL_ROWS, HALF_WIDTH), bf16)
    keep, send = pl.pallas_call(
        unit_kernel, out_shape=(half, half),
        in_specs=[SCALARS, WHOLE, WHOLE], out_specs=(WHOLE, WHOLE), compiler_params=params(12), name="unit",
    )(where, embeddings, cluster_ids.reshape(1, ROWS))
    got = lax.ppermute(send, "c", [(0, 1), (1, 0)])
    packed, code = pl.pallas_call(
        pack_kernel,
        out_shape=(shape((CHIPS, BLOCK, WIDTH), bf16), shape((8, ROWS), i32)),
        in_specs=[SCALARS, WHOLE, WHOLE], out_specs=(WHOLE, WHOLE), compiler_params=params(20), name="pack",
    )(where, keep, got)
    packed = lax.all_to_all(packed, ("x", "z", "y"), 0, 0, tiled=True)
    ordered, pos, meta = pl.pallas_call(
        sort_kernel,
        out_shape=(shape((SORTED, WIDTH), bf16), shape((CHIPS, LANES), i32), shape((8, LANES), f32)),
        in_specs=[SCALARS, WHOLE], out_specs=(WHOLE, WHOLE, WHOLE), compiler_params=params(28), name="sort",
    )(where, packed)

    def within_bins(embeddings, cluster_ids):
        other = lax.ppermute(ordered, "c", [(0, 1), (1, 0)])
        partial = pl.pallas_call(
            gram_kernel,
            out_shape=[shape((CHUNK, LANES), f32)] * 4,
            in_specs=[SCALARS, WHOLE, WHOLE, WHOLE], out_specs=[WHOLE] * 4,
            scratch_shapes=[pltpu.VMEM((4, CHUNK, LANES), f32)],
            compiler_params=params(20), name="gram",
        )(where, ordered, other, meta)
        arrived = [partial[0]] + [
            lax.ppermute(partial[s], "y", [(i, (i + s) % 4) for i in range(4)]) for s in (1, 2, 3)
        ]
        best = pl.pallas_call(
            max_kernel,
            out_shape=shape((CHIPS, LANES), f32),
            in_specs=[SCALARS] * 2 + [WHOLE] * 5, out_specs=WHOLE,
            scratch_shapes=[pltpu.VMEM((16, LANES), f32)],
            compiler_params=params(8), name="maxima",
        )(where, tables(), *arrived, pos)
        sent = jnp.broadcast_to(best[:, None, :], (CHIPS, 2, LANES)).reshape(2 * CHIPS, 1, LANES)
        back = lax.all_to_all(sent, ("x", "z", "y", "c"), 0, 0, tiled=True)
        return pl.pallas_call(
            pick_kernel,
            out_shape=shape((1, ROWS), f32),
            in_specs=[SCALARS, WHOLE, WHOLE], out_specs=WHOLE, compiler_params=params(8), name="pick",
        )(where, back.reshape(2 * CHIPS, LANES), code).reshape(ROWS)

    return lax.cond(meta[4, 0] < 0.5, within_bins, gather_groups, embeddings, cluster_ids)


def solution(mesh):
    axes = ("x", "z", "y", "c")
    grid = Mesh(mesh.devices.reshape(4, 4, 4, 2), axes)
    return jax.shard_map(
        on_device, mesh=grid, in_specs=(P(axes, None), P(axes)), out_specs=P(axes), check_vma=False
    )
```

```python
import jax
import jax.numpy as jnp
from jax import lax
from jax.experimental import pallas as pl
from jax.experimental.pallas import tpu as pltpu
from jax.sharding import Mesh, PartitionSpec as P

ROWS = 128
HALF_WIDTH = 2048
WIDTH = 512
LABEL_ROWS = 16
BINS = 16
CHIPS = 64
BLOCK = 40
SLOTS = BLOCK - 1
LANES = 128
CAPS = (704, 512, 320, 192)
STARTS = (0, 704, 1216, 1536)
HALF = 64
COUNT = 7
CHUNK = COUNT * HALF
PARTIAL = 4 * CHUNK
SHARES = (
    tuple((q, first) for q, first in ((0, 0), (0, 128), (2, 0), (2, 128), (2, 256))),
    tuple((q, first) for q, first in (
        (0, 256), (0, 384), (0, 512), (0, 640), (1, 0), (1, 128), (1, 256), (1, 384), (3, 0), (3, 128))),
)
BASES = ({0: 0, 2: 704}, {0: -256, 1: 448, 3: 960})
SHARE_ROWS = 1216
SEGMENTS = (
    (0, 256, 0, None), (256, 448, 256, 0), (704, 256, None, 448), (960, 256, None, 704),
    (1216, 320, 704, None), (1536, 192, None, 960),
)
f32, bf16, i32 = jnp.float32, jnp.bfloat16, jnp.int32
WHOLE = pl.BlockSpec(memory_space=pltpu.VMEM)
SCALARS = pl.BlockSpec(memory_space=pltpu.SMEM)


def params(mib):
    return pltpu.CompilerParams(vmem_limit_bytes=mib * 1024 * 1024)


def iota(shape, dim):
    return lax.broadcasted_iota(i32, shape, dim)


def dot_last(a, b):
    return lax.dot_general(a, b, (((1,), (1,)), ((), ())), preferred_element_type=f32)


def dot(a, b):
    return lax.dot_general(a, b, (((1,), (0,)), ((), ())), preferred_element_type=f32)


def as_bf16(mask):
    return jnp.where(mask, 1.0, 0.0).astype(bf16)


def bin_of(labels):
    rank, residue = labels >> 2, labels & 3
    row, col = rank >> 2, rank & 3
    col = jnp.where((row & 1) == 1, 3 - col, col)
    return 4 * col + ((row - residue) & 3)


def unit_kernel(where_ref, x_ref, ids_ref, keep_ref, send_ref):
    c = where_ref[3]
    x = x_ref[...]
    scale = lax.rsqrt(jnp.sum(x * x, axis=1, keepdims=True) + 1e-06)
    ids = jnp.concatenate([ids_ref[...].astype(f32), jnp.zeros((1, HALF_WIDTH - ROWS), f32)], axis=1)
    ids = jnp.broadcast_to(ids, (LABEL_ROWS, HALF_WIDTH)).astype(bf16)
    for half, out_ref in ((c, keep_ref), (1 - c, send_ref)):
        columns = pl.ds(pl.multiple_of(half * HALF_WIDTH, HALF_WIDTH), HALF_WIDTH)
        out_ref[:ROWS, :] = (x_ref[:, columns] * scale).astype(bf16)
        out_ref[ROWS:, :] = ids


def pack_kernel(where_ref, keep_ref, got_ref, out_ref, code_ref, block_ref, sems):
    first = where_ref[3] == 0
    kept = jnp.max(keep_ref[ROWS:, :ROWS].astype(f32), axis=0, keepdims=True)
    got = jnp.max(got_ref[ROWS:, :ROWS].astype(f32), axis=0, keepdims=True)
    labels = jnp.concatenate([jnp.where(first, kept, got), jnp.where(first, got, kept)], axis=0).astype(i32)
    bins = bin_of(labels)
    member = jnp.concatenate([jnp.where(bins == b, 1.0, 0.0) for b in range(BINS)], axis=0)
    member16 = member.astype(bf16)
    along = dot(member16, as_bf16(iota((ROWS, ROWS), 0) < iota((ROWS, ROWS), 1)))
    row, col = iota((2 * BINS, 2 * BINS), 0), iota((2 * BINS, 2 * BINS), 1)
    earlier = dot(as_bf16(((row >> 1) == (col >> 1)) & (col < row)), member16)
    ranks = member * (along + jnp.sum(earlier, axis=1, keepdims=True))
    rank = sum(ranks[2 * b:2 * b + 2] for b in range(BINS)).astype(i32)
    code = jnp.where(rank < SLOTS, bins * BLOCK + rank, -1)
    code_ref[...] = jnp.concatenate([code] * 4, axis=0)
    docs = 2 * ROWS
    flat = lambda v: jnp.concatenate([v[:1], v[1:]], axis=1)
    rank_row, bin_row, label_row = flat(rank), flat(bins), flat(labels)
    counts = dot_last(jnp.ones((8, docs), bf16), as_bf16(iota((LANES, docs), 0) == label_row))[:1]
    named = jnp.where(iota((BINS, docs), 0) == bin_row, (label_row + 1).astype(f32), 0.0).astype(bf16)
    names = dot_last(named, as_bf16((iota((LANES, docs), 0) == rank_row) & (rank_row < SLOTS)))
    own = jnp.where(first, code[:1], code[1:])
    other = jnp.where(first, code[1:], code[:1])
    onehot = as_bf16(iota((BINS * BLOCK, docs), 0) == jnp.concatenate([own, other], axis=1))
    is_last = iota((BLOCK, WIDTH), 0) == SLOTS
    for y in range(4):
        columns = slice(y * WIDTH, (y + 1) * WIDTH)
        x = jnp.concatenate([keep_ref[:ROWS, columns], got_ref[:ROWS, columns]], axis=0)
        packed = dot(onehot, x)
        for b in range(BINS):
            extra = jnp.concatenate([names[b:b + 1], counts, jnp.zeros((1, 2 * LANES), f32)], axis=1)
            block_ref[y, b] = jnp.where(is_last, extra, packed[b * BLOCK:(b + 1) * BLOCK]).astype(bf16)
        pltpu.make_async_copy(block_ref.at[y], out_ref.at[:, y], sems.at[y]).start()
    for y in range(4):
        pltpu.make_async_copy(block_ref.at[y], out_ref.at[:, y], sems.at[y]).wait()


def sort_kernel(where_ref, x_ref, mine_ref, send_ref, pos_ref, meta_ref):
    mine = where_ref[0] * 4 + where_ref[1]
    tail = x_ref[:, BLOCK - 8:, :2 * LANES].astype(f32)
    tail = jnp.max(jnp.where(iota(tail.shape, 1) == 7, tail, 0.0), axis=1)
    labels, chip_counts = tail[:, :LANES].astype(i32) - 1, tail[:, LANES:].astype(bf16)
    row, col = iota((LANES, LANES), 0), iota((LANES, LANES), 1)
    in_bin = (bin_of(row) == col) & (row < 4 * BINS)
    sizes, total = [], 0.0
    for r in range(4):
        counts = dot(chip_counts, as_bf16(in_bin & ((row & 3) == r)))
        total = total + counts
        sizes.append(jnp.sum(counts, axis=0, keepdims=True))
    a, b = jnp.maximum(sizes[0], sizes[1]), jnp.minimum(sizes[0], sizes[1])
    c, d = jnp.maximum(sizes[2], sizes[3]), jnp.minimum(sizes[2], sizes[3])
    first, e = jnp.maximum(a, c), jnp.minimum(a, c)
    g, fourth = jnp.maximum(b, d), jnp.minimum(b, d)
    ordered = (first, jnp.maximum(e, g), jnp.minimum(e, g), fourth)
    over = jnp.max(jnp.where(total > SLOTS, 1.0, 0.0), axis=0, keepdims=True)
    for size, cap in zip(ordered, CAPS):
        over = jnp.maximum(over, jnp.where(size > cap, 1.0, 0.0))
    for share in SHARES:
        length = sum(jnp.maximum(jnp.floor((ordered[q] + 63.0) * (1 / 64)) - first // HALF, 0.0) for q, first in share)
        over = jnp.maximum(over, jnp.where(length > 4 * COUNT, 1.0, 0.0))
    over = jnp.max(over, axis=1, keepdims=True)
    here = iota((1, LANES), 1) == mine
    own = lambda v: jnp.sum(jnp.where(here, v, 0.0), axis=1, keepdims=True)
    wide = lambda v: jnp.broadcast_to(v, (1, LANES))
    meta_ref[...] = jnp.concatenate([wide(own(v)) for v in ordered] + [wide(over)] * 4, axis=0).astype(i32)

    n = [own(v) for v in sizes]
    valid = (labels >= 0) & (iota(labels.shape, 1) < SLOTS)
    upper = as_bf16(row < col)
    lower = as_bf16(iota((CHIPS, CHIPS), 1) < iota((CHIPS, CHIPS), 0))
    pos = jnp.full(labels.shape, -1.0, f32)
    for r in range(4):
        place = sum(
            jnp.where((n[q] > n[r]) | ((n[q] == n[r]) & (q < r)), 1.0, 0.0) for q in range(4) if q != r
        )
        start = jnp.where(
            place < 0.5, float(STARTS[0]),
            jnp.where(place < 1.5, float(STARTS[1]), jnp.where(place < 2.5, float(STARTS[2]), float(STARTS[3]))),
        )
        member = valid & ((labels & 3) == r)
        member16 = as_bf16(member)
        rank = dot(member16, upper) + jnp.sum(dot(lower, member16), axis=1, keepdims=True)
        pos = jnp.where(member, start + rank, pos)
    pos_ref[...] = pos.astype(i32)
    per, groups = 16, CHIPS // 16
    plus = jnp.where(iota(pos.shape, 1) < BLOCK, pos + 1.0, 0.0)
    lined = jnp.zeros((8, per * BLOCK), f32)
    for t in range(per):
        rows = jnp.concatenate([plus[per * g + t:per * g + t + 1] for g in range(groups)] * 2, axis=0)
        rows = jnp.concatenate([rows, jnp.zeros((8, per * BLOCK - LANES), f32)], axis=1)
        lined = lined + (pltpu.roll(rows, t * BLOCK, 1) if t else rows)
    pos_row = jnp.concatenate([lined[g:g + 1] for g in range(groups)], axis=1).astype(i32) - 1
    x = x_ref[...].reshape(CHIPS * BLOCK, WIDTH)
    core = where_ref[3]
    for first, rows, *offsets in SEGMENTS:
        onehot = as_bf16(iota((rows, CHIPS * BLOCK), 0) + first == pos_row)
        part = dot(onehot, x).astype(bf16)
        for me in range(2):
            @pl.when(core == me)
            def _():
                for share, at in enumerate(offsets):
                    if at is not None:
                        (mine_ref if share == me else send_ref)[at:at + rows, :] = part


def blocks_of(core):
    for q, first in SHARES[core]:
        at = BASES[core][q] + first
        yield q, first, pl.ds(at, CAPS[q] - first), pl.ds(at, LANES)


RAW_ROWS = max(sum(CAPS[q] - first for q, first in share) for share in SHARES)


def own_kernel(where_ref, x_ref, raw_ref):
    for core in range(2):
        @pl.when(where_ref[3] == core)
        def _():
            at = 0
            for q, first, left, right in blocks_of(core):
                rows = CAPS[q] - first
                raw_ref[at:at + rows, :] = dot_last(x_ref[left, :], x_ref[right, :])
                at += rows


def length_of(size, first):
    return jnp.maximum(((size + HALF - 1) >> 6) - first // HALF, 0)


def gram_kernel(where_ref, meta_ref, x_ref, raw_ref, out0, out1, out2, out3, part_ref):
    y, c = where_ref[2], where_ref[3]
    part_ref[...] = jnp.full(part_ref.shape, -4.0, f32)
    for core in range(2):
        @pl.when(c == core)
        def _():
            at, to = 0, jnp.zeros((), i32)
            for q, first, left, right in blocks_of(core):
                rows = CAPS[q] - first
                score = raw_ref[at:at + rows, :] + dot_last(x_ref[left, :], x_ref[right, :])
                at += rows
                size = meta_ref[q, 0]
                i, j = iota(score.shape, 0), iota(score.shape, 1)
                keep = (i < size - first) & (j < size - first) & (i != j)
                part_ref[pl.ds(pl.multiple_of(to, HALF), rows), :] = jnp.where(keep, score, -4.0)
                to = jnp.minimum(to + HALF * length_of(size, first), PARTIAL)
    for shift, out in enumerate((out0, out1, out2, out3)):
        out[...] = part_ref[pl.ds(pl.multiple_of(lax.rem(y + shift, 4) * CHUNK, HALF), CHUNK), :]


FIRST_ROW = (0, 6, 10, 13)


def max_kernel(where_ref, meta_ref, p0, p1, p2, p3, pos_ref, out_ref, best_ref):
    y, c = where_ref[2], where_ref[3]
    best_ref[...] = jnp.full(best_ref.shape, -1.0, f32)
    sub, lane = iota((HALF, LANES), 0), iota((HALF, LANES), 1)
    blocks = []
    for core, share in enumerate(SHARES):
        at = jnp.zeros((), i32)
        for q, first in share:
            length = length_of(meta_ref[q, 0], first)
            col = FIRST_ROW[q] + first // LANES
            blocks.append((jnp.where((c == core) & (length > 0), at, PARTIAL), col, 2 * col - at))
            at = at + length
    for t in range(COUNT):
        at = slice(t * HALF, (t + 1) * HALF)
        block = (p0[at, :] + p1[at, :]) + (p2[at, :] + p3[at, :])
        index = y * COUNT + t
        col, shift = jnp.asarray(15, i32), jnp.asarray(0, i32)
        for start, block_col, block_shift in blocks:
            inside = index >= start
            col, shift = jnp.where(inside, block_col, col), jnp.where(inside, block_shift, shift)
        row = jnp.minimum(jnp.maximum(index + shift, 0), 31)
        along = jnp.max(block, axis=1, keepdims=True)
        along = jnp.max(jnp.where(sub + (row & 1) * HALF == lane, along, -1.0), axis=0, keepdims=True)
        row = row >> 1
        best_ref[pl.ds(row, 1), :] = jnp.maximum(best_ref[pl.ds(row, 1), :], along)
        down = jnp.max(block, axis=0, keepdims=True)
        best_ref[pl.ds(col, 1), :] = jnp.maximum(best_ref[pl.ds(col, 1), :], down)
    pos = pos_ref[...]
    pos = jnp.where(pos >= STARTS[1], pos + HALF, pos)
    pos = jnp.where(pos >= STARTS[3] + HALF, pos + HALF, pos)
    row, lane = pos >> 7, pos & (LANES - 1)
    out = jnp.full(pos.shape, -1.0, f32)
    for r in range(15):
        value = jnp.broadcast_to(best_ref[r:r + 1, :], pos.shape)
        value = jnp.take_along_axis(value, lane, axis=1, mode="promise_in_bounds")
        out = jnp.where(row == r, value, out)
    out_ref[...] = out


def pick_kernel(where_ref, v_ref, code_ref, out_ref):
    c = where_ref[3]
    values = jnp.max(v_ref[...].reshape(BINS, 8, LANES), axis=1)
    eye = iota((LANES, LANES), 0) == iota((LANES, LANES), 1)
    code = jnp.max(jnp.where(iota((8, ROWS), 0) == c, code_ref[...], -1), axis=0, keepdims=True)
    code = jnp.max(jnp.where(eye, code.astype(f32), -1.0), axis=1, keepdims=True).astype(i32)
    slot = iota((ROWS, LANES), 1)
    best = jnp.full((ROWS, LANES), -1.0, f32)
    for b in range(BINS):
        best = jnp.where((slot + b * BLOCK == code) & (slot < BLOCK), values[b:b + 1], best)
    best = jnp.max(best, axis=1, keepdims=True)
    out_ref[...] = jnp.max(jnp.where(eye, best, -1.0), axis=0, keepdims=True)


def gather_groups(embeddings, cluster_ids):
    split = ("z", "y", "c")
    rows = embeddings.shape[0]
    groups = lax.axis_size("x")
    cap = 2 * rows // groups
    slots = groups * cap
    owner_of = cluster_ids % groups
    onehot = (owner_of[:, None] == jnp.arange(groups, dtype=i32)[None, :]).astype(i32)
    before = jnp.cumsum(onehot, axis=0) - onehot
    rank = jnp.sum(before * onehot, axis=1)
    place = owner_of * cap + rank
    picked = place[None, :] == jnp.arange(slots, dtype=i32)[:, None]
    filled = jnp.any(picked, axis=1)
    source = jnp.sum(jnp.where(picked, jnp.arange(rows, dtype=i32)[None, :], 0), axis=1)
    out_labels = jnp.where(filled, cluster_ids[source], -1)
    squares = jnp.sum(embeddings * embeddings, axis=1, keepdims=True)
    local_unit = (embeddings * lax.rsqrt(squares + 1e-06)).astype(bf16)
    outgoing_unit = jnp.where(filled[:, None], local_unit[source], jnp.zeros((), bf16))
    unit = lax.all_to_all(outgoing_unit, "x", split_axis=0, concat_axis=0, tiled=True)
    labels = lax.all_to_all(out_labels, "x", split_axis=0, concat_axis=0, tiled=True)
    members = lax.axis_size(split)

    def everywhere(v):
        copies = jnp.broadcast_to(v[None], (members,) + v.shape).reshape((members * slots,) + v.shape[1:])
        return lax.all_to_all(copies, split, split_axis=0, concat_axis=0, tiled=True)

    def add_slice(i, scores):
        part = lax.dynamic_slice_in_dim(unit, i * WIDTH, WIDTH, 1)
        return scores + dot_last(part, everywhere(part))

    scores = lax.fori_loop(0, embeddings.shape[1] // WIDTH, add_slice, jnp.zeros((slots, members * slots), f32))
    all_labels = everywhere(labels)
    own = lax.axis_index(split) * slots + jnp.arange(slots, dtype=i32)
    mask = (
        (labels[:, None] == all_labels[None, :])
        & (labels[:, None] >= 0)
        & (own[:, None] != jnp.arange(members * slots, dtype=i32)[None, :])
    )
    scores = jnp.where(mask, scores, -1.0)
    best = jnp.maximum(-1.0, jnp.max(scores, axis=1))
    returned = lax.all_to_all(best, "x", split_axis=0, concat_axis=0, tiled=True)
    return returned[place]


def on_device(embeddings, cluster_ids):
    where = jnp.stack([lax.axis_index(a) for a in ("x", "z", "y", "c")]).astype(i32)
    shape = jax.ShapeDtypeStruct
    half = shape((ROWS + LABEL_ROWS, HALF_WIDTH), bf16)
    keep, send = pl.pallas_call(
        unit_kernel, out_shape=(half, half),
        in_specs=[SCALARS, WHOLE, WHOLE], out_specs=(WHOLE, WHOLE), compiler_params=params(12), name="unit",
    )(where, embeddings, cluster_ids.reshape(1, ROWS))
    got = lax.ppermute(send, "c", [(0, 1), (1, 0)])
    packed, code = pl.pallas_call(
        pack_kernel,
        out_shape=(shape((BINS, 4, BLOCK, WIDTH), bf16), shape((8, ROWS), i32)),
        in_specs=[SCALARS, WHOLE, WHOLE], out_specs=(pl.BlockSpec(memory_space=pltpu.HBM), WHOLE),
        scratch_shapes=[pltpu.VMEM((4, BINS, BLOCK, WIDTH), bf16), pltpu.SemaphoreType.DMA((4,))],
        compiler_params=params(20), name="pack",
    )(where, keep, got)
    packed = lax.all_to_all(packed.reshape(CHIPS, BLOCK, WIDTH), ("x", "z", "y"), 0, 0, tiled=True)
    mine, send, pos, meta = pl.pallas_call(
        sort_kernel,
        out_shape=(
            shape((SHARE_ROWS, WIDTH), bf16), shape((SHARE_ROWS, WIDTH), bf16),
            shape((CHIPS, LANES), i32), shape((8, LANES), i32),
        ),
        in_specs=[SCALARS, WHOLE], out_specs=(WHOLE,) * 4, compiler_params=params(28), name="sort",
    )(where, packed)
    other = lax.ppermute(send, "c", [(0, 1), (1, 0)])
    raw = pl.pallas_call(
        own_kernel, out_shape=shape((RAW_ROWS, LANES), f32),
        in_specs=[SCALARS, WHOLE], out_specs=WHOLE, compiler_params=params(12), name="own",
        cost_estimate=pl.CostEstimate(flops=2 * RAW_ROWS * LANES * WIDTH, bytes_accessed=3 << 20, transcendentals=0),
    )(where, mine)
    partial = pl.pallas_call(
        gram_kernel,
        out_shape=[shape((CHUNK, LANES), f32)] * 4,
        in_specs=[SCALARS, SCALARS, WHOLE, WHOLE], out_specs=[WHOLE] * 4,
        scratch_shapes=[pltpu.VMEM((PARTIAL + CAPS[0], LANES), f32)],
        compiler_params=params(16), name="gram",
    )(where, meta, other, raw)
    arrived = [partial[0]] + [
        lax.ppermute(partial[s], "y", [(i, (i + s) % 4) for i in range(4)]) for s in (1, 2, 3)
    ]
    best = pl.pallas_call(
        max_kernel,
        out_shape=shape((CHIPS, LANES), f32),
        in_specs=[SCALARS] * 2 + [WHOLE] * 5, out_specs=WHOLE,
        scratch_shapes=[pltpu.VMEM((16, LANES), f32)],
        compiler_params=params(8), name="maxima",
    )(where, meta, *arrived, pos)
    sent = jnp.broadcast_to(best[:, None, :], (CHIPS, 2, LANES)).reshape(2 * CHIPS, 1, LANES)
    back = lax.all_to_all(sent, ("x", "z", "y", "c"), 0, 0, tiled=True)
    fitted = pl.pallas_call(
        pick_kernel,
        out_shape=shape((1, ROWS), f32),
        in_specs=[SCALARS, WHOLE, WHOLE], out_specs=WHOLE, compiler_params=params(8), name="pick",
    )(where, back.reshape(2 * CHIPS, LANES), code).reshape(ROWS)
    return lax.cond(
        meta[4, 0] == 0,
        lambda fitted, embeddings, cluster_ids: fitted,
        lambda fitted, embeddings, cluster_ids: gather_groups(embeddings, cluster_ids),
        fitted, embeddings, cluster_ids,
    )


def solution(mesh):
    axes = ("x", "z", "y", "c")
    grid = Mesh(mesh.devices.reshape(4, 4, 4, 2), axes)
    return jax.shard_map(
        on_device, mesh=grid, in_specs=(P(axes, None), P(axes)), out_specs=P(axes), check_vma=False
    )
```

```python
import jax
import jax.numpy as jnp
from jax import lax
from jax.experimental import pallas as pl
from jax.experimental.pallas import tpu as pltpu
from jax.sharding import Mesh, PartitionSpec as P

ROWS = 128
HALF_WIDTH = 2048
WIDTH = 512
LABEL_ROWS = 16
BINS = 16
CHIPS = 64
BLOCK = 40
SLOTS = BLOCK - 1
LANES = 128
CAPS = (704, 512, 320, 192)
STARTS = (0, 704, 1216, 1536)
HALF = 64
COUNT = 7
CHUNK = COUNT * HALF
PARTIAL = 4 * CHUNK
SHARES = (
    tuple((q, first) for q, first in ((0, 0), (0, 128), (2, 0), (2, 128), (2, 256))),
    tuple((q, first) for q, first in (
        (0, 256), (0, 384), (0, 512), (0, 640), (1, 0), (1, 128), (1, 256), (1, 384), (3, 0), (3, 128))),
)
BASES = ({0: 0, 2: 704}, {0: -256, 1: 448, 3: 960})
SHARE_ROWS = 1216
SEGMENTS = (
    (0, 256, 0, None), (256, 448, 256, 0), (704, 256, None, 448), (960, 256, None, 704),
    (1216, 320, 704, None), (1536, 192, None, 960),
)
f32, bf16, i32 = jnp.float32, jnp.bfloat16, jnp.int32
WHOLE = pl.BlockSpec(memory_space=pltpu.VMEM)
SCALARS = pl.BlockSpec(memory_space=pltpu.SMEM)


def params(mib):
    return pltpu.CompilerParams(vmem_limit_bytes=mib * 1024 * 1024)


def iota(shape, dim):
    return lax.broadcasted_iota(i32, shape, dim)


def dot_last(a, b):
    return lax.dot_general(a, b, (((1,), (1,)), ((), ())), preferred_element_type=f32)


def dot(a, b):
    return lax.dot_general(a, b, (((1,), (0,)), ((), ())), preferred_element_type=f32)


def as_bf16(mask):
    return jnp.where(mask, 1.0, 0.0).astype(bf16)


def bin_of(labels):
    rank, residue = labels >> 2, labels & 3
    row, col = rank >> 2, rank & 3
    col = jnp.where((row & 1) == 1, 3 - col, col)
    return 4 * col + ((row - residue) & 3)


PIECE = 32


def unit_kernel(where_ref, x_ref, ids_ref, keep_ref, send_ref, rows_ref, sems):
    c = where_ref[3]
    copies = [
        pltpu.make_async_copy(x_ref.at[pl.ds(at, PIECE)], rows_ref.at[pl.ds(at, PIECE)], sems.at[at // PIECE])
        for at in range(0, ROWS, PIECE)
    ]
    for copy in copies:
        copy.start()
    ids = jnp.concatenate([ids_ref[...].astype(f32), jnp.zeros((1, HALF_WIDTH - ROWS), f32)], axis=1)
    ids = jnp.broadcast_to(ids, (LABEL_ROWS, HALF_WIDTH)).astype(bf16)
    keep_ref[ROWS:, :] = ids
    send_ref[ROWS:, :] = ids
    for piece, copy in enumerate(copies):
        at = slice(piece * PIECE, (piece + 1) * PIECE)
        copy.wait()
        x = rows_ref[at, :]
        scale = lax.rsqrt(jnp.sum(x * x, axis=1, keepdims=True) + 1e-06)
        for half, out_ref in ((c, keep_ref), (1 - c, send_ref)):
            columns = pl.ds(pl.multiple_of(half * HALF_WIDTH, HALF_WIDTH), HALF_WIDTH)
            out_ref[at, :] = (rows_ref[at, columns] * scale).astype(bf16)


def pack_kernel(where_ref, keep_ref, got_ref, out_ref, code_ref):
    first = where_ref[3] == 0
    kept = jnp.max(keep_ref[ROWS:, :ROWS].astype(f32), axis=0, keepdims=True)
    got = jnp.max(got_ref[ROWS:, :ROWS].astype(f32), axis=0, keepdims=True)
    labels = jnp.concatenate([jnp.where(first, kept, got), jnp.where(first, got, kept)], axis=0).astype(i32)
    bins = bin_of(labels)
    member = jnp.concatenate([jnp.where(bins == b, 1.0, 0.0) for b in range(BINS)], axis=0)
    member16 = member.astype(bf16)
    along = dot(member16, as_bf16(iota((ROWS, ROWS), 0) < iota((ROWS, ROWS), 1)))
    row, col = iota((2 * BINS, 2 * BINS), 0), iota((2 * BINS, 2 * BINS), 1)
    earlier = dot(as_bf16(((row >> 1) == (col >> 1)) & (col < row)), member16)
    ranks = member * (along + jnp.sum(earlier, axis=1, keepdims=True))
    rank = sum(ranks[2 * b:2 * b + 2] for b in range(BINS)).astype(i32)
    code = jnp.where(rank < SLOTS, bins * BLOCK + rank, -1)
    code_ref[...] = jnp.concatenate([code] * 4, axis=0)
    docs = 2 * ROWS
    flat = lambda v: jnp.concatenate([v[:1], v[1:]], axis=1)
    rank_row, bin_row, label_row = flat(rank), flat(bins), flat(labels)
    counts = dot_last(jnp.ones((8, docs), bf16), as_bf16(iota((LANES, docs), 0) == label_row))[:1]
    named = jnp.where(iota((BINS, docs), 0) == bin_row, (label_row + 1).astype(f32), 0.0).astype(bf16)
    names = dot_last(named, as_bf16((iota((LANES, docs), 0) == rank_row) & (rank_row < SLOTS)))
    own = jnp.where(first, code[:1], code[1:])
    other = jnp.where(first, code[1:], code[:1])
    onehot = as_bf16(iota((BINS * BLOCK, docs), 0) == jnp.concatenate([own, other], axis=1))
    is_last = iota((BLOCK, WIDTH), 0) == SLOTS
    for y in range(4):
        columns = slice(y * WIDTH, (y + 1) * WIDTH)
        x = jnp.concatenate([keep_ref[:ROWS, columns], got_ref[:ROWS, columns]], axis=0)
        packed = dot(onehot, x)
        for b in range(BINS):
            extra = jnp.concatenate([names[b:b + 1], counts, jnp.zeros((1, 2 * LANES), f32)], axis=1)
            out_ref[4 * b + y] = jnp.where(is_last, extra, packed[b * BLOCK:(b + 1) * BLOCK]).astype(bf16)


def send_kernel(where_ref, x_ref, send_ref, line_ref, pos_ref, meta_ref):
    mine = where_ref[0] * 4 + where_ref[1]
    tail = x_ref[:, BLOCK - 8:, :2 * LANES].astype(f32)
    tail = jnp.max(jnp.where(iota(tail.shape, 1) == 7, tail, 0.0), axis=1)
    labels, chip_counts = tail[:, :LANES].astype(i32) - 1, tail[:, LANES:].astype(bf16)
    row, col = iota((LANES, LANES), 0), iota((LANES, LANES), 1)
    in_bin = (bin_of(row) == col) & (row < 4 * BINS)
    sizes, total = [], 0.0
    for r in range(4):
        counts = dot(chip_counts, as_bf16(in_bin & ((row & 3) == r)))
        total = total + counts
        sizes.append(jnp.sum(counts, axis=0, keepdims=True))
    a, b = jnp.maximum(sizes[0], sizes[1]), jnp.minimum(sizes[0], sizes[1])
    c, d = jnp.maximum(sizes[2], sizes[3]), jnp.minimum(sizes[2], sizes[3])
    first, e = jnp.maximum(a, c), jnp.minimum(a, c)
    g, fourth = jnp.maximum(b, d), jnp.minimum(b, d)
    ordered = (first, jnp.maximum(e, g), jnp.minimum(e, g), fourth)
    over = jnp.max(jnp.where(total > SLOTS, 1.0, 0.0), axis=0, keepdims=True)
    for size, cap in zip(ordered, CAPS):
        over = jnp.maximum(over, jnp.where(size > cap, 1.0, 0.0))
    for share in SHARES:
        length = sum(jnp.maximum(jnp.floor((ordered[q] + 63.0) * (1 / 64)) - first // HALF, 0.0) for q, first in share)
        over = jnp.maximum(over, jnp.where(length > 4 * COUNT, 1.0, 0.0))
    over = jnp.max(over, axis=1, keepdims=True)
    here = iota((1, LANES), 1) == mine
    own = lambda v: jnp.sum(jnp.where(here, v, 0.0), axis=1, keepdims=True)
    wide = lambda v: jnp.broadcast_to(v, (1, LANES))
    meta_ref[...] = jnp.concatenate([wide(own(v)) for v in ordered] + [wide(over)] * 4, axis=0).astype(i32)

    n = [own(v) for v in sizes]
    valid = (labels >= 0) & (iota(labels.shape, 1) < SLOTS)
    upper = as_bf16(row < col)
    lower = as_bf16(iota((CHIPS, CHIPS), 1) < iota((CHIPS, CHIPS), 0))
    pos = jnp.full(labels.shape, -1.0, f32)
    for r in range(4):
        place = sum(
            jnp.where((n[q] > n[r]) | ((n[q] == n[r]) & (q < r)), 1.0, 0.0) for q in range(4) if q != r
        )
        start = jnp.where(
            place < 0.5, float(STARTS[0]),
            jnp.where(place < 1.5, float(STARTS[1]), jnp.where(place < 2.5, float(STARTS[2]), float(STARTS[3]))),
        )
        member = valid & ((labels & 3) == r)
        member16 = as_bf16(member)
        rank = dot(member16, upper) + jnp.sum(dot(lower, member16), axis=1, keepdims=True)
        pos = jnp.where(member, start + rank, pos)
    pos_ref[...] = pos.astype(i32)
    per, groups = 16, CHIPS // 16
    plus = jnp.where(iota(pos.shape, 1) < BLOCK, pos + 1.0, 0.0)
    lined = jnp.zeros((8, per * BLOCK), f32)
    for t in range(per):
        rows = jnp.concatenate([plus[per * g + t:per * g + t + 1] for g in range(groups)] * 2, axis=0)
        rows = jnp.concatenate([rows, jnp.zeros((8, per * BLOCK - LANES), f32)], axis=1)
        lined = lined + (pltpu.roll(rows, t * BLOCK, 1) if t else rows)
    pos_row = jnp.concatenate([lined[g:g + 1] for g in range(groups)], axis=1).astype(i32) - 1
    line_ref[...] = jnp.broadcast_to(pos_row, line_ref.shape)
    x = x_ref[...].reshape(CHIPS * BLOCK, WIDTH)
    for me in range(2):
        @pl.when(where_ref[3] == me)
        def _():
            for segment in SEGMENTS:
                at = segment[2 + 1 - me]
                if at is not None:
                    send_ref[at:at + segment[1], :] = sorted_rows(segment, pos_row, x)


def sorted_rows(segment, pos_row, x):
    onehot = as_bf16(iota((segment[1], CHIPS * BLOCK), 0) + segment[0] == pos_row)
    return dot(onehot, x).astype(bf16)


def blocks_of(core):
    for q, first in SHARES[core]:
        at = BASES[core][q] + first
        yield q, first, pl.ds(at, CAPS[q] - first), pl.ds(at, LANES)


RAW_ROWS = max(sum(CAPS[q] - first for q, first in share) for share in SHARES)


def own_kernel(where_ref, x_ref, line_ref, send_ref, raw_ref, mine_ref):
    x = x_ref[...].reshape(CHIPS * BLOCK, WIDTH)
    pos_row = line_ref[:1, :]
    for core in range(2):
        @pl.when(where_ref[3] == core)
        def _():
            for segment in SEGMENTS:
                at, sent = segment[2 + core], segment[2 + 1 - core]
                if at is not None:
                    rows = segment[1]
                    both = sent is not None
                    mine_ref[at:at + rows, :] = (
                        send_ref[sent:sent + rows, :] if both else sorted_rows(segment, pos_row, x)
                    )
            at = 0
            for q, first, left, right in blocks_of(core):
                rows = CAPS[q] - first
                raw_ref[at:at + rows, :] = dot_last(mine_ref[left, :], mine_ref[right, :])
                at += rows


def length_of(size, first):
    return jnp.maximum(((size + HALF - 1) >> 6) - first // HALF, 0)


def gram_kernel(where_ref, meta_ref, x_ref, raw_ref, out0, out1, out2, out3, part_ref):
    y, c = where_ref[2], where_ref[3]
    part_ref[...] = jnp.full(part_ref.shape, -4.0, f32)
    for core in range(2):
        @pl.when(c == core)
        def _():
            at, to = 0, jnp.zeros((), i32)
            for q, first, left, right in blocks_of(core):
                rows = CAPS[q] - first
                score = raw_ref[at:at + rows, :] + dot_last(x_ref[left, :], x_ref[right, :])
                at += rows
                size = meta_ref[q, 0]
                i, j = iota(score.shape, 0), iota(score.shape, 1)
                keep = (i < size - first) & (j < size - first) & (i != j)
                part_ref[pl.ds(pl.multiple_of(to, HALF), rows), :] = jnp.where(keep, score, -4.0)
                to = jnp.minimum(to + HALF * length_of(size, first), PARTIAL)
    for shift, out in enumerate((out0, out1, out2, out3)):
        out[...] = part_ref[pl.ds(pl.multiple_of(lax.rem(y + shift, 4) * CHUNK, HALF), CHUNK), :]


FIRST_ROW = (0, 6, 10, 13)


def max_kernel(where_ref, meta_ref, p0, p1, p2, p3, pos_ref, out_ref, best_ref):
    y, c = where_ref[2], where_ref[3]
    best_ref[...] = jnp.full(best_ref.shape, -1.0, f32)
    sub, lane = iota((HALF, LANES), 0), iota((HALF, LANES), 1)
    blocks = []
    for core, share in enumerate(SHARES):
        at = jnp.zeros((), i32)
        for q, first in share:
            length = length_of(meta_ref[q, 0], first)
            col = FIRST_ROW[q] + first // LANES
            blocks.append((jnp.where((c == core) & (length > 0), at, PARTIAL), col, 2 * col - at))
            at = at + length
    for t in range(COUNT):
        at = slice(t * HALF, (t + 1) * HALF)
        block = (p0[at, :] + p1[at, :]) + (p2[at, :] + p3[at, :])
        index = y * COUNT + t
        col, shift = jnp.asarray(15, i32), jnp.asarray(0, i32)
        for start, block_col, block_shift in blocks:
            inside = index >= start
            col, shift = jnp.where(inside, block_col, col), jnp.where(inside, block_shift, shift)
        row = jnp.minimum(jnp.maximum(index + shift, 0), 31)
        along = jnp.max(block, axis=1, keepdims=True)
        along = jnp.max(jnp.where(sub + (row & 1) * HALF == lane, along, -1.0), axis=0, keepdims=True)
        row = row >> 1
        best_ref[pl.ds(row, 1), :] = jnp.maximum(best_ref[pl.ds(row, 1), :], along)
        down = jnp.max(block, axis=0, keepdims=True)
        best_ref[pl.ds(col, 1), :] = jnp.maximum(best_ref[pl.ds(col, 1), :], down)
    pos = pos_ref[...]
    pos = jnp.where(pos >= STARTS[1], pos + HALF, pos)
    pos = jnp.where(pos >= STARTS[3] + HALF, pos + HALF, pos)
    row, lane = pos >> 7, pos & (LANES - 1)
    out = jnp.full(pos.shape, -1.0, f32)
    for r in range(15):
        value = jnp.broadcast_to(best_ref[r:r + 1, :], pos.shape)
        value = jnp.take_along_axis(value, lane, axis=1, mode="promise_in_bounds")
        out = jnp.where(row == r, value, out)
    for s in range(CHIPS):
        out_ref[2 * s] = out[s:s + 1]
        out_ref[2 * s + 1] = out[s:s + 1]


def pick_kernel(where_ref, v_ref, code_ref, out_ref):
    c = where_ref[3]
    values = jnp.max(v_ref[...].reshape(BINS, 8, LANES), axis=1)
    eye = iota((LANES, LANES), 0) == iota((LANES, LANES), 1)
    code = jnp.max(jnp.where(iota((8, ROWS), 0) == c, code_ref[...], -1), axis=0, keepdims=True)
    code = jnp.max(jnp.where(eye, code.astype(f32), -1.0), axis=1, keepdims=True).astype(i32)
    slot = iota((ROWS, LANES), 1)
    best = jnp.full((ROWS, LANES), -1.0, f32)
    for b in range(BINS):
        best = jnp.where((slot + b * BLOCK == code) & (slot < BLOCK), values[b:b + 1], best)
    best = jnp.max(best, axis=1, keepdims=True)
    out_ref[...] = jnp.max(jnp.where(eye, best, -1.0), axis=0, keepdims=True)


def gather_groups(embeddings, cluster_ids):
    split = ("z", "y", "c")
    rows = embeddings.shape[0]
    groups = lax.axis_size("x")
    cap = 2 * rows // groups
    slots = groups * cap
    owner_of = cluster_ids % groups
    onehot = (owner_of[:, None] == jnp.arange(groups, dtype=i32)[None, :]).astype(i32)
    before = jnp.cumsum(onehot, axis=0) - onehot
    rank = jnp.sum(before * onehot, axis=1)
    place = owner_of * cap + rank
    picked = place[None, :] == jnp.arange(slots, dtype=i32)[:, None]
    filled = jnp.any(picked, axis=1)
    source = jnp.sum(jnp.where(picked, jnp.arange(rows, dtype=i32)[None, :], 0), axis=1)
    out_labels = jnp.where(filled, cluster_ids[source], -1)
    squares = jnp.sum(embeddings * embeddings, axis=1, keepdims=True)
    local_unit = (embeddings * lax.rsqrt(squares + 1e-06)).astype(bf16)
    outgoing_unit = jnp.where(filled[:, None], local_unit[source], jnp.zeros((), bf16))
    unit = lax.all_to_all(outgoing_unit, "x", split_axis=0, concat_axis=0, tiled=True)
    labels = lax.all_to_all(out_labels, "x", split_axis=0, concat_axis=0, tiled=True)
    members = lax.axis_size(split)

    def everywhere(v):
        copies = jnp.broadcast_to(v[None], (members,) + v.shape).reshape((members * slots,) + v.shape[1:])
        return lax.all_to_all(copies, split, split_axis=0, concat_axis=0, tiled=True)

    def add_slice(i, scores):
        part = lax.dynamic_slice_in_dim(unit, i * WIDTH, WIDTH, 1)
        return scores + dot_last(part, everywhere(part))

    scores = lax.fori_loop(0, embeddings.shape[1] // WIDTH, add_slice, jnp.zeros((slots, members * slots), f32))
    all_labels = everywhere(labels)
    own = lax.axis_index(split) * slots + jnp.arange(slots, dtype=i32)
    mask = (
        (labels[:, None] == all_labels[None, :])
        & (labels[:, None] >= 0)
        & (own[:, None] != jnp.arange(members * slots, dtype=i32)[None, :])
    )
    scores = jnp.where(mask, scores, -1.0)
    best = jnp.maximum(-1.0, jnp.max(scores, axis=1))
    returned = lax.all_to_all(best, "x", split_axis=0, concat_axis=0, tiled=True)
    return returned[place]


def on_device(embeddings, cluster_ids):
    where = jnp.stack([lax.axis_index(a) for a in ("x", "z", "y", "c")]).astype(i32)
    shape = jax.ShapeDtypeStruct
    half = shape((ROWS + LABEL_ROWS, HALF_WIDTH), bf16)
    keep, send = pl.pallas_call(
        unit_kernel, out_shape=(half, half),
        in_specs=[SCALARS, pl.BlockSpec(memory_space=pl.ANY), WHOLE], out_specs=(WHOLE, WHOLE),
        scratch_shapes=[pltpu.VMEM(embeddings.shape, f32), pltpu.SemaphoreType.DMA((ROWS // PIECE,))],
        compiler_params=params(12), name="unit",
    )(where, embeddings, cluster_ids.reshape(1, ROWS))
    got = lax.ppermute(send, "c", [(0, 1), (1, 0)])
    packed, code = pl.pallas_call(
        pack_kernel,
        out_shape=(shape((CHIPS, BLOCK, WIDTH), bf16), shape((8, ROWS), i32)),
        in_specs=[SCALARS, WHOLE, WHOLE], out_specs=(WHOLE, WHOLE), compiler_params=params(20), name="pack",
    )(where, keep, got)
    packed = lax.all_to_all(packed, ("x", "z", "y"), 0, 0, tiled=True)
    send, line, pos, meta = pl.pallas_call(
        send_kernel,
        out_shape=(
            shape((SHARE_ROWS, WIDTH), bf16), shape((8, CHIPS * BLOCK), i32),
            shape((CHIPS, LANES), i32), shape((8, LANES), i32),
        ),
        in_specs=[SCALARS, WHOLE], out_specs=(WHOLE,) * 4, compiler_params=params(24), name="sort",
    )(where, packed)
    other = lax.ppermute(send, "c", [(0, 1), (1, 0)])
    flops = 2 * LANES * WIDTH * (RAW_ROWS + 5 * CHIPS * BLOCK)
    raw = pl.pallas_call(
        own_kernel, out_shape=shape((RAW_ROWS, LANES), f32),
        in_specs=[SCALARS, WHOLE, WHOLE, WHOLE], out_specs=WHOLE,
        scratch_shapes=[pltpu.VMEM((SHARE_ROWS, WIDTH), bf16)],
        compiler_params=params(20), name="own",
        cost_estimate=pl.CostEstimate(flops=flops, bytes_accessed=8 << 20, transcendentals=0),
    )(where, packed, line, send)
    partial = pl.pallas_call(
        gram_kernel,
        out_shape=[shape((CHUNK, LANES), f32)] * 4,
        in_specs=[SCALARS, SCALARS, WHOLE, WHOLE], out_specs=[WHOLE] * 4,
        scratch_shapes=[pltpu.VMEM((PARTIAL + CAPS[0], LANES), f32)],
        compiler_params=params(16), name="gram",
    )(where, meta, other, raw)
    arrived = [partial[0]] + [
        lax.ppermute(partial[s], "y", [(i, (i + s) % 4) for i in range(4)]) for s in (1, 2, 3)
    ]
    best = pl.pallas_call(
        max_kernel,
        out_shape=shape((2 * CHIPS, 1, LANES), f32),
        in_specs=[SCALARS] * 2 + [WHOLE] * 5, out_specs=WHOLE,
        scratch_shapes=[pltpu.VMEM((16, LANES), f32)],
        compiler_params=params(8), name="maxima",
    )(where, meta, *arrived, pos)
    back = lax.all_to_all(best, ("x", "z", "y", "c"), 0, 0, tiled=True)
    fitted = pl.pallas_call(
        pick_kernel,
        out_shape=shape((1, ROWS), f32),
        in_specs=[SCALARS, WHOLE, WHOLE], out_specs=WHOLE, compiler_params=params(8), name="pick",
    )(where, back.reshape(2 * CHIPS, LANES), code).reshape(ROWS)
    return lax.cond(
        meta[4, 0] == 0,
        lambda fitted, embeddings, cluster_ids: fitted,
        lambda fitted, embeddings, cluster_ids: gather_groups(embeddings, cluster_ids),
        fitted, embeddings, cluster_ids,
    )


def solution(mesh):
    axes = ("x", "z", "y", "c")
    grid = Mesh(mesh.devices.reshape(4, 4, 4, 2), axes)
    return jax.shard_map(
        on_device, mesh=grid, in_specs=(P(axes, None), P(axes)), out_specs=P(axes), check_vma=False
    )
```

```python
import jax
import jax.numpy as jnp
from jax import lax
from jax.experimental import pallas as pl
from jax.experimental.pallas import tpu as pltpu
from jax.sharding import Mesh, PartitionSpec as P

ROWS = 128
HALF_WIDTH = 2048
WIDTH = 512
LABEL_ROWS = 16
BINS = 16
CHIPS = 64
BLOCK = 24
SLOTS = BLOCK - 1
GROUP = 32
GUESTS = 64
ALL_GUESTS = 4 * GUESTS
GUEST = 4096
LANES = 128
CAPS = (704, 512, 320, 192)
STARTS = (0, 704, 1216, 1536)
HALF = 64
COUNT = 7
CHUNK = COUNT * HALF
PARTIAL = 4 * CHUNK
SHARES = (
    tuple((q, first) for q, first in ((0, 0), (0, 128), (2, 0), (2, 128), (2, 256))),
    tuple((q, first) for q, first in (
        (0, 256), (0, 384), (0, 512), (0, 640), (1, 0), (1, 128), (1, 256), (1, 384), (3, 0), (3, 128))),
)
BASES = ({0: 0, 2: 704}, {0: -256, 1: 448, 3: 960})
SHARE_ROWS = 1216
SEGMENTS = (
    (0, 256, 0, None), (256, 448, 256, 0), (704, 256, None, 448), (960, 256, None, 704),
    (1216, 320, 704, None), (1536, 192, None, 960),
)
f32, bf16, i32 = jnp.float32, jnp.bfloat16, jnp.int32
WHOLE = pl.BlockSpec(memory_space=pltpu.VMEM)
SCALARS = pl.BlockSpec(memory_space=pltpu.SMEM)


def params(mib):
    return pltpu.CompilerParams(vmem_limit_bytes=mib * 1024 * 1024)


def iota(shape, dim):
    return lax.broadcasted_iota(i32, shape, dim)


def dot_last(a, b):
    return lax.dot_general(a, b, (((1,), (1,)), ((), ())), preferred_element_type=f32)


def dot(a, b):
    return lax.dot_general(a, b, (((1,), (0,)), ((), ())), preferred_element_type=f32)


def as_bf16(mask):
    return jnp.where(mask, 1.0, 0.0).astype(bf16)


def bin_of(labels):
    rank, residue = labels >> 2, labels & 3
    row, col = rank >> 2, rank & 3
    col = jnp.where((row & 1) == 1, 3 - col, col)
    return 4 * col + ((row - residue) & 3)


def unit_kernel(where_ref, x_ref, ids_ref, keep_ref, send_ref):
    c = where_ref[3]
    x = x_ref[...]
    scale = lax.rsqrt(jnp.sum(x * x, axis=1, keepdims=True) + 1e-06)
    ids = jnp.concatenate([ids_ref[...].astype(f32), jnp.zeros((1, HALF_WIDTH - ROWS), f32)], axis=1)
    ids = jnp.broadcast_to(ids, (LABEL_ROWS, HALF_WIDTH)).astype(bf16)
    for half, out_ref in ((c, keep_ref), (1 - c, send_ref)):
        columns = pl.ds(pl.multiple_of(half * HALF_WIDTH, HALF_WIDTH), HALF_WIDTH)
        out_ref[:ROWS, :] = (x_ref[:, columns] * scale).astype(bf16)
        out_ref[ROWS:, :] = ids


def pack_kernel(where_ref, keep_ref, got_ref, out_ref, code_ref):
    y, first = where_ref[2], where_ref[3] == 0
    kept = jnp.max(keep_ref[ROWS:, :ROWS].astype(f32), axis=0, keepdims=True)
    got = jnp.max(got_ref[ROWS:, :ROWS].astype(f32), axis=0, keepdims=True)
    labels = jnp.concatenate([jnp.where(first, kept, got), jnp.where(first, got, kept)], axis=0).astype(i32)
    bins = bin_of(labels)
    upper = as_bf16(iota((ROWS, ROWS), 0) < iota((ROWS, ROWS), 1))

    def ranks_within(masks):
        member = jnp.concatenate([jnp.where(mask, 1.0, 0.0) for mask in masks], axis=0)
        row, col = iota((member.shape[0],) * 2, 0), iota((member.shape[0],) * 2, 1)
        earlier = dot(as_bf16(((row >> 1) == (col >> 1)) & (col < row)), member.astype(bf16))
        ranks = member * (dot(member.astype(bf16), upper) + jnp.sum(earlier, axis=1, keepdims=True))
        rank = sum(ranks[2 * b:2 * b + 2] for b in range(len(masks)))
        return rank.astype(i32), jnp.sum(member, axis=1, keepdims=True)

    rank, sizes = ranks_within([bins == b for b in range(BINS)])
    quad, line = bins >> 2, bins & 3
    extra = rank >= SLOTS
    turn, _ = ranks_within([extra & (quad == q) for q in range(4)])
    room, used = [], []
    for step in range(4):
        taken = jnp.zeros(labels.shape, f32)
        for at in range(4):
            size = jnp.zeros(labels.shape, f32)
            for q in range(4):
                b = 4 * q + at
                size = jnp.where(quad == q, sizes[2 * b:2 * b + 1] + sizes[2 * b + 1:2 * b + 2], size)
            taken = jnp.where(((at - y) & 3) == step, size, taken)
        taken = jnp.minimum(taken.astype(i32), SLOTS)
        used.append(taken)
        room.append(SLOTS - taken)
    placed = jnp.logical_not(extra)
    to_line, to_slot, start = line, rank, jnp.zeros(labels.shape, i32)
    for step in range(4):
        here = extra & (turn >= start) & (turn < start + room[step])
        to_line = jnp.where(here, (y + step) & 3, to_line)
        to_slot = jnp.where(here, used[step] + turn - start, to_slot)
        placed = placed | here
        start = start + room[step]
    lane = jnp.where(placed, to_line * GROUP + to_slot, -1)
    place = jnp.where(placed, (quad * 4 + to_line) * BLOCK + to_slot, -1)
    code_ref[...] = jnp.concatenate([jnp.where(placed, bins * LANES + lane, -1)] * 4, axis=0)
    docs = 2 * ROWS
    flat = lambda v: jnp.concatenate([v[:1], v[1:]], axis=1)
    label_row = flat(labels)
    counts = dot_last(jnp.ones((8, docs), bf16), as_bf16(iota((LANES, docs), 0) == label_row))[:1]
    named = jnp.where(iota((8, docs), 0) == flat(quad), (label_row + 1).astype(f32), 0.0).astype(bf16)
    names = dot_last(named, as_bf16(iota((LANES, docs), 0) == flat(lane)))
    own = jnp.where(first, place[:1], place[1:])
    other = jnp.where(first, place[1:], place[:1])
    onehot = as_bf16(iota((BINS * BLOCK, docs), 0) == jnp.concatenate([own, other], axis=1))
    is_last = iota((BLOCK, WIDTH), 0) == SLOTS
    for y in range(4):
        columns = slice(y * WIDTH, (y + 1) * WIDTH)
        x = jnp.concatenate([keep_ref[:ROWS, columns], got_ref[:ROWS, columns]], axis=0)
        packed = dot(onehot, x)
        for b in range(BINS):
            extra = jnp.concatenate([names[b // 4:b // 4 + 1], counts, jnp.zeros((1, 2 * LANES), f32)], axis=1)
            out_ref[4 * b + y] = jnp.where(is_last, extra, packed[b * BLOCK:(b + 1) * BLOCK]).astype(bf16)


def labels_of(x_ref):
    tail = x_ref[:, BLOCK - 8:, :2 * LANES].astype(f32)
    tail = jnp.max(jnp.where(iota(tail.shape, 1) == 7, tail, 0.0), axis=1)
    return tail[:, :LANES].astype(i32) - 1, tail[:, LANES:].astype(bf16)


def counts_of(chip_counts):
    row, col = iota((LANES, LANES), 0), iota((LANES, LANES), 1)
    in_bin = (bin_of(row) == col) & (row < 4 * BINS)
    counts = [dot(chip_counts, as_bf16(in_bin & ((row & 3) == r))) for r in range(4)]
    return counts, [jnp.sum(v, axis=0, keepdims=True) for v in counts]


def in_order(sizes):
    a, b = jnp.maximum(sizes[0], sizes[1]), jnp.minimum(sizes[0], sizes[1])
    c, d = jnp.maximum(sizes[2], sizes[3]), jnp.minimum(sizes[2], sizes[3])
    first, e = jnp.maximum(a, c), jnp.minimum(a, c)
    g, fourth = jnp.maximum(b, d), jnp.minimum(b, d)
    return first, jnp.maximum(e, g), jnp.minimum(e, g), fourth


def names_kernel(where_ref, x_ref, guest_ref, line_ref, key_ref, pos_ref, meta_ref):
    mine, z = where_ref[0] * 4 + where_ref[1], where_ref[1]
    labels, chip_counts = labels_of(x_ref)
    _, sizes = counts_of(chip_counts)
    here = iota((1, LANES), 1) == mine
    own = lambda v: jnp.sum(jnp.where(here, v, 0.0), axis=1, keepdims=True)
    wide = lambda v: jnp.broadcast_to(v, (1, LANES))
    ordered = in_order(sizes)
    meta_ref[...] = jnp.concatenate([wide(own(v)) for v in ordered] * 2, axis=0).astype(i32)

    n = [own(v) for v in sizes]
    row, col = iota((LANES, LANES), 0), iota((LANES, LANES), 1)
    lane = iota(labels.shape, 1)
    group = lane >> 5
    valid = labels >= 0
    home = bin_of(labels) & 3
    at_home = valid & (home == z)
    upper = as_bf16(row < col)
    lower = as_bf16(iota((CHIPS, CHIPS), 1) < iota((CHIPS, CHIPS), 0))
    pos = jnp.full(labels.shape, -1.0, f32)
    for r in range(4):
        place = sum(
            jnp.where((n[q] > n[r]) | ((n[q] == n[r]) & (q < r)), 1.0, 0.0) for q in range(4) if q != r
        )
        start = jnp.where(
            place < 0.5, float(STARTS[0]),
            jnp.where(place < 1.5, float(STARTS[1]), jnp.where(place < 2.5, float(STARTS[2]), float(STARTS[3]))),
        )
        member = at_home & ((labels & 3) == r)
        member16 = as_bf16(member)
        rank = dot(member16, upper) + jnp.sum(dot(lower, member16), axis=1, keepdims=True)
        pos = jnp.where(member, start + rank, pos)
    pos = pos.astype(i32)
    pos_ref[...] = pos
    guest = valid & (home != group)
    guest16 = as_bf16(guest)
    same = (row >> 5) == (col >> 5)
    turn = dot(guest16, as_bf16(same & (row < col))) + dot(dot(lower, guest16).astype(bf16), as_bf16(same))
    turn = turn.astype(i32)
    away = at_home & (group != z) & (turn < GUESTS)
    key_ref[...] = jnp.where(away, (((z - group) & 3) - 1) * GUESTS + turn, -1)
    per, groups = 16, CHIPS // 16
    value = jnp.where(group == z, jnp.where(guest, GUEST + turn, pos + 1), 0).astype(f32)
    value = pltpu.roll(value, lax.rem(LANES - GROUP * z, LANES), 1)
    value = jnp.where(lane < BLOCK, value, 0.0)
    lined = jnp.zeros((8, per * BLOCK), f32)
    for t in range(per):
        rows = jnp.concatenate([value[per * g + t:per * g + t + 1] for g in range(groups)] * 2, axis=0)
        rows = jnp.concatenate([rows, jnp.zeros((8, per * BLOCK - LANES), f32)], axis=1)
        lined = lined + (pltpu.roll(rows, t * BLOCK, 1) if t else rows)
    slots = jnp.concatenate([lined[g:g + 1] for g in range(groups)], axis=1).astype(i32)
    line_ref[...] = jnp.broadcast_to(slots, line_ref.shape)
    onehot = as_bf16(iota((GUESTS, CHIPS * BLOCK), 0) + GUEST == slots)
    guest_ref[...] = dot(onehot, x_ref[...].reshape(CHIPS * BLOCK, WIDTH)).astype(bf16)


def sorted_rows(segment, slots, x):
    onehot = as_bf16(iota((segment[1], x.shape[0]), 0) + (segment[0] + 1) == slots)
    return dot(onehot, x).astype(bf16)


def send_kernel(where_ref, x_ref, line_ref, send_ref):
    x = x_ref[...].reshape(CHIPS * BLOCK, WIDTH)
    slots = line_ref[:1, :]
    for me in range(2):
        @pl.when(where_ref[3] == me)
        def _():
            for segment in SEGMENTS:
                at = segment[2 + 1 - me]
                if at is not None:
                    send_ref[at:at + segment[1], :] = sorted_rows(segment, slots, x)


def mine_kernel(where_ref, x_ref, line_ref, send_ref, key_ref, pos_ref, mine_ref, far_ref, over_ref):
    x = x_ref[...].reshape(CHIPS * BLOCK, WIDTH)
    slots = line_ref[:1, :]
    for core in range(2):
        @pl.when(where_ref[3] == core)
        def _():
            for segment in SEGMENTS:
                at, sent = segment[2 + core], segment[2 + 1 - core]
                if at is not None:
                    rows = segment[1]
                    mine_ref[at:at + rows, :] = (
                        send_ref[sent:sent + rows, :] if sent is not None else sorted_rows(segment, slots, x)
                    )
    total = jnp.zeros((8, ALL_GUESTS), f32)
    step = 16
    for first in range(0, CHIPS, step):
        flat = lambda ref: jnp.concatenate([ref[s:s + 1, :] for s in range(first, first + step)], axis=1)
        places = flat(pos_ref) + 1
        parts = jnp.where(iota((8, step * LANES), 0) == 0, places >> 5, places & 31).astype(f32).astype(bf16)
        total = total + dot_last(parts, as_bf16(iota((ALL_GUESTS, step * LANES), 0) == flat(key_ref)))
    far_ref[...] = jnp.broadcast_to((32.0 * total[:1] + total[1:2]).astype(i32), far_ref.shape)
    _, chip_counts = labels_of(x_ref)
    counts, sizes = counts_of(chip_counts)
    ordered = in_order(sizes)
    over = jnp.zeros((1, LANES), f32)
    for size, cap in zip(ordered, CAPS):
        over = jnp.maximum(over, jnp.where(size > cap, 1.0, 0.0))
    for share in SHARES:
        length = sum(jnp.maximum(jnp.floor((ordered[q] + 63.0) * (1 / 64)) - first // HALF, 0.0) for q, first in share)
        over = jnp.maximum(over, jnp.where(length > 4 * COUNT, 1.0, 0.0))
    taken = counts[0] + counts[1] + counts[2] + counts[3]
    extra, room = jnp.maximum(taken - SLOTS, 0.0), jnp.maximum(SLOTS - taken, 0.0)
    row, col = iota((LANES, LANES), 0), iota((LANES, LANES), 1)
    same = (row >> 2) == (col >> 2)
    wanted = dot(extra.astype(bf16), as_bf16(same))
    before = jnp.zeros(taken.shape, f32)
    for turn in range(4):
        earlier = same & (((row - turn) & 3) < ((col - turn) & 3))
        before = jnp.where((iota(taken.shape, 0) & 3) == turn, dot(room.astype(bf16), as_bf16(earlier)), before)
    held = jnp.sum(jnp.minimum(jnp.maximum(wanted - before, 0.0), room), axis=0, keepdims=True)
    over = jnp.maximum(over, jnp.where(held > GUESTS, 1.0, 0.0))
    full = jnp.where(wanted > dot(room.astype(bf16), as_bf16(same)), 1.0, 0.0)
    over = jnp.maximum(over, jnp.max(full, axis=0, keepdims=True))
    over_ref[...] = jnp.broadcast_to(jnp.max(over, axis=1, keepdims=True), over_ref.shape).astype(i32)


def add_guests(core, base_ref, guests, far_ref, out_ref):
    guests = jnp.concatenate([ref[...] for ref in guests] + [guests[0][...]], axis=0)
    far = far_ref[:1, :]
    for segment in SEGMENTS:
        at, rows = segment[2 + core], segment[1]
        if at is not None:
            out_ref[at:at + rows, :] = base_ref[at:at + rows, :] + sorted_rows(segment, far, guests)


def blocks_of(core):
    for q, first in SHARES[core]:
        at = BASES[core][q] + first
        yield q, first, pl.ds(at, CAPS[q] - first), pl.ds(at, LANES)


RAW_ROWS = max(sum(CAPS[q] - first for q, first in share) for share in SHARES)


def own_kernel(where_ref, x_ref, g1, g2, g3, far_ref, raw_ref, rows_ref):
    for core in range(2):
        @pl.when(where_ref[3] == core)
        def _():
            add_guests(core, x_ref, (g1, g2, g3), far_ref, rows_ref)
            at = 0
            for q, first, left, right in blocks_of(core):
                rows = CAPS[q] - first
                raw_ref[at:at + rows, :] = dot_last(rows_ref[left, :], rows_ref[right, :])
                at += rows


def length_of(size, first):
    return jnp.maximum(((size + HALF - 1) >> 6) - first // HALF, 0)


def gram_kernel(where_ref, meta_ref, x_ref, g1, g2, g3, far_ref, raw_ref, out0, out1, out2, out3, part_ref, rows_ref):
    y, c = where_ref[2], where_ref[3]
    part_ref[...] = jnp.full(part_ref.shape, -4.0, f32)
    for core in range(2):
        @pl.when(c == core)
        def _():
            add_guests(core, x_ref, (g1, g2, g3), far_ref, rows_ref)
            at, to = 0, jnp.zeros((), i32)
            for q, first, left, right in blocks_of(core):
                rows = CAPS[q] - first
                score = raw_ref[at:at + rows, :] + dot_last(rows_ref[left, :], rows_ref[right, :])
                at += rows
                size = meta_ref[q, 0]
                i, j = iota(score.shape, 0), iota(score.shape, 1)
                keep = (i < size - first) & (j < size - first) & (i != j)
                part_ref[pl.ds(pl.multiple_of(to, HALF), rows), :] = jnp.where(keep, score, -4.0)
                to = jnp.minimum(to + HALF * length_of(size, first), PARTIAL)
    for shift, out in enumerate((out0, out1, out2, out3)):
        out[...] = part_ref[pl.ds(pl.multiple_of(lax.rem(y + shift, 4) * CHUNK, HALF), CHUNK), :]


FIRST_ROW = (0, 6, 10, 13)


def max_kernel(where_ref, meta_ref, p0, p1, p2, p3, pos_ref, out_ref, best_ref):
    y, c = where_ref[2], where_ref[3]
    best_ref[...] = jnp.full(best_ref.shape, -1.0, f32)
    sub, lane = iota((HALF, LANES), 0), iota((HALF, LANES), 1)
    blocks = []
    for core, share in enumerate(SHARES):
        at = jnp.zeros((), i32)
        for q, first in share:
            length = length_of(meta_ref[q, 0], first)
            col = FIRST_ROW[q] + first // LANES
            blocks.append((jnp.where((c == core) & (length > 0), at, PARTIAL), col, 2 * col - at))
            at = at + length
    for t in range(COUNT):
        at = slice(t * HALF, (t + 1) * HALF)
        block = (p0[at, :] + p1[at, :]) + (p2[at, :] + p3[at, :])
        index = y * COUNT + t
        col, shift = jnp.asarray(15, i32), jnp.asarray(0, i32)
        for start, block_col, block_shift in blocks:
            inside = index >= start
            col, shift = jnp.where(inside, block_col, col), jnp.where(inside, block_shift, shift)
        row = jnp.minimum(jnp.maximum(index + shift, 0), 31)
        along = jnp.max(block, axis=1, keepdims=True)
        along = jnp.max(jnp.where(sub + (row & 1) * HALF == lane, along, -1.0), axis=0, keepdims=True)
        row = row >> 1
        best_ref[pl.ds(row, 1), :] = jnp.maximum(best_ref[pl.ds(row, 1), :], along)
        down = jnp.max(block, axis=0, keepdims=True)
        best_ref[pl.ds(col, 1), :] = jnp.maximum(best_ref[pl.ds(col, 1), :], down)
    pos = pos_ref[...]
    pos = jnp.where(pos >= STARTS[1], pos + HALF, pos)
    pos = jnp.where(pos >= STARTS[3] + HALF, pos + HALF, pos)
    row, lane = pos >> 7, pos & (LANES - 1)
    out = jnp.full(pos.shape, -1.0, f32)
    for r in range(15):
        value = jnp.broadcast_to(best_ref[r:r + 1, :], pos.shape)
        value = jnp.take_along_axis(value, lane, axis=1, mode="promise_in_bounds")
        out = jnp.where(row == r, value, out)
    out_ref[:CHIPS, :] = out
    out_ref[CHIPS:, :] = out


def pick_kernel(where_ref, v_ref, code_ref, out_ref):
    c = where_ref[3]
    values = jnp.maximum(v_ref[:CHIPS, :], v_ref[CHIPS:, :])
    values = jnp.max(values.reshape(BINS, 4, LANES), axis=1)
    eye = iota((LANES, LANES), 0) == iota((LANES, LANES), 1)
    code = jnp.max(jnp.where(iota((8, ROWS), 0) == c, code_ref[...], -1), axis=0, keepdims=True)
    code = jnp.max(jnp.where(eye, code.astype(f32), -1.0), axis=1, keepdims=True).astype(i32)
    slot = iota((ROWS, LANES), 1)
    best = jnp.full((ROWS, LANES), -1.0, f32)
    for b in range(BINS):
        best = jnp.where(slot + b * LANES == code, values[b:b + 1], best)
    best = jnp.max(best, axis=1, keepdims=True)
    out_ref[...] = jnp.max(jnp.where(eye, best, -1.0), axis=0, keepdims=True)


def gather_groups(embeddings, cluster_ids):
    split = ("z", "y", "c")
    rows = embeddings.shape[0]
    groups = lax.axis_size("x")
    cap = 2 * rows // groups
    slots = groups * cap
    owner_of = cluster_ids % groups
    onehot = (owner_of[:, None] == jnp.arange(groups, dtype=i32)[None, :]).astype(i32)
    before = jnp.cumsum(onehot, axis=0) - onehot
    rank = jnp.sum(before * onehot, axis=1)
    place = owner_of * cap + rank
    picked = place[None, :] == jnp.arange(slots, dtype=i32)[:, None]
    filled = jnp.any(picked, axis=1)
    source = jnp.sum(jnp.where(picked, jnp.arange(rows, dtype=i32)[None, :], 0), axis=1)
    out_labels = jnp.where(filled, cluster_ids[source], -1)
    squares = jnp.sum(embeddings * embeddings, axis=1, keepdims=True)
    local_unit = (embeddings * lax.rsqrt(squares + 1e-06)).astype(bf16)
    outgoing_unit = jnp.where(filled[:, None], local_unit[source], jnp.zeros((), bf16))
    unit = lax.all_to_all(outgoing_unit, "x", split_axis=0, concat_axis=0, tiled=True)
    labels = lax.all_to_all(out_labels, "x", split_axis=0, concat_axis=0, tiled=True)
    members = lax.axis_size(split)

    def everywhere(v):
        copies = jnp.broadcast_to(v[None], (members,) + v.shape).reshape((members * slots,) + v.shape[1:])
        return lax.all_to_all(copies, split, split_axis=0, concat_axis=0, tiled=True)

    def add_slice(i, scores):
        part = lax.dynamic_slice_in_dim(unit, i * WIDTH, WIDTH, 1)
        return scores + dot_last(part, everywhere(part))

    scores = lax.fori_loop(0, embeddings.shape[1] // WIDTH, add_slice, jnp.zeros((slots, members * slots), f32))
    all_labels = everywhere(labels)
    own = lax.axis_index(split) * slots + jnp.arange(slots, dtype=i32)
    mask = (
        (labels[:, None] == all_labels[None, :])
        & (labels[:, None] >= 0)
        & (own[:, None] != jnp.arange(members * slots, dtype=i32)[None, :])
    )
    scores = jnp.where(mask, scores, -1.0)
    best = jnp.maximum(-1.0, jnp.max(scores, axis=1))
    returned = lax.all_to_all(best, "x", split_axis=0, concat_axis=0, tiled=True)
    return returned[place]


def on_device(embeddings, cluster_ids):
    where = jnp.stack([lax.axis_index(a) for a in ("x", "z", "y", "c")]).astype(i32)
    shape = jax.ShapeDtypeStruct
    half = shape((ROWS + LABEL_ROWS, HALF_WIDTH), bf16)
    keep, send = pl.pallas_call(
        unit_kernel, out_shape=(half, half),
        in_specs=[SCALARS, WHOLE, WHOLE], out_specs=(WHOLE, WHOLE), compiler_params=params(12), name="unit",
    )(where, embeddings, cluster_ids.reshape(1, ROWS))
    got = lax.ppermute(send, "c", [(0, 1), (1, 0)])
    packed, code = pl.pallas_call(
        pack_kernel,
        out_shape=(shape((CHIPS, BLOCK, WIDTH), bf16), shape((8, ROWS), i32)),
        in_specs=[SCALARS, WHOLE, WHOLE], out_specs=(WHOLE, WHOLE), compiler_params=params(20), name="pack",
    )(where, keep, got)
    packed = lax.all_to_all(packed, ("x", "z", "y"), 0, 0, tiled=True)
    table = shape((CHIPS, LANES), i32)
    guests, line, key, pos, meta = pl.pallas_call(
        names_kernel,
        out_shape=(shape((GUESTS, WIDTH), bf16), shape((8, CHIPS * BLOCK), i32), table, table, shape((8, LANES), i32)),
        in_specs=[SCALARS, WHOLE], out_specs=(WHOLE,) * 5, compiler_params=params(12), name="names",
    )(where, packed)
    brought = [lax.ppermute(guests, "z", [(i, (i + s) % 4) for i in range(4)]) for s in (1, 2, 3)]
    share = shape((SHARE_ROWS, WIDTH), bf16)
    slots = CHIPS * BLOCK
    send = pl.pallas_call(
        send_kernel, out_shape=share,
        in_specs=[SCALARS, WHOLE, WHOLE], out_specs=WHOLE, compiler_params=params(16), name="send",
        cost_estimate=pl.CostEstimate(flops=2 * SHARE_ROWS * WIDTH * slots, bytes_accessed=4 << 20, transcendentals=0),
    )(where, packed, line)
    other = lax.ppermute(send, "c", [(0, 1), (1, 0)])
    mine, far, over = pl.pallas_call(
        mine_kernel, out_shape=(share, shape((8, ALL_GUESTS), i32), shape((8, LANES), i32)),
        in_specs=[SCALARS] + [WHOLE] * 5, out_specs=(WHOLE,) * 3, compiler_params=params(20), name="mine",
        cost_estimate=pl.CostEstimate(flops=2 * SHARE_ROWS * WIDTH * slots, bytes_accessed=4 << 20, transcendentals=0),
    )(where, packed, line, send, key, pos)
    swapped = [lax.ppermute(v, "c", [(0, 1), (1, 0)]) for v in brought]
    raw = pl.pallas_call(
        own_kernel, out_shape=shape((RAW_ROWS, LANES), f32),
        in_specs=[SCALARS] + [WHOLE] * 5, out_specs=WHOLE,
        scratch_shapes=[pltpu.VMEM((SHARE_ROWS, WIDTH), bf16)],
        compiler_params=params(16), name="own",
        cost_estimate=pl.CostEstimate(flops=2 * RAW_ROWS * LANES * WIDTH, bytes_accessed=4 << 20, transcendentals=0),
    )(where, mine, *brought, far)
    partial = pl.pallas_call(
        gram_kernel,
        out_shape=[shape((CHUNK, LANES), f32)] * 4,
        in_specs=[SCALARS, SCALARS] + [WHOLE] * 6, out_specs=[WHOLE] * 4,
        scratch_shapes=[pltpu.VMEM((PARTIAL + CAPS[0], LANES), f32), pltpu.VMEM((SHARE_ROWS, WIDTH), bf16)],
        compiler_params=params(16), name="gram",
    )(where, meta, other, *swapped, far, raw)
    arrived = [partial[0]] + [
        lax.ppermute(partial[s], "y", [(i, (i + s) % 4) for i in range(4)]) for s in (1, 2, 3)
    ]
    best = pl.pallas_call(
        max_kernel,
        out_shape=shape((2 * CHIPS, LANES), f32),
        in_specs=[SCALARS] * 2 + [WHOLE] * 5, out_specs=WHOLE,
        scratch_shapes=[pltpu.VMEM((16, LANES), f32)],
        compiler_params=params(8), name="maxima",
    )(where, meta, *arrived, pos)
    back = lax.all_to_all(best.reshape(2 * CHIPS, 1, LANES), ("c", "x", "z", "y"), 0, 0, tiled=True)
    fitted = pl.pallas_call(
        pick_kernel,
        out_shape=shape((1, ROWS), f32),
        in_specs=[SCALARS, WHOLE, WHOLE], out_specs=WHOLE, compiler_params=params(8), name="pick",
    )(where, back.reshape(2 * CHIPS, LANES), code).reshape(ROWS)
    return lax.cond(
        over[0, 0] == 0,
        lambda fitted, embeddings, cluster_ids: fitted,
        lambda fitted, embeddings, cluster_ids: gather_groups(embeddings, cluster_ids),
        fitted, embeddings, cluster_ids,
    )


def solution(mesh):
    axes = ("x", "z", "y", "c")
    grid = Mesh(mesh.devices.reshape(4, 4, 4, 2), axes)
    return jax.shard_map(
        on_device, mesh=grid, in_specs=(P(axes, None), P(axes)), out_specs=P(axes), check_vma=False
    )
```

```python
import jax
import jax.numpy as jnp
from jax import lax
from jax.experimental import pallas as pl
from jax.experimental.pallas import tpu as pltpu
from jax.sharding import Mesh, PartitionSpec as P

ROWS = 128
HALF_WIDTH = 2048
WIDTH = 512
LABEL_ROWS = 16
BINS = 16
CHIPS = 64
BLOCK = 24
SLOTS = BLOCK - 1
GROUP = 32
GUESTS = 64
ALL_GUESTS = 4 * GUESTS
GUEST = 4096
LANES = 128
CAPS = (704, 512, 320, 192)
STARTS = (0, 704, 1216, 1536)
HALF = 64
COUNT = 7
CHUNK = COUNT * HALF
PARTIAL = 4 * CHUNK
SHARES = (
    tuple((q, first) for q, first in ((0, 0), (0, 128), (2, 0), (2, 128), (2, 256))),
    tuple((q, first) for q, first in (
        (0, 256), (0, 384), (0, 512), (0, 640), (1, 0), (1, 128), (1, 256), (1, 384), (3, 0), (3, 128))),
)
BASES = ({0: 0, 2: 704}, {0: -256, 1: 448, 3: 960})
SHARE_ROWS = 1216
SEGMENTS = (
    (0, 256, 0, None), (256, 448, 256, 0), (704, 256, None, 448), (960, 256, None, 704),
    (1216, 320, 704, None), (1536, 192, None, 960),
)
f32, bf16, i32 = jnp.float32, jnp.bfloat16, jnp.int32
WHOLE = pl.BlockSpec(memory_space=pltpu.VMEM)
SCALARS = pl.BlockSpec(memory_space=pltpu.SMEM)


def params(mib):
    return pltpu.CompilerParams(vmem_limit_bytes=mib * 1024 * 1024)


def iota(shape, dim):
    return lax.broadcasted_iota(i32, shape, dim)


def dot_last(a, b):
    return lax.dot_general(a, b, (((1,), (1,)), ((), ())), preferred_element_type=f32)


def dot(a, b):
    return lax.dot_general(a, b, (((1,), (0,)), ((), ())), preferred_element_type=f32)


def as_bf16(mask):
    return jnp.where(mask, 1.0, 0.0).astype(bf16)


def bin_of(labels):
    rank, residue = labels >> 2, labels & 3
    row, col = rank >> 2, rank & 3
    col = jnp.where((row & 1) == 1, 3 - col, col)
    return 4 * col + ((row - residue) & 3)


def unit_kernel(where_ref, x_ref, ids_ref, keep_ref, send_ref):
    c = where_ref[3]
    x = x_ref[...]
    scale = lax.rsqrt(jnp.sum(x * x, axis=1, keepdims=True) + 1e-06)
    ids = jnp.concatenate([ids_ref[...].astype(f32), jnp.zeros((1, HALF_WIDTH - ROWS), f32)], axis=1)
    ids = jnp.broadcast_to(ids, (LABEL_ROWS, HALF_WIDTH)).astype(bf16)
    for half, out_ref in ((c, keep_ref), (1 - c, send_ref)):
        columns = pl.ds(pl.multiple_of(half * HALF_WIDTH, HALF_WIDTH), HALF_WIDTH)
        out_ref[:ROWS, :] = (x_ref[:, columns] * scale).astype(bf16)
        out_ref[ROWS:, :] = ids


def pack_kernel(where_ref, keep_ref, got_ref, out_ref, code_ref):
    y, first = where_ref[2], where_ref[3] == 0
    kept = jnp.max(keep_ref[ROWS:, :ROWS].astype(f32), axis=0, keepdims=True)
    got = jnp.max(got_ref[ROWS:, :ROWS].astype(f32), axis=0, keepdims=True)
    labels = jnp.concatenate([jnp.where(first, kept, got), jnp.where(first, got, kept)], axis=0).astype(i32)
    bins = bin_of(labels)
    upper = as_bf16(iota((ROWS, ROWS), 0) < iota((ROWS, ROWS), 1))

    def ranks_within(masks):
        member = jnp.concatenate([jnp.where(mask, 1.0, 0.0) for mask in masks], axis=0)
        row, col = iota((member.shape[0],) * 2, 0), iota((member.shape[0],) * 2, 1)
        earlier = dot(as_bf16(((row >> 1) == (col >> 1)) & (col < row)), member.astype(bf16))
        ranks = member * (dot(member.astype(bf16), upper) + jnp.sum(earlier, axis=1, keepdims=True))
        rank = sum(ranks[2 * b:2 * b + 2] for b in range(len(masks)))
        return rank.astype(i32), jnp.sum(member, axis=1, keepdims=True)

    rank, sizes = ranks_within([bins == b for b in range(BINS)])
    quad, line = bins >> 2, bins & 3
    extra = rank >= SLOTS
    turn, _ = ranks_within([extra & (quad == q) for q in range(4)])
    room, used = [], []
    for step in range(4):
        taken = jnp.zeros(labels.shape, f32)
        for at in range(4):
            size = jnp.zeros(labels.shape, f32)
            for q in range(4):
                b = 4 * q + at
                size = jnp.where(quad == q, sizes[2 * b:2 * b + 1] + sizes[2 * b + 1:2 * b + 2], size)
            taken = jnp.where(((at - y) & 3) == step, size, taken)
        taken = jnp.minimum(taken.astype(i32), SLOTS)
        used.append(taken)
        room.append(SLOTS - taken)
    placed = jnp.logical_not(extra)
    to_line, to_slot, start = line, rank, jnp.zeros(labels.shape, i32)
    for step in range(4):
        here = extra & (turn >= start) & (turn < start + room[step])
        to_line = jnp.where(here, (y + step) & 3, to_line)
        to_slot = jnp.where(here, used[step] + turn - start, to_slot)
        placed = placed | here
        start = start + room[step]
    lane = jnp.where(placed, to_line * GROUP + to_slot, -1)
    place = jnp.where(placed, (quad * 4 + to_line) * BLOCK + to_slot, -1)
    code_ref[...] = jnp.concatenate([jnp.where(placed, bins * LANES + lane, -1)] * 4, axis=0)
    docs = 2 * ROWS
    flat = lambda v: jnp.concatenate([v[:1], v[1:]], axis=1)
    label_row = flat(labels)
    counts = dot_last(jnp.ones((8, docs), bf16), as_bf16(iota((LANES, docs), 0) == label_row))[:1]
    named = jnp.where(iota((8, docs), 0) == flat(quad), (label_row + 1).astype(f32), 0.0).astype(bf16)
    names = dot_last(named, as_bf16(iota((LANES, docs), 0) == flat(lane)))
    own = jnp.where(first, place[:1], place[1:])
    other = jnp.where(first, place[1:], place[:1])
    onehot = as_bf16(iota((BINS * BLOCK, docs), 0) == jnp.concatenate([own, other], axis=1))
    is_last = iota((BLOCK, WIDTH), 0) == SLOTS
    for y in range(4):
        columns = slice(y * WIDTH, (y + 1) * WIDTH)
        x = jnp.concatenate([keep_ref[:ROWS, columns], got_ref[:ROWS, columns]], axis=0)
        packed = dot(onehot, x)
        for b in range(BINS):
            extra = jnp.concatenate([names[b // 4:b // 4 + 1], counts, jnp.zeros((1, 2 * LANES), f32)], axis=1)
            out_ref[4 * b + y] = jnp.where(is_last, extra, packed[b * BLOCK:(b + 1) * BLOCK]).astype(bf16)


def labels_of(x_ref):
    tail = x_ref[:, BLOCK - 8:, :2 * LANES].astype(f32)
    tail = jnp.max(jnp.where(iota(tail.shape, 1) == 7, tail, 0.0), axis=1)
    return tail[:, :LANES].astype(i32) - 1, tail[:, LANES:].astype(bf16)


def counts_of(chip_counts):
    row, col = iota((LANES, LANES), 0), iota((LANES, LANES), 1)
    in_bin = (bin_of(row) == col) & (row < 4 * BINS)
    counts = [dot(chip_counts, as_bf16(in_bin & ((row & 3) == r))) for r in range(4)]
    return counts, [jnp.sum(v, axis=0, keepdims=True) for v in counts]


def in_order(sizes):
    a, b = jnp.maximum(sizes[0], sizes[1]), jnp.minimum(sizes[0], sizes[1])
    c, d = jnp.maximum(sizes[2], sizes[3]), jnp.minimum(sizes[2], sizes[3])
    first, e = jnp.maximum(a, c), jnp.minimum(a, c)
    g, fourth = jnp.maximum(b, d), jnp.minimum(b, d)
    return first, jnp.maximum(e, g), jnp.minimum(e, g), fourth


def names_kernel(where_ref, x_ref, guest_ref, line_ref, key_ref, pos_ref, meta_ref):
    mine, z = where_ref[0] * 4 + where_ref[1], where_ref[1]
    labels, chip_counts = labels_of(x_ref)
    _, sizes = counts_of(chip_counts)
    here = iota((1, LANES), 1) == mine
    own = lambda v: jnp.sum(jnp.where(here, v, 0.0), axis=1, keepdims=True)
    wide = lambda v: jnp.broadcast_to(v, (1, LANES))
    ordered = in_order(sizes)
    meta_ref[...] = jnp.concatenate([wide(own(v)) for v in ordered] * 2, axis=0).astype(i32)

    n = [own(v) for v in sizes]
    row, col = iota((LANES, LANES), 0), iota((LANES, LANES), 1)
    lane = iota(labels.shape, 1)
    group = lane >> 5
    valid = labels >= 0
    home = bin_of(labels) & 3
    at_home = valid & (home == z)
    upper = as_bf16(row < col)
    lower = as_bf16(iota((CHIPS, CHIPS), 1) < iota((CHIPS, CHIPS), 0))
    pos = jnp.full(labels.shape, -1.0, f32)
    for r in range(4):
        place = sum(
            jnp.where((n[q] > n[r]) | ((n[q] == n[r]) & (q < r)), 1.0, 0.0) for q in range(4) if q != r
        )
        start = jnp.where(
            place < 0.5, float(STARTS[0]),
            jnp.where(place < 1.5, float(STARTS[1]), jnp.where(place < 2.5, float(STARTS[2]), float(STARTS[3]))),
        )
        member = at_home & ((labels & 3) == r)
        member16 = as_bf16(member)
        rank = dot(member16, upper) + jnp.sum(dot(lower, member16), axis=1, keepdims=True)
        pos = jnp.where(member, start + rank, pos)
    pos = pos.astype(i32)
    pos_ref[...] = pos
    guest = valid & (home != group)
    guest16 = as_bf16(guest)
    same = (row >> 5) == (col >> 5)
    turn = dot(guest16, as_bf16(same & (row < col))) + dot(dot(lower, guest16).astype(bf16), as_bf16(same))
    turn = turn.astype(i32)
    away = at_home & (group != z) & (turn < GUESTS)
    key_ref[...] = jnp.where(away, (((z - group) & 3) - 1) * GUESTS + turn, -1)
    per, groups = 16, CHIPS // 16
    value = jnp.where(group == z, jnp.where(guest, GUEST + turn, pos + 1), 0).astype(f32)
    value = pltpu.roll(value, lax.rem(LANES - GROUP * z, LANES), 1)
    value = jnp.where(lane < BLOCK, value, 0.0)
    lined = jnp.zeros((8, per * BLOCK), f32)
    for t in range(per):
        rows = jnp.concatenate([value[per * g + t:per * g + t + 1] for g in range(groups)] * 2, axis=0)
        rows = jnp.concatenate([rows, jnp.zeros((8, per * BLOCK - LANES), f32)], axis=1)
        lined = lined + (pltpu.roll(rows, t * BLOCK, 1) if t else rows)
    slots = jnp.concatenate([lined[g:g + 1] for g in range(groups)], axis=1).astype(i32)
    line_ref[...] = jnp.broadcast_to(slots, line_ref.shape)
    onehot = as_bf16(iota((GUESTS, CHIPS * BLOCK), 0) + GUEST == slots)
    guest_ref[...] = dot(onehot, x_ref[...].reshape(CHIPS * BLOCK, WIDTH)).astype(bf16)


def sorted_rows(segment, slots, x):
    onehot = as_bf16(iota((segment[1], x.shape[0]), 0) + (segment[0] + 1) == slots)
    return dot(onehot, x).astype(bf16)


def send_kernel(where_ref, x_ref, line_ref, send_ref):
    x = x_ref[...].reshape(CHIPS * BLOCK, WIDTH)
    slots = line_ref[:1, :]
    for me in range(2):
        @pl.when(where_ref[3] == me)
        def _():
            for segment in SEGMENTS:
                at = segment[2 + 1 - me]
                if at is not None:
                    send_ref[at:at + segment[1], :] = sorted_rows(segment, slots, x)


def mine_kernel(where_ref, x_ref, line_ref, send_ref, key_ref, pos_ref, mine_ref, far_ref, over_ref):
    x = x_ref[...].reshape(CHIPS * BLOCK, WIDTH)
    slots = line_ref[:1, :]
    for core in range(2):
        @pl.when(where_ref[3] == core)
        def _():
            for segment in SEGMENTS:
                at, sent = segment[2 + core], segment[2 + 1 - core]
                if at is not None:
                    rows = segment[1]
                    mine_ref[at:at + rows, :] = (
                        send_ref[sent:sent + rows, :] if sent is not None else sorted_rows(segment, slots, x)
                    )
    total = jnp.zeros((8, ALL_GUESTS), f32)
    step = 16
    for first in range(0, CHIPS, step):
        flat = lambda ref: jnp.concatenate([ref[s:s + 1, :] for s in range(first, first + step)], axis=1)
        places = flat(pos_ref) + 1
        parts = jnp.where(iota((8, step * LANES), 0) == 0, places >> 5, places & 31).astype(f32).astype(bf16)
        total = total + dot_last(parts, as_bf16(iota((ALL_GUESTS, step * LANES), 0) == flat(key_ref)))
    far_ref[...] = jnp.broadcast_to((32.0 * total[:1] + total[1:2]).astype(i32), far_ref.shape)
    _, chip_counts = labels_of(x_ref)
    counts, sizes = counts_of(chip_counts)
    ordered = in_order(sizes)
    over = jnp.zeros((1, LANES), f32)
    for size, cap in zip(ordered, CAPS):
        over = jnp.maximum(over, jnp.where(size > cap, 1.0, 0.0))
    for share in SHARES:
        length = sum(jnp.maximum(jnp.floor((ordered[q] + 63.0) * (1 / 64)) - first // HALF, 0.0) for q, first in share)
        over = jnp.maximum(over, jnp.where(length > 4 * COUNT, 1.0, 0.0))
    taken = counts[0] + counts[1] + counts[2] + counts[3]
    extra, room = jnp.maximum(taken - SLOTS, 0.0), jnp.maximum(SLOTS - taken, 0.0)
    row, col = iota((LANES, LANES), 0), iota((LANES, LANES), 1)
    same = (row >> 2) == (col >> 2)
    wanted = dot(extra.astype(bf16), as_bf16(same))
    before = jnp.zeros(taken.shape, f32)
    for turn in range(4):
        earlier = same & (((row - turn) & 3) < ((col - turn) & 3))
        before = jnp.where((iota(taken.shape, 0) & 3) == turn, dot(room.astype(bf16), as_bf16(earlier)), before)
    held = jnp.sum(jnp.minimum(jnp.maximum(wanted - before, 0.0), room), axis=0, keepdims=True)
    over = jnp.maximum(over, jnp.where(held > GUESTS, 1.0, 0.0))
    full = jnp.where(wanted > dot(room.astype(bf16), as_bf16(same)), 1.0, 0.0)
    over = jnp.maximum(over, jnp.max(full, axis=0, keepdims=True))
    over_ref[...] = jnp.broadcast_to(jnp.max(over, axis=1, keepdims=True), over_ref.shape).astype(i32)


def add_guests(core, base_ref, guests, far_ref, out_ref):
    guests = jnp.concatenate([ref[...] for ref in guests] + [guests[0][...]], axis=0)
    far = far_ref[:1, :]
    for segment in SEGMENTS:
        at, rows = segment[2 + core], segment[1]
        if at is not None:
            out_ref[at:at + rows, :] = base_ref[at:at + rows, :] + sorted_rows(segment, far, guests)


def blocks_of(core):
    for q, first in SHARES[core]:
        at = BASES[core][q] + first
        yield q, first, pl.ds(at, CAPS[q] - first), pl.ds(at, LANES)


RAW_ROWS = max(sum(CAPS[q] - first for q, first in share) for share in SHARES)


def own_kernel(where_ref, x_ref, g1, g2, g3, far_ref, raw_ref, rows_ref):
    for core in range(2):
        @pl.when(where_ref[3] == core)
        def _():
            add_guests(core, x_ref, (g1, g2, g3), far_ref, rows_ref)
            at = 0
            for q, first, left, right in blocks_of(core):
                rows = CAPS[q] - first
                raw_ref[at:at + rows, :] = dot_last(rows_ref[left, :], rows_ref[right, :])
                at += rows


def length_of(size, first):
    return jnp.maximum(((size + HALF - 1) >> 6) - first // HALF, 0)


def gram_kernel(where_ref, meta_ref, x_ref, g1, g2, g3, far_ref, raw_ref, out0, out1, out2, out3, part_ref, rows_ref):
    y, c = where_ref[2], where_ref[3]
    part_ref[...] = jnp.full(part_ref.shape, -4.0, f32)
    for core in range(2):
        @pl.when(c == core)
        def _():
            add_guests(core, x_ref, (g1, g2, g3), far_ref, rows_ref)
            at, to = 0, jnp.zeros((), i32)
            for q, first, left, right in blocks_of(core):
                rows = CAPS[q] - first
                score = raw_ref[at:at + rows, :] + dot_last(rows_ref[left, :], rows_ref[right, :])
                at += rows
                size = meta_ref[q, 0]
                i, j = iota(score.shape, 0), iota(score.shape, 1)
                keep = (i < size - first) & (j < size - first) & (i != j)
                part_ref[pl.ds(pl.multiple_of(to, HALF), rows), :] = jnp.where(keep, score, -4.0)
                to = jnp.minimum(to + HALF * length_of(size, first), PARTIAL)
    for shift, out in enumerate((out0, out1, out2, out3)):
        out[...] = part_ref[pl.ds(pl.multiple_of(lax.rem(y + shift, 4) * CHUNK, HALF), CHUNK), :]


FIRST_ROW = (0, 6, 10, 13)


def max_kernel(where_ref, meta_ref, p0, p1, p2, p3, pos_ref, out_ref, best_ref):
    y, c = where_ref[2], where_ref[3]
    best_ref[...] = jnp.full(best_ref.shape, -1.0, f32)
    sub, lane = iota((HALF, LANES), 0), iota((HALF, LANES), 1)
    blocks = []
    for core, share in enumerate(SHARES):
        at = jnp.zeros((), i32)
        for q, first in share:
            length = length_of(meta_ref[q, 0], first)
            col = FIRST_ROW[q] + first // LANES
            blocks.append((jnp.where((c == core) & (length > 0), at, PARTIAL), col, 2 * col - at))
            at = at + length
    for t in range(COUNT):
        at = slice(t * HALF, (t + 1) * HALF)
        block = (p0[at, :] + p1[at, :]) + (p2[at, :] + p3[at, :])
        index = y * COUNT + t
        col, shift = jnp.asarray(15, i32), jnp.asarray(0, i32)
        for start, block_col, block_shift in blocks:
            inside = index >= start
            col, shift = jnp.where(inside, block_col, col), jnp.where(inside, block_shift, shift)
        row = jnp.minimum(jnp.maximum(index + shift, 0), 31)
        along = jnp.max(block, axis=1, keepdims=True)
        along = jnp.max(jnp.where(sub + (row & 1) * HALF == lane, along, -1.0), axis=0, keepdims=True)
        row = row >> 1
        best_ref[pl.ds(row, 1), :] = jnp.maximum(best_ref[pl.ds(row, 1), :], along)
        down = jnp.max(block, axis=0, keepdims=True)
        best_ref[pl.ds(col, 1), :] = jnp.maximum(best_ref[pl.ds(col, 1), :], down)
    pos = pos_ref[...]
    pos = jnp.where(pos >= STARTS[1], pos + HALF, pos)
    pos = jnp.where(pos >= STARTS[3] + HALF, pos + HALF, pos)
    row, lane = pos >> 7, pos & (LANES - 1)
    out = jnp.full(pos.shape, -1.0, f32)
    for r in range(15):
        value = jnp.broadcast_to(best_ref[r:r + 1, :], pos.shape)
        value = jnp.take_along_axis(value, lane, axis=1, mode="promise_in_bounds")
        out = jnp.where(row == r, value, out)
    out_ref[:CHIPS, :] = out
    out_ref[CHIPS:, :] = out


def pick_kernel(where_ref, v_ref, code_ref, out_ref):
    c = where_ref[3]
    values = jnp.maximum(v_ref[:CHIPS, :], v_ref[CHIPS:, :])
    values = jnp.max(values.reshape(BINS, 4, LANES), axis=1)
    eye = iota((LANES, LANES), 0) == iota((LANES, LANES), 1)
    code = jnp.max(jnp.where(iota((8, ROWS), 0) == c, code_ref[...], -1), axis=0, keepdims=True)
    code = jnp.max(jnp.where(eye, code.astype(f32), -1.0), axis=1, keepdims=True).astype(i32)
    slot = iota((ROWS, LANES), 1)
    best = jnp.full((ROWS, LANES), -1.0, f32)
    for b in range(BINS):
        best = jnp.where(slot + b * LANES == code, values[b:b + 1], best)
    best = jnp.max(best, axis=1, keepdims=True)
    out_ref[...] = jnp.max(jnp.where(eye, best, -1.0), axis=0, keepdims=True)


def gather_groups(embeddings, cluster_ids):
    split = ("z", "y", "c")
    rows = embeddings.shape[0]
    groups = lax.axis_size("x")
    cap = 2 * rows // groups
    slots = groups * cap
    owner_of = cluster_ids % groups
    onehot = (owner_of[:, None] == jnp.arange(groups, dtype=i32)[None, :]).astype(i32)
    before = jnp.cumsum(onehot, axis=0) - onehot
    rank = jnp.sum(before * onehot, axis=1)
    place = owner_of * cap + rank
    picked = place[None, :] == jnp.arange(slots, dtype=i32)[:, None]
    filled = jnp.any(picked, axis=1)
    source = jnp.sum(jnp.where(picked, jnp.arange(rows, dtype=i32)[None, :], 0), axis=1)
    out_labels = jnp.where(filled, cluster_ids[source], -1)
    squares = jnp.sum(embeddings * embeddings, axis=1, keepdims=True)
    local_unit = (embeddings * lax.rsqrt(squares + 1e-06)).astype(bf16)
    outgoing_unit = jnp.where(filled[:, None], local_unit[source], jnp.zeros((), bf16))
    unit = lax.all_to_all(outgoing_unit, "x", split_axis=0, concat_axis=0, tiled=True)
    labels = lax.all_to_all(out_labels, "x", split_axis=0, concat_axis=0, tiled=True)
    members = lax.axis_size(split)

    def everywhere(v):
        copies = jnp.broadcast_to(v[None], (members,) + v.shape).reshape((members * slots,) + v.shape[1:])
        return lax.all_to_all(copies, split, split_axis=0, concat_axis=0, tiled=True)

    def add_slice(i, scores):
        part = lax.dynamic_slice_in_dim(unit, i * WIDTH, WIDTH, 1)
        return scores + dot_last(part, everywhere(part))

    scores = lax.fori_loop(0, embeddings.shape[1] // WIDTH, add_slice, jnp.zeros((slots, members * slots), f32))
    all_labels = everywhere(labels)
    own = lax.axis_index(split) * slots + jnp.arange(slots, dtype=i32)
    mask = (
        (labels[:, None] == all_labels[None, :])
        & (labels[:, None] >= 0)
        & (own[:, None] != jnp.arange(members * slots, dtype=i32)[None, :])
    )
    scores = jnp.where(mask, scores, -1.0)
    best = jnp.maximum(-1.0, jnp.max(scores, axis=1))
    returned = lax.all_to_all(best, "x", split_axis=0, concat_axis=0, tiled=True)
    return returned[place]


def on_device(embeddings, cluster_ids):
    where = jnp.stack([lax.axis_index(a) for a in ("x", "z", "y", "c")]).astype(i32)
    shape = jax.ShapeDtypeStruct
    half = shape((ROWS + LABEL_ROWS, HALF_WIDTH), bf16)
    keep, send = pl.pallas_call(
        unit_kernel, out_shape=(half, half),
        in_specs=[SCALARS, WHOLE, WHOLE], out_specs=(WHOLE, WHOLE), compiler_params=params(12), name="unit",
    )(where, embeddings, cluster_ids.reshape(1, ROWS))
    got = lax.ppermute(send, "c", [(0, 1), (1, 0)])
    packed, code = pl.pallas_call(
        pack_kernel,
        out_shape=(shape((CHIPS, BLOCK, WIDTH), bf16), shape((8, ROWS), i32)),
        in_specs=[SCALARS, WHOLE, WHOLE], out_specs=(WHOLE, WHOLE), compiler_params=params(20), name="pack",
    )(where, keep, got)
    packed = lax.all_to_all(packed, ("x", "z", "y"), 0, 0, tiled=True)
    table = shape((CHIPS, LANES), i32)
    guests, line, key, pos, meta = pl.pallas_call(
        names_kernel,
        out_shape=(shape((GUESTS, WIDTH), bf16), shape((8, CHIPS * BLOCK), i32), table, table, shape((8, LANES), i32)),
        in_specs=[SCALARS, WHOLE], out_specs=(WHOLE,) * 5, compiler_params=params(12), name="names",
    )(where, packed)
    brought = [lax.ppermute(guests, "z", [(i, (i + s) % 4) for i in range(4)]) for s in (1, 2, 3)]
    share = shape((SHARE_ROWS, WIDTH), bf16)
    slots = CHIPS * BLOCK
    send = pl.pallas_call(
        send_kernel, out_shape=share,
        in_specs=[SCALARS, WHOLE, WHOLE], out_specs=WHOLE, compiler_params=params(16), name="send",
        cost_estimate=pl.CostEstimate(flops=2 * SHARE_ROWS * WIDTH * slots, bytes_accessed=4 << 20, transcendentals=0),
    )(where, packed, line)
    other = lax.ppermute(send, "c", [(0, 1), (1, 0)])
    mine, far, over = pl.pallas_call(
        mine_kernel, out_shape=(share, shape((8, ALL_GUESTS), i32), shape((8, LANES), i32)),
        in_specs=[SCALARS] + [WHOLE] * 5, out_specs=(WHOLE,) * 3, compiler_params=params(20), name="mine",
        cost_estimate=pl.CostEstimate(flops=2 * SHARE_ROWS * WIDTH * slots, bytes_accessed=4 << 20, transcendentals=0),
    )(where, packed, line, send, key, pos)
    brought, mine = lax.optimization_barrier((brought, mine))
    swapped = [lax.ppermute(v, "c", [(0, 1), (1, 0)]) for v in brought]
    raw = pl.pallas_call(
        own_kernel, out_shape=shape((RAW_ROWS, LANES), f32),
        in_specs=[SCALARS] + [WHOLE] * 5, out_specs=WHOLE,
        scratch_shapes=[pltpu.VMEM((SHARE_ROWS, WIDTH), bf16)],
        compiler_params=params(16), name="own",
        cost_estimate=pl.CostEstimate(flops=2 * RAW_ROWS * LANES * WIDTH, bytes_accessed=4 << 20, transcendentals=0),
    )(where, mine, *brought, far)
    partial = pl.pallas_call(
        gram_kernel,
        out_shape=[shape((CHUNK, LANES), f32)] * 4,
        in_specs=[SCALARS, SCALARS] + [WHOLE] * 6, out_specs=[WHOLE] * 4,
        scratch_shapes=[pltpu.VMEM((PARTIAL + CAPS[0], LANES), f32), pltpu.VMEM((SHARE_ROWS, WIDTH), bf16)],
        compiler_params=params(16), name="gram",
    )(where, meta, other, *swapped, far, raw)
    arrived = [partial[0]] + [
        lax.ppermute(partial[s], "y", [(i, (i + s) % 4) for i in range(4)]) for s in (1, 2, 3)
    ]
    arrived, fits = lax.optimization_barrier((arrived, over[0, 0] == 0))
    best = pl.pallas_call(
        max_kernel,
        out_shape=shape((2 * CHIPS, LANES), f32),
        in_specs=[SCALARS] * 2 + [WHOLE] * 5, out_specs=WHOLE,
        scratch_shapes=[pltpu.VMEM((16, LANES), f32)],
        compiler_params=params(8), name="maxima",
    )(where, meta, *arrived, pos)
    back = lax.all_to_all(best.reshape(2 * CHIPS, 1, LANES), ("c", "x", "z", "y"), 0, 0, tiled=True)
    fitted = pl.pallas_call(
        pick_kernel,
        out_shape=shape((1, ROWS), f32),
        in_specs=[SCALARS, WHOLE, WHOLE], out_specs=WHOLE, compiler_params=params(8), name="pick",
    )(where, back.reshape(2 * CHIPS, LANES), code).reshape(ROWS)
    return lax.cond(
        fits,
        lambda fitted, embeddings, cluster_ids: fitted,
        lambda fitted, embeddings, cluster_ids: gather_groups(embeddings, cluster_ids),
        fitted, embeddings, cluster_ids,
    )


def solution(mesh):
    axes = ("x", "z", "y", "c")
    grid = Mesh(mesh.devices.reshape(4, 4, 4, 2), axes)
    return jax.shard_map(
        on_device, mesh=grid, in_specs=(P(axes, None), P(axes)), out_specs=P(axes), check_vma=False
    )
```

```python
import jax
import jax.numpy as jnp
from jax import lax
from jax.experimental import pallas as pl
from jax.experimental.pallas import tpu as pltpu
from jax.sharding import Mesh, PartitionSpec as P

ROWS = 128
HALF_WIDTH = 2048
WIDTH = 512
LABEL_ROWS = 16
BINS = 16
CHIPS = 64
BLOCK = 24
SLOTS = BLOCK - 1
GROUP = 32
GUESTS = 64
ALL_GUESTS = 4 * GUESTS
GUEST = 4096
LANES = 128
CAPS = (704, 512, 320, 192)
STARTS = (0, 704, 1216, 1536)
HALF = 64
COUNT = 7
CHUNK = COUNT * HALF
PARTIAL = 4 * CHUNK
SHARES = (
    tuple((q, first) for q, first in ((0, 0), (0, 128), (2, 0), (2, 128), (2, 256))),
    tuple((q, first) for q, first in (
        (0, 256), (0, 384), (0, 512), (0, 640), (1, 0), (1, 128), (1, 256), (1, 384), (3, 0), (3, 128))),
)
BASES = ({0: 0, 2: 704}, {0: -256, 1: 448, 3: 960})
SHARE_ROWS = 1216
SEGMENTS = (
    (0, 256, 0, None), (256, 448, 256, 0), (704, 256, None, 448), (960, 256, None, 704),
    (1216, 320, 704, None), (1536, 192, None, 960),
)
f32, bf16, i32 = jnp.float32, jnp.bfloat16, jnp.int32
WHOLE = pl.BlockSpec(memory_space=pltpu.VMEM)
SCALARS = pl.BlockSpec(memory_space=pltpu.SMEM)


def params(mib):
    return pltpu.CompilerParams(vmem_limit_bytes=mib * 1024 * 1024)


def index_on(axis):
    return lax.axis_index(axis)


def iota(shape, dim):
    return lax.broadcasted_iota(i32, shape, dim)


def dot_last(a, b):
    return lax.dot_general(a, b, (((1,), (1,)), ((), ())), preferred_element_type=f32)


def dot(a, b):
    return lax.dot_general(a, b, (((1,), (0,)), ((), ())), preferred_element_type=f32)


def as_bf16(mask):
    return jnp.where(mask, 1.0, 0.0).astype(bf16)


def bin_of(labels):
    rank, residue = labels >> 2, labels & 3
    row, col = rank >> 2, rank & 3
    col = jnp.where((row & 1) == 1, 3 - col, col)
    return 4 * col + ((row - residue) & 3)


def unit_kernel(x_ref, ids_ref, keep_ref, send_ref):
    c = index_on("c")
    x = x_ref[...]
    scale = lax.rsqrt(jnp.sum(x * x, axis=1, keepdims=True) + 1e-06)
    ids = jnp.concatenate([ids_ref[...].astype(f32), jnp.zeros((1, HALF_WIDTH - ROWS), f32)], axis=1)
    ids = jnp.broadcast_to(ids, (LABEL_ROWS, HALF_WIDTH)).astype(bf16)
    for half, out_ref in ((c, keep_ref), (1 - c, send_ref)):
        columns = pl.ds(pl.multiple_of(half * HALF_WIDTH, HALF_WIDTH), HALF_WIDTH)
        out_ref[:ROWS, :] = (x_ref[:, columns] * scale).astype(bf16)
        out_ref[ROWS:, :] = ids


def pack_kernel(keep_ref, got_ref, out_ref, code_ref):
    y, first = index_on("y"), index_on("c") == 0
    kept = jnp.max(keep_ref[ROWS:, :ROWS].astype(f32), axis=0, keepdims=True)
    got = jnp.max(got_ref[ROWS:, :ROWS].astype(f32), axis=0, keepdims=True)
    labels = jnp.concatenate([jnp.where(first, kept, got), jnp.where(first, got, kept)], axis=0).astype(i32)
    bins = bin_of(labels)
    upper = as_bf16(iota((ROWS, ROWS), 0) < iota((ROWS, ROWS), 1))

    def ranks_within(masks):
        member = jnp.concatenate([jnp.where(mask, 1.0, 0.0) for mask in masks], axis=0)
        row, col = iota((member.shape[0],) * 2, 0), iota((member.shape[0],) * 2, 1)
        earlier = dot(as_bf16(((row >> 1) == (col >> 1)) & (col < row)), member.astype(bf16))
        ranks = member * (dot(member.astype(bf16), upper) + jnp.sum(earlier, axis=1, keepdims=True))
        rank = sum(ranks[2 * b:2 * b + 2] for b in range(len(masks)))
        return rank.astype(i32), jnp.sum(member, axis=1, keepdims=True)

    rank, sizes = ranks_within([bins == b for b in range(BINS)])
    quad, line = bins >> 2, bins & 3
    extra = rank >= SLOTS
    turn, _ = ranks_within([extra & (quad == q) for q in range(4)])
    room, used = [], []
    for step in range(4):
        taken = jnp.zeros(labels.shape, f32)
        for at in range(4):
            size = jnp.zeros(labels.shape, f32)
            for q in range(4):
                b = 4 * q + at
                size = jnp.where(quad == q, sizes[2 * b:2 * b + 1] + sizes[2 * b + 1:2 * b + 2], size)
            taken = jnp.where(((at - y) & 3) == step, size, taken)
        taken = jnp.minimum(taken.astype(i32), SLOTS)
        used.append(taken)
        room.append(SLOTS - taken)
    placed = jnp.logical_not(extra)
    to_line, to_slot, start = line, rank, jnp.zeros(labels.shape, i32)
    for step in range(4):
        here = extra & (turn >= start) & (turn < start + room[step])
        to_line = jnp.where(here, (y + step) & 3, to_line)
        to_slot = jnp.where(here, used[step] + turn - start, to_slot)
        placed = placed | here
        start = start + room[step]
    lane = jnp.where(placed, to_line * GROUP + to_slot, -1)
    place = jnp.where(placed, (quad * 4 + to_line) * BLOCK + to_slot, -1)
    code_ref[...] = jnp.concatenate([jnp.where(placed, bins * LANES + lane, -1)] * 4, axis=0)
    docs = 2 * ROWS
    flat = lambda v: jnp.concatenate([v[:1], v[1:]], axis=1)
    label_row = flat(labels)
    counts = dot_last(jnp.ones((8, docs), bf16), as_bf16(iota((LANES, docs), 0) == label_row))[:1]
    named = jnp.where(iota((8, docs), 0) == flat(quad), (label_row + 1).astype(f32), 0.0).astype(bf16)
    names = dot_last(named, as_bf16(iota((LANES, docs), 0) == flat(lane)))
    own = jnp.where(first, place[:1], place[1:])
    other = jnp.where(first, place[1:], place[:1])
    onehot = as_bf16(iota((BINS * BLOCK, docs), 0) == jnp.concatenate([own, other], axis=1))
    is_last = iota((BLOCK, WIDTH), 0) == SLOTS
    for y in range(4):
        columns = slice(y * WIDTH, (y + 1) * WIDTH)
        x = jnp.concatenate([keep_ref[:ROWS, columns], got_ref[:ROWS, columns]], axis=0)
        packed = dot(onehot, x)
        for b in range(BINS):
            extra = jnp.concatenate([names[b // 4:b // 4 + 1], counts, jnp.zeros((1, 2 * LANES), f32)], axis=1)
            out_ref[4 * b + y] = jnp.where(is_last, extra, packed[b * BLOCK:(b + 1) * BLOCK]).astype(bf16)


def labels_of(x_ref):
    tail = x_ref[:, BLOCK - 8:, :2 * LANES].astype(f32)
    tail = jnp.max(jnp.where(iota(tail.shape, 1) == 7, tail, 0.0), axis=1)
    return tail[:, :LANES].astype(i32) - 1, tail[:, LANES:].astype(bf16)


def counts_of(chip_counts):
    row, col = iota((LANES, LANES), 0), iota((LANES, LANES), 1)
    in_bin = (bin_of(row) == col) & (row < 4 * BINS)
    counts = [dot(chip_counts, as_bf16(in_bin & ((row & 3) == r))) for r in range(4)]
    return counts, [jnp.sum(v, axis=0, keepdims=True) for v in counts]


def in_order(sizes):
    a, b = jnp.maximum(sizes[0], sizes[1]), jnp.minimum(sizes[0], sizes[1])
    c, d = jnp.maximum(sizes[2], sizes[3]), jnp.minimum(sizes[2], sizes[3])
    first, e = jnp.maximum(a, c), jnp.minimum(a, c)
    g, fourth = jnp.maximum(b, d), jnp.minimum(b, d)
    return first, jnp.maximum(e, g), jnp.minimum(e, g), fourth


def names_kernel(x_ref, guest_ref, line_ref, key_ref, pos_ref, meta_ref):
    mine, z = index_on("x") * 4 + index_on("z"), index_on("z")
    labels, chip_counts = labels_of(x_ref)
    _, sizes = counts_of(chip_counts)
    here = iota((1, LANES), 1) == mine
    own = lambda v: jnp.sum(jnp.where(here, v, 0.0), axis=1, keepdims=True)
    wide = lambda v: jnp.broadcast_to(v, (1, LANES))
    ordered = in_order(sizes)
    meta_ref[...] = jnp.concatenate([wide(own(v)) for v in ordered] * 2, axis=0).astype(i32)

    n = [own(v) for v in sizes]
    row, col = iota((LANES, LANES), 0), iota((LANES, LANES), 1)
    lane = iota(labels.shape, 1)
    group = lane >> 5
    valid = labels >= 0
    home = bin_of(labels) & 3
    at_home = valid & (home == z)
    upper = as_bf16(row < col)
    lower = as_bf16(iota((CHIPS, CHIPS), 1) < iota((CHIPS, CHIPS), 0))
    pos = jnp.full(labels.shape, -1.0, f32)
    for r in range(4):
        place = sum(
            jnp.where((n[q] > n[r]) | ((n[q] == n[r]) & (q < r)), 1.0, 0.0) for q in range(4) if q != r
        )
        start = jnp.where(
            place < 0.5, float(STARTS[0]),
            jnp.where(place < 1.5, float(STARTS[1]), jnp.where(place < 2.5, float(STARTS[2]), float(STARTS[3]))),
        )
        member = at_home & ((labels & 3) == r)
        member16 = as_bf16(member)
        rank = dot(member16, upper) + jnp.sum(dot(lower, member16), axis=1, keepdims=True)
        pos = jnp.where(member, start + rank, pos)
    pos = pos.astype(i32)
    pos_ref[...] = pos
    guest = valid & (home != group)
    guest16 = as_bf16(guest)
    same = (row >> 5) == (col >> 5)
    turn = dot(guest16, as_bf16(same & (row < col))) + dot(dot(lower, guest16).astype(bf16), as_bf16(same))
    turn = turn.astype(i32)
    away = at_home & (group != z) & (turn < GUESTS)
    key_ref[...] = jnp.where(away, (((z - group) & 3) - 1) * GUESTS + turn, -1)
    per, groups = 16, CHIPS // 16
    value = jnp.where(group == z, jnp.where(guest, GUEST + turn, pos + 1), 0).astype(f32)
    value = pltpu.roll(value, lax.rem(LANES - GROUP * z, LANES), 1)
    value = jnp.where(lane < BLOCK, value, 0.0)
    lined = jnp.zeros((8, per * BLOCK), f32)
    for t in range(per):
        rows = jnp.concatenate([value[per * g + t:per * g + t + 1] for g in range(groups)] * 2, axis=0)
        rows = jnp.concatenate([rows, jnp.zeros((8, per * BLOCK - LANES), f32)], axis=1)
        lined = lined + (pltpu.roll(rows, t * BLOCK, 1) if t else rows)
    slots = jnp.concatenate([lined[g:g + 1] for g in range(groups)], axis=1).astype(i32)
    line_ref[...] = jnp.broadcast_to(slots, line_ref.shape)
    onehot = as_bf16(iota((GUESTS, CHIPS * BLOCK), 0) + GUEST == slots)
    guest_ref[...] = dot(onehot, x_ref[...].reshape(CHIPS * BLOCK, WIDTH)).astype(bf16)


def sorted_rows(segment, slots, x):
    onehot = as_bf16(iota((segment[1], x.shape[0]), 0) + (segment[0] + 1) == slots)
    return dot(onehot, x).astype(bf16)


def send_kernel(x_ref, line_ref, send_ref):
    x = x_ref[...].reshape(CHIPS * BLOCK, WIDTH)
    slots = line_ref[:1, :]
    for me in range(2):
        @pl.when(index_on("c") == me)
        def _():
            for segment in SEGMENTS:
                at = segment[2 + 1 - me]
                if at is not None:
                    send_ref[at:at + segment[1], :] = sorted_rows(segment, slots, x)


def mine_kernel(x_ref, line_ref, send_ref, key_ref, pos_ref, mine_ref, far_ref, over_ref):
    x = x_ref[...].reshape(CHIPS * BLOCK, WIDTH)
    slots = line_ref[:1, :]
    for core in range(2):
        @pl.when(index_on("c") == core)
        def _():
            for segment in SEGMENTS:
                at, sent = segment[2 + core], segment[2 + 1 - core]
                if at is not None:
                    rows = segment[1]
                    mine_ref[at:at + rows, :] = (
                        send_ref[sent:sent + rows, :] if sent is not None else sorted_rows(segment, slots, x)
                    )
    total = jnp.zeros((8, ALL_GUESTS), f32)
    step = 16
    for first in range(0, CHIPS, step):
        flat = lambda ref: jnp.concatenate([ref[s:s + 1, :] for s in range(first, first + step)], axis=1)
        places = flat(pos_ref) + 1
        parts = jnp.where(iota((8, step * LANES), 0) == 0, places >> 5, places & 31).astype(f32).astype(bf16)
        total = total + dot_last(parts, as_bf16(iota((ALL_GUESTS, step * LANES), 0) == flat(key_ref)))
    far_ref[...] = jnp.broadcast_to((32.0 * total[:1] + total[1:2]).astype(i32), far_ref.shape)
    _, chip_counts = labels_of(x_ref)
    counts, sizes = counts_of(chip_counts)
    ordered = in_order(sizes)
    over = jnp.zeros((1, LANES), f32)
    for size, cap in zip(ordered, CAPS):
        over = jnp.maximum(over, jnp.where(size > cap, 1.0, 0.0))
    for share in SHARES:
        length = sum(jnp.maximum(jnp.floor((ordered[q] + 63.0) * (1 / 64)) - first // HALF, 0.0) for q, first in share)
        over = jnp.maximum(over, jnp.where(length > 4 * COUNT, 1.0, 0.0))
    taken = counts[0] + counts[1] + counts[2] + counts[3]
    extra, room = jnp.maximum(taken - SLOTS, 0.0), jnp.maximum(SLOTS - taken, 0.0)
    row, col = iota((LANES, LANES), 0), iota((LANES, LANES), 1)
    same = (row >> 2) == (col >> 2)
    wanted = dot(extra.astype(bf16), as_bf16(same))
    before = jnp.zeros(taken.shape, f32)
    for turn in range(4):
        earlier = same & (((row - turn) & 3) < ((col - turn) & 3))
        before = jnp.where((iota(taken.shape, 0) & 3) == turn, dot(room.astype(bf16), as_bf16(earlier)), before)
    held = jnp.sum(jnp.minimum(jnp.maximum(wanted - before, 0.0), room), axis=0, keepdims=True)
    over = jnp.maximum(over, jnp.where(held > GUESTS, 1.0, 0.0))
    full = jnp.where(wanted > dot(room.astype(bf16), as_bf16(same)), 1.0, 0.0)
    over = jnp.maximum(over, jnp.max(full, axis=0, keepdims=True))
    over_ref[...] = jnp.broadcast_to(jnp.max(over, axis=1, keepdims=True), over_ref.shape).astype(i32)


def add_guests(core, base_ref, guests, far_ref, out_ref):
    guests = jnp.concatenate([ref[...] for ref in guests] + [guests[0][...]], axis=0)
    far = far_ref[:1, :]
    for segment in SEGMENTS:
        at, rows = segment[2 + core], segment[1]
        if at is not None:
            out_ref[at:at + rows, :] = base_ref[at:at + rows, :] + sorted_rows(segment, far, guests)


def blocks_of(core):
    for q, first in SHARES[core]:
        at = BASES[core][q] + first
        yield q, first, pl.ds(at, CAPS[q] - first), pl.ds(at, LANES)


RAW_ROWS = max(sum(CAPS[q] - first for q, first in share) for share in SHARES)


def own_kernel(x_ref, g1, g2, g3, far_ref, raw_ref, rows_ref):
    for core in range(2):
        @pl.when(index_on("c") == core)
        def _():
            add_guests(core, x_ref, (g1, g2, g3), far_ref, rows_ref)
            at = 0
            for q, first, left, right in blocks_of(core):
                rows = CAPS[q] - first
                raw_ref[at:at + rows, :] = dot_last(rows_ref[left, :], rows_ref[right, :])
                at += rows


def length_of(size, first):
    return jnp.maximum(((size + HALF - 1) >> 6) - first // HALF, 0)


def gram_kernel(meta_ref, x_ref, g1, g2, g3, far_ref, raw_ref, out0, out1, out2, out3, part_ref, rows_ref):
    y, c = index_on("y"), index_on("c")
    part_ref[...] = jnp.full(part_ref.shape, -4.0, f32)
    for core in range(2):
        @pl.when(c == core)
        def _():
            add_guests(core, x_ref, (g1, g2, g3), far_ref, rows_ref)
            at, to = 0, jnp.zeros((), i32)
            for q, first, left, right in blocks_of(core):
                rows = CAPS[q] - first
                score = raw_ref[at:at + rows, :] + dot_last(rows_ref[left, :], rows_ref[right, :])
                at += rows
                size = meta_ref[q, 0]
                i, j = iota(score.shape, 0), iota(score.shape, 1)
                keep = (i < size - first) & (j < size - first) & (i != j)
                part_ref[pl.ds(pl.multiple_of(to, HALF), rows), :] = jnp.where(keep, score, -4.0)
                to = jnp.minimum(to + HALF * length_of(size, first), PARTIAL)
    for shift, out in enumerate((out0, out1, out2, out3)):
        out[...] = part_ref[pl.ds(pl.multiple_of(lax.rem(y + shift, 4) * CHUNK, HALF), CHUNK), :]


FIRST_ROW = (0, 6, 10, 13)


def max_kernel(meta_ref, p0, p1, p2, p3, pos_ref, out_ref, best_ref):
    y, c = index_on("y"), index_on("c")
    best_ref[...] = jnp.full(best_ref.shape, -1.0, f32)
    sub, lane = iota((HALF, LANES), 0), iota((HALF, LANES), 1)
    blocks = []
    for core, share in enumerate(SHARES):
        at = jnp.zeros((), i32)
        for q, first in share:
            length = length_of(meta_ref[q, 0], first)
            col = FIRST_ROW[q] + first // LANES
            blocks.append((jnp.where((c == core) & (length > 0), at, PARTIAL), col, 2 * col - at))
            at = at + length
    for t in range(COUNT):
        at = slice(t * HALF, (t + 1) * HALF)
        block = (p0[at, :] + p1[at, :]) + (p2[at, :] + p3[at, :])
        index = y * COUNT + t
        col, shift = jnp.asarray(15, i32), jnp.asarray(0, i32)
        for start, block_col, block_shift in blocks:
            inside = index >= start
            col, shift = jnp.where(inside, block_col, col), jnp.where(inside, block_shift, shift)
        row = jnp.minimum(jnp.maximum(index + shift, 0), 31)
        along = jnp.max(block, axis=1, keepdims=True)
        along = jnp.max(jnp.where(sub + (row & 1) * HALF == lane, along, -1.0), axis=0, keepdims=True)
        row = row >> 1
        best_ref[pl.ds(row, 1), :] = jnp.maximum(best_ref[pl.ds(row, 1), :], along)
        down = jnp.max(block, axis=0, keepdims=True)
        best_ref[pl.ds(col, 1), :] = jnp.maximum(best_ref[pl.ds(col, 1), :], down)
    pos = pos_ref[...]
    pos = jnp.where(pos >= STARTS[1], pos + HALF, pos)
    pos = jnp.where(pos >= STARTS[3] + HALF, pos + HALF, pos)
    row, lane = pos >> 7, pos & (LANES - 1)
    out = jnp.full(pos.shape, -1.0, f32)
    for r in range(15):
        value = jnp.broadcast_to(best_ref[r:r + 1, :], pos.shape)
        value = jnp.take_along_axis(value, lane, axis=1, mode="promise_in_bounds")
        out = jnp.where(row == r, value, out)
    out_ref[:CHIPS, :] = out
    out_ref[CHIPS:, :] = out


def pick_kernel(v_ref, code_ref, out_ref):
    c = index_on("c")
    values = jnp.maximum(v_ref[:CHIPS, :], v_ref[CHIPS:, :])
    values = jnp.max(values.reshape(BINS, 4, LANES), axis=1)
    eye = iota((LANES, LANES), 0) == iota((LANES, LANES), 1)
    code = jnp.max(jnp.where(iota((8, ROWS), 0) == c, code_ref[...], -1), axis=0, keepdims=True)
    code = jnp.max(jnp.where(eye, code.astype(f32), -1.0), axis=1, keepdims=True).astype(i32)
    slot = iota((ROWS, LANES), 1)
    best = jnp.full((ROWS, LANES), -1.0, f32)
    for b in range(BINS):
        best = jnp.where(slot + b * LANES == code, values[b:b + 1], best)
    best = jnp.max(best, axis=1, keepdims=True)
    out_ref[...] = jnp.max(jnp.where(eye, best, -1.0), axis=0, keepdims=True)


def gather_groups(embeddings, cluster_ids):
    split = ("z", "y", "c")
    rows = embeddings.shape[0]
    groups = lax.axis_size("x")
    cap = 2 * rows // groups
    slots = groups * cap
    owner_of = cluster_ids % groups
    onehot = (owner_of[:, None] == jnp.arange(groups, dtype=i32)[None, :]).astype(i32)
    before = jnp.cumsum(onehot, axis=0) - onehot
    rank = jnp.sum(before * onehot, axis=1)
    place = owner_of * cap + rank
    picked = place[None, :] == jnp.arange(slots, dtype=i32)[:, None]
    filled = jnp.any(picked, axis=1)
    source = jnp.sum(jnp.where(picked, jnp.arange(rows, dtype=i32)[None, :], 0), axis=1)
    out_labels = jnp.where(filled, cluster_ids[source], -1)
    squares = jnp.sum(embeddings * embeddings, axis=1, keepdims=True)
    local_unit = (embeddings * lax.rsqrt(squares + 1e-06)).astype(bf16)
    outgoing_unit = jnp.where(filled[:, None], local_unit[source], jnp.zeros((), bf16))
    unit = lax.all_to_all(outgoing_unit, "x", split_axis=0, concat_axis=0, tiled=True)
    labels = lax.all_to_all(out_labels, "x", split_axis=0, concat_axis=0, tiled=True)
    members = lax.axis_size(split)

    def everywhere(v):
        copies = jnp.broadcast_to(v[None], (members,) + v.shape).reshape((members * slots,) + v.shape[1:])
        return lax.all_to_all(copies, split, split_axis=0, concat_axis=0, tiled=True)

    def add_slice(i, scores):
        part = lax.dynamic_slice_in_dim(unit, i * WIDTH, WIDTH, 1)
        return scores + dot_last(part, everywhere(part))

    scores = lax.fori_loop(0, embeddings.shape[1] // WIDTH, add_slice, jnp.zeros((slots, members * slots), f32))
    all_labels = everywhere(labels)
    own = lax.axis_index(split) * slots + jnp.arange(slots, dtype=i32)
    mask = (
        (labels[:, None] == all_labels[None, :])
        & (labels[:, None] >= 0)
        & (own[:, None] != jnp.arange(members * slots, dtype=i32)[None, :])
    )
    scores = jnp.where(mask, scores, -1.0)
    best = jnp.maximum(-1.0, jnp.max(scores, axis=1))
    returned = lax.all_to_all(best, "x", split_axis=0, concat_axis=0, tiled=True)
    return returned[place]


def on_device(embeddings, cluster_ids):
    shape = jax.ShapeDtypeStruct
    half = shape((ROWS + LABEL_ROWS, HALF_WIDTH), bf16)
    keep, send = pl.pallas_call(
        unit_kernel, out_shape=(half, half),
        in_specs=[WHOLE, WHOLE], out_specs=(WHOLE, WHOLE), compiler_params=params(12), name="unit",
    )(embeddings, cluster_ids.reshape(1, ROWS))
    got = lax.ppermute(send, "c", [(0, 1), (1, 0)])
    packed, code = pl.pallas_call(
        pack_kernel,
        out_shape=(shape((CHIPS, BLOCK, WIDTH), bf16), shape((8, ROWS), i32)),
        in_specs=[WHOLE, WHOLE], out_specs=(WHOLE, WHOLE), compiler_params=params(20), name="pack",
    )(keep, got)
    packed = lax.all_to_all(packed, ("x", "z", "y"), 0, 0, tiled=True)
    table = shape((CHIPS, LANES), i32)
    guests, line, key, pos, meta = pl.pallas_call(
        names_kernel,
        out_shape=(shape((GUESTS, WIDTH), bf16), shape((8, CHIPS * BLOCK), i32), table, table, shape((8, LANES), i32)),
        in_specs=[WHOLE], out_specs=(WHOLE,) * 5, compiler_params=params(12), name="names",
    )(packed)
    brought = [lax.ppermute(guests, "z", [(i, (i + s) % 4) for i in range(4)]) for s in (1, 2, 3)]
    share = shape((SHARE_ROWS, WIDTH), bf16)
    slots = CHIPS * BLOCK
    send = pl.pallas_call(
        send_kernel, out_shape=share,
        in_specs=[WHOLE, WHOLE], out_specs=WHOLE, compiler_params=params(16), name="send",
        cost_estimate=pl.CostEstimate(flops=2 * SHARE_ROWS * WIDTH * slots, bytes_accessed=4 << 20, transcendentals=0),
    )(packed, line)
    other = lax.ppermute(send, "c", [(0, 1), (1, 0)])
    mine, far, over = pl.pallas_call(
        mine_kernel, out_shape=(share, shape((8, ALL_GUESTS), i32), shape((8, LANES), i32)),
        in_specs=[WHOLE] * 5, out_specs=(WHOLE,) * 3, compiler_params=params(20), name="mine",
        cost_estimate=pl.CostEstimate(flops=2 * SHARE_ROWS * WIDTH * slots, bytes_accessed=4 << 20, transcendentals=0),
    )(packed, line, send, key, pos)
    brought, mine = lax.optimization_barrier((brought, mine))
    swapped = [lax.ppermute(v, "c", [(0, 1), (1, 0)]) for v in brought]
    raw = pl.pallas_call(
        own_kernel, out_shape=shape((RAW_ROWS, LANES), f32),
        in_specs=[WHOLE] * 5, out_specs=WHOLE,
        scratch_shapes=[pltpu.VMEM((SHARE_ROWS, WIDTH), bf16)],
        compiler_params=params(16), name="own",
        cost_estimate=pl.CostEstimate(flops=2 * RAW_ROWS * LANES * WIDTH, bytes_accessed=4 << 20, transcendentals=0),
    )(mine, *brought, far)
    partial = pl.pallas_call(
        gram_kernel,
        out_shape=[shape((CHUNK, LANES), f32)] * 4,
        in_specs=[SCALARS] + [WHOLE] * 6, out_specs=[WHOLE] * 4,
        scratch_shapes=[pltpu.VMEM((PARTIAL + CAPS[0], LANES), f32), pltpu.VMEM((SHARE_ROWS, WIDTH), bf16)],
        compiler_params=params(16), name="gram",
    )(meta, other, *swapped, far, raw)
    arrived = [partial[0]] + [
        lax.ppermute(partial[s], "y", [(i, (i + s) % 4) for i in range(4)]) for s in (1, 2, 3)
    ]
    arrived, fits = lax.optimization_barrier((arrived, over[0, 0] == 0))
    best = pl.pallas_call(
        max_kernel,
        out_shape=shape((2 * CHIPS, LANES), f32),
        in_specs=[SCALARS] + [WHOLE] * 5, out_specs=WHOLE,
        scratch_shapes=[pltpu.VMEM((16, LANES), f32)],
        compiler_params=params(8), name="maxima",
    )(meta, *arrived, pos)
    back = lax.all_to_all(best.reshape(2 * CHIPS, 1, LANES), ("c", "x", "z", "y"), 0, 0, tiled=True)
    fitted = pl.pallas_call(
        pick_kernel,
        out_shape=shape((1, ROWS), f32),
        in_specs=[WHOLE, WHOLE], out_specs=WHOLE, compiler_params=params(8), name="pick",
    )(back.reshape(2 * CHIPS, LANES), code).reshape(ROWS)
    return lax.cond(
        fits,
        lambda fitted, embeddings, cluster_ids: fitted,
        lambda fitted, embeddings, cluster_ids: gather_groups(embeddings, cluster_ids),
        fitted, embeddings, cluster_ids,
    )


def solution(mesh):
    axes = ("x", "z", "y", "c")
    grid = Mesh(mesh.devices.reshape(4, 4, 4, 2), axes)
    return jax.shard_map(
        on_device, mesh=grid, in_specs=(P(axes, None), P(axes)), out_specs=P(axes), check_vma=False
    )
```

```python
import functools

import jax
import jax.numpy as jnp
from jax import lax
from jax.experimental import pallas as pl
from jax.experimental.pallas import tpu as pltpu
from jax.sharding import Mesh, PartitionSpec as P

ROWS = 128
HALF_WIDTH = 2048
WIDTH = 512
LABEL_ROWS = 16
BINS = 16
CHIPS = 64
BLOCKS = (24, 32)
GROUP = 32
GUESTS = 64
ALL_GUESTS = 4 * GUESTS
GUEST = 4096
LANES = 128
CAPS = (704, 512, 320, 192)
STARTS = (0, 704, 1216, 1536)
HALF = 64
COUNT = 7
CHUNK = COUNT * HALF
PARTIAL = 4 * CHUNK
SHARES = (
    tuple((q, first) for q, first in ((0, 0), (0, 128), (2, 0), (2, 128), (2, 256))),
    tuple((q, first) for q, first in (
        (0, 256), (0, 384), (0, 512), (0, 640), (1, 0), (1, 128), (1, 256), (1, 384), (3, 0), (3, 128))),
)
BASES = ({0: 0, 2: 704}, {0: -256, 1: 448, 3: 960})
SHARE_ROWS = 1216
SEGMENTS = (
    (0, 256, 0, None), (256, 448, 256, 0), (704, 256, None, 448), (960, 256, None, 704),
    (1216, 320, 704, None), (1536, 192, None, 960),
)
f32, bf16, i32 = jnp.float32, jnp.bfloat16, jnp.int32
WHOLE = pl.BlockSpec(memory_space=pltpu.VMEM)


def params(mib):
    return pltpu.CompilerParams(vmem_limit_bytes=mib * 1024 * 1024)


def index_on(axis):
    return lax.axis_index(axis)


def iota(shape, dim):
    return lax.broadcasted_iota(i32, shape, dim)


def dot_last(a, b):
    return lax.dot_general(a, b, (((1,), (1,)), ((), ())), preferred_element_type=f32)


def dot(a, b):
    return lax.dot_general(a, b, (((1,), (0,)), ((), ())), preferred_element_type=f32)


def as_bf16(mask):
    return jnp.where(mask, 1.0, 0.0).astype(bf16)


def bin_of(labels):
    rank, residue = labels >> 2, labels & 3
    row, col = rank >> 2, rank & 3
    col = jnp.where((row & 1) == 1, 3 - col, col)
    return 4 * col + ((row - residue) & 3)


def unit_kernel(x_ref, ids_ref, keep_ref, send_ref):
    c = index_on("c")
    x = x_ref[...]
    scale = lax.rsqrt(jnp.sum(x * x, axis=1, keepdims=True) + 1e-06)
    ids = jnp.concatenate([ids_ref[...].astype(f32), jnp.zeros((1, HALF_WIDTH - ROWS), f32)], axis=1)
    ids = jnp.broadcast_to(ids, (LABEL_ROWS, HALF_WIDTH)).astype(bf16)
    for half, out_ref in ((c, keep_ref), (1 - c, send_ref)):
        columns = pl.ds(pl.multiple_of(half * HALF_WIDTH, HALF_WIDTH), HALF_WIDTH)
        out_ref[:ROWS, :] = (x_ref[:, columns] * scale).astype(bf16)
        out_ref[ROWS:, :] = ids


def pack_kernel(block, keep_ref, got_ref, out_ref, code_ref):
    y, first = index_on("y"), index_on("c") == 0
    kept = jnp.max(keep_ref[ROWS:, :ROWS].astype(f32), axis=0, keepdims=True)
    got = jnp.max(got_ref[ROWS:, :ROWS].astype(f32), axis=0, keepdims=True)
    labels = jnp.concatenate([jnp.where(first, kept, got), jnp.where(first, got, kept)], axis=0).astype(i32)
    bins = bin_of(labels)
    upper = as_bf16(iota((ROWS, ROWS), 0) < iota((ROWS, ROWS), 1))

    def ranks_within(masks):
        member = jnp.concatenate([jnp.where(mask, 1.0, 0.0) for mask in masks], axis=0)
        row, col = iota((member.shape[0],) * 2, 0), iota((member.shape[0],) * 2, 1)
        earlier = dot(as_bf16(((row >> 1) == (col >> 1)) & (col < row)), member.astype(bf16))
        ranks = member * (dot(member.astype(bf16), upper) + jnp.sum(earlier, axis=1, keepdims=True))
        rank = sum(ranks[2 * b:2 * b + 2] for b in range(len(masks)))
        return rank.astype(i32), jnp.sum(member, axis=1, keepdims=True)

    rank, sizes = ranks_within([bins == b for b in range(BINS)])
    quad, line = bins >> 2, bins & 3
    extra = rank >= (block - 1)
    turn, _ = ranks_within([extra & (quad == q) for q in range(4)])
    room, used = [], []
    for step in range(4):
        taken = jnp.zeros(labels.shape, f32)
        for at in range(4):
            size = jnp.zeros(labels.shape, f32)
            for q in range(4):
                b = 4 * q + at
                size = jnp.where(quad == q, sizes[2 * b:2 * b + 1] + sizes[2 * b + 1:2 * b + 2], size)
            taken = jnp.where(((at - y) & 3) == step, size, taken)
        taken = jnp.minimum(taken.astype(i32), (block - 1))
        used.append(taken)
        room.append((block - 1) - taken)
    placed = jnp.logical_not(extra)
    to_line, to_slot, start = line, rank, jnp.zeros(labels.shape, i32)
    for step in range(4):
        here = extra & (turn >= start) & (turn < start + room[step])
        to_line = jnp.where(here, (y + step) & 3, to_line)
        to_slot = jnp.where(here, used[step] + turn - start, to_slot)
        placed = placed | here
        start = start + room[step]
    lane = jnp.where(placed, to_line * GROUP + to_slot, -1)
    place = jnp.where(placed, (quad * 4 + to_line) * block + to_slot, -1)
    code_ref[...] = jnp.concatenate([jnp.where(placed, bins * LANES + lane, -1)] * 4, axis=0)
    docs = 2 * ROWS
    flat = lambda v: jnp.concatenate([v[:1], v[1:]], axis=1)
    label_row = flat(labels)
    counts = dot_last(jnp.ones((8, docs), bf16), as_bf16(iota((LANES, docs), 0) == label_row))[:1]
    named = jnp.where(iota((8, docs), 0) == flat(quad), (label_row + 1).astype(f32), 0.0).astype(bf16)
    names = dot_last(named, as_bf16(iota((LANES, docs), 0) == flat(lane)))
    own = jnp.where(first, place[:1], place[1:])
    other = jnp.where(first, place[1:], place[:1])
    onehot = as_bf16(iota((BINS * block, docs), 0) == jnp.concatenate([own, other], axis=1))
    is_last = iota((block, WIDTH), 0) == (block - 1)
    for y in range(4):
        columns = slice(y * WIDTH, (y + 1) * WIDTH)
        x = jnp.concatenate([keep_ref[:ROWS, columns], got_ref[:ROWS, columns]], axis=0)
        packed = dot(onehot, x)
        for b in range(BINS):
            extra = jnp.concatenate([names[b // 4:b // 4 + 1], counts, jnp.zeros((1, 2 * LANES), f32)], axis=1)
            out_ref[4 * b + y] = jnp.where(is_last, extra, packed[b * block:(b + 1) * block]).astype(bf16)


def labels_of(block, x_ref):
    tail = x_ref[:, block - 8:, :2 * LANES].astype(f32)
    tail = jnp.max(jnp.where(iota(tail.shape, 1) == 7, tail, 0.0), axis=1)
    return tail[:, :LANES].astype(i32) - 1, tail[:, LANES:].astype(bf16)


def counts_of(chip_counts):
    row, col = iota((LANES, LANES), 0), iota((LANES, LANES), 1)
    in_bin = (bin_of(row) == col) & (row < 4 * BINS)
    counts = [dot(chip_counts, as_bf16(in_bin & ((row & 3) == r))) for r in range(4)]
    return counts, [jnp.sum(v, axis=0, keepdims=True) for v in counts]


def in_order(sizes):
    a, b = jnp.maximum(sizes[0], sizes[1]), jnp.minimum(sizes[0], sizes[1])
    c, d = jnp.maximum(sizes[2], sizes[3]), jnp.minimum(sizes[2], sizes[3])
    first, e = jnp.maximum(a, c), jnp.minimum(a, c)
    g, fourth = jnp.maximum(b, d), jnp.minimum(b, d)
    return first, jnp.maximum(e, g), jnp.minimum(e, g), fourth


def names_kernel(block, x_ref, guest_ref, line_ref, key_ref, pos_ref, meta_ref):
    mine, z = index_on("x") * 4 + index_on("z"), index_on("z")
    labels, chip_counts = labels_of(block, x_ref)
    _, sizes = counts_of(chip_counts)
    here = iota((1, LANES), 1) == mine
    own = lambda v: jnp.sum(jnp.where(here, v, 0.0), axis=1, keepdims=True)
    wide = lambda v: jnp.broadcast_to(v, (1, LANES))
    ordered = in_order(sizes)
    meta_ref[...] = jnp.concatenate([wide(own(v)) for v in ordered] * 2, axis=0).astype(i32)

    n = [own(v) for v in sizes]
    row, col = iota((LANES, LANES), 0), iota((LANES, LANES), 1)
    lane = iota(labels.shape, 1)
    group = lane >> 5
    valid = labels >= 0
    home = bin_of(labels) & 3
    at_home = valid & (home == z)
    upper = as_bf16(row < col)
    lower = as_bf16(iota((CHIPS, CHIPS), 1) < iota((CHIPS, CHIPS), 0))
    pos = jnp.full(labels.shape, -1.0, f32)
    for r in range(4):
        place = sum(
            jnp.where((n[q] > n[r]) | ((n[q] == n[r]) & (q < r)), 1.0, 0.0) for q in range(4) if q != r
        )
        start = jnp.where(
            place < 0.5, float(STARTS[0]),
            jnp.where(place < 1.5, float(STARTS[1]), jnp.where(place < 2.5, float(STARTS[2]), float(STARTS[3]))),
        )
        member = at_home & ((labels & 3) == r)
        member16 = as_bf16(member)
        rank = dot(member16, upper) + jnp.sum(dot(lower, member16), axis=1, keepdims=True)
        pos = jnp.where(member, start + rank, pos)
    pos = pos.astype(i32)
    pos_ref[...] = pos
    guest = valid & (home != group)
    guest16 = as_bf16(guest)
    same = (row >> 5) == (col >> 5)
    turn = dot(guest16, as_bf16(same & (row < col))) + dot(dot(lower, guest16).astype(bf16), as_bf16(same))
    turn = turn.astype(i32)
    away = at_home & (group != z) & (turn < GUESTS)
    key_ref[...] = jnp.where(away, (((z - group) & 3) - 1) * GUESTS + turn, -1)
    per, groups = 16, CHIPS // 16
    value = jnp.where(group == z, jnp.where(guest, GUEST + turn, pos + 1), 0).astype(f32)
    value = pltpu.roll(value, lax.rem(LANES - GROUP * z, LANES), 1)
    value = jnp.where(lane < block, value, 0.0)
    lined = jnp.zeros((8, per * block), f32)
    for t in range(per):
        rows = jnp.concatenate([value[per * g + t:per * g + t + 1] for g in range(groups)] * 2, axis=0)
        rows = jnp.concatenate([rows, jnp.zeros((8, per * block - LANES), f32)], axis=1)
        lined = lined + (pltpu.roll(rows, t * block, 1) if t else rows)
    slots = jnp.concatenate([lined[g:g + 1] for g in range(groups)], axis=1).astype(i32)
    line_ref[...] = jnp.broadcast_to(slots, line_ref.shape)
    onehot = as_bf16(iota((GUESTS, CHIPS * block), 0) + GUEST == slots)
    guest_ref[...] = dot(onehot, x_ref[...].reshape(CHIPS * block, WIDTH)).astype(bf16)


def sorted_rows(segment, slots, x):
    onehot = as_bf16(iota((segment[1], x.shape[0]), 0) + (segment[0] + 1) == slots)
    return dot(onehot, x).astype(bf16)


def send_kernel(block, x_ref, line_ref, send_ref):
    x = x_ref[...].reshape(CHIPS * block, WIDTH)
    slots = line_ref[:1, :]
    for me in range(2):
        @pl.when(index_on("c") == me)
        def _():
            for segment in SEGMENTS:
                at = segment[2 + 1 - me]
                if at is not None:
                    send_ref[at:at + segment[1], :] = sorted_rows(segment, slots, x)


def mine_kernel(block, x_ref, line_ref, send_ref, key_ref, pos_ref, mine_ref, far_ref):
    x = x_ref[...].reshape(CHIPS * block, WIDTH)
    slots = line_ref[:1, :]
    for core in range(2):
        @pl.when(index_on("c") == core)
        def _():
            for segment in SEGMENTS:
                at, sent = segment[2 + core], segment[2 + 1 - core]
                if at is not None:
                    rows = segment[1]
                    mine_ref[at:at + rows, :] = (
                        send_ref[sent:sent + rows, :] if sent is not None else sorted_rows(segment, slots, x)
                    )
    total = jnp.zeros((8, ALL_GUESTS), f32)
    step = 16
    for first in range(0, CHIPS, step):
        flat = lambda ref: jnp.concatenate([ref[s:s + 1, :] for s in range(first, first + step)], axis=1)
        places = flat(pos_ref) + 1
        parts = jnp.where(iota((8, step * LANES), 0) == 0, places >> 5, places & 31).astype(f32).astype(bf16)
        total = total + dot_last(parts, as_bf16(iota((ALL_GUESTS, step * LANES), 0) == flat(key_ref)))
    far_ref[...] = jnp.broadcast_to((32.0 * total[:1] + total[1:2]).astype(i32), far_ref.shape)


def fit_kernel(block, x_ref, over_ref):
    _, chip_counts = labels_of(block, x_ref)
    counts, sizes = counts_of(chip_counts)
    ordered = in_order(sizes)
    over = jnp.zeros((1, LANES), f32)
    for size, cap in zip(ordered, CAPS):
        over = jnp.maximum(over, jnp.where(size > cap, 1.0, 0.0))
    for share in SHARES:
        length = sum(jnp.maximum(jnp.floor((ordered[q] + 63.0) * (1 / 64)) - first // HALF, 0.0) for q, first in share)
        over = jnp.maximum(over, jnp.where(length > 4 * COUNT, 1.0, 0.0))
    taken = counts[0] + counts[1] + counts[2] + counts[3]
    extra, room = jnp.maximum(taken - (block - 1), 0.0), jnp.maximum((block - 1) - taken, 0.0)
    row, col = iota((LANES, LANES), 0), iota((LANES, LANES), 1)
    same = (row >> 2) == (col >> 2)
    wanted = dot(extra.astype(bf16), as_bf16(same))
    before = jnp.zeros(taken.shape, f32)
    for turn in range(4):
        earlier = same & (((row - turn) & 3) < ((col - turn) & 3))
        before = jnp.where((iota(taken.shape, 0) & 3) == turn, dot(room.astype(bf16), as_bf16(earlier)), before)
    held = jnp.sum(jnp.minimum(jnp.maximum(wanted - before, 0.0), room), axis=0, keepdims=True)
    over = jnp.maximum(over, jnp.where(held > GUESTS, 1.0, 0.0))
    full = jnp.where(wanted > dot(room.astype(bf16), as_bf16(same)), 1.0, 0.0)
    over = jnp.maximum(over, jnp.max(full, axis=0, keepdims=True))
    over_ref[...] = jnp.broadcast_to(jnp.max(over, axis=1, keepdims=True), over_ref.shape).astype(i32)


def add_guests(core, base_ref, guests, far_ref, out_ref):
    guests = jnp.concatenate([ref[...] for ref in guests] + [guests[0][...]], axis=0)
    far = far_ref[:1, :]
    for segment in SEGMENTS:
        at, rows = segment[2 + core], segment[1]
        if at is not None:
            out_ref[at:at + rows, :] = base_ref[at:at + rows, :] + sorted_rows(segment, far, guests)


def blocks_of(core):
    for q, first in SHARES[core]:
        at = BASES[core][q] + first
        yield q, first, pl.ds(at, CAPS[q] - first), pl.ds(at, LANES)


RAW_ROWS = max(sum(CAPS[q] - first for q, first in share) for share in SHARES)


def own_kernel(x_ref, g1, g2, g3, far_ref, raw_ref, rows_ref):
    for core in range(2):
        @pl.when(index_on("c") == core)
        def _():
            add_guests(core, x_ref, (g1, g2, g3), far_ref, rows_ref)
            at = 0
            for q, first, left, right in blocks_of(core):
                rows = CAPS[q] - first
                raw_ref[at:at + rows, :] = dot_last(rows_ref[left, :], rows_ref[right, :])
                at += rows


def size_of(meta_ref, q):
    return jnp.max(meta_ref[q:q + 1, :].astype(f32)).astype(i32)


def length_of(size, first):
    return jnp.maximum(((size + HALF - 1) >> 6) - first // HALF, 0)


def gram_kernel(meta_ref, x_ref, g1, g2, g3, far_ref, raw_ref, out0, out1, out2, out3, part_ref, rows_ref):
    y, c = index_on("y"), index_on("c")
    part_ref[...] = jnp.full(part_ref.shape, -4.0, f32)
    for core in range(2):
        @pl.when(c == core)
        def _():
            add_guests(core, x_ref, (g1, g2, g3), far_ref, rows_ref)
            at, to = 0, jnp.zeros((), i32)
            for q, first, left, right in blocks_of(core):
                rows = CAPS[q] - first
                score = raw_ref[at:at + rows, :] + dot_last(rows_ref[left, :], rows_ref[right, :])
                at += rows
                size = size_of(meta_ref, q)
                i, j = iota(score.shape, 0), iota(score.shape, 1)
                keep = (i < size - first) & (j < size - first) & (i != j)
                part_ref[pl.ds(pl.multiple_of(to, HALF), rows), :] = jnp.where(keep, score, -4.0)
                to = jnp.minimum(to + HALF * length_of(size, first), PARTIAL)
    for shift, out in enumerate((out0, out1, out2, out3)):
        out[...] = part_ref[pl.ds(pl.multiple_of(lax.rem(y + shift, 4) * CHUNK, HALF), CHUNK), :]


FIRST_ROW = (0, 6, 10, 13)


def max_kernel(meta_ref, p0, p1, p2, p3, pos_ref, out_ref, best_ref):
    y, c = index_on("y"), index_on("c")
    best_ref[...] = jnp.full(best_ref.shape, -1.0, f32)
    sub, lane = iota((HALF, LANES), 0), iota((HALF, LANES), 1)
    blocks, sizes = [], [size_of(meta_ref, q) for q in range(4)]
    for core, share in enumerate(SHARES):
        at = jnp.zeros((), i32)
        for q, first in share:
            length = length_of(sizes[q], first)
            col = FIRST_ROW[q] + first // LANES
            blocks.append((jnp.where((c == core) & (length > 0), at, PARTIAL), col, 2 * col - at))
            at = at + length
    for t in range(COUNT):
        at = slice(t * HALF, (t + 1) * HALF)
        block = (p0[at, :] + p1[at, :]) + (p2[at, :] + p3[at, :])
        index = y * COUNT + t
        col, shift = jnp.asarray(15, i32), jnp.asarray(0, i32)
        for start, block_col, block_shift in blocks:
            inside = index >= start
            col, shift = jnp.where(inside, block_col, col), jnp.where(inside, block_shift, shift)
        row = jnp.minimum(jnp.maximum(index + shift, 0), 31)
        along = jnp.max(block, axis=1, keepdims=True)
        along = jnp.max(jnp.where(sub + (row & 1) * HALF == lane, along, -1.0), axis=0, keepdims=True)
        row = row >> 1
        best_ref[pl.ds(row, 1), :] = jnp.maximum(best_ref[pl.ds(row, 1), :], along)
        down = jnp.max(block, axis=0, keepdims=True)
        best_ref[pl.ds(col, 1), :] = jnp.maximum(best_ref[pl.ds(col, 1), :], down)
    pos = pos_ref[...]
    pos = jnp.where(pos >= STARTS[1], pos + HALF, pos)
    pos = jnp.where(pos >= STARTS[3] + HALF, pos + HALF, pos)
    row, lane = pos >> 7, pos & (LANES - 1)
    out = jnp.full(pos.shape, -1.0, f32)
    for r in range(15):
        value = jnp.broadcast_to(best_ref[r:r + 1, :], pos.shape)
        value = jnp.take_along_axis(value, lane, axis=1, mode="promise_in_bounds")
        out = jnp.where(row == r, value, out)
    out_ref[:CHIPS, :] = out
    out_ref[CHIPS:, :] = out


def pick_kernel(v_ref, code_ref, out_ref):
    c = index_on("c")
    values = jnp.maximum(v_ref[:CHIPS, :], v_ref[CHIPS:, :])
    values = jnp.max(values.reshape(BINS, 4, LANES), axis=1)
    eye = iota((LANES, LANES), 0) == iota((LANES, LANES), 1)
    code = jnp.max(jnp.where(iota((8, ROWS), 0) == c, code_ref[...], -1), axis=0, keepdims=True)
    code = jnp.max(jnp.where(eye, code.astype(f32), -1.0), axis=1, keepdims=True).astype(i32)
    slot = iota((ROWS, LANES), 1)
    best = jnp.full((ROWS, LANES), -1.0, f32)
    for b in range(BINS):
        best = jnp.where(slot + b * LANES == code, values[b:b + 1], best)
    best = jnp.max(best, axis=1, keepdims=True)
    out_ref[...] = jnp.max(jnp.where(eye, best, -1.0), axis=0, keepdims=True)


def gather_groups(embeddings, cluster_ids):
    split = ("z", "y", "c")
    rows = embeddings.shape[0]
    groups = lax.axis_size("x")
    cap = 2 * rows // groups
    slots = groups * cap
    owner_of = cluster_ids % groups
    onehot = (owner_of[:, None] == jnp.arange(groups, dtype=i32)[None, :]).astype(i32)
    before = jnp.cumsum(onehot, axis=0) - onehot
    rank = jnp.sum(before * onehot, axis=1)
    place = owner_of * cap + rank
    picked = place[None, :] == jnp.arange(slots, dtype=i32)[:, None]
    filled = jnp.any(picked, axis=1)
    source = jnp.sum(jnp.where(picked, jnp.arange(rows, dtype=i32)[None, :], 0), axis=1)
    out_labels = jnp.where(filled, cluster_ids[source], -1)
    squares = jnp.sum(embeddings * embeddings, axis=1, keepdims=True)
    local_unit = (embeddings * lax.rsqrt(squares + 1e-06)).astype(bf16)
    outgoing_unit = jnp.where(filled[:, None], local_unit[source], jnp.zeros((), bf16))
    unit = lax.all_to_all(outgoing_unit, "x", split_axis=0, concat_axis=0, tiled=True)
    labels = lax.all_to_all(out_labels, "x", split_axis=0, concat_axis=0, tiled=True)
    members = lax.axis_size(split)

    def everywhere(v):
        copies = jnp.broadcast_to(v[None], (members,) + v.shape).reshape((members * slots,) + v.shape[1:])
        return lax.all_to_all(copies, split, split_axis=0, concat_axis=0, tiled=True)

    def add_slice(i, scores):
        part = lax.dynamic_slice_in_dim(unit, i * WIDTH, WIDTH, 1)
        return scores + dot_last(part, everywhere(part))

    scores = lax.fori_loop(0, embeddings.shape[1] // WIDTH, add_slice, jnp.zeros((slots, members * slots), f32))
    all_labels = everywhere(labels)
    own = lax.axis_index(split) * slots + jnp.arange(slots, dtype=i32)
    mask = (
        (labels[:, None] == all_labels[None, :])
        & (labels[:, None] >= 0)
        & (own[:, None] != jnp.arange(members * slots, dtype=i32)[None, :])
    )
    scores = jnp.where(mask, scores, -1.0)
    best = jnp.maximum(-1.0, jnp.max(scores, axis=1))
    returned = lax.all_to_all(best, "x", split_axis=0, concat_axis=0, tiled=True)
    return returned[place]


def route(block, embeddings, cluster_ids):
    shape = jax.ShapeDtypeStruct
    half = shape((ROWS + LABEL_ROWS, HALF_WIDTH), bf16)
    keep, send = pl.pallas_call(
        unit_kernel, out_shape=(half, half),
        in_specs=[WHOLE, WHOLE], out_specs=(WHOLE, WHOLE), compiler_params=params(12), name="unit",
    )(embeddings, cluster_ids.reshape(1, ROWS))
    got = lax.ppermute(send, "c", [(0, 1), (1, 0)])
    packed, code = pl.pallas_call(
        functools.partial(pack_kernel, block),
        out_shape=(shape((CHIPS, block, WIDTH), bf16), shape((8, ROWS), i32)),
        in_specs=[WHOLE, WHOLE], out_specs=(WHOLE, WHOLE), compiler_params=params(20), name="pack",
    )(keep, got)
    packed = lax.all_to_all(packed, ("x", "z", "y"), 0, 0, tiled=True)
    table = shape((CHIPS, LANES), i32)
    guests, line, key, pos, meta = pl.pallas_call(
        functools.partial(names_kernel, block),
        out_shape=(shape((GUESTS, WIDTH), bf16), shape((8, CHIPS * block), i32), table, table, shape((8, LANES), i32)),
        in_specs=[WHOLE], out_specs=(WHOLE,) * 5, compiler_params=params(12), name="names",
    )(packed)
    brought = [lax.ppermute(guests, "z", [(i, (i + s) % 4) for i in range(4)]) for s in (1, 2, 3)]
    share = shape((SHARE_ROWS, WIDTH), bf16)
    slots = CHIPS * block
    send = pl.pallas_call(
        functools.partial(send_kernel, block), out_shape=share,
        in_specs=[WHOLE, WHOLE], out_specs=WHOLE, compiler_params=params(16), name="send",
        cost_estimate=pl.CostEstimate(flops=2 * SHARE_ROWS * WIDTH * slots, bytes_accessed=4 << 20, transcendentals=0),
    )(packed, line)
    other = lax.ppermute(send, "c", [(0, 1), (1, 0)])
    mine, far = pl.pallas_call(
        functools.partial(mine_kernel, block), out_shape=(share, shape((8, ALL_GUESTS), i32)),
        in_specs=[WHOLE] * 5, out_specs=(WHOLE,) * 2, compiler_params=params(20), name="mine",
        cost_estimate=pl.CostEstimate(flops=2 * SHARE_ROWS * WIDTH * slots, bytes_accessed=4 << 20, transcendentals=0),
    )(packed, line, send, key, pos)
    brought, mine = lax.optimization_barrier((brought, mine))
    swapped = [lax.ppermute(v, "c", [(0, 1), (1, 0)]) for v in brought]
    raw = pl.pallas_call(
        own_kernel, out_shape=shape((RAW_ROWS, LANES), f32),
        in_specs=[WHOLE] * 5, out_specs=WHOLE,
        scratch_shapes=[pltpu.VMEM((SHARE_ROWS, WIDTH), bf16)],
        compiler_params=params(16), name="own",
        cost_estimate=pl.CostEstimate(flops=2 * RAW_ROWS * LANES * WIDTH, bytes_accessed=4 << 20, transcendentals=0),
    )(mine, *brought, far)
    partial = pl.pallas_call(
        gram_kernel,
        out_shape=[shape((CHUNK, LANES), f32)] * 4,
        in_specs=[WHOLE] * 7, out_specs=[WHOLE] * 4,
        scratch_shapes=[pltpu.VMEM((PARTIAL + CAPS[0], LANES), f32), pltpu.VMEM((SHARE_ROWS, WIDTH), bf16)],
        compiler_params=params(16), name="gram",
    )(meta, other, *swapped, far, raw)
    arrived = [partial[0]] + [
        lax.ppermute(partial[s], "y", [(i, (i + s) % 4) for i in range(4)]) for s in (1, 2, 3)
    ]
    over = pl.pallas_call(
        functools.partial(fit_kernel, block), out_shape=shape((8, LANES), i32),
        in_specs=[WHOLE], out_specs=WHOLE, compiler_params=params(8), name="fit",
    )(packed)
    arrived, fits = lax.optimization_barrier((arrived, over[0, 0] == 0))
    best = pl.pallas_call(
        max_kernel,
        out_shape=shape((2 * CHIPS, LANES), f32),
        in_specs=[WHOLE] * 6, out_specs=WHOLE,
        scratch_shapes=[pltpu.VMEM((16, LANES), f32)],
        compiler_params=params(8), name="maxima",
    )(meta, *arrived, pos)
    back = lax.all_to_all(best.reshape(2 * CHIPS, 1, LANES), ("c", "x", "z", "y"), 0, 0, tiled=True)
    back, fits = lax.optimization_barrier((back, fits))
    best = pl.pallas_call(
        pick_kernel,
        out_shape=shape((1, ROWS), f32),
        in_specs=[WHOLE, WHOLE], out_specs=WHOLE, compiler_params=params(8), name="pick",
    )(back.reshape(2 * CHIPS, LANES), code).reshape(ROWS)
    return best, fits


def on_device(embeddings, cluster_ids, blocks=BLOCKS):
    if not blocks:
        return gather_groups(embeddings, cluster_ids)
    best, fits = route(blocks[0], embeddings, cluster_ids)
    return lax.cond(
        fits,
        lambda best, embeddings, cluster_ids: best,
        lambda best, embeddings, cluster_ids: on_device(embeddings, cluster_ids, blocks[1:]),
        best, embeddings, cluster_ids,
    )


def solution(mesh):
    axes = ("x", "z", "y", "c")
    grid = Mesh(mesh.devices.reshape(4, 4, 4, 2), axes)
    return jax.shard_map(
        on_device, mesh=grid, in_specs=(P(axes, None), P(axes)), out_specs=P(axes), check_vma=False
    )
```

```python
import functools

import jax
import jax.numpy as jnp
from jax import lax
from jax.experimental import pallas as pl
from jax.experimental.pallas import tpu as pltpu
from jax.sharding import Mesh, PartitionSpec as P

ROWS = 128
HALF_WIDTH = 2048
WIDTH = 512
LABEL_ROWS = 16
BINS = 16
CHIPS = 64
TRIES = ((24, 11), (32, 16))
GROUP = 32
GUESTS = 64
ALL_GUESTS = 4 * GUESTS
GUEST = 4096
LANES = 128
CAPS = (704, 512, 320, 192)
STARTS = (0, 704, 1216, 1536)
UNIT = 32
SHARES = (
    ((0, 0), (0, 256), (2, 0), (2, 128), (2, 256), (3, 0)),
    ((0, 128), (0, 384), (0, 512), (0, 640), (1, 0), (1, 128), (1, 256), (1, 384), (3, 128)),
)
BASES = ({0: 0, 2: 704, 3: 1024}, {0: -128, 1: 576, 3: 960})
SHARE_ROWS = 1216
SEGMENTS = (
    (0, 128, 0, None), (128, 576, 128, 0), (704, 256, None, 576), (960, 256, None, 832),
    (1216, 320, 704, None), (1536, 128, 1024, None), (1664, 64, 1152, 1088),
)
f32, bf16, i32 = jnp.float32, jnp.bfloat16, jnp.int32
WHOLE = pl.BlockSpec(memory_space=pltpu.VMEM)


def params(mib):
    return pltpu.CompilerParams(vmem_limit_bytes=mib * 1024 * 1024)


def index_on(axis):
    return lax.axis_index(axis)


def iota(shape, dim):
    return lax.broadcasted_iota(i32, shape, dim)


def dot_last(a, b):
    return lax.dot_general(a, b, (((1,), (1,)), ((), ())), preferred_element_type=f32)


def dot(a, b):
    return lax.dot_general(a, b, (((1,), (0,)), ((), ())), preferred_element_type=f32)


def as_bf16(mask):
    return jnp.where(mask, 1.0, 0.0).astype(bf16)


def bin_of(labels):
    rank, residue = labels >> 2, labels & 3
    row, col = rank >> 2, rank & 3
    col = jnp.where((row & 1) == 1, 3 - col, col)
    return 4 * col + ((row - residue) & 3)


def unit_kernel(x_ref, ids_ref, keep_ref, send_ref):
    c = index_on("c")
    x = x_ref[...]
    scale = lax.rsqrt(jnp.sum(x * x, axis=1, keepdims=True) + 1e-06)
    ids = jnp.concatenate([ids_ref[...].astype(f32), jnp.zeros((1, HALF_WIDTH - ROWS), f32)], axis=1)
    ids = jnp.broadcast_to(ids, (LABEL_ROWS, HALF_WIDTH)).astype(bf16)
    for half, out_ref in ((c, keep_ref), (1 - c, send_ref)):
        columns = pl.ds(pl.multiple_of(half * HALF_WIDTH, HALF_WIDTH), HALF_WIDTH)
        out_ref[:ROWS, :] = (x_ref[:, columns] * scale).astype(bf16)
        out_ref[ROWS:, :] = ids


def pack_kernel(block, keep_ref, got_ref, out_ref, code_ref):
    y, first = index_on("y"), index_on("c") == 0
    kept = jnp.max(keep_ref[ROWS:, :ROWS].astype(f32), axis=0, keepdims=True)
    got = jnp.max(got_ref[ROWS:, :ROWS].astype(f32), axis=0, keepdims=True)
    labels = jnp.concatenate([jnp.where(first, kept, got), jnp.where(first, got, kept)], axis=0).astype(i32)
    bins = bin_of(labels)
    upper = as_bf16(iota((ROWS, ROWS), 0) < iota((ROWS, ROWS), 1))

    def ranks_within(masks):
        member = jnp.concatenate([jnp.where(mask, 1.0, 0.0) for mask in masks], axis=0)
        row, col = iota((member.shape[0],) * 2, 0), iota((member.shape[0],) * 2, 1)
        earlier = dot(as_bf16(((row >> 1) == (col >> 1)) & (col < row)), member.astype(bf16))
        ranks = member * (dot(member.astype(bf16), upper) + jnp.sum(earlier, axis=1, keepdims=True))
        rank = sum(ranks[2 * b:2 * b + 2] for b in range(len(masks)))
        return rank.astype(i32), jnp.sum(member, axis=1, keepdims=True)

    rank, sizes = ranks_within([bins == b for b in range(BINS)])
    quad, line = bins >> 2, bins & 3
    extra = rank >= (block - 1)
    turn, _ = ranks_within([extra & (quad == q) for q in range(4)])
    room, used = [], []
    for step in range(4):
        taken = jnp.zeros(labels.shape, f32)
        for at in range(4):
            size = jnp.zeros(labels.shape, f32)
            for q in range(4):
                b = 4 * q + at
                size = jnp.where(quad == q, sizes[2 * b:2 * b + 1] + sizes[2 * b + 1:2 * b + 2], size)
            taken = jnp.where(((at - y) & 3) == step, size, taken)
        taken = jnp.minimum(taken.astype(i32), (block - 1))
        used.append(taken)
        room.append((block - 1) - taken)
    placed = jnp.logical_not(extra)
    to_line, to_slot, start = line, rank, jnp.zeros(labels.shape, i32)
    for step in range(4):
        here = extra & (turn >= start) & (turn < start + room[step])
        to_line = jnp.where(here, (y + step) & 3, to_line)
        to_slot = jnp.where(here, used[step] + turn - start, to_slot)
        placed = placed | here
        start = start + room[step]
    lane = jnp.where(placed, to_line * GROUP + to_slot, -1)
    place = jnp.where(placed, (quad * 4 + to_line) * block + to_slot, -1)
    code_ref[...] = jnp.concatenate([jnp.where(placed, bins * LANES + lane, -1)] * 4, axis=0)
    docs = 2 * ROWS
    flat = lambda v: jnp.concatenate([v[:1], v[1:]], axis=1)
    label_row = flat(labels)
    counts = dot_last(jnp.ones((8, docs), bf16), as_bf16(iota((LANES, docs), 0) == label_row))[:1]
    named = jnp.where(iota((8, docs), 0) == flat(quad), (label_row + 1).astype(f32), 0.0).astype(bf16)
    names = dot_last(named, as_bf16(iota((LANES, docs), 0) == flat(lane)))
    own = jnp.where(first, place[:1], place[1:])
    other = jnp.where(first, place[1:], place[:1])
    onehot = as_bf16(iota((BINS * block, docs), 0) == jnp.concatenate([own, other], axis=1))
    is_last = iota((block, WIDTH), 0) == (block - 1)
    for y in range(4):
        columns = slice(y * WIDTH, (y + 1) * WIDTH)
        x = jnp.concatenate([keep_ref[:ROWS, columns], got_ref[:ROWS, columns]], axis=0)
        packed = dot(onehot, x)
        for b in range(BINS):
            extra = jnp.concatenate([names[b // 4:b // 4 + 1], counts, jnp.zeros((1, 2 * LANES), f32)], axis=1)
            out_ref[4 * b + y] = jnp.where(is_last, extra, packed[b * block:(b + 1) * block]).astype(bf16)


def labels_of(block, x_ref):
    tail = x_ref[:, block - 8:, :2 * LANES].astype(f32)
    tail = jnp.max(jnp.where(iota(tail.shape, 1) == 7, tail, 0.0), axis=1)
    return tail[:, :LANES].astype(i32) - 1, tail[:, LANES:].astype(bf16)


def counts_of(chip_counts):
    row, col = iota((LANES, LANES), 0), iota((LANES, LANES), 1)
    in_bin = (bin_of(row) == col) & (row < 4 * BINS)
    counts = [dot(chip_counts, as_bf16(in_bin & ((row & 3) == r))) for r in range(4)]
    return counts, [jnp.sum(v, axis=0, keepdims=True) for v in counts]


def in_order(sizes):
    a, b = jnp.maximum(sizes[0], sizes[1]), jnp.minimum(sizes[0], sizes[1])
    c, d = jnp.maximum(sizes[2], sizes[3]), jnp.minimum(sizes[2], sizes[3])
    first, e = jnp.maximum(a, c), jnp.minimum(a, c)
    g, fourth = jnp.maximum(b, d), jnp.minimum(b, d)
    return first, jnp.maximum(e, g), jnp.minimum(e, g), fourth


def names_kernel(block, x_ref, guest_ref, line_ref, key_ref, pos_ref, meta_ref):
    mine, z = index_on("x") * 4 + index_on("z"), index_on("z")
    labels, chip_counts = labels_of(block, x_ref)
    _, sizes = counts_of(chip_counts)
    here = iota((1, LANES), 1) == mine
    own = lambda v: jnp.sum(jnp.where(here, v, 0.0), axis=1, keepdims=True)
    wide = lambda v: jnp.broadcast_to(v, (1, LANES))
    ordered = in_order(sizes)
    meta_ref[...] = jnp.concatenate([wide(own(v)) for v in ordered] * 2, axis=0).astype(i32)

    n = [own(v) for v in sizes]
    row, col = iota((LANES, LANES), 0), iota((LANES, LANES), 1)
    lane = iota(labels.shape, 1)
    group = lane >> 5
    valid = labels >= 0
    home = bin_of(labels) & 3
    at_home = valid & (home == z)
    upper = as_bf16(row < col)
    lower = as_bf16(iota((CHIPS, CHIPS), 1) < iota((CHIPS, CHIPS), 0))
    pos = jnp.full(labels.shape, -1.0, f32)
    for r in range(4):
        place = sum(
            jnp.where((n[q] > n[r]) | ((n[q] == n[r]) & (q < r)), 1.0, 0.0) for q in range(4) if q != r
        )
        start = jnp.where(
            place < 0.5, float(STARTS[0]),
            jnp.where(place < 1.5, float(STARTS[1]), jnp.where(place < 2.5, float(STARTS[2]), float(STARTS[3]))),
        )
        member = at_home & ((labels & 3) == r)
        member16 = as_bf16(member)
        rank = dot(member16, upper) + jnp.sum(dot(lower, member16), axis=1, keepdims=True)
        pos = jnp.where(member, start + rank, pos)
    pos = pos.astype(i32)
    pos_ref[...] = pos
    guest = valid & (home != group)
    guest16 = as_bf16(guest)
    same = (row >> 5) == (col >> 5)
    turn = dot(guest16, as_bf16(same & (row < col))) + dot(dot(lower, guest16).astype(bf16), as_bf16(same))
    turn = turn.astype(i32)
    away = at_home & (group != z) & (turn < GUESTS)
    key_ref[...] = jnp.where(away, (((z - group) & 3) - 1) * GUESTS + turn, -1)
    per, groups = 16, CHIPS // 16
    value = jnp.where(group == z, jnp.where(guest, GUEST + turn, pos + 1), 0).astype(f32)
    value = pltpu.roll(value, lax.rem(LANES - GROUP * z, LANES), 1)
    value = jnp.where(lane < block, value, 0.0)
    lined = jnp.zeros((8, per * block), f32)
    for t in range(per):
        rows = jnp.concatenate([value[per * g + t:per * g + t + 1] for g in range(groups)] * 2, axis=0)
        rows = jnp.concatenate([rows, jnp.zeros((8, per * block - LANES), f32)], axis=1)
        lined = lined + (pltpu.roll(rows, t * block, 1) if t else rows)
    slots = jnp.concatenate([lined[g:g + 1] for g in range(groups)], axis=1).astype(i32)
    line_ref[...] = jnp.broadcast_to(slots, line_ref.shape)
    onehot = as_bf16(iota((GUESTS, CHIPS * block), 0) + GUEST == slots)
    guest_ref[...] = dot(onehot, x_ref[...].reshape(CHIPS * block, WIDTH)).astype(bf16)


def sorted_rows(segment, slots, x):
    onehot = as_bf16(iota((segment[1], x.shape[0]), 0) + (segment[0] + 1) == slots)
    return dot(onehot, x).astype(bf16)


def send_kernel(block, x_ref, line_ref, send_ref):
    x = x_ref[...].reshape(CHIPS * block, WIDTH)
    slots = line_ref[:1, :]
    for me in range(2):
        @pl.when(index_on("c") == me)
        def _():
            for segment in SEGMENTS:
                at = segment[2 + 1 - me]
                if at is not None:
                    send_ref[at:at + segment[1], :] = sorted_rows(segment, slots, x)


def mine_kernel(block, x_ref, line_ref, send_ref, key_ref, pos_ref, mine_ref, far_ref):
    x = x_ref[...].reshape(CHIPS * block, WIDTH)
    slots = line_ref[:1, :]
    for core in range(2):
        @pl.when(index_on("c") == core)
        def _():
            for segment in SEGMENTS:
                at, sent = segment[2 + core], segment[2 + 1 - core]
                if at is not None:
                    rows = segment[1]
                    mine_ref[at:at + rows, :] = (
                        send_ref[sent:sent + rows, :] if sent is not None else sorted_rows(segment, slots, x)
                    )
    total = jnp.zeros((8, ALL_GUESTS), f32)
    step = 16
    for first in range(0, CHIPS, step):
        flat = lambda ref: jnp.concatenate([ref[s:s + 1, :] for s in range(first, first + step)], axis=1)
        places = flat(pos_ref) + 1
        parts = jnp.where(iota((8, step * LANES), 0) == 0, places >> 5, places & 31).astype(f32).astype(bf16)
        total = total + dot_last(parts, as_bf16(iota((ALL_GUESTS, step * LANES), 0) == flat(key_ref)))
    far_ref[...] = jnp.broadcast_to((32.0 * total[:1] + total[1:2]).astype(i32), far_ref.shape)


def fit_kernel(block, units, x_ref, over_ref):
    _, chip_counts = labels_of(block, x_ref)
    counts, sizes = counts_of(chip_counts)
    ordered = in_order(sizes)
    over = jnp.zeros((1, LANES), f32)
    for size, cap in zip(ordered, CAPS):
        over = jnp.maximum(over, jnp.where(size > cap, 1.0, 0.0))
    for share in SHARES:
        length = 0.0
        for q, first in share:
            rows = jnp.maximum(jnp.floor((ordered[q] + (UNIT - 1.0)) * (1 / UNIT)) - first // UNIT, 0.0)
            length = length + jnp.where(rows >= 3.0, rows - 1.0, rows)
        over = jnp.maximum(over, jnp.where(length > 4 * units, 1.0, 0.0))
    taken = counts[0] + counts[1] + counts[2] + counts[3]
    extra, room = jnp.maximum(taken - (block - 1), 0.0), jnp.maximum((block - 1) - taken, 0.0)
    row, col = iota((LANES, LANES), 0), iota((LANES, LANES), 1)
    same = (row >> 2) == (col >> 2)
    wanted = dot(extra.astype(bf16), as_bf16(same))
    before = jnp.zeros(taken.shape, f32)
    for turn in range(4):
        earlier = same & (((row - turn) & 3) < ((col - turn) & 3))
        before = jnp.where((iota(taken.shape, 0) & 3) == turn, dot(room.astype(bf16), as_bf16(earlier)), before)
    held = jnp.sum(jnp.minimum(jnp.maximum(wanted - before, 0.0), room), axis=0, keepdims=True)
    over = jnp.maximum(over, jnp.where(held > GUESTS, 1.0, 0.0))
    full = jnp.where(wanted > dot(room.astype(bf16), as_bf16(same)), 1.0, 0.0)
    over = jnp.maximum(over, jnp.max(full, axis=0, keepdims=True))
    over_ref[...] = jnp.broadcast_to(jnp.max(over, axis=1, keepdims=True), over_ref.shape).astype(i32)


def add_guests(core, base_ref, guests, far_ref, out_ref):
    guests = jnp.concatenate([ref[...] for ref in guests] + [guests[0][...]], axis=0)
    far = far_ref[:1, :]
    for segment in SEGMENTS:
        at, rows = segment[2 + core], segment[1]
        if at is not None:
            out_ref[at:at + rows, :] = base_ref[at:at + rows, :] + sorted_rows(segment, far, guests)


def blocks_of(core):
    for q, first in SHARES[core]:
        at = BASES[core][q] + first
        yield q, first, pl.ds(at, CAPS[q] - first), pl.ds(at, LANES)


RAW_ROWS = max(sum(CAPS[q] - first for q, first in share) for share in SHARES)


def own_kernel(x_ref, g1, g2, g3, far_ref, raw_ref, rows_ref):
    for core in range(2):
        @pl.when(index_on("c") == core)
        def _():
            add_guests(core, x_ref, (g1, g2, g3), far_ref, rows_ref)
            at = 0
            for q, first, left, right in blocks_of(core):
                rows = CAPS[q] - first
                raw_ref[at:at + rows, :] = dot_last(rows_ref[left, :], rows_ref[right, :])
                at += rows


def size_of(meta_ref, q):
    return jnp.max(meta_ref[q:q + 1, :].astype(f32)).astype(i32)


def length_of(size, first):
    units = jnp.maximum(((size + UNIT - 1) >> 5) - first // UNIT, 0)
    return jnp.where(units >= 3, units - 1, units)


def folded(score):
    away = jnp.full((UNIT, LANES), -4.0, f32) if score.shape[0] < LANES else score[2 * UNIT:3 * UNIT]
    both = jnp.where(iota(away.shape, 1) < 3 * UNIT, away, pltpu.roll(score[:UNIT], 3 * UNIT, 1))
    rest = [score[3 * UNIT:]] if score.shape[0] > 3 * UNIT else []
    return jnp.concatenate([both, score[UNIT:2 * UNIT]] + rest, axis=0)


def gram_kernel(units, meta_ref, x_ref, g1, g2, g3, far_ref, raw_ref, out0, out1, out2, out3, part_ref, rows_ref):
    y, c = index_on("y"), index_on("c")
    part_ref[...] = jnp.full(part_ref.shape, -4.0, f32)
    for core in range(2):
        @pl.when(c == core)
        def _():
            add_guests(core, x_ref, (g1, g2, g3), far_ref, rows_ref)
            at, to = 0, jnp.zeros((), i32)
            for q, first, left, right in blocks_of(core):
                rows = CAPS[q] - first
                score = raw_ref[at:at + rows, :] + dot_last(rows_ref[left, :], rows_ref[right, :])
                at += rows
                size = size_of(meta_ref, q)
                i, j = iota(score.shape, 0), iota(score.shape, 1)
                keep = (i < size - first) & (j < size - first) & (i != j)
                score = folded(jnp.where(keep, score, -4.0))
                part_ref[pl.ds(pl.multiple_of(to, UNIT), score.shape[0]), :] = score
                to = jnp.minimum(to + UNIT * length_of(size, first), 4 * units * UNIT)
    chunk = units * UNIT
    for shift, out in enumerate((out0, out1, out2, out3)):
        out[...] = part_ref[pl.ds(pl.multiple_of(lax.rem(y + shift, 4) * chunk, UNIT), chunk), :]


FIRST_ROW = (0, 6, 10, 13)


def max_kernel(units, meta_ref, p0, p1, p2, p3, pos_ref, out_ref, best_ref):
    y, c = index_on("y"), index_on("c")
    best_ref[...] = jnp.full(best_ref.shape, -1.0, f32)
    sub, lane = iota((UNIT, LANES), 0), iota((UNIT, LANES), 1)
    blocks, sizes = [], [size_of(meta_ref, q) for q in range(4)]
    for core, share in enumerate(SHARES):
        at = jnp.zeros((), i32)
        for q, first in share:
            length = length_of(sizes[q], first)
            blocks.append((jnp.where((c == core) & (length > 0), at, 4 * units), FIRST_ROW[q] + first // LANES, at))
            at = at + length
    for t in range(units):
        at = slice(t * UNIT, (t + 1) * UNIT)
        block = (p0[at, :] + p1[at, :]) + (p2[at, :] + p3[at, :])
        index = y * units + t
        col, start = jnp.asarray(15, i32), jnp.asarray(0, i32)
        for block_start, block_col, block_at in blocks:
            inside = index >= block_start
            col, start = jnp.where(inside, block_col, col), jnp.where(inside, block_at, start)
        turn = index - start
        unit = 4 * col + jnp.where(turn == 0, 2, jnp.where(turn == 1, 1, turn + 1))
        unit = jnp.minimum(jnp.maximum(unit, 0), 63)
        beside = (lane >= 3 * UNIT) & (turn == 0)
        one, two = jnp.where(beside, -4.0, block), jnp.where(beside, block, -4.0)
        along = jnp.max(one, axis=1, keepdims=True)
        along = jnp.max(jnp.where(sub + (unit & 3) * UNIT == lane, along, -1.0), axis=0, keepdims=True)
        row = unit >> 2
        best_ref[pl.ds(row, 1), :] = jnp.maximum(best_ref[pl.ds(row, 1), :], along)
        down = jnp.max(one, axis=0, keepdims=True)
        along = jnp.max(two, axis=1, keepdims=True)
        two = jnp.maximum(jnp.where(sub == lane, along, -1.0), pltpu.roll(two, UNIT, 1))
        down = jnp.maximum(down, jnp.max(two, axis=0, keepdims=True))
        best_ref[pl.ds(col, 1), :] = jnp.maximum(best_ref[pl.ds(col, 1), :], down)
    pos = pos_ref[...]
    pos = jnp.where(pos >= STARTS[1], pos + 64, pos)
    pos = jnp.where(pos >= STARTS[3] + 64, pos + 64, pos)
    row, lane = pos >> 7, pos & (LANES - 1)
    out = jnp.full(pos.shape, -1.0, f32)
    for r in range(15):
        value = jnp.broadcast_to(best_ref[r:r + 1, :], pos.shape)
        value = jnp.take_along_axis(value, lane, axis=1, mode="promise_in_bounds")
        out = jnp.where(row == r, value, out)
    out_ref[:CHIPS, :] = out
    out_ref[CHIPS:, :] = out


def pick_kernel(v_ref, code_ref, out_ref):
    c = index_on("c")
    values = jnp.maximum(v_ref[:CHIPS, :], v_ref[CHIPS:, :])
    values = jnp.max(values.reshape(BINS, 4, LANES), axis=1)
    eye = iota((LANES, LANES), 0) == iota((LANES, LANES), 1)
    code = jnp.max(jnp.where(iota((8, ROWS), 0) == c, code_ref[...], -1), axis=0, keepdims=True)
    code = jnp.max(jnp.where(eye, code.astype(f32), -1.0), axis=1, keepdims=True).astype(i32)
    slot = iota((ROWS, LANES), 1)
    best = jnp.full((ROWS, LANES), -1.0, f32)
    for b in range(BINS):
        best = jnp.where(slot + b * LANES == code, values[b:b + 1], best)
    best = jnp.max(best, axis=1, keepdims=True)
    out_ref[...] = jnp.max(jnp.where(eye, best, -1.0), axis=0, keepdims=True)


def gather_groups(embeddings, cluster_ids):
    split = ("z", "y", "c")
    rows = embeddings.shape[0]
    groups = lax.axis_size("x")
    cap = 2 * rows // groups
    slots = groups * cap
    owner_of = cluster_ids % groups
    onehot = (owner_of[:, None] == jnp.arange(groups, dtype=i32)[None, :]).astype(i32)
    before = jnp.cumsum(onehot, axis=0) - onehot
    rank = jnp.sum(before * onehot, axis=1)
    place = owner_of * cap + rank
    picked = place[None, :] == jnp.arange(slots, dtype=i32)[:, None]
    filled = jnp.any(picked, axis=1)
    source = jnp.sum(jnp.where(picked, jnp.arange(rows, dtype=i32)[None, :], 0), axis=1)
    out_labels = jnp.where(filled, cluster_ids[source], -1)
    squares = jnp.sum(embeddings * embeddings, axis=1, keepdims=True)
    local_unit = (embeddings * lax.rsqrt(squares + 1e-06)).astype(bf16)
    outgoing_unit = jnp.where(filled[:, None], local_unit[source], jnp.zeros((), bf16))
    unit = lax.all_to_all(outgoing_unit, "x", split_axis=0, concat_axis=0, tiled=True)
    labels = lax.all_to_all(out_labels, "x", split_axis=0, concat_axis=0, tiled=True)
    members = lax.axis_size(split)

    def everywhere(v):
        copies = jnp.broadcast_to(v[None], (members,) + v.shape).reshape((members * slots,) + v.shape[1:])
        return lax.all_to_all(copies, split, split_axis=0, concat_axis=0, tiled=True)

    def add_slice(i, scores):
        part = lax.dynamic_slice_in_dim(unit, i * WIDTH, WIDTH, 1)
        return scores + dot_last(part, everywhere(part))

    scores = lax.fori_loop(0, embeddings.shape[1] // WIDTH, add_slice, jnp.zeros((slots, members * slots), f32))
    all_labels = everywhere(labels)
    own = lax.axis_index(split) * slots + jnp.arange(slots, dtype=i32)
    mask = (
        (labels[:, None] == all_labels[None, :])
        & (labels[:, None] >= 0)
        & (own[:, None] != jnp.arange(members * slots, dtype=i32)[None, :])
    )
    scores = jnp.where(mask, scores, -1.0)
    best = jnp.maximum(-1.0, jnp.max(scores, axis=1))
    returned = lax.all_to_all(best, "x", split_axis=0, concat_axis=0, tiled=True)
    return returned[place]


def route(block, units, embeddings, cluster_ids):
    shape = jax.ShapeDtypeStruct
    half = shape((ROWS + LABEL_ROWS, HALF_WIDTH), bf16)
    keep, send = pl.pallas_call(
        unit_kernel, out_shape=(half, half),
        in_specs=[WHOLE, WHOLE], out_specs=(WHOLE, WHOLE), compiler_params=params(12), name="unit",
    )(embeddings, cluster_ids.reshape(1, ROWS))
    got = lax.ppermute(send, "c", [(0, 1), (1, 0)])
    packed, code = pl.pallas_call(
        functools.partial(pack_kernel, block),
        out_shape=(shape((CHIPS, block, WIDTH), bf16), shape((8, ROWS), i32)),
        in_specs=[WHOLE, WHOLE], out_specs=(WHOLE, WHOLE), compiler_params=params(20), name="pack",
    )(keep, got)
    packed = lax.all_to_all(packed, ("x", "z", "y"), 0, 0, tiled=True)
    table = shape((CHIPS, LANES), i32)
    guests, line, key, pos, meta = pl.pallas_call(
        functools.partial(names_kernel, block),
        out_shape=(shape((GUESTS, WIDTH), bf16), shape((8, CHIPS * block), i32), table, table, shape((8, LANES), i32)),
        in_specs=[WHOLE], out_specs=(WHOLE,) * 5, compiler_params=params(12), name="names",
    )(packed)
    brought = [lax.ppermute(guests, "z", [(i, (i + s) % 4) for i in range(4)]) for s in (1, 2, 3)]
    share = shape((SHARE_ROWS, WIDTH), bf16)
    slots = CHIPS * block
    send = pl.pallas_call(
        functools.partial(send_kernel, block), out_shape=share,
        in_specs=[WHOLE, WHOLE], out_specs=WHOLE, compiler_params=params(16), name="send",
        cost_estimate=pl.CostEstimate(flops=2 * SHARE_ROWS * WIDTH * slots, bytes_accessed=4 << 20, transcendentals=0),
    )(packed, line)
    other = lax.ppermute(send, "c", [(0, 1), (1, 0)])
    mine, far = pl.pallas_call(
        functools.partial(mine_kernel, block), out_shape=(share, shape((8, ALL_GUESTS), i32)),
        in_specs=[WHOLE] * 5, out_specs=(WHOLE,) * 2, compiler_params=params(20), name="mine",
        cost_estimate=pl.CostEstimate(flops=2 * SHARE_ROWS * WIDTH * slots, bytes_accessed=4 << 20, transcendentals=0),
    )(packed, line, send, key, pos)
    brought, mine = lax.optimization_barrier((brought, mine))
    swapped = [lax.ppermute(v, "c", [(0, 1), (1, 0)]) for v in brought]
    raw = pl.pallas_call(
        own_kernel, out_shape=shape((RAW_ROWS, LANES), f32),
        in_specs=[WHOLE] * 5, out_specs=WHOLE,
        scratch_shapes=[pltpu.VMEM((SHARE_ROWS, WIDTH), bf16)],
        compiler_params=params(16), name="own",
        cost_estimate=pl.CostEstimate(flops=2 * RAW_ROWS * LANES * WIDTH, bytes_accessed=4 << 20, transcendentals=0),
    )(mine, *brought, far)
    partial = pl.pallas_call(
        functools.partial(gram_kernel, units),
        out_shape=[shape((units * UNIT, LANES), f32)] * 4,
        in_specs=[WHOLE] * 7, out_specs=[WHOLE] * 4,
        scratch_shapes=[pltpu.VMEM((4 * units * UNIT + CAPS[0], LANES), f32), pltpu.VMEM((SHARE_ROWS, WIDTH), bf16)],
        compiler_params=params(16), name="gram",
    )(meta, other, *swapped, far, raw)
    arrived = [partial[0]] + [
        lax.ppermute(partial[s], "y", [(i, (i + s) % 4) for i in range(4)]) for s in (1, 2, 3)
    ]
    over = pl.pallas_call(
        functools.partial(fit_kernel, block, units), out_shape=shape((8, LANES), i32),
        in_specs=[WHOLE], out_specs=WHOLE, compiler_params=params(8), name="fit",
    )(packed)
    arrived, fits = lax.optimization_barrier((arrived, over[0, 0] == 0))
    best = pl.pallas_call(
        functools.partial(max_kernel, units),
        out_shape=shape((2 * CHIPS, LANES), f32),
        in_specs=[WHOLE] * 6, out_specs=WHOLE,
        scratch_shapes=[pltpu.VMEM((16, LANES), f32)],
        compiler_params=params(8), name="maxima",
    )(meta, *arrived, pos)
    back = lax.all_to_all(best.reshape(2 * CHIPS, 1, LANES), ("c", "x", "z", "y"), 0, 0, tiled=True)
    back, fits = lax.optimization_barrier((back, fits))
    best = pl.pallas_call(
        pick_kernel,
        out_shape=shape((1, ROWS), f32),
        in_specs=[WHOLE, WHOLE], out_specs=WHOLE, compiler_params=params(8), name="pick",
    )(back.reshape(2 * CHIPS, LANES), code).reshape(ROWS)
    return best, fits


def on_device(embeddings, cluster_ids, tries=TRIES):
    if not tries:
        return gather_groups(embeddings, cluster_ids)
    best, fits = route(*tries[0], embeddings, cluster_ids)
    return lax.cond(
        fits,
        lambda best, embeddings, cluster_ids: best,
        lambda best, embeddings, cluster_ids: on_device(embeddings, cluster_ids, tries[1:]),
        best, embeddings, cluster_ids,
    )


def solution(mesh):
    axes = ("x", "z", "y", "c")
    grid = Mesh(mesh.devices.reshape(4, 4, 4, 2), axes)
    return jax.shard_map(
        on_device, mesh=grid, in_specs=(P(axes, None), P(axes)), out_specs=P(axes), check_vma=False
    )
```

```python
import functools

import jax
import jax.numpy as jnp
from jax import lax
from jax.experimental import pallas as pl
from jax.experimental.pallas import tpu as pltpu
from jax.sharding import Mesh, PartitionSpec as P

ROWS = 128
HALF_WIDTH = 2048
WIDTH = 512
LABEL_ROWS = 16
BINS = 16
CHIPS = 64
TRIES = ((24, 11), (32, 16))
GROUP = 32
GUESTS = 64
GUEST = 4096
LANES = 128
CAPS = (704, 512, 320, 192)
STARTS = (0, 704, 1216, 1536)
UNIT = 32
SHARES = (
    ((0, 0), (0, 256), (2, 0), (2, 128), (2, 256), (3, 0)),
    ((0, 128), (0, 384), (0, 512), (0, 640), (1, 0), (1, 128), (1, 256), (1, 384), (3, 128)),
)
BASES = ({0: 0, 2: 704, 3: 1024}, {0: -128, 1: 576, 3: 960})
SHARE_ROWS = 1216
SEGMENTS = (
    (0, 128, 0, None), (128, 576, 128, 0), (704, 256, None, 576), (960, 256, None, 832),
    (1216, 320, 704, None), (1536, 128, 1024, None), (1664, 64, 1152, 1088),
)
f32, bf16, i32 = jnp.float32, jnp.bfloat16, jnp.int32
WHOLE = pl.BlockSpec(memory_space=pltpu.VMEM)


def params(mib):
    return pltpu.CompilerParams(vmem_limit_bytes=mib * 1024 * 1024)


def index_on(axis):
    return lax.axis_index(axis)


def iota(shape, dim):
    return lax.broadcasted_iota(i32, shape, dim)


def dot_last(a, b):
    return lax.dot_general(a, b, (((1,), (1,)), ((), ())), preferred_element_type=f32)


def dot(a, b):
    return lax.dot_general(a, b, (((1,), (0,)), ((), ())), preferred_element_type=f32)


def as_bf16(mask):
    return jnp.where(mask, 1.0, 0.0).astype(bf16)


def bin_of(labels):
    rank, residue = labels >> 2, labels & 3
    row, col = rank >> 2, rank & 3
    col = jnp.where((row & 1) == 1, 3 - col, col)
    return 4 * col + ((row - residue) & 3)


def unit_kernel(x_ref, ids_ref, keep_ref, send_ref):
    c = index_on("c")
    x = x_ref[...]
    scale = lax.rsqrt(jnp.sum(x * x, axis=1, keepdims=True) + 1e-06)
    ids = jnp.concatenate([ids_ref[...].astype(f32), jnp.zeros((1, HALF_WIDTH - ROWS), f32)], axis=1)
    ids = jnp.broadcast_to(ids, (LABEL_ROWS, HALF_WIDTH)).astype(bf16)
    for half, out_ref in ((c, keep_ref), (1 - c, send_ref)):
        columns = pl.ds(pl.multiple_of(half * HALF_WIDTH, HALF_WIDTH), HALF_WIDTH)
        out_ref[:ROWS, :] = (x_ref[:, columns] * scale).astype(bf16)
        out_ref[ROWS:, :] = ids


def passed_on(over, before):
    once = before(over, 1)
    twice = before(over, 2)
    return jnp.maximum(jnp.maximum(over, 0), jnp.maximum(over + once, over + once + twice))


def pack_kernel(block, keep_ref, got_ref, out_ref, code_ref):
    first = index_on("c") == 0
    kept = jnp.max(keep_ref[ROWS:, :ROWS].astype(f32), axis=0, keepdims=True)
    got = jnp.max(got_ref[ROWS:, :ROWS].astype(f32), axis=0, keepdims=True)
    labels = jnp.concatenate([jnp.where(first, kept, got), jnp.where(first, got, kept)], axis=0).astype(i32)
    bins = bin_of(labels)
    upper = as_bf16(iota((ROWS, ROWS), 0) < iota((ROWS, ROWS), 1))

    def ranks_within(masks):
        member = jnp.concatenate([jnp.where(mask, 1.0, 0.0) for mask in masks], axis=0)
        row, col = iota((member.shape[0],) * 2, 0), iota((member.shape[0],) * 2, 1)
        earlier = dot(as_bf16(((row >> 1) == (col >> 1)) & (col < row)), member.astype(bf16))
        ranks = member * (dot(member.astype(bf16), upper) + jnp.sum(earlier, axis=1, keepdims=True))
        rank = sum(ranks[2 * b:2 * b + 2] for b in range(len(masks)))
        return rank.astype(i32), jnp.sum(member, axis=1, keepdims=True)

    rank, sizes = ranks_within([bins == b for b in range(BINS)])
    quad, line = bins >> 2, bins & 3
    taken = []
    for at in range(4):
        size = jnp.zeros(labels.shape, f32)
        for b in range(at, BINS, 4):
            size = jnp.where(quad == b >> 2, sizes[2 * b:2 * b + 1] + sizes[2 * b + 1:2 * b + 2], size)
        taken.append(size.astype(i32) - (block - 1))
    stays = []
    for at in range(4):
        moved = passed_on(taken[at], lambda _, back: taken[(at - back) & 3])
        stays.append(taken[at] + (block - 1) - moved)

    def of_line(values, which):
        out = values[0]
        for at in range(1, 4):
            out = jnp.where(which == at, values[at], out)
        return out

    stay = of_line(stays, line)
    to_line = jnp.where(rank < stay, line, (line + 1) & 3)
    to_slot = jnp.where(rank < stay, rank, of_line(stays, to_line) + rank - stay)
    placed = to_slot < (block - 1)
    lane = jnp.where(placed, to_line * GROUP + to_slot, -1)
    place = jnp.where(placed, (quad * 4 + to_line) * block + to_slot, -1)
    code_ref[...] = jnp.concatenate([jnp.where(placed, bins * LANES + lane, -1)] * 4, axis=0)
    docs = 2 * ROWS
    flat = lambda v: jnp.concatenate([v[:1], v[1:]], axis=1)
    label_row = flat(labels)
    counts = dot_last(jnp.ones((8, docs), bf16), as_bf16(iota((LANES, docs), 0) == label_row))[:1]
    named = jnp.where(iota((8, docs), 0) == flat(quad), (label_row + 1).astype(f32), 0.0).astype(bf16)
    names = dot_last(named, as_bf16(iota((LANES, docs), 0) == flat(lane)))
    own = jnp.where(first, place[:1], place[1:])
    other = jnp.where(first, place[1:], place[:1])
    onehot = as_bf16(iota((BINS * block, docs), 0) == jnp.concatenate([own, other], axis=1))
    is_last = iota((block, WIDTH), 0) == (block - 1)
    for y in range(4):
        columns = slice(y * WIDTH, (y + 1) * WIDTH)
        x = jnp.concatenate([keep_ref[:ROWS, columns], got_ref[:ROWS, columns]], axis=0)
        packed = dot(onehot, x)
        for b in range(BINS):
            extra = jnp.concatenate([names[b // 4:b // 4 + 1], counts, jnp.zeros((1, 2 * LANES), f32)], axis=1)
            out_ref[4 * b + y] = jnp.where(is_last, extra, packed[b * block:(b + 1) * block]).astype(bf16)


def labels_of(block, x_ref):
    tail = x_ref[:, block - 8:, :2 * LANES].astype(f32)
    tail = jnp.max(jnp.where(iota(tail.shape, 1) == 7, tail, 0.0), axis=1)
    return tail[:, :LANES].astype(i32) - 1, tail[:, LANES:].astype(bf16)


def counts_of(chip_counts):
    row, col = iota((LANES, LANES), 0), iota((LANES, LANES), 1)
    in_bin = (bin_of(row) == col) & (row < 4 * BINS)
    counts = [dot(chip_counts, as_bf16(in_bin & ((row & 3) == r))) for r in range(4)]
    return counts, [jnp.sum(v, axis=0, keepdims=True) for v in counts]


def in_order(sizes):
    a, b = jnp.maximum(sizes[0], sizes[1]), jnp.minimum(sizes[0], sizes[1])
    c, d = jnp.maximum(sizes[2], sizes[3]), jnp.minimum(sizes[2], sizes[3])
    first, e = jnp.maximum(a, c), jnp.minimum(a, c)
    g, fourth = jnp.maximum(b, d), jnp.minimum(b, d)
    return first, jnp.maximum(e, g), jnp.minimum(e, g), fourth


def names_kernel(block, x_ref, guest_ref, line_ref, key_ref, pos_ref, meta_ref):
    z = index_on("z")
    labels, _ = labels_of(block, x_ref)
    row, col = iota((LANES, LANES), 0), iota((LANES, LANES), 1)
    lane = iota(labels.shape, 1)
    group = lane >> 5
    valid = labels >= 0
    home = bin_of(labels) & 3
    at_home = valid & (home == z)
    upper = as_bf16(row < col)
    lower = as_bf16(iota((CHIPS, CHIPS), 1) < iota((CHIPS, CHIPS), 0))
    members, n = [at_home & ((labels & 3) == r) for r in range(4)], []
    for member in members:
        size = jnp.sum(jnp.where(member, 1.0, 0.0), axis=0, keepdims=True)
        n.append(jnp.sum(size, axis=1, keepdims=True))
    wide = lambda v: jnp.broadcast_to(v, (1, LANES))
    meta_ref[...] = jnp.concatenate([wide(v) for v in in_order(n)] * 2, axis=0).astype(i32)
    pos = jnp.full(labels.shape, -1.0, f32)
    for r, member in enumerate(members):
        place = sum(
            jnp.where((n[q] > n[r]) | ((n[q] == n[r]) & (q < r)), 1.0, 0.0) for q in range(4) if q != r
        )
        start = jnp.where(
            place < 0.5, float(STARTS[0]),
            jnp.where(place < 1.5, float(STARTS[1]), jnp.where(place < 2.5, float(STARTS[2]), float(STARTS[3]))),
        )
        member16 = as_bf16(member)
        rank = dot(member16, upper) + jnp.sum(dot(lower, member16), axis=1, keepdims=True)
        pos = jnp.where(member, start + rank, pos)
    pos = pos.astype(i32)
    pos_ref[...] = pos
    guest = valid & (home != group)
    guest16 = as_bf16(guest)
    same = (row >> 5) == (col >> 5)
    turn = dot(guest16, as_bf16(same & (row < col))) + dot(dot(lower, guest16).astype(bf16), as_bf16(same))
    turn = turn.astype(i32)
    away = at_home & (group != z) & (turn < GUESTS)
    key_ref[...] = jnp.where(away, turn, -1)
    per, groups = 16, CHIPS // 16
    value = jnp.where(group == z, jnp.where(guest, GUEST + turn, pos + 1), 0).astype(f32)
    value = pltpu.roll(value, lax.rem(LANES - GROUP * z, LANES), 1)
    value = jnp.where(lane < block, value, 0.0)
    lined = jnp.zeros((8, per * block), f32)
    for t in range(per):
        rows = jnp.concatenate([value[per * g + t:per * g + t + 1] for g in range(groups)] * 2, axis=0)
        rows = jnp.concatenate([rows, jnp.zeros((8, per * block - LANES), f32)], axis=1)
        lined = lined + (pltpu.roll(rows, t * block, 1) if t else rows)
    slots = jnp.concatenate([lined[g:g + 1] for g in range(groups)], axis=1).astype(i32)
    line_ref[...] = jnp.broadcast_to(slots, line_ref.shape)
    onehot = as_bf16(iota((GUESTS, CHIPS * block), 0) + GUEST == slots)
    guest_ref[...] = dot(onehot, x_ref[...].reshape(CHIPS * block, WIDTH)).astype(bf16)


def sorted_rows(segment, slots, x):
    onehot = as_bf16(iota((segment[1], x.shape[0]), 0) + (segment[0] + 1) == slots)
    return dot(onehot, x).astype(bf16)


def send_kernel(block, x_ref, line_ref, send_ref):
    x = x_ref[...].reshape(CHIPS * block, WIDTH)
    slots = line_ref[:1, :]
    for me in range(2):
        @pl.when(index_on("c") == me)
        def _():
            for segment in SEGMENTS:
                at = segment[2 + 1 - me]
                if at is not None:
                    send_ref[at:at + segment[1], :] = sorted_rows(segment, slots, x)


def mine_kernel(block, x_ref, line_ref, send_ref, key_ref, pos_ref, mine_ref, far_ref):
    x = x_ref[...].reshape(CHIPS * block, WIDTH)
    slots = line_ref[:1, :]
    for core in range(2):
        @pl.when(index_on("c") == core)
        def _():
            for segment in SEGMENTS:
                at, sent = segment[2 + core], segment[2 + 1 - core]
                if at is not None:
                    rows = segment[1]
                    mine_ref[at:at + rows, :] = (
                        send_ref[sent:sent + rows, :] if sent is not None else sorted_rows(segment, slots, x)
                    )
    total = jnp.zeros((8, GUESTS), f32)
    step = 16
    for first in range(0, CHIPS, step):
        flat = lambda ref: jnp.concatenate([ref[s:s + 1, :] for s in range(first, first + step)], axis=1)
        places = flat(pos_ref) + 1
        parts = jnp.where(iota((8, step * LANES), 0) == 0, places >> 5, places & 31).astype(f32).astype(bf16)
        total = total + dot_last(parts, as_bf16(iota((GUESTS, step * LANES), 0) == flat(key_ref)))
    far_ref[...] = jnp.broadcast_to((32.0 * total[:1] + total[1:2]).astype(i32), far_ref.shape)


def fit_kernel(block, units, x_ref, over_ref):
    _, chip_counts = labels_of(block, x_ref)
    counts, sizes = counts_of(chip_counts)
    ordered = in_order(sizes)
    over = jnp.zeros((1, LANES), f32)
    for size, cap in zip(ordered, CAPS):
        over = jnp.maximum(over, jnp.where(size > cap, 1.0, 0.0))
    for share in SHARES:
        length = 0.0
        for q, first in share:
            rows = jnp.maximum(jnp.floor((ordered[q] + (UNIT - 1.0)) * (1 / UNIT)) - first // UNIT, 0.0)
            length = length + jnp.where(rows >= 3.0, rows - 1.0, rows)
        over = jnp.maximum(over, jnp.where(length > 4 * units, 1.0, 0.0))
    taken = counts[0] + counts[1] + counts[2] + counts[3]
    lane = iota(taken.shape, 1) & 3
    before = lambda v, back: jnp.where(lane >= back, pltpu.roll(v, back, 1), pltpu.roll(v, LANES - 4 + back, 1))
    extra = taken - (block - 1)
    moved = passed_on(extra, before)
    held = jnp.sum(moved, axis=0, keepdims=True)
    over = jnp.maximum(over, jnp.where(held > GUESTS, 1.0, 0.0))
    full = extra + before(extra, 1) + before(extra, 2) + before(extra, 3) > 0
    full = jnp.where(full | (moved > block - 1), 1.0, 0.0)
    over = jnp.maximum(over, jnp.max(full, axis=0, keepdims=True))
    over_ref[...] = jnp.broadcast_to(jnp.max(over, axis=1, keepdims=True), over_ref.shape).astype(i32)


def add_guests(core, base_ref, guest_ref, far_ref, out_ref):
    guests, far = guest_ref[...], far_ref[:1, :]
    for segment in SEGMENTS:
        at, rows = segment[2 + core], segment[1]
        if at is not None:
            out_ref[at:at + rows, :] = base_ref[at:at + rows, :] + sorted_rows(segment, far, guests)


def blocks_of(core):
    for q, first in SHARES[core]:
        at = BASES[core][q] + first
        yield q, first, pl.ds(at, CAPS[q] - first), pl.ds(at, LANES)


RAW_ROWS = max(sum(CAPS[q] - first for q, first in share) for share in SHARES)


def own_kernel(x_ref, guest_ref, far_ref, raw_ref, rows_ref):
    for core in range(2):
        @pl.when(index_on("c") == core)
        def _():
            add_guests(core, x_ref, guest_ref, far_ref, rows_ref)
            at = 0
            for q, first, left, right in blocks_of(core):
                rows = CAPS[q] - first
                raw_ref[at:at + rows, :] = dot_last(rows_ref[left, :], rows_ref[right, :])
                at += rows


def size_of(meta_ref, q):
    return jnp.max(meta_ref[q:q + 1, :].astype(f32)).astype(i32)


def length_of(size, first):
    units = jnp.maximum(((size + UNIT - 1) >> 5) - first // UNIT, 0)
    return jnp.where(units >= 3, units - 1, units)


def folded(score):
    away = jnp.full((UNIT, LANES), -4.0, f32) if score.shape[0] < LANES else score[2 * UNIT:3 * UNIT]
    both = jnp.where(iota(away.shape, 1) < 3 * UNIT, away, pltpu.roll(score[:UNIT], 3 * UNIT, 1))
    rest = [score[3 * UNIT:]] if score.shape[0] > 3 * UNIT else []
    return jnp.concatenate([both, score[UNIT:2 * UNIT]] + rest, axis=0)


def gram_kernel(units, meta_ref, x_ref, guest_ref, far_ref, raw_ref, out0, out1, out2, out3, part_ref, rows_ref):
    y, c = index_on("y"), index_on("c")
    part_ref[...] = jnp.full(part_ref.shape, -4.0, f32)
    for core in range(2):
        @pl.when(c == core)
        def _():
            add_guests(core, x_ref, guest_ref, far_ref, rows_ref)
            at, to = 0, jnp.zeros((), i32)
            for q, first, left, right in blocks_of(core):
                rows = CAPS[q] - first
                score = raw_ref[at:at + rows, :] + dot_last(rows_ref[left, :], rows_ref[right, :])
                at += rows
                size = size_of(meta_ref, q)
                i, j = iota(score.shape, 0), iota(score.shape, 1)
                keep = (i < size - first) & (j < size - first) & (i != j)
                score = folded(jnp.where(keep, score, -4.0))
                part_ref[pl.ds(pl.multiple_of(to, UNIT), score.shape[0]), :] = score
                to = jnp.minimum(to + UNIT * length_of(size, first), 4 * units * UNIT)
    chunk = units * UNIT
    for shift, out in enumerate((out0, out1, out2, out3)):
        out[...] = part_ref[pl.ds(pl.multiple_of(lax.rem(y + shift, 4) * chunk, UNIT), chunk), :]


FIRST_ROW = (0, 6, 10, 13)


def max_kernel(units, meta_ref, p0, p1, p2, p3, pos_ref, out_ref, best_ref):
    y, c = index_on("y"), index_on("c")
    best_ref[...] = jnp.full(best_ref.shape, -1.0, f32)
    sub, lane = iota((UNIT, LANES), 0), iota((UNIT, LANES), 1)
    blocks, sizes = [], [size_of(meta_ref, q) for q in range(4)]
    for core, share in enumerate(SHARES):
        at = jnp.zeros((), i32)
        for q, first in share:
            length = length_of(sizes[q], first)
            blocks.append((jnp.where((c == core) & (length > 0), at, 4 * units), FIRST_ROW[q] + first // LANES, at))
            at = at + length
    for t in range(units):
        at = slice(t * UNIT, (t + 1) * UNIT)
        block = (p0[at, :] + p1[at, :]) + (p2[at, :] + p3[at, :])
        index = y * units + t
        col, start = jnp.asarray(15, i32), jnp.asarray(0, i32)
        for block_start, block_col, block_at in blocks:
            inside = index >= block_start
            col, start = jnp.where(inside, block_col, col), jnp.where(inside, block_at, start)
        turn = index - start
        unit = 4 * col + jnp.where(turn == 0, 2, jnp.where(turn == 1, 1, turn + 1))
        unit = jnp.minimum(jnp.maximum(unit, 0), 63)
        beside = (lane >= 3 * UNIT) & (turn == 0)
        one, two = jnp.where(beside, -4.0, block), jnp.where(beside, block, -4.0)
        along = jnp.max(one, axis=1, keepdims=True)
        along = jnp.max(jnp.where(sub + (unit & 3) * UNIT == lane, along, -1.0), axis=0, keepdims=True)
        row = unit >> 2
        best_ref[pl.ds(row, 1), :] = jnp.maximum(best_ref[pl.ds(row, 1), :], along)
        down = jnp.max(one, axis=0, keepdims=True)
        along = jnp.max(two, axis=1, keepdims=True)
        two = jnp.maximum(jnp.where(sub == lane, along, -1.0), pltpu.roll(two, UNIT, 1))
        down = jnp.maximum(down, jnp.max(two, axis=0, keepdims=True))
        best_ref[pl.ds(col, 1), :] = jnp.maximum(best_ref[pl.ds(col, 1), :], down)
    pos = pos_ref[...]
    pos = jnp.where(pos >= STARTS[1], pos + 64, pos)
    pos = jnp.where(pos >= STARTS[3] + 64, pos + 64, pos)
    row, lane = pos >> 7, pos & (LANES - 1)
    out = jnp.full(pos.shape, -1.0, f32)
    for r in range(15):
        value = jnp.broadcast_to(best_ref[r:r + 1, :], pos.shape)
        value = jnp.take_along_axis(value, lane, axis=1, mode="promise_in_bounds")
        out = jnp.where(row == r, value, out)
    out_ref[:CHIPS, :] = out
    out_ref[CHIPS:, :] = out


def pick_kernel(v_ref, code_ref, out_ref):
    c = index_on("c")
    values = jnp.maximum(v_ref[:CHIPS, :], v_ref[CHIPS:, :])
    values = jnp.max(values.reshape(BINS, 4, LANES), axis=1)
    eye = iota((LANES, LANES), 0) == iota((LANES, LANES), 1)
    code = jnp.max(jnp.where(iota((8, ROWS), 0) == c, code_ref[...], -1), axis=0, keepdims=True)
    code = jnp.max(jnp.where(eye, code.astype(f32), -1.0), axis=1, keepdims=True).astype(i32)
    slot = iota((ROWS, LANES), 1)
    best = jnp.full((ROWS, LANES), -1.0, f32)
    for b in range(BINS):
        best = jnp.where(slot + b * LANES == code, values[b:b + 1], best)
    best = jnp.max(best, axis=1, keepdims=True)
    out_ref[...] = jnp.max(jnp.where(eye, best, -1.0), axis=0, keepdims=True)


def gather_groups(embeddings, cluster_ids):
    split = ("z", "y", "c")
    rows = embeddings.shape[0]
    groups = lax.axis_size("x")
    cap = 2 * rows // groups
    slots = groups * cap
    owner_of = cluster_ids % groups
    onehot = (owner_of[:, None] == jnp.arange(groups, dtype=i32)[None, :]).astype(i32)
    before = jnp.cumsum(onehot, axis=0) - onehot
    rank = jnp.sum(before * onehot, axis=1)
    place = owner_of * cap + rank
    picked = place[None, :] == jnp.arange(slots, dtype=i32)[:, None]
    filled = jnp.any(picked, axis=1)
    source = jnp.sum(jnp.where(picked, jnp.arange(rows, dtype=i32)[None, :], 0), axis=1)
    out_labels = jnp.where(filled, cluster_ids[source], -1)
    squares = jnp.sum(embeddings * embeddings, axis=1, keepdims=True)
    local_unit = (embeddings * lax.rsqrt(squares + 1e-06)).astype(bf16)
    outgoing_unit = jnp.where(filled[:, None], local_unit[source], jnp.zeros((), bf16))
    unit = lax.all_to_all(outgoing_unit, "x", split_axis=0, concat_axis=0, tiled=True)
    labels = lax.all_to_all(out_labels, "x", split_axis=0, concat_axis=0, tiled=True)
    members = lax.axis_size(split)

    def everywhere(v):
        copies = jnp.broadcast_to(v[None], (members,) + v.shape).reshape((members * slots,) + v.shape[1:])
        return lax.all_to_all(copies, split, split_axis=0, concat_axis=0, tiled=True)

    def add_slice(i, scores):
        part = lax.dynamic_slice_in_dim(unit, i * WIDTH, WIDTH, 1)
        return scores + dot_last(part, everywhere(part))

    scores = lax.fori_loop(0, embeddings.shape[1] // WIDTH, add_slice, jnp.zeros((slots, members * slots), f32))
    all_labels = everywhere(labels)
    own = lax.axis_index(split) * slots + jnp.arange(slots, dtype=i32)
    mask = (
        (labels[:, None] == all_labels[None, :])
        & (labels[:, None] >= 0)
        & (own[:, None] != jnp.arange(members * slots, dtype=i32)[None, :])
    )
    scores = jnp.where(mask, scores, -1.0)
    best = jnp.maximum(-1.0, jnp.max(scores, axis=1))
    returned = lax.all_to_all(best, "x", split_axis=0, concat_axis=0, tiled=True)
    return returned[place]


def route(block, units, embeddings, cluster_ids):
    shape = jax.ShapeDtypeStruct
    half = shape((ROWS + LABEL_ROWS, HALF_WIDTH), bf16)
    keep, send = pl.pallas_call(
        unit_kernel, out_shape=(half, half),
        in_specs=[WHOLE, WHOLE], out_specs=(WHOLE, WHOLE), compiler_params=params(12), name="unit",
    )(embeddings, cluster_ids.reshape(1, ROWS))
    got = lax.ppermute(send, "c", [(0, 1), (1, 0)])
    packed, code = pl.pallas_call(
        functools.partial(pack_kernel, block),
        out_shape=(shape((CHIPS, block, WIDTH), bf16), shape((8, ROWS), i32)),
        in_specs=[WHOLE, WHOLE], out_specs=(WHOLE, WHOLE), compiler_params=params(20), name="pack",
    )(keep, got)
    packed = lax.all_to_all(packed, ("x", "z", "y"), 0, 0, tiled=True)
    table = shape((CHIPS, LANES), i32)
    guests, line, key, pos, meta = pl.pallas_call(
        functools.partial(names_kernel, block),
        out_shape=(shape((GUESTS, WIDTH), bf16), shape((8, CHIPS * block), i32), table, table, shape((8, LANES), i32)),
        in_specs=[WHOLE], out_specs=(WHOLE,) * 5, compiler_params=params(12), name="names",
    )(packed)
    brought = lax.ppermute(guests, "z", [(i, (i + 3) % 4) for i in range(4)])
    share = shape((SHARE_ROWS, WIDTH), bf16)
    slots = CHIPS * block
    send = pl.pallas_call(
        functools.partial(send_kernel, block), out_shape=share,
        in_specs=[WHOLE, WHOLE], out_specs=WHOLE, compiler_params=params(16), name="send",
        cost_estimate=pl.CostEstimate(flops=2 * SHARE_ROWS * WIDTH * slots, bytes_accessed=4 << 20, transcendentals=0),
    )(packed, line)
    other = lax.ppermute(send, "c", [(0, 1), (1, 0)])
    mine, far = pl.pallas_call(
        functools.partial(mine_kernel, block), out_shape=(share, shape((8, GUESTS), i32)),
        in_specs=[WHOLE] * 5, out_specs=(WHOLE,) * 2, compiler_params=params(20), name="mine",
        cost_estimate=pl.CostEstimate(flops=2 * SHARE_ROWS * WIDTH * slots, bytes_accessed=4 << 20, transcendentals=0),
    )(packed, line, send, key, pos)
    brought, mine = lax.optimization_barrier((brought, mine))
    swapped = lax.ppermute(brought, "c", [(0, 1), (1, 0)])
    raw = pl.pallas_call(
        own_kernel, out_shape=shape((RAW_ROWS, LANES), f32),
        in_specs=[WHOLE] * 3, out_specs=WHOLE,
        scratch_shapes=[pltpu.VMEM((SHARE_ROWS, WIDTH), bf16)],
        compiler_params=params(16), name="own",
        cost_estimate=pl.CostEstimate(flops=2 * RAW_ROWS * LANES * WIDTH, bytes_accessed=4 << 20, transcendentals=0),
    )(mine, brought, far)
    partial = pl.pallas_call(
        functools.partial(gram_kernel, units),
        out_shape=[shape((units * UNIT, LANES), f32)] * 4,
        in_specs=[WHOLE] * 5, out_specs=[WHOLE] * 4,
        scratch_shapes=[pltpu.VMEM((4 * units * UNIT + CAPS[0], LANES), f32), pltpu.VMEM((SHARE_ROWS, WIDTH), bf16)],
        compiler_params=params(16), name="gram",
    )(meta, other, swapped, far, raw)
    arrived = [partial[0]] + [
        lax.ppermute(partial[s], "y", [(i, (i + s) % 4) for i in range(4)]) for s in (1, 2, 3)
    ]
    over = pl.pallas_call(
        functools.partial(fit_kernel, block, units), out_shape=shape((8, LANES), i32),
        in_specs=[WHOLE], out_specs=WHOLE, compiler_params=params(8), name="fit",
    )(packed)
    arrived, fits = lax.optimization_barrier((arrived, over[0, 0] == 0))
    best = pl.pallas_call(
        functools.partial(max_kernel, units),
        out_shape=shape((2 * CHIPS, LANES), f32),
        in_specs=[WHOLE] * 6, out_specs=WHOLE,
        scratch_shapes=[pltpu.VMEM((16, LANES), f32)],
        compiler_params=params(8), name="maxima",
    )(meta, *arrived, pos)
    back = lax.all_to_all(best.reshape(2 * CHIPS, 1, LANES), ("c", "x", "z", "y"), 0, 0, tiled=True)
    back, fits = lax.optimization_barrier((back, fits))
    best = pl.pallas_call(
        pick_kernel,
        out_shape=shape((1, ROWS), f32),
        in_specs=[WHOLE, WHOLE], out_specs=WHOLE, compiler_params=params(8), name="pick",
    )(back.reshape(2 * CHIPS, LANES), code).reshape(ROWS)
    return best, fits


def on_device(embeddings, cluster_ids, tries=TRIES):
    if not tries:
        return gather_groups(embeddings, cluster_ids)
    best, fits = route(*tries[0], embeddings, cluster_ids)
    return lax.cond(
        fits,
        lambda best, embeddings, cluster_ids: best,
        lambda best, embeddings, cluster_ids: on_device(embeddings, cluster_ids, tries[1:]),
        best, embeddings, cluster_ids,
    )


def solution(mesh):
    axes = ("x", "z", "y", "c")
    grid = Mesh(mesh.devices.reshape(4, 4, 4, 2), axes)
    return jax.shard_map(
        on_device, mesh=grid, in_specs=(P(axes, None), P(axes)), out_specs=P(axes), check_vma=False
    )
```

```python
import functools

import jax
import jax.numpy as jnp
from jax import lax
from jax.experimental import pallas as pl
from jax.experimental.pallas import tpu as pltpu
from jax.sharding import Mesh, PartitionSpec as P

ROWS = 128
HALF_WIDTH = 2048
WIDTH = 512
LABEL_ROWS = 16
BINS = 16
CHIPS = 64
TRIES = ((24, 11), (32, 16))
GROUP = 32
GUESTS = 64
GUEST = 4096
LANES = 128
CAPS = (704, 512, 320, 192)
STARTS = (0, 704, 1216, 1536)
UNIT = 32
SHARES = (
    ((0, 0), (0, 256), (2, 0), (2, 128), (2, 256), (3, 0)),
    ((0, 128), (0, 384), (0, 512), (0, 640), (1, 0), (1, 128), (1, 256), (1, 384), (3, 128)),
)
BASES = ({0: 0, 2: 704, 3: 1024}, {0: -128, 1: 576, 3: 960})
SHARE_ROWS = 1216
SEGMENTS = (
    (0, 128, 0, None), (128, 576, 128, 0), (704, 256, None, 576), (960, 256, None, 832),
    (1216, 320, 704, None), (1536, 128, 1024, None), (1664, 64, 1152, 1088),
)
f32, bf16, i32 = jnp.float32, jnp.bfloat16, jnp.int32
WHOLE = pl.BlockSpec(memory_space=pltpu.VMEM)


def params(mib):
    return pltpu.CompilerParams(vmem_limit_bytes=mib * 1024 * 1024)


def index_on(axis):
    return lax.axis_index(axis)


def iota(shape, dim):
    return lax.broadcasted_iota(i32, shape, dim)


def dot_last(a, b):
    return lax.dot_general(a, b, (((1,), (1,)), ((), ())), preferred_element_type=f32)


def dot(a, b):
    return lax.dot_general(a, b, (((1,), (0,)), ((), ())), preferred_element_type=f32)


def as_bf16(mask):
    return jnp.where(mask, 1.0, 0.0).astype(bf16)


def bin_of(labels):
    rank, residue = labels >> 2, labels & 3
    row, col = rank >> 2, rank & 3
    col = jnp.where((row & 1) == 1, 3 - col, col)
    return 4 * col + ((row - residue) & 3)


def unit_kernel(x_ref, ids_ref, keep_ref, send_ref):
    c = index_on("c")
    x = x_ref[...]
    scale = lax.rsqrt(jnp.sum(x * x, axis=1, keepdims=True) + 1e-06)
    ids = jnp.concatenate([ids_ref[...].astype(f32), jnp.zeros((1, HALF_WIDTH - ROWS), f32)], axis=1)
    ids = jnp.broadcast_to(ids, (LABEL_ROWS, HALF_WIDTH)).astype(bf16)
    for half, out_ref in ((c, keep_ref), (1 - c, send_ref)):
        columns = pl.ds(pl.multiple_of(half * HALF_WIDTH, HALF_WIDTH), HALF_WIDTH)
        out_ref[:ROWS, :] = (x_ref[:, columns] * scale).astype(bf16)
        out_ref[ROWS:, :] = ids


def passed_on(over, before):
    once = before(over, 1)
    twice = before(over, 2)
    return jnp.maximum(jnp.maximum(over, 0), jnp.maximum(over + once, over + once + twice))


def pack_kernel(block, keep_ref, got_ref, out_ref, code_ref):
    first = index_on("c") == 0
    kept = jnp.max(keep_ref[ROWS:, :ROWS].astype(f32), axis=0, keepdims=True)
    got = jnp.max(got_ref[ROWS:, :ROWS].astype(f32), axis=0, keepdims=True)
    labels = jnp.concatenate([jnp.where(first, kept, got), jnp.where(first, got, kept)], axis=0).astype(i32)
    bins = bin_of(labels)
    upper = as_bf16(iota((ROWS, ROWS), 0) < iota((ROWS, ROWS), 1))

    def ranks_within(masks):
        member = jnp.concatenate([jnp.where(mask, 1.0, 0.0) for mask in masks], axis=0)
        row, col = iota((member.shape[0],) * 2, 0), iota((member.shape[0],) * 2, 1)
        earlier = dot(as_bf16(((row >> 1) == (col >> 1)) & (col < row)), member.astype(bf16))
        ranks = member * (dot(member.astype(bf16), upper) + jnp.sum(earlier, axis=1, keepdims=True))
        rank = sum(ranks[2 * b:2 * b + 2] for b in range(len(masks)))
        return rank.astype(i32), jnp.sum(member, axis=1, keepdims=True)

    rank, sizes = ranks_within([bins == b for b in range(BINS)])
    quad, line = bins >> 2, bins & 3
    taken = []
    for at in range(4):
        size = jnp.zeros(labels.shape, f32)
        for b in range(at, BINS, 4):
            size = jnp.where(quad == b >> 2, sizes[2 * b:2 * b + 1] + sizes[2 * b + 1:2 * b + 2], size)
        taken.append(size.astype(i32) - (block - 1))
    stays = []
    for at in range(4):
        moved = passed_on(taken[at], lambda _, back: taken[(at - back) & 3])
        stays.append(taken[at] + (block - 1) - moved)

    def of_line(values, which):
        out = values[0]
        for at in range(1, 4):
            out = jnp.where(which == at, values[at], out)
        return out

    stay = of_line(stays, line)
    to_line = jnp.where(rank < stay, line, (line + 1) & 3)
    to_slot = jnp.where(rank < stay, rank, of_line(stays, to_line) + rank - stay)
    placed = to_slot < (block - 1)
    lane = jnp.where(placed, to_line * GROUP + to_slot, -1)
    place = jnp.where(placed, (quad * 4 + to_line) * block + to_slot, -1)
    code_ref[...] = jnp.concatenate([jnp.where(placed, bins * LANES + lane, -1)] * 4, axis=0)
    docs = 2 * ROWS
    flat = lambda v: jnp.concatenate([v[:1], v[1:]], axis=1)
    label_row = flat(labels)
    counts = dot_last(jnp.ones((8, docs), bf16), as_bf16(iota((LANES, docs), 0) == label_row))[:1]
    named = jnp.where(iota((8, docs), 0) == flat(quad), (label_row + 1).astype(f32), 0.0).astype(bf16)
    names = dot_last(named, as_bf16(iota((LANES, docs), 0) == flat(lane)))
    own = jnp.where(first, place[:1], place[1:])
    other = jnp.where(first, place[1:], place[:1])
    onehot = as_bf16(iota((BINS * block, docs), 0) == jnp.concatenate([own, other], axis=1))
    is_last = iota((block, WIDTH), 0) == (block - 1)
    for y in range(4):
        columns = slice(y * WIDTH, (y + 1) * WIDTH)
        x = jnp.concatenate([keep_ref[:ROWS, columns], got_ref[:ROWS, columns]], axis=0)
        packed = dot(onehot, x)
        for b in range(BINS):
            extra = jnp.concatenate([names[b // 4:b // 4 + 1], counts, jnp.zeros((1, 2 * LANES), f32)], axis=1)
            out_ref[4 * b + y] = jnp.where(is_last, extra, packed[b * block:(b + 1) * block]).astype(bf16)


def labels_of(block, x_ref):
    tail = x_ref[:, block - 8:, :2 * LANES].astype(f32)
    tail = jnp.max(jnp.where(iota(tail.shape, 1) == 7, tail, 0.0), axis=1)
    return tail[:, :LANES].astype(i32) - 1, tail[:, LANES:].astype(bf16)


def counts_of(chip_counts):
    row, col = iota((LANES, LANES), 0), iota((LANES, LANES), 1)
    in_bin = (bin_of(row) == col) & (row < 4 * BINS)
    counts = [dot(chip_counts, as_bf16(in_bin & ((row & 3) == r))) for r in range(4)]
    return counts, [jnp.sum(v, axis=0, keepdims=True) for v in counts]


def in_order(sizes):
    a, b = jnp.maximum(sizes[0], sizes[1]), jnp.minimum(sizes[0], sizes[1])
    c, d = jnp.maximum(sizes[2], sizes[3]), jnp.minimum(sizes[2], sizes[3])
    first, e = jnp.maximum(a, c), jnp.minimum(a, c)
    g, fourth = jnp.maximum(b, d), jnp.minimum(b, d)
    return first, jnp.maximum(e, g), jnp.minimum(e, g), fourth


def names_kernel(block, x_ref, guest_ref, line_ref, key_ref, pos_ref, meta_ref):
    z = index_on("z")
    labels, _ = labels_of(block, x_ref)
    row, col = iota((LANES, LANES), 0), iota((LANES, LANES), 1)
    lane = iota(labels.shape, 1)
    group = lane >> 5
    valid = labels >= 0
    home = bin_of(labels) & 3
    at_home = valid & (home == z)
    upper = as_bf16(row < col)
    lower = as_bf16(iota((CHIPS, CHIPS), 1) < iota((CHIPS, CHIPS), 0))
    members, n = [at_home & ((labels & 3) == r) for r in range(4)], []
    for member in members:
        size = jnp.sum(jnp.where(member, 1.0, 0.0), axis=0, keepdims=True)
        n.append(jnp.sum(size, axis=1, keepdims=True))
    wide = lambda v: jnp.broadcast_to(v, (1, LANES))
    meta_ref[...] = jnp.concatenate([wide(v) for v in in_order(n)] * 2, axis=0).astype(i32)
    pos = jnp.full(labels.shape, -1.0, f32)
    for r, member in enumerate(members):
        place = sum(
            jnp.where((n[q] > n[r]) | ((n[q] == n[r]) & (q < r)), 1.0, 0.0) for q in range(4) if q != r
        )
        start = jnp.where(
            place < 0.5, float(STARTS[0]),
            jnp.where(place < 1.5, float(STARTS[1]), jnp.where(place < 2.5, float(STARTS[2]), float(STARTS[3]))),
        )
        member16 = as_bf16(member)
        rank = dot(member16, upper) + jnp.sum(dot(lower, member16), axis=1, keepdims=True)
        pos = jnp.where(member, start + rank, pos)
    pos = pos.astype(i32)
    pos_ref[...] = pos
    guest = valid & (home != group)
    guest16 = as_bf16(guest)
    same = (row >> 5) == (col >> 5)
    turn = dot(guest16, as_bf16(same & (row < col))) + dot(dot(lower, guest16).astype(bf16), as_bf16(same))
    turn = turn.astype(i32)
    away = at_home & (group != z) & (turn < GUESTS)
    key_ref[...] = jnp.where(away, turn, -1)
    per, groups = 16, CHIPS // 16
    value = jnp.where(group == z, jnp.where(guest, GUEST + turn, pos + 1), 0).astype(f32)
    value = pltpu.roll(value, lax.rem(LANES - GROUP * z, LANES), 1)
    value = jnp.where(lane < block, value, 0.0)
    lined = jnp.zeros((8, per * block), f32)
    for t in range(per):
        rows = jnp.concatenate([value[per * g + t:per * g + t + 1] for g in range(groups)] * 2, axis=0)
        rows = jnp.concatenate([rows, jnp.zeros((8, per * block - LANES), f32)], axis=1)
        lined = lined + (pltpu.roll(rows, t * block, 1) if t else rows)
    slots = jnp.concatenate([lined[g:g + 1] for g in range(groups)], axis=1).astype(i32)
    line_ref[...] = jnp.broadcast_to(slots, line_ref.shape)
    onehot = as_bf16(iota((GUESTS, CHIPS * block), 0) + GUEST == slots)
    guest_ref[...] = dot(onehot, x_ref[...].reshape(CHIPS * block, WIDTH)).astype(bf16)


def sorted_rows(segment, slots, x):
    onehot = as_bf16(iota((segment[1], x.shape[0]), 0) + (segment[0] + 1) == slots)
    return dot(onehot, x).astype(bf16)


def sort_kernel(block, x_ref, line_ref, key_ref, pos_ref, send_ref, mine_ref, far_ref):
    x = x_ref[...].reshape(CHIPS * block, WIDTH)
    slots = line_ref[:1, :]
    for core in range(2):
        @pl.when(index_on("c") == core)
        def _():
            for segment in SEGMENTS:
                rows = sorted_rows(segment, slots, x)
                for out_ref, at in ((mine_ref, segment[2 + core]), (send_ref, segment[2 + 1 - core])):
                    if at is not None:
                        out_ref[at:at + segment[1], :] = rows
    total = jnp.zeros((8, GUESTS), f32)
    step = 16
    for first in range(0, CHIPS, step):
        flat = lambda ref: jnp.concatenate([ref[s:s + 1, :] for s in range(first, first + step)], axis=1)
        places = flat(pos_ref) + 1
        parts = jnp.where(iota((8, step * LANES), 0) == 0, places >> 5, places & 31).astype(f32).astype(bf16)
        total = total + dot_last(parts, as_bf16(iota((GUESTS, step * LANES), 0) == flat(key_ref)))
    far_ref[...] = jnp.broadcast_to((32.0 * total[:1] + total[1:2]).astype(i32), far_ref.shape)


def fit_kernel(block, units, x_ref, over_ref):
    _, chip_counts = labels_of(block, x_ref)
    counts, sizes = counts_of(chip_counts)
    ordered = in_order(sizes)
    over = jnp.zeros((1, LANES), f32)
    for size, cap in zip(ordered, CAPS):
        over = jnp.maximum(over, jnp.where(size > cap, 1.0, 0.0))
    for share in SHARES:
        length = 0.0
        for q, first in share:
            rows = jnp.maximum(jnp.floor((ordered[q] + (UNIT - 1.0)) * (1 / UNIT)) - first // UNIT, 0.0)
            length = length + jnp.where(rows >= 3.0, rows - 1.0, rows)
        over = jnp.maximum(over, jnp.where(length > 4 * units, 1.0, 0.0))
    taken = counts[0] + counts[1] + counts[2] + counts[3]
    lane = iota(taken.shape, 1) & 3
    before = lambda v, back: jnp.where(lane >= back, pltpu.roll(v, back, 1), pltpu.roll(v, LANES - 4 + back, 1))
    extra = taken - (block - 1)
    moved = passed_on(extra, before)
    held = jnp.sum(moved, axis=0, keepdims=True)
    over = jnp.maximum(over, jnp.where(held > GUESTS, 1.0, 0.0))
    full = extra + before(extra, 1) + before(extra, 2) + before(extra, 3) > 0
    full = jnp.where(full | (moved > block - 1), 1.0, 0.0)
    over = jnp.maximum(over, jnp.max(full, axis=0, keepdims=True))
    over_ref[...] = jnp.broadcast_to(jnp.max(over, axis=1, keepdims=True), over_ref.shape).astype(i32)


def add_guests(core, base_ref, guest_ref, far_ref, out_ref):
    guests, far = guest_ref[...], far_ref[:1, :]
    for segment in SEGMENTS:
        at, rows = segment[2 + core], segment[1]
        if at is not None:
            out_ref[at:at + rows, :] = base_ref[at:at + rows, :] + sorted_rows(segment, far, guests)


def blocks_of(core):
    for q, first in SHARES[core]:
        at = BASES[core][q] + first
        yield q, first, pl.ds(at, CAPS[q] - first), pl.ds(at, LANES)


RAW_ROWS = max(sum(CAPS[q] - first for q, first in share) for share in SHARES)


def own_kernel(x_ref, guest_ref, far_ref, raw_ref, rows_ref):
    for core in range(2):
        @pl.when(index_on("c") == core)
        def _():
            add_guests(core, x_ref, guest_ref, far_ref, rows_ref)
            at = 0
            for q, first, left, right in blocks_of(core):
                rows = CAPS[q] - first
                raw_ref[at:at + rows, :] = dot_last(rows_ref[left, :], rows_ref[right, :])
                at += rows


def size_of(meta_ref, q):
    return jnp.max(meta_ref[q:q + 1, :].astype(f32)).astype(i32)


def length_of(size, first):
    units = jnp.maximum(((size + UNIT - 1) >> 5) - first // UNIT, 0)
    return jnp.where(units >= 3, units - 1, units)


def folded(score):
    away = jnp.full((UNIT, LANES), -4.0, f32) if score.shape[0] < LANES else score[2 * UNIT:3 * UNIT]
    both = jnp.where(iota(away.shape, 1) < 3 * UNIT, away, pltpu.roll(score[:UNIT], 3 * UNIT, 1))
    rest = [score[3 * UNIT:]] if score.shape[0] > 3 * UNIT else []
    return jnp.concatenate([both, score[UNIT:2 * UNIT]] + rest, axis=0)


def gram_kernel(units, meta_ref, x_ref, guest_ref, far_ref, raw_ref, out0, out1, out2, out3, part_ref, rows_ref):
    y, c = index_on("y"), index_on("c")
    part_ref[...] = jnp.full(part_ref.shape, -4.0, f32)
    for core in range(2):
        @pl.when(c == core)
        def _():
            add_guests(core, x_ref, guest_ref, far_ref, rows_ref)
            at, to = 0, jnp.zeros((), i32)
            for q, first, left, right in blocks_of(core):
                rows = CAPS[q] - first
                score = raw_ref[at:at + rows, :] + dot_last(rows_ref[left, :], rows_ref[right, :])
                at += rows
                size = size_of(meta_ref, q)
                i, j = iota(score.shape, 0), iota(score.shape, 1)
                keep = (i < size - first) & (j < size - first) & (i != j)
                score = folded(jnp.where(keep, score, -4.0))
                part_ref[pl.ds(pl.multiple_of(to, UNIT), score.shape[0]), :] = score
                to = jnp.minimum(to + UNIT * length_of(size, first), 4 * units * UNIT)
    chunk = units * UNIT
    for shift, out in enumerate((out0, out1, out2, out3)):
        out[...] = part_ref[pl.ds(pl.multiple_of(lax.rem(y + shift, 4) * chunk, UNIT), chunk), :]


FIRST_ROW = (0, 6, 10, 13)


def max_kernel(units, meta_ref, p0, p1, p2, p3, pos_ref, out_ref, best_ref):
    y, c = index_on("y"), index_on("c")
    best_ref[...] = jnp.full(best_ref.shape, -1.0, f32)
    sub, lane = iota((UNIT, LANES), 0), iota((UNIT, LANES), 1)
    blocks, sizes = [], [size_of(meta_ref, q) for q in range(4)]
    for core, share in enumerate(SHARES):
        at = jnp.zeros((), i32)
        for q, first in share:
            length = length_of(sizes[q], first)
            blocks.append((jnp.where((c == core) & (length > 0), at, 4 * units), FIRST_ROW[q] + first // LANES, at))
            at = at + length
    for t in range(units):
        at = slice(t * UNIT, (t + 1) * UNIT)
        block = (p0[at, :] + p1[at, :]) + (p2[at, :] + p3[at, :])
        index = y * units + t
        col, start = jnp.asarray(15, i32), jnp.asarray(0, i32)
        for block_start, block_col, block_at in blocks:
            inside = index >= block_start
            col, start = jnp.where(inside, block_col, col), jnp.where(inside, block_at, start)
        turn = index - start
        unit = 4 * col + jnp.where(turn == 0, 2, jnp.where(turn == 1, 1, turn + 1))
        unit = jnp.minimum(jnp.maximum(unit, 0), 63)
        beside = (lane >= 3 * UNIT) & (turn == 0)
        one, two = jnp.where(beside, -4.0, block), jnp.where(beside, block, -4.0)
        along = jnp.max(one, axis=1, keepdims=True)
        along = jnp.max(jnp.where(sub + (unit & 3) * UNIT == lane, along, -1.0), axis=0, keepdims=True)
        row = unit >> 2
        best_ref[pl.ds(row, 1), :] = jnp.maximum(best_ref[pl.ds(row, 1), :], along)
        down = jnp.max(one, axis=0, keepdims=True)
        along = jnp.max(two, axis=1, keepdims=True)
        two = jnp.maximum(jnp.where(sub == lane, along, -1.0), pltpu.roll(two, UNIT, 1))
        down = jnp.maximum(down, jnp.max(two, axis=0, keepdims=True))
        best_ref[pl.ds(col, 1), :] = jnp.maximum(best_ref[pl.ds(col, 1), :], down)
    pos = pos_ref[...]
    pos = jnp.where(pos >= STARTS[1], pos + 64, pos)
    pos = jnp.where(pos >= STARTS[3] + 64, pos + 64, pos)
    row, lane = pos >> 7, pos & (LANES - 1)
    out = jnp.full(pos.shape, -1.0, f32)
    for r in range(15):
        value = jnp.broadcast_to(best_ref[r:r + 1, :], pos.shape)
        value = jnp.take_along_axis(value, lane, axis=1, mode="promise_in_bounds")
        out = jnp.where(row == r, value, out)
    out_ref[:CHIPS, :] = out
    out_ref[CHIPS:, :] = out


def pick_kernel(v_ref, code_ref, out_ref):
    c = index_on("c")
    values = jnp.maximum(v_ref[:CHIPS, :], v_ref[CHIPS:, :])
    values = jnp.max(values.reshape(BINS, 4, LANES), axis=1)
    eye = iota((LANES, LANES), 0) == iota((LANES, LANES), 1)
    code = jnp.max(jnp.where(iota((8, ROWS), 0) == c, code_ref[...], -1), axis=0, keepdims=True)
    code = jnp.max(jnp.where(eye, code.astype(f32), -1.0), axis=1, keepdims=True).astype(i32)
    slot = iota((ROWS, LANES), 1)
    best = jnp.full((ROWS, LANES), -1.0, f32)
    for b in range(BINS):
        best = jnp.where(slot + b * LANES == code, values[b:b + 1], best)
    best = jnp.max(best, axis=1, keepdims=True)
    out_ref[...] = jnp.max(jnp.where(eye, best, -1.0), axis=0, keepdims=True)


def gather_groups(embeddings, cluster_ids):
    split = ("z", "y", "c")
    rows = embeddings.shape[0]
    groups = lax.axis_size("x")
    cap = 2 * rows // groups
    slots = groups * cap
    owner_of = cluster_ids % groups
    onehot = (owner_of[:, None] == jnp.arange(groups, dtype=i32)[None, :]).astype(i32)
    before = jnp.cumsum(onehot, axis=0) - onehot
    rank = jnp.sum(before * onehot, axis=1)
    place = owner_of * cap + rank
    picked = place[None, :] == jnp.arange(slots, dtype=i32)[:, None]
    filled = jnp.any(picked, axis=1)
    source = jnp.sum(jnp.where(picked, jnp.arange(rows, dtype=i32)[None, :], 0), axis=1)
    out_labels = jnp.where(filled, cluster_ids[source], -1)
    squares = jnp.sum(embeddings * embeddings, axis=1, keepdims=True)
    local_unit = (embeddings * lax.rsqrt(squares + 1e-06)).astype(bf16)
    outgoing_unit = jnp.where(filled[:, None], local_unit[source], jnp.zeros((), bf16))
    unit = lax.all_to_all(outgoing_unit, "x", split_axis=0, concat_axis=0, tiled=True)
    labels = lax.all_to_all(out_labels, "x", split_axis=0, concat_axis=0, tiled=True)
    members = lax.axis_size(split)

    def everywhere(v):
        copies = jnp.broadcast_to(v[None], (members,) + v.shape).reshape((members * slots,) + v.shape[1:])
        return lax.all_to_all(copies, split, split_axis=0, concat_axis=0, tiled=True)

    def add_slice(i, scores):
        part = lax.dynamic_slice_in_dim(unit, i * WIDTH, WIDTH, 1)
        return scores + dot_last(part, everywhere(part))

    scores = lax.fori_loop(0, embeddings.shape[1] // WIDTH, add_slice, jnp.zeros((slots, members * slots), f32))
    all_labels = everywhere(labels)
    own = lax.axis_index(split) * slots + jnp.arange(slots, dtype=i32)
    mask = (
        (labels[:, None] == all_labels[None, :])
        & (labels[:, None] >= 0)
        & (own[:, None] != jnp.arange(members * slots, dtype=i32)[None, :])
    )
    scores = jnp.where(mask, scores, -1.0)
    best = jnp.maximum(-1.0, jnp.max(scores, axis=1))
    returned = lax.all_to_all(best, "x", split_axis=0, concat_axis=0, tiled=True)
    return returned[place]


def route(block, units, embeddings, cluster_ids):
    shape = jax.ShapeDtypeStruct
    half = shape((ROWS + LABEL_ROWS, HALF_WIDTH), bf16)
    keep, send = pl.pallas_call(
        unit_kernel, out_shape=(half, half),
        in_specs=[WHOLE, WHOLE], out_specs=(WHOLE, WHOLE), compiler_params=params(12), name="unit",
    )(embeddings, cluster_ids.reshape(1, ROWS))
    got = lax.ppermute(send, "c", [(0, 1), (1, 0)])
    packed, code = pl.pallas_call(
        functools.partial(pack_kernel, block),
        out_shape=(shape((CHIPS, block, WIDTH), bf16), shape((8, ROWS), i32)),
        in_specs=[WHOLE, WHOLE], out_specs=(WHOLE, WHOLE), compiler_params=params(20), name="pack",
    )(keep, got)
    packed = lax.all_to_all(packed, ("x", "z", "y"), 0, 0, tiled=True)
    table = shape((CHIPS, LANES), i32)
    guests, line, key, pos, meta = pl.pallas_call(
        functools.partial(names_kernel, block),
        out_shape=(shape((GUESTS, WIDTH), bf16), shape((8, CHIPS * block), i32), table, table, shape((8, LANES), i32)),
        in_specs=[WHOLE], out_specs=(WHOLE,) * 5, compiler_params=params(12), name="names",
    )(packed)
    brought = lax.ppermute(guests, "z", [(i, (i + 3) % 4) for i in range(4)])
    share = shape((SHARE_ROWS, WIDTH), bf16)
    send, mine, far = pl.pallas_call(
        functools.partial(sort_kernel, block), out_shape=(share, share, shape((8, GUESTS), i32)),
        in_specs=[WHOLE] * 4, out_specs=(WHOLE,) * 3, compiler_params=params(24), name="sort",
    )(packed, line, key, pos)
    other = lax.ppermute(send, "c", [(0, 1), (1, 0)])
    brought, mine = lax.optimization_barrier((brought, mine))
    swapped = lax.ppermute(brought, "c", [(0, 1), (1, 0)])
    raw = pl.pallas_call(
        own_kernel, out_shape=shape((RAW_ROWS, LANES), f32),
        in_specs=[WHOLE] * 3, out_specs=WHOLE,
        scratch_shapes=[pltpu.VMEM((SHARE_ROWS, WIDTH), bf16)],
        compiler_params=params(16), name="own",
        cost_estimate=pl.CostEstimate(flops=2 * RAW_ROWS * LANES * WIDTH, bytes_accessed=4 << 20, transcendentals=0),
    )(mine, brought, far)
    partial = pl.pallas_call(
        functools.partial(gram_kernel, units),
        out_shape=[shape((units * UNIT, LANES), f32)] * 4,
        in_specs=[WHOLE] * 5, out_specs=[WHOLE] * 4,
        scratch_shapes=[pltpu.VMEM((4 * units * UNIT + CAPS[0], LANES), f32), pltpu.VMEM((SHARE_ROWS, WIDTH), bf16)],
        compiler_params=params(16), name="gram",
    )(meta, other, swapped, far, raw)
    arrived = [partial[0]] + [
        lax.ppermute(partial[s], "y", [(i, (i + s) % 4) for i in range(4)]) for s in (1, 2, 3)
    ]
    over = pl.pallas_call(
        functools.partial(fit_kernel, block, units), out_shape=shape((8, LANES), i32),
        in_specs=[WHOLE], out_specs=WHOLE, compiler_params=params(8), name="fit",
    )(packed)
    arrived, fits = lax.optimization_barrier((arrived, over[0, 0] == 0))
    best = pl.pallas_call(
        functools.partial(max_kernel, units),
        out_shape=shape((2 * CHIPS, LANES), f32),
        in_specs=[WHOLE] * 6, out_specs=WHOLE,
        scratch_shapes=[pltpu.VMEM((16, LANES), f32)],
        compiler_params=params(8), name="maxima",
    )(meta, *arrived, pos)
    back = lax.all_to_all(best.reshape(2 * CHIPS, 1, LANES), ("c", "x", "z", "y"), 0, 0, tiled=True)
    back, fits = lax.optimization_barrier((back, fits))
    best = pl.pallas_call(
        pick_kernel,
        out_shape=shape((1, ROWS), f32),
        in_specs=[WHOLE, WHOLE], out_specs=WHOLE, compiler_params=params(8), name="pick",
    )(back.reshape(2 * CHIPS, LANES), code).reshape(ROWS)
    return best, fits


def on_device(embeddings, cluster_ids, tries=TRIES):
    if not tries:
        return gather_groups(embeddings, cluster_ids)
    best, fits = route(*tries[0], embeddings, cluster_ids)
    return lax.cond(
        fits,
        lambda best, embeddings, cluster_ids: best,
        lambda best, embeddings, cluster_ids: on_device(embeddings, cluster_ids, tries[1:]),
        best, embeddings, cluster_ids,
    )


def solution(mesh):
    axes = ("x", "z", "y", "c")
    grid = Mesh(mesh.devices.reshape(4, 4, 4, 2), axes)
    return jax.shard_map(
        on_device, mesh=grid, in_specs=(P(axes, None), P(axes)), out_specs=P(axes), check_vma=False
    )
```

```python
import functools

import jax
import jax.numpy as jnp
from jax import lax
from jax.experimental import pallas as pl
from jax.experimental.pallas import tpu as pltpu
from jax.sharding import Mesh, PartitionSpec as P

ROWS = 128
HALF_WIDTH = 2048
WIDTH = 512
LABEL_ROWS = 16
BINS = 16
CHIPS = 64
TRIES = ((24, 11), (32, 16))
GROUP = 32
GUESTS = 64
GUEST = 4096
LANES = 128
CAPS = (704, 512, 320, 192)
STARTS = (0, 704, 1216, 1536)
UNIT = 32
SHARES = (
    ((0, 0), (0, 256), (2, 0), (2, 128), (2, 256), (3, 0)),
    ((0, 128), (0, 384), (0, 512), (0, 640), (1, 0), (1, 128), (1, 256), (1, 384), (3, 128)),
)
BASES = ({0: 0, 2: 704, 3: 1024}, {0: -128, 1: 576, 3: 960})
SHARE_ROWS = 1216
SEGMENTS = (
    (0, 128, 0, None), (128, 576, 128, 0), (704, 256, None, 576), (960, 256, None, 832),
    (1216, 320, 704, None), (1536, 128, 1024, None), (1664, 64, 1152, 1088),
)
f32, bf16, i32 = jnp.float32, jnp.bfloat16, jnp.int32
WHOLE = pl.BlockSpec(memory_space=pltpu.VMEM)


def params(mib):
    return pltpu.CompilerParams(vmem_limit_bytes=mib * 1024 * 1024)


def index_on(axis):
    return lax.axis_index(axis)


def iota(shape, dim):
    return lax.broadcasted_iota(i32, shape, dim)


def dot_last(a, b):
    return lax.dot_general(a, b, (((1,), (1,)), ((), ())), preferred_element_type=f32)


def dot(a, b):
    return lax.dot_general(a, b, (((1,), (0,)), ((), ())), preferred_element_type=f32)


def as_bf16(mask):
    return jnp.where(mask, 1.0, 0.0).astype(bf16)


def bin_of(labels):
    rank, residue = labels >> 2, labels & 3
    row, col = rank >> 2, rank & 3
    col = jnp.where((row & 1) == 1, 3 - col, col)
    return 4 * col + ((row - residue) & 3)


def unit_kernel(x_ref, ids_ref, keep_ref, send_ref):
    c = index_on("c")
    x = x_ref[...]
    scale = lax.rsqrt(jnp.sum(x * x, axis=1, keepdims=True) + 1e-06)
    ids = jnp.concatenate([ids_ref[...].astype(f32), jnp.zeros((1, HALF_WIDTH - ROWS), f32)], axis=1)
    ids = jnp.broadcast_to(ids, (LABEL_ROWS, HALF_WIDTH)).astype(bf16)
    for half, out_ref in ((c, keep_ref), (1 - c, send_ref)):
        columns = pl.ds(pl.multiple_of(half * HALF_WIDTH, HALF_WIDTH), HALF_WIDTH)
        out_ref[:ROWS, :] = (x_ref[:, columns] * scale).astype(bf16)
        out_ref[ROWS:, :] = ids


def passed_on(over, before):
    once = before(over, 1)
    twice = before(over, 2)
    return jnp.maximum(jnp.maximum(over, 0), jnp.maximum(over + once, over + once + twice))


def pack_kernel(block, keep_ref, got_ref, out_ref, code_ref):
    first = index_on("c") == 0
    kept = jnp.max(keep_ref[ROWS:, :ROWS].astype(f32), axis=0, keepdims=True)
    got = jnp.max(got_ref[ROWS:, :ROWS].astype(f32), axis=0, keepdims=True)
    labels = jnp.concatenate([jnp.where(first, kept, got), jnp.where(first, got, kept)], axis=0).astype(i32)
    bins = bin_of(labels)
    upper = as_bf16(iota((ROWS, ROWS), 0) < iota((ROWS, ROWS), 1))

    def ranks_within(masks):
        member = jnp.concatenate([jnp.where(mask, 1.0, 0.0) for mask in masks], axis=0)
        row, col = iota((member.shape[0],) * 2, 0), iota((member.shape[0],) * 2, 1)
        earlier = dot(as_bf16(((row >> 1) == (col >> 1)) & (col < row)), member.astype(bf16))
        ranks = member * (dot(member.astype(bf16), upper) + jnp.sum(earlier, axis=1, keepdims=True))
        rank = sum(ranks[2 * b:2 * b + 2] for b in range(len(masks)))
        return rank.astype(i32), jnp.sum(member, axis=1, keepdims=True)

    rank, sizes = ranks_within([bins == b for b in range(BINS)])
    quad, line = bins >> 2, bins & 3
    taken = []
    for at in range(4):
        size = jnp.zeros(labels.shape, f32)
        for b in range(at, BINS, 4):
            size = jnp.where(quad == b >> 2, sizes[2 * b:2 * b + 1] + sizes[2 * b + 1:2 * b + 2], size)
        taken.append(size.astype(i32) - (block - 1))
    stays = []
    for at in range(4):
        moved = passed_on(taken[at], lambda _, back: taken[(at - back) & 3])
        stays.append(taken[at] + (block - 1) - moved)

    def of_line(values, which):
        out = values[0]
        for at in range(1, 4):
            out = jnp.where(which == at, values[at], out)
        return out

    stay = of_line(stays, line)
    to_line = jnp.where(rank < stay, line, (line + 1) & 3)
    to_slot = jnp.where(rank < stay, rank, of_line(stays, to_line) + rank - stay)
    placed = to_slot < (block - 1)
    lane = jnp.where(placed, to_line * GROUP + to_slot, -1)
    place = jnp.where(placed, (quad * 4 + to_line) * block + to_slot, -1)
    code_ref[...] = jnp.concatenate([jnp.where(placed, bins * LANES + lane, -1)] * 4, axis=0)
    docs = 2 * ROWS
    flat = lambda v: jnp.concatenate([v[:1], v[1:]], axis=1)
    label_row = flat(labels)
    counts = dot_last(jnp.ones((8, docs), bf16), as_bf16(iota((LANES, docs), 0) == label_row))[:1]
    named = jnp.where(iota((8, docs), 0) == flat(quad), (label_row + 1).astype(f32), 0.0).astype(bf16)
    names = dot_last(named, as_bf16(iota((LANES, docs), 0) == flat(lane)))
    own = jnp.where(first, place[:1], place[1:])
    other = jnp.where(first, place[1:], place[:1])
    onehot = as_bf16(iota((BINS * block, docs), 0) == jnp.concatenate([own, other], axis=1))
    is_last = iota((block, WIDTH), 0) == (block - 1)
    for y in range(4):
        columns = slice(y * WIDTH, (y + 1) * WIDTH)
        x = jnp.concatenate([keep_ref[:ROWS, columns], got_ref[:ROWS, columns]], axis=0)
        packed = dot(onehot, x)
        for b in range(BINS):
            extra = jnp.concatenate([names[b // 4:b // 4 + 1], counts, jnp.zeros((1, 2 * LANES), f32)], axis=1)
            out_ref[4 * b + y] = jnp.where(is_last, extra, packed[b * block:(b + 1) * block]).astype(bf16)


def labels_of(block, x_ref):
    tail = x_ref[:, block - 8:, :2 * LANES].astype(f32)
    tail = jnp.max(jnp.where(iota(tail.shape, 1) == 7, tail, 0.0), axis=1)
    return tail[:, :LANES].astype(i32) - 1, tail[:, LANES:].astype(bf16)


def counts_of(chip_counts):
    row, col = iota((LANES, LANES), 0), iota((LANES, LANES), 1)
    in_bin = (bin_of(row) == col) & (row < 4 * BINS)
    counts = [dot(chip_counts, as_bf16(in_bin & ((row & 3) == r))) for r in range(4)]
    return counts, [jnp.sum(v, axis=0, keepdims=True) for v in counts]


def in_order(sizes):
    a, b = jnp.maximum(sizes[0], sizes[1]), jnp.minimum(sizes[0], sizes[1])
    c, d = jnp.maximum(sizes[2], sizes[3]), jnp.minimum(sizes[2], sizes[3])
    first, e = jnp.maximum(a, c), jnp.minimum(a, c)
    g, fourth = jnp.maximum(b, d), jnp.minimum(b, d)
    return first, jnp.maximum(e, g), jnp.minimum(e, g), fourth


def names_kernel(block, x_ref, guest_ref, line_ref, key_ref, pos_ref, meta_ref):
    z = index_on("z")
    labels, _ = labels_of(block, x_ref)
    row, col = iota((LANES, LANES), 0), iota((LANES, LANES), 1)
    lane = iota(labels.shape, 1)
    group = lane >> 5
    valid = labels >= 0
    home = bin_of(labels) & 3
    at_home = valid & (home == z)
    upper = as_bf16(row < col)
    lower = as_bf16(iota((CHIPS, CHIPS), 1) < iota((CHIPS, CHIPS), 0))
    members, n = [at_home & ((labels & 3) == r) for r in range(4)], []
    for member in members:
        size = jnp.sum(jnp.where(member, 1.0, 0.0), axis=0, keepdims=True)
        n.append(jnp.sum(size, axis=1, keepdims=True))
    wide = lambda v: jnp.broadcast_to(v, (1, LANES))
    meta_ref[...] = jnp.concatenate([wide(v) for v in in_order(n)] * 2, axis=0).astype(i32)
    pos = jnp.full(labels.shape, -1.0, f32)
    for r, member in enumerate(members):
        place = sum(
            jnp.where((n[q] > n[r]) | ((n[q] == n[r]) & (q < r)), 1.0, 0.0) for q in range(4) if q != r
        )
        start = jnp.where(
            place < 0.5, float(STARTS[0]),
            jnp.where(place < 1.5, float(STARTS[1]), jnp.where(place < 2.5, float(STARTS[2]), float(STARTS[3]))),
        )
        member16 = as_bf16(member)
        rank = dot(member16, upper) + jnp.sum(dot(lower, member16), axis=1, keepdims=True)
        pos = jnp.where(member, start + rank, pos)
    pos = pos.astype(i32)
    pos_ref[...] = pos
    guest = valid & (home != group)
    guest16 = as_bf16(guest)
    same = (row >> 5) == (col >> 5)
    turn = dot(guest16, as_bf16(same & (row < col))) + dot(dot(lower, guest16).astype(bf16), as_bf16(same))
    turn = turn.astype(i32)
    away = at_home & (group != z) & (turn < GUESTS)
    key_ref[...] = jnp.where(away, turn, -1)
    per, groups = 16, CHIPS // 16
    value = jnp.where(group == z, jnp.where(guest, GUEST + turn, pos + 1), 0).astype(f32)
    value = pltpu.roll(value, lax.rem(LANES - GROUP * z, LANES), 1)
    value = jnp.where(lane < block, value, 0.0)
    lined = jnp.zeros((8, per * block), f32)
    for t in range(per):
        rows = jnp.concatenate([value[per * g + t:per * g + t + 1] for g in range(groups)] * 2, axis=0)
        rows = jnp.concatenate([rows, jnp.zeros((8, per * block - LANES), f32)], axis=1)
        lined = lined + (pltpu.roll(rows, t * block, 1) if t else rows)
    slots = jnp.concatenate([lined[g:g + 1] for g in range(groups)], axis=1).astype(i32)
    line_ref[...] = jnp.broadcast_to(slots, line_ref.shape)
    onehot = as_bf16(iota((GUESTS, CHIPS * block), 0) + GUEST == slots)
    guest_ref[...] = dot(onehot, x_ref[...].reshape(CHIPS * block, WIDTH)).astype(bf16)


def sorted_rows(segment, slots, x):
    onehot = as_bf16(iota((segment[1], x.shape[0]), 0) + (segment[0] + 1) == slots)
    return dot(onehot, x).astype(bf16)


def sort_kernel(block, x_ref, line_ref, send_ref, mine_ref):
    x = x_ref[...].reshape(CHIPS * block, WIDTH)
    slots = line_ref[:1, :]
    for core in range(2):
        @pl.when(index_on("c") == core)
        def _():
            for segment in SEGMENTS:
                rows = sorted_rows(segment, slots, x)
                for out_ref, at in ((mine_ref, segment[2 + core]), (send_ref, segment[2 + 1 - core])):
                    if at is not None:
                        out_ref[at:at + segment[1], :] = rows


def fit_kernel(block, units, x_ref, over_ref):
    _, chip_counts = labels_of(block, x_ref)
    counts, sizes = counts_of(chip_counts)
    ordered = in_order(sizes)
    over = jnp.zeros((1, LANES), f32)
    for size, cap in zip(ordered, CAPS):
        over = jnp.maximum(over, jnp.where(size > cap, 1.0, 0.0))
    for share in SHARES:
        length = 0.0
        for q, first in share:
            rows = jnp.maximum(jnp.floor((ordered[q] + (UNIT - 1.0)) * (1 / UNIT)) - first // UNIT, 0.0)
            length = length + jnp.where(rows >= 3.0, rows - 1.0, rows)
        over = jnp.maximum(over, jnp.where(length > 4 * units, 1.0, 0.0))
    taken = counts[0] + counts[1] + counts[2] + counts[3]
    lane = iota(taken.shape, 1) & 3
    before = lambda v, back: jnp.where(lane >= back, pltpu.roll(v, back, 1), pltpu.roll(v, LANES - 4 + back, 1))
    extra = taken - (block - 1)
    moved = passed_on(extra, before)
    held = jnp.sum(moved, axis=0, keepdims=True)
    over = jnp.maximum(over, jnp.where(held > GUESTS, 1.0, 0.0))
    full = extra + before(extra, 1) + before(extra, 2) + before(extra, 3) > 0
    full = jnp.where(full | (moved > block - 1), 1.0, 0.0)
    over = jnp.maximum(over, jnp.max(full, axis=0, keepdims=True))
    over_ref[...] = jnp.broadcast_to(jnp.max(over, axis=1, keepdims=True), over_ref.shape).astype(i32)


def add_guests(core, base_ref, guest_ref, far_ref, out_ref):
    guests, far = guest_ref[...], far_ref[:1, :]
    for segment in SEGMENTS:
        at, rows = segment[2 + core], segment[1]
        if at is not None:
            out_ref[at:at + rows, :] = base_ref[at:at + rows, :] + sorted_rows(segment, far, guests)


def blocks_of(core):
    for q, first in SHARES[core]:
        at = BASES[core][q] + first
        yield q, first, pl.ds(at, CAPS[q] - first), pl.ds(at, LANES)


RAW_ROWS = max(sum(CAPS[q] - first for q, first in share) for share in SHARES)


def own_kernel(x_ref, guest_ref, key_ref, pos_ref, raw_ref, far_ref, rows_ref):
    total = jnp.zeros((8, GUESTS), f32)
    step = 16
    for first in range(0, CHIPS, step):
        flat = lambda ref: jnp.concatenate([ref[s:s + 1, :] for s in range(first, first + step)], axis=1)
        places = flat(pos_ref) + 1
        parts = jnp.where(iota((8, step * LANES), 0) == 0, places >> 5, places & 31).astype(f32).astype(bf16)
        total = total + dot_last(parts, as_bf16(iota((GUESTS, step * LANES), 0) == flat(key_ref)))
    far_ref[...] = jnp.broadcast_to((32.0 * total[:1] + total[1:2]).astype(i32), far_ref.shape)
    for core in range(2):
        @pl.when(index_on("c") == core)
        def _():
            add_guests(core, x_ref, guest_ref, far_ref, rows_ref)
            at = 0
            for q, first, left, right in blocks_of(core):
                rows = CAPS[q] - first
                raw_ref[at:at + rows, :] = dot_last(rows_ref[left, :], rows_ref[right, :])
                at += rows


def size_of(meta_ref, q):
    return jnp.max(meta_ref[q:q + 1, :].astype(f32)).astype(i32)


def length_of(size, first):
    units = jnp.maximum(((size + UNIT - 1) >> 5) - first // UNIT, 0)
    return jnp.where(units >= 3, units - 1, units)


def folded(score):
    away = jnp.full((UNIT, LANES), -4.0, f32) if score.shape[0] < LANES else score[2 * UNIT:3 * UNIT]
    both = jnp.where(iota(away.shape, 1) < 3 * UNIT, away, pltpu.roll(score[:UNIT], 3 * UNIT, 1))
    rest = [score[3 * UNIT:]] if score.shape[0] > 3 * UNIT else []
    return jnp.concatenate([both, score[UNIT:2 * UNIT]] + rest, axis=0)


def gram_kernel(units, meta_ref, x_ref, guest_ref, far_ref, raw_ref, out0, out1, out2, out3, part_ref, rows_ref):
    y, c = index_on("y"), index_on("c")
    part_ref[...] = jnp.full(part_ref.shape, -4.0, f32)
    for core in range(2):
        @pl.when(c == core)
        def _():
            add_guests(core, x_ref, guest_ref, far_ref, rows_ref)
            at, to = 0, jnp.zeros((), i32)
            for q, first, left, right in blocks_of(core):
                rows = CAPS[q] - first
                score = raw_ref[at:at + rows, :] + dot_last(rows_ref[left, :], rows_ref[right, :])
                at += rows
                size = size_of(meta_ref, q)
                i, j = iota(score.shape, 0), iota(score.shape, 1)
                keep = (i < size - first) & (j < size - first) & (i != j)
                score = folded(jnp.where(keep, score, -4.0))
                part_ref[pl.ds(pl.multiple_of(to, UNIT), score.shape[0]), :] = score
                to = jnp.minimum(to + UNIT * length_of(size, first), 4 * units * UNIT)
    chunk = units * UNIT
    for shift, out in enumerate((out0, out1, out2, out3)):
        out[...] = part_ref[pl.ds(pl.multiple_of(lax.rem(y + shift, 4) * chunk, UNIT), chunk), :]


FIRST_ROW = (0, 6, 10, 13)


def max_kernel(units, meta_ref, p0, p1, p2, p3, pos_ref, out_ref, best_ref):
    y, c = index_on("y"), index_on("c")
    best_ref[...] = jnp.full(best_ref.shape, -1.0, f32)
    sub, lane = iota((UNIT, LANES), 0), iota((UNIT, LANES), 1)
    blocks, sizes = [], [size_of(meta_ref, q) for q in range(4)]
    for core, share in enumerate(SHARES):
        at = jnp.zeros((), i32)
        for q, first in share:
            length = length_of(sizes[q], first)
            blocks.append((jnp.where((c == core) & (length > 0), at, 4 * units), FIRST_ROW[q] + first // LANES, at))
            at = at + length
    for t in range(units):
        at = slice(t * UNIT, (t + 1) * UNIT)
        block = (p0[at, :] + p1[at, :]) + (p2[at, :] + p3[at, :])
        index = y * units + t
        col, start = jnp.asarray(15, i32), jnp.asarray(0, i32)
        for block_start, block_col, block_at in blocks:
            inside = index >= block_start
            col, start = jnp.where(inside, block_col, col), jnp.where(inside, block_at, start)
        turn = index - start
        unit = 4 * col + jnp.where(turn == 0, 2, jnp.where(turn == 1, 1, turn + 1))
        unit = jnp.minimum(jnp.maximum(unit, 0), 63)
        beside = (lane >= 3 * UNIT) & (turn == 0)
        one, two = jnp.where(beside, -4.0, block), jnp.where(beside, block, -4.0)
        along = jnp.max(one, axis=1, keepdims=True)
        along = jnp.max(jnp.where(sub + (unit & 3) * UNIT == lane, along, -1.0), axis=0, keepdims=True)
        row = unit >> 2
        best_ref[pl.ds(row, 1), :] = jnp.maximum(best_ref[pl.ds(row, 1), :], along)
        down = jnp.max(one, axis=0, keepdims=True)
        along = jnp.max(two, axis=1, keepdims=True)
        two = jnp.maximum(jnp.where(sub == lane, along, -1.0), pltpu.roll(two, UNIT, 1))
        down = jnp.maximum(down, jnp.max(two, axis=0, keepdims=True))
        best_ref[pl.ds(col, 1), :] = jnp.maximum(best_ref[pl.ds(col, 1), :], down)
    pos = pos_ref[...]
    pos = jnp.where(pos >= STARTS[1], pos + 64, pos)
    pos = jnp.where(pos >= STARTS[3] + 64, pos + 64, pos)
    row, lane = pos >> 7, pos & (LANES - 1)
    out = jnp.full(pos.shape, -1.0, f32)
    for r in range(15):
        value = jnp.broadcast_to(best_ref[r:r + 1, :], pos.shape)
        value = jnp.take_along_axis(value, lane, axis=1, mode="promise_in_bounds")
        out = jnp.where(row == r, value, out)
    out_ref[:CHIPS, :] = out
    out_ref[CHIPS:, :] = out


def pick_kernel(v_ref, code_ref, out_ref):
    c = index_on("c")
    values = jnp.maximum(v_ref[:CHIPS, :], v_ref[CHIPS:, :])
    values = jnp.max(values.reshape(BINS, 4, LANES), axis=1)
    eye = iota((LANES, LANES), 0) == iota((LANES, LANES), 1)
    code = jnp.max(jnp.where(iota((8, ROWS), 0) == c, code_ref[...], -1), axis=0, keepdims=True)
    code = jnp.max(jnp.where(eye, code.astype(f32), -1.0), axis=1, keepdims=True).astype(i32)
    slot = iota((ROWS, LANES), 1)
    best = jnp.full((ROWS, LANES), -1.0, f32)
    for b in range(BINS):
        best = jnp.where(slot + b * LANES == code, values[b:b + 1], best)
    best = jnp.max(best, axis=1, keepdims=True)
    out_ref[...] = jnp.max(jnp.where(eye, best, -1.0), axis=0, keepdims=True)


def gather_groups(embeddings, cluster_ids):
    split = ("z", "y", "c")
    rows = embeddings.shape[0]
    groups = lax.axis_size("x")
    cap = 2 * rows // groups
    slots = groups * cap
    owner_of = cluster_ids % groups
    onehot = (owner_of[:, None] == jnp.arange(groups, dtype=i32)[None, :]).astype(i32)
    before = jnp.cumsum(onehot, axis=0) - onehot
    rank = jnp.sum(before * onehot, axis=1)
    place = owner_of * cap + rank
    picked = place[None, :] == jnp.arange(slots, dtype=i32)[:, None]
    filled = jnp.any(picked, axis=1)
    source = jnp.sum(jnp.where(picked, jnp.arange(rows, dtype=i32)[None, :], 0), axis=1)
    out_labels = jnp.where(filled, cluster_ids[source], -1)
    squares = jnp.sum(embeddings * embeddings, axis=1, keepdims=True)
    local_unit = (embeddings * lax.rsqrt(squares + 1e-06)).astype(bf16)
    outgoing_unit = jnp.where(filled[:, None], local_unit[source], jnp.zeros((), bf16))
    unit = lax.all_to_all(outgoing_unit, "x", split_axis=0, concat_axis=0, tiled=True)
    labels = lax.all_to_all(out_labels, "x", split_axis=0, concat_axis=0, tiled=True)
    members = lax.axis_size(split)

    def everywhere(v):
        copies = jnp.broadcast_to(v[None], (members,) + v.shape).reshape((members * slots,) + v.shape[1:])
        return lax.all_to_all(copies, split, split_axis=0, concat_axis=0, tiled=True)

    def add_slice(i, scores):
        part = lax.dynamic_slice_in_dim(unit, i * WIDTH, WIDTH, 1)
        return scores + dot_last(part, everywhere(part))

    scores = lax.fori_loop(0, embeddings.shape[1] // WIDTH, add_slice, jnp.zeros((slots, members * slots), f32))
    all_labels = everywhere(labels)
    own = lax.axis_index(split) * slots + jnp.arange(slots, dtype=i32)
    mask = (
        (labels[:, None] == all_labels[None, :])
        & (labels[:, None] >= 0)
        & (own[:, None] != jnp.arange(members * slots, dtype=i32)[None, :])
    )
    scores = jnp.where(mask, scores, -1.0)
    best = jnp.maximum(-1.0, jnp.max(scores, axis=1))
    returned = lax.all_to_all(best, "x", split_axis=0, concat_axis=0, tiled=True)
    return returned[place]


def route(block, units, embeddings, cluster_ids):
    shape = jax.ShapeDtypeStruct
    half = shape((ROWS + LABEL_ROWS, HALF_WIDTH), bf16)
    keep, send = pl.pallas_call(
        unit_kernel, out_shape=(half, half),
        in_specs=[WHOLE, WHOLE], out_specs=(WHOLE, WHOLE), compiler_params=params(12), name="unit",
    )(embeddings, cluster_ids.reshape(1, ROWS))
    got = lax.ppermute(send, "c", [(0, 1), (1, 0)])
    packed, code = pl.pallas_call(
        functools.partial(pack_kernel, block),
        out_shape=(shape((CHIPS, block, WIDTH), bf16), shape((8, ROWS), i32)),
        in_specs=[WHOLE, WHOLE], out_specs=(WHOLE, WHOLE), compiler_params=params(20), name="pack",
    )(keep, got)
    packed = lax.all_to_all(packed, ("x", "z", "y"), 0, 0, tiled=True)
    table = shape((CHIPS, LANES), i32)
    guests, line, key, pos, meta = pl.pallas_call(
        functools.partial(names_kernel, block),
        out_shape=(shape((GUESTS, WIDTH), bf16), shape((8, CHIPS * block), i32), table, table, shape((8, LANES), i32)),
        in_specs=[WHOLE], out_specs=(WHOLE,) * 5, compiler_params=params(12), name="names",
    )(packed)
    brought = lax.ppermute(guests, "z", [(i, (i + 3) % 4) for i in range(4)])
    share = shape((SHARE_ROWS, WIDTH), bf16)
    send, mine = pl.pallas_call(
        functools.partial(sort_kernel, block), out_shape=(share, share),
        in_specs=[WHOLE] * 2, out_specs=(WHOLE,) * 2, compiler_params=params(24), name="sort",
    )(packed, line)
    brought, mine, send = lax.optimization_barrier((brought, mine, send))
    other = lax.ppermute(send, "c", [(0, 1), (1, 0)])
    swapped = lax.ppermute(brought, "c", [(0, 1), (1, 0)])
    raw, far = pl.pallas_call(
        own_kernel, out_shape=(shape((RAW_ROWS, LANES), f32), shape((8, GUESTS), i32)),
        in_specs=[WHOLE] * 4, out_specs=(WHOLE,) * 2,
        scratch_shapes=[pltpu.VMEM((SHARE_ROWS, WIDTH), bf16)],
        compiler_params=params(16), name="own",
        cost_estimate=pl.CostEstimate(flops=2 * RAW_ROWS * LANES * WIDTH, bytes_accessed=4 << 20, transcendentals=0),
    )(mine, brought, key, pos)
    partial = pl.pallas_call(
        functools.partial(gram_kernel, units),
        out_shape=[shape((units * UNIT, LANES), f32)] * 4,
        in_specs=[WHOLE] * 5, out_specs=[WHOLE] * 4,
        scratch_shapes=[pltpu.VMEM((4 * units * UNIT + CAPS[0], LANES), f32), pltpu.VMEM((SHARE_ROWS, WIDTH), bf16)],
        compiler_params=params(16), name="gram",
    )(meta, other, swapped, far, raw)
    arrived = [partial[0]] + [
        lax.ppermute(partial[s], "y", [(i, (i + s) % 4) for i in range(4)]) for s in (1, 2, 3)
    ]
    over = pl.pallas_call(
        functools.partial(fit_kernel, block, units), out_shape=shape((8, LANES), i32),
        in_specs=[WHOLE], out_specs=WHOLE, compiler_params=params(8), name="fit",
    )(packed)
    arrived, fits = lax.optimization_barrier((arrived, over[0, 0] == 0))
    best = pl.pallas_call(
        functools.partial(max_kernel, units),
        out_shape=shape((2 * CHIPS, LANES), f32),
        in_specs=[WHOLE] * 6, out_specs=WHOLE,
        scratch_shapes=[pltpu.VMEM((16, LANES), f32)],
        compiler_params=params(8), name="maxima",
    )(meta, *arrived, pos)
    back = lax.all_to_all(best.reshape(2 * CHIPS, 1, LANES), ("c", "x", "z", "y"), 0, 0, tiled=True)
    back, fits = lax.optimization_barrier((back, fits))
    best = pl.pallas_call(
        pick_kernel,
        out_shape=shape((1, ROWS), f32),
        in_specs=[WHOLE, WHOLE], out_specs=WHOLE, compiler_params=params(8), name="pick",
    )(back.reshape(2 * CHIPS, LANES), code).reshape(ROWS)
    return best, fits


def on_device(embeddings, cluster_ids, tries=TRIES):
    if not tries:
        return gather_groups(embeddings, cluster_ids)
    best, fits = route(*tries[0], embeddings, cluster_ids)
    return lax.cond(
        fits,
        lambda best, embeddings, cluster_ids: best,
        lambda best, embeddings, cluster_ids: on_device(embeddings, cluster_ids, tries[1:]),
        best, embeddings, cluster_ids,
    )


def solution(mesh):
    axes = ("x", "z", "y", "c")
    grid = Mesh(mesh.devices.reshape(4, 4, 4, 2), axes)
    return jax.shard_map(
        on_device, mesh=grid, in_specs=(P(axes, None), P(axes)), out_specs=P(axes), check_vma=False
    )
```

```python
import functools

import jax
import jax.numpy as jnp
from jax import lax
from jax.experimental import pallas as pl
from jax.experimental.pallas import tpu as pltpu
from jax.sharding import Mesh, PartitionSpec as P

ROWS = 128
HALF_WIDTH = 2048
WIDTH = 512
LABEL_ROWS = 16
BINS = 16
CHIPS = 64
TRIES = ((24, 11), (32, 16))
GROUP = 32
GUESTS = 64
GUEST = 4096
LANES = 128
CAPS = (704, 512, 320, 192)
STARTS = (0, 704, 1216, 1536)
UNIT = 32
SHARES = (
    ((0, 0), (0, 256), (2, 0), (2, 128), (2, 256), (3, 0)),
    ((0, 128), (0, 384), (0, 512), (0, 640), (1, 0), (1, 128), (1, 256), (1, 384), (3, 128)),
)
BASES = ({0: 0, 2: 704, 3: 1024}, {0: -128, 1: 576, 3: 960})
SHARE_ROWS = 1216
SEGMENTS = (
    (0, 128, 0, None), (128, 576, 128, 0), (704, 256, None, 576), (960, 256, None, 832),
    (1216, 320, 704, None), (1536, 128, 1024, None), (1664, 64, 1152, 1088),
)
f32, bf16, i32 = jnp.float32, jnp.bfloat16, jnp.int32
WHOLE = pl.BlockSpec(memory_space=pltpu.VMEM)


def params(mib):
    return pltpu.CompilerParams(vmem_limit_bytes=mib * 1024 * 1024)


def index_on(axis):
    return lax.axis_index(axis)


def iota(shape, dim):
    return lax.broadcasted_iota(i32, shape, dim)


def dot_last(a, b):
    return lax.dot_general(a, b, (((1,), (1,)), ((), ())), preferred_element_type=f32)


def dot(a, b):
    return lax.dot_general(a, b, (((1,), (0,)), ((), ())), preferred_element_type=f32)


def as_bf16(mask):
    return jnp.where(mask, 1.0, 0.0).astype(bf16)


def bin_of(labels):
    rank, residue = labels >> 2, labels & 3
    row, col = rank >> 2, rank & 3
    col = jnp.where((row & 1) == 1, 3 - col, col)
    return 4 * col + ((row - residue) & 3)


def label_rows(ids_ref):
    ids = jnp.concatenate([ids_ref[...].astype(f32), jnp.zeros((1, HALF_WIDTH - ROWS), f32)], axis=1)
    return jnp.broadcast_to(ids, (LABEL_ROWS, HALF_WIDTH)).astype(bf16)


def half_of(core):
    return pl.ds(pl.multiple_of(core * HALF_WIDTH, HALF_WIDTH), HALF_WIDTH)


def unit_send_kernel(x_ref, ids_ref, out_ref, scale_ref):
    x = x_ref[...]
    scale = lax.rsqrt(jnp.sum(x * x, axis=1, keepdims=True) + 1e-06)
    scale_ref[...] = jnp.broadcast_to(scale, scale_ref.shape)
    out_ref[:ROWS, :] = (x_ref[:, half_of(1 - index_on("c"))] * scale).astype(bf16)
    out_ref[ROWS:, :] = label_rows(ids_ref)


def unit_keep_kernel(x_ref, ids_ref, scale_ref, out_ref, half_ref, sem):
    copy = pltpu.make_async_copy(x_ref.at[:, half_of(index_on("c"))], half_ref, sem)
    copy.start()
    out_ref[ROWS:, :] = label_rows(ids_ref)
    copy.wait()
    out_ref[:ROWS, :] = (half_ref[...] * scale_ref[:, :1]).astype(bf16)


def passed_on(over, before):
    once = before(over, 1)
    twice = before(over, 2)
    return jnp.maximum(jnp.maximum(over, 0), jnp.maximum(over + once, over + once + twice))


def pack_kernel(block, keep_ref, got_ref, out_ref, code_ref):
    first = index_on("c") == 0
    kept = jnp.max(keep_ref[ROWS:, :ROWS].astype(f32), axis=0, keepdims=True)
    got = jnp.max(got_ref[ROWS:, :ROWS].astype(f32), axis=0, keepdims=True)
    labels = jnp.concatenate([jnp.where(first, kept, got), jnp.where(first, got, kept)], axis=0).astype(i32)
    bins = bin_of(labels)
    upper = as_bf16(iota((ROWS, ROWS), 0) < iota((ROWS, ROWS), 1))

    def ranks_within(masks):
        member = jnp.concatenate([jnp.where(mask, 1.0, 0.0) for mask in masks], axis=0)
        row, col = iota((member.shape[0],) * 2, 0), iota((member.shape[0],) * 2, 1)
        earlier = dot(as_bf16(((row >> 1) == (col >> 1)) & (col < row)), member.astype(bf16))
        ranks = member * (dot(member.astype(bf16), upper) + jnp.sum(earlier, axis=1, keepdims=True))
        rank = sum(ranks[2 * b:2 * b + 2] for b in range(len(masks)))
        return rank.astype(i32), jnp.sum(member, axis=1, keepdims=True)

    rank, sizes = ranks_within([bins == b for b in range(BINS)])
    quad, line = bins >> 2, bins & 3
    taken = []
    for at in range(4):
        size = jnp.zeros(labels.shape, f32)
        for b in range(at, BINS, 4):
            size = jnp.where(quad == b >> 2, sizes[2 * b:2 * b + 1] + sizes[2 * b + 1:2 * b + 2], size)
        taken.append(size.astype(i32) - (block - 1))
    stays = []
    for at in range(4):
        moved = passed_on(taken[at], lambda _, back: taken[(at - back) & 3])
        stays.append(taken[at] + (block - 1) - moved)

    def of_line(values, which):
        out = values[0]
        for at in range(1, 4):
            out = jnp.where(which == at, values[at], out)
        return out

    stay = of_line(stays, line)
    to_line = jnp.where(rank < stay, line, (line + 1) & 3)
    to_slot = jnp.where(rank < stay, rank, of_line(stays, to_line) + rank - stay)
    placed = to_slot < (block - 1)
    lane = jnp.where(placed, to_line * GROUP + to_slot, -1)
    place = jnp.where(placed, (quad * 4 + to_line) * block + to_slot, -1)
    code_ref[...] = jnp.concatenate([jnp.where(placed, bins * LANES + lane, -1)] * 4, axis=0)
    docs = 2 * ROWS
    flat = lambda v: jnp.concatenate([v[:1], v[1:]], axis=1)
    label_row = flat(labels)
    counts = dot_last(jnp.ones((8, docs), bf16), as_bf16(iota((LANES, docs), 0) == label_row))[:1]
    named = jnp.where(iota((8, docs), 0) == flat(quad), (label_row + 1).astype(f32), 0.0).astype(bf16)
    names = dot_last(named, as_bf16(iota((LANES, docs), 0) == flat(lane)))
    own = jnp.where(first, place[:1], place[1:])
    other = jnp.where(first, place[1:], place[:1])
    onehot = as_bf16(iota((BINS * block, docs), 0) == jnp.concatenate([own, other], axis=1))
    is_last = iota((block, WIDTH), 0) == (block - 1)
    for y in range(4):
        columns = slice(y * WIDTH, (y + 1) * WIDTH)
        x = jnp.concatenate([keep_ref[:ROWS, columns], got_ref[:ROWS, columns]], axis=0)
        packed = dot(onehot, x)
        for b in range(BINS):
            extra = jnp.concatenate([names[b // 4:b // 4 + 1], counts, jnp.zeros((1, 2 * LANES), f32)], axis=1)
            out_ref[4 * b + y] = jnp.where(is_last, extra, packed[b * block:(b + 1) * block]).astype(bf16)


def labels_of(block, x_ref):
    tail = x_ref[:, block - 8:, :2 * LANES].astype(f32)
    tail = jnp.max(jnp.where(iota(tail.shape, 1) == 7, tail, 0.0), axis=1)
    return tail[:, :LANES].astype(i32) - 1, tail[:, LANES:].astype(bf16)


def counts_of(chip_counts):
    row, col = iota((LANES, LANES), 0), iota((LANES, LANES), 1)
    in_bin = (bin_of(row) == col) & (row < 4 * BINS)
    counts = [dot(chip_counts, as_bf16(in_bin & ((row & 3) == r))) for r in range(4)]
    return counts, [jnp.sum(v, axis=0, keepdims=True) for v in counts]


def in_order(sizes):
    a, b = jnp.maximum(sizes[0], sizes[1]), jnp.minimum(sizes[0], sizes[1])
    c, d = jnp.maximum(sizes[2], sizes[3]), jnp.minimum(sizes[2], sizes[3])
    first, e = jnp.maximum(a, c), jnp.minimum(a, c)
    g, fourth = jnp.maximum(b, d), jnp.minimum(b, d)
    return first, jnp.maximum(e, g), jnp.minimum(e, g), fourth


def names_kernel(block, x_ref, guest_ref, line_ref, key_ref, pos_ref, meta_ref):
    z = index_on("z")
    labels, _ = labels_of(block, x_ref)
    row, col = iota((LANES, LANES), 0), iota((LANES, LANES), 1)
    lane = iota(labels.shape, 1)
    group = lane >> 5
    valid = labels >= 0
    home = bin_of(labels) & 3
    at_home = valid & (home == z)
    upper = as_bf16(row < col)
    lower = as_bf16(iota((CHIPS, CHIPS), 1) < iota((CHIPS, CHIPS), 0))
    members, n = [at_home & ((labels & 3) == r) for r in range(4)], []
    for member in members:
        size = jnp.sum(jnp.where(member, 1.0, 0.0), axis=0, keepdims=True)
        n.append(jnp.sum(size, axis=1, keepdims=True))
    wide = lambda v: jnp.broadcast_to(v, (1, LANES))
    meta_ref[...] = jnp.concatenate([wide(v) for v in in_order(n)] * 2, axis=0).astype(i32)
    pos = jnp.full(labels.shape, -1.0, f32)
    for r, member in enumerate(members):
        place = sum(
            jnp.where((n[q] > n[r]) | ((n[q] == n[r]) & (q < r)), 1.0, 0.0) for q in range(4) if q != r
        )
        start = jnp.where(
            place < 0.5, float(STARTS[0]),
            jnp.where(place < 1.5, float(STARTS[1]), jnp.where(place < 2.5, float(STARTS[2]), float(STARTS[3]))),
        )
        member16 = as_bf16(member)
        rank = dot(member16, upper) + jnp.sum(dot(lower, member16), axis=1, keepdims=True)
        pos = jnp.where(member, start + rank, pos)
    pos = pos.astype(i32)
    pos_ref[...] = pos
    guest = valid & (home != group)
    guest16 = as_bf16(guest)
    same = (row >> 5) == (col >> 5)
    turn = dot(guest16, as_bf16(same & (row < col))) + dot(dot(lower, guest16).astype(bf16), as_bf16(same))
    turn = turn.astype(i32)
    away = at_home & (group != z) & (turn < GUESTS)
    key_ref[...] = jnp.where(away, turn, -1)
    per, groups = 16, CHIPS // 16
    value = jnp.where(group == z, jnp.where(guest, GUEST + turn, pos + 1), 0).astype(f32)
    value = pltpu.roll(value, lax.rem(LANES - GROUP * z, LANES), 1)
    value = jnp.where(lane < block, value, 0.0)
    lined = jnp.zeros((8, per * block), f32)
    for t in range(per):
        rows = jnp.concatenate([value[per * g + t:per * g + t + 1] for g in range(groups)] * 2, axis=0)
        rows = jnp.concatenate([rows, jnp.zeros((8, per * block - LANES), f32)], axis=1)
        lined = lined + (pltpu.roll(rows, t * block, 1) if t else rows)
    slots = jnp.concatenate([lined[g:g + 1] for g in range(groups)], axis=1).astype(i32)
    line_ref[...] = jnp.broadcast_to(slots, line_ref.shape)
    onehot = as_bf16(iota((GUESTS, CHIPS * block), 0) + GUEST == slots)
    guest_ref[...] = dot(onehot, x_ref[...].reshape(CHIPS * block, WIDTH)).astype(bf16)


def sorted_rows(segment, slots, x):
    onehot = as_bf16(iota((segment[1], x.shape[0]), 0) + (segment[0] + 1) == slots)
    return dot(onehot, x).astype(bf16)


def sort_kernel(block, x_ref, line_ref, send_ref, mine_ref):
    x = x_ref[...].reshape(CHIPS * block, WIDTH)
    slots = line_ref[:1, :]
    for core in range(2):
        @pl.when(index_on("c") == core)
        def _():
            for segment in SEGMENTS:
                rows = sorted_rows(segment, slots, x)
                for out_ref, at in ((mine_ref, segment[2 + core]), (send_ref, segment[2 + 1 - core])):
                    if at is not None:
                        out_ref[at:at + segment[1], :] = rows


def fit_kernel(block, units, x_ref, meta_ref, over_ref, table_ref):
    _, chip_counts = labels_of(block, x_ref)
    counts, sizes = counts_of(chip_counts)
    ordered = in_order(sizes)
    over = jnp.zeros((1, LANES), f32)
    for size, cap in zip(ordered, CAPS):
        over = jnp.maximum(over, jnp.where(size > cap, 1.0, 0.0))
    for share in SHARES:
        length = 0.0
        for q, first in share:
            rows = jnp.maximum(jnp.floor((ordered[q] + (UNIT - 1.0)) * (1 / UNIT)) - first // UNIT, 0.0)
            length = length + jnp.where(rows >= 3.0, rows - 1.0, rows)
        over = jnp.maximum(over, jnp.where(length > 4 * units, 1.0, 0.0))
    taken = counts[0] + counts[1] + counts[2] + counts[3]
    lane = iota(taken.shape, 1) & 3
    before = lambda v, back: jnp.where(lane >= back, pltpu.roll(v, back, 1), pltpu.roll(v, LANES - 4 + back, 1))
    extra = taken - (block - 1)
    moved = passed_on(extra, before)
    held = jnp.sum(moved, axis=0, keepdims=True)
    over = jnp.maximum(over, jnp.where(held > GUESTS, 1.0, 0.0))
    full = extra + before(extra, 1) + before(extra, 2) + before(extra, 3) > 0
    full = jnp.where(full | (moved > block - 1), 1.0, 0.0)
    over = jnp.maximum(over, jnp.max(full, axis=0, keepdims=True))
    over_ref[...] = jnp.broadcast_to(jnp.max(over, axis=1, keepdims=True), over_ref.shape).astype(i32)
    y, c = index_on("y"), index_on("c")
    blocks, sizes = [], [size_of(meta_ref, q) for q in range(4)]
    for core, share in enumerate(SHARES):
        at = jnp.zeros((), i32)
        for q, first in share:
            length = length_of(sizes[q], first)
            blocks.append((jnp.where((c == core) & (length > 0), at, 4 * units), FIRST_ROW[q] + first // LANES, at))
            at = at + length
    for t in range(units):
        index = y * units + t
        col, start = jnp.asarray(15, i32), jnp.asarray(0, i32)
        for block_start, block_col, block_at in blocks:
            inside = index >= block_start
            col, start = jnp.where(inside, block_col, col), jnp.where(inside, block_at, start)
        turn = index - start
        unit = 4 * col + jnp.where(turn == 0, 2, jnp.where(turn == 1, 1, turn + 1))
        beside = jnp.where(turn == 0, 3 * UNIT, LANES)
        for entry, value in enumerate((unit >> 2, (unit & 3) * UNIT, beside, col)):
            table_ref[4 * t + entry:4 * t + entry + 1, :] = jnp.full((1, LANES), value, i32)


def add_guests(core, base_ref, guest_ref, far_ref, out_ref):
    guests, far = guest_ref[...], far_ref[:1, :]
    for segment in SEGMENTS:
        at, rows = segment[2 + core], segment[1]
        if at is not None:
            out_ref[at:at + rows, :] = base_ref[at:at + rows, :] + sorted_rows(segment, far, guests)


def blocks_of(core):
    for q, first in SHARES[core]:
        at = BASES[core][q] + first
        yield q, first, pl.ds(at, CAPS[q] - first), pl.ds(at, LANES)


RAW_ROWS = max(sum(CAPS[q] - first for q, first in share) for share in SHARES)


def own_kernel(x_ref, guest_ref, key_ref, pos_ref, raw_ref, far_ref, rows_ref):
    total = jnp.zeros((8, GUESTS), f32)
    step = 16
    for first in range(0, CHIPS, step):
        flat = lambda ref: jnp.concatenate([ref[s:s + 1, :] for s in range(first, first + step)], axis=1)
        places = flat(pos_ref) + 1
        parts = jnp.where(iota((8, step * LANES), 0) == 0, places >> 5, places & 31).astype(f32).astype(bf16)
        total = total + dot_last(parts, as_bf16(iota((GUESTS, step * LANES), 0) == flat(key_ref)))
    far_ref[...] = jnp.broadcast_to((32.0 * total[:1] + total[1:2]).astype(i32), far_ref.shape)
    for core in range(2):
        @pl.when(index_on("c") == core)
        def _():
            add_guests(core, x_ref, guest_ref, far_ref, rows_ref)
            at = 0
            for q, first, left, right in blocks_of(core):
                rows = CAPS[q] - first
                raw_ref[at:at + rows, :] = dot_last(rows_ref[left, :], rows_ref[right, :])
                at += rows


def size_of(meta_ref, q):
    return jnp.max(meta_ref[q:q + 1, :].astype(f32)).astype(i32)


def length_of(size, first):
    units = jnp.maximum(((size + UNIT - 1) >> 5) - first // UNIT, 0)
    return jnp.where(units >= 3, units - 1, units)


def folded(score):
    away = jnp.full((UNIT, LANES), -4.0, f32) if score.shape[0] < LANES else score[2 * UNIT:3 * UNIT]
    both = jnp.where(iota(away.shape, 1) < 3 * UNIT, away, pltpu.roll(score[:UNIT], 3 * UNIT, 1))
    rest = [score[3 * UNIT:]] if score.shape[0] > 3 * UNIT else []
    return jnp.concatenate([both, score[UNIT:2 * UNIT]] + rest, axis=0)


def gram_kernel(units, meta_ref, x_ref, guest_ref, far_ref, raw_ref, out0, out1, out2, out3, part_ref, rows_ref):
    y, c = index_on("y"), index_on("c")
    part_ref[...] = jnp.full(part_ref.shape, -4.0, f32)
    for core in range(2):
        @pl.when(c == core)
        def _():
            add_guests(core, x_ref, guest_ref, far_ref, rows_ref)
            at, to = 0, jnp.zeros((), i32)
            for q, first, left, right in blocks_of(core):
                rows = CAPS[q] - first
                score = raw_ref[at:at + rows, :] + dot_last(rows_ref[left, :], rows_ref[right, :])
                at += rows
                size = size_of(meta_ref, q)
                i, j = iota(score.shape, 0), iota(score.shape, 1)
                keep = (i < size - first) & (j < size - first) & (i != j)
                score = folded(jnp.where(keep, score, -4.0))
                part_ref[pl.ds(pl.multiple_of(to, UNIT), score.shape[0]), :] = score
                to = jnp.minimum(to + UNIT * length_of(size, first), 4 * units * UNIT)
    chunk = units * UNIT
    for shift, out in enumerate((out0, out1, out2, out3)):
        out[...] = part_ref[pl.ds(pl.multiple_of(lax.rem(y + shift, 4) * chunk, UNIT), chunk), :]


FIRST_ROW = (0, 6, 10, 13)


def max_kernel(units, table_ref, p0, p1, p2, p3, pos_ref, out_ref):
    best = jnp.full((16, LANES), -1.0, f32)
    sub, lane, row = iota((UNIT, LANES), 0), iota((UNIT, LANES), 1), iota((16, LANES), 0)
    for t in range(units):
        at = slice(t * UNIT, (t + 1) * UNIT)
        block = (p0[at, :] + p1[at, :]) + (p2[at, :] + p3[at, :])
        unit_row, offset, beside, col = (table_ref[4 * t + entry:4 * t + entry + 1, :] for entry in range(4))
        one, two = jnp.where(lane < beside, block, -4.0), jnp.where(lane < beside, -4.0, block)
        along = jnp.max(one, axis=1, keepdims=True)
        along = jnp.max(jnp.where(sub + offset == lane, along, -1.0), axis=0, keepdims=True)
        best = jnp.maximum(best, jnp.where(row == unit_row, along, -1.0))
        along = jnp.max(two, axis=1, keepdims=True)
        two = jnp.maximum(jnp.where(sub == lane, along, -1.0), pltpu.roll(two, UNIT, 1))
        down = jnp.max(jnp.maximum(one, two), axis=0, keepdims=True)
        best = jnp.maximum(best, jnp.where(row == col, down, -1.0))
    pos = pos_ref[...]
    pos = jnp.where(pos >= STARTS[1], pos + 64, pos)
    pos = jnp.where(pos >= STARTS[3] + 64, pos + 64, pos)
    row, lane = pos >> 7, pos & (LANES - 1)
    out = jnp.full(pos.shape, -1.0, f32)
    for r in range(15):
        value = jnp.broadcast_to(best[r:r + 1, :], pos.shape)
        value = jnp.take_along_axis(value, lane, axis=1, mode="promise_in_bounds")
        out = jnp.where(row == r, value, out)
    out_ref[:CHIPS, :] = out
    out_ref[CHIPS:, :] = out


def pick_kernel(v_ref, code_ref, out_ref):
    c = index_on("c")
    values = jnp.maximum(v_ref[:CHIPS, :], v_ref[CHIPS:, :])
    values = jnp.max(values.reshape(BINS, 4, LANES), axis=1)
    eye = iota((LANES, LANES), 0) == iota((LANES, LANES), 1)
    code = jnp.max(jnp.where(iota((8, ROWS), 0) == c, code_ref[...], -1), axis=0, keepdims=True)
    code = jnp.max(jnp.where(eye, code.astype(f32), -1.0), axis=1, keepdims=True).astype(i32)
    slot = iota((ROWS, LANES), 1)
    best = jnp.full((ROWS, LANES), -1.0, f32)
    for b in range(BINS):
        best = jnp.where(slot + b * LANES == code, values[b:b + 1], best)
    best = jnp.max(best, axis=1, keepdims=True)
    out_ref[...] = jnp.max(jnp.where(eye, best, -1.0), axis=0, keepdims=True)


def gather_groups(embeddings, cluster_ids):
    split = ("z", "y", "c")
    rows = embeddings.shape[0]
    groups = lax.axis_size("x")
    cap = 2 * rows // groups
    slots = groups * cap
    owner_of = cluster_ids % groups
    onehot = (owner_of[:, None] == jnp.arange(groups, dtype=i32)[None, :]).astype(i32)
    before = jnp.cumsum(onehot, axis=0) - onehot
    rank = jnp.sum(before * onehot, axis=1)
    place = owner_of * cap + rank
    picked = place[None, :] == jnp.arange(slots, dtype=i32)[:, None]
    filled = jnp.any(picked, axis=1)
    source = jnp.sum(jnp.where(picked, jnp.arange(rows, dtype=i32)[None, :], 0), axis=1)
    out_labels = jnp.where(filled, cluster_ids[source], -1)
    squares = jnp.sum(embeddings * embeddings, axis=1, keepdims=True)
    local_unit = (embeddings * lax.rsqrt(squares + 1e-06)).astype(bf16)
    outgoing_unit = jnp.where(filled[:, None], local_unit[source], jnp.zeros((), bf16))
    unit = lax.all_to_all(outgoing_unit, "x", split_axis=0, concat_axis=0, tiled=True)
    labels = lax.all_to_all(out_labels, "x", split_axis=0, concat_axis=0, tiled=True)
    members = lax.axis_size(split)

    def everywhere(v):
        copies = jnp.broadcast_to(v[None], (members,) + v.shape).reshape((members * slots,) + v.shape[1:])
        return lax.all_to_all(copies, split, split_axis=0, concat_axis=0, tiled=True)

    def add_slice(i, scores):
        part = lax.dynamic_slice_in_dim(unit, i * WIDTH, WIDTH, 1)
        return scores + dot_last(part, everywhere(part))

    scores = lax.fori_loop(0, embeddings.shape[1] // WIDTH, add_slice, jnp.zeros((slots, members * slots), f32))
    all_labels = everywhere(labels)
    own = lax.axis_index(split) * slots + jnp.arange(slots, dtype=i32)
    mask = (
        (labels[:, None] == all_labels[None, :])
        & (labels[:, None] >= 0)
        & (own[:, None] != jnp.arange(members * slots, dtype=i32)[None, :])
    )
    scores = jnp.where(mask, scores, -1.0)
    best = jnp.maximum(-1.0, jnp.max(scores, axis=1))
    returned = lax.all_to_all(best, "x", split_axis=0, concat_axis=0, tiled=True)
    return returned[place]


def route(block, units, embeddings, cluster_ids):
    shape = jax.ShapeDtypeStruct
    half = shape((ROWS + LABEL_ROWS, HALF_WIDTH), bf16)
    ids = cluster_ids.reshape(1, ROWS)
    send, scale = pl.pallas_call(
        unit_send_kernel, out_shape=(half, shape((ROWS, LANES), f32)),
        in_specs=[WHOLE, WHOLE], out_specs=(WHOLE, WHOLE), compiler_params=params(12), name="unit_send",
    )(embeddings, ids)
    got = lax.ppermute(send, "c", [(0, 1), (1, 0)])
    keep = pl.pallas_call(
        unit_keep_kernel, out_shape=half,
        in_specs=[pl.BlockSpec(memory_space=pl.ANY), WHOLE, WHOLE], out_specs=WHOLE,
        scratch_shapes=[pltpu.VMEM((ROWS, HALF_WIDTH), f32), pltpu.SemaphoreType.DMA],
        compiler_params=params(8), name="unit_keep",
    )(embeddings, ids, scale)
    packed, code = pl.pallas_call(
        functools.partial(pack_kernel, block),
        out_shape=(shape((CHIPS, block, WIDTH), bf16), shape((8, ROWS), i32)),
        in_specs=[WHOLE, WHOLE], out_specs=(WHOLE, WHOLE), compiler_params=params(20), name="pack",
    )(keep, got)
    packed = lax.all_to_all(packed, ("x", "z", "y"), 0, 0, tiled=True)
    table = shape((CHIPS, LANES), i32)
    guests, line, key, pos, meta = pl.pallas_call(
        functools.partial(names_kernel, block),
        out_shape=(shape((GUESTS, WIDTH), bf16), shape((8, CHIPS * block), i32), table, table, shape((8, LANES), i32)),
        in_specs=[WHOLE], out_specs=(WHOLE,) * 5, compiler_params=params(12), name="names",
    )(packed)
    brought = lax.ppermute(guests, "z", [(i, (i + 3) % 4) for i in range(4)])
    share = shape((SHARE_ROWS, WIDTH), bf16)
    send, mine = pl.pallas_call(
        functools.partial(sort_kernel, block), out_shape=(share, share),
        in_specs=[WHOLE] * 2, out_specs=(WHOLE,) * 2, compiler_params=params(24), name="sort",
    )(packed, line)
    brought, mine, send = lax.optimization_barrier((brought, mine, send))
    other = lax.ppermute(send, "c", [(0, 1), (1, 0)])
    swapped = lax.ppermute(brought, "c", [(0, 1), (1, 0)])
    raw, far = pl.pallas_call(
        own_kernel, out_shape=(shape((RAW_ROWS, LANES), f32), shape((8, GUESTS), i32)),
        in_specs=[WHOLE] * 4, out_specs=(WHOLE,) * 2,
        scratch_shapes=[pltpu.VMEM((SHARE_ROWS, WIDTH), bf16)],
        compiler_params=params(16), name="own",
        cost_estimate=pl.CostEstimate(flops=2 * RAW_ROWS * LANES * WIDTH, bytes_accessed=4 << 20, transcendentals=0),
    )(mine, brought, key, pos)
    partial = pl.pallas_call(
        functools.partial(gram_kernel, units),
        out_shape=[shape((units * UNIT, LANES), f32)] * 4,
        in_specs=[WHOLE] * 5, out_specs=[WHOLE] * 4,
        scratch_shapes=[pltpu.VMEM((4 * units * UNIT + CAPS[0], LANES), f32), pltpu.VMEM((SHARE_ROWS, WIDTH), bf16)],
        compiler_params=params(16), name="gram",
    )(meta, other, swapped, far, raw)
    arrived = [partial[0]] + [
        lax.ppermute(partial[s], "y", [(i, (i + s) % 4) for i in range(4)]) for s in (1, 2, 3)
    ]
    over, table = pl.pallas_call(
        functools.partial(fit_kernel, block, units),
        out_shape=(shape((8, LANES), i32), shape((4 * units, LANES), i32)),
        in_specs=[WHOLE, WHOLE], out_specs=(WHOLE, WHOLE), compiler_params=params(8), name="fit",
    )(packed, meta)
    arrived, fits, table = lax.optimization_barrier((arrived, over[0, 0] == 0, table))
    best = pl.pallas_call(
        functools.partial(max_kernel, units),
        out_shape=shape((2 * CHIPS, LANES), f32),
        in_specs=[WHOLE] * 6, out_specs=WHOLE, compiler_params=params(8), name="maxima",
    )(table, *arrived, pos)
    back = lax.all_to_all(best.reshape(2 * CHIPS, 1, LANES), ("c", "x", "z", "y"), 0, 0, tiled=True)
    back, fits = lax.optimization_barrier((back, fits))
    best = pl.pallas_call(
        pick_kernel,
        out_shape=shape((1, ROWS), f32),
        in_specs=[WHOLE, WHOLE], out_specs=WHOLE, compiler_params=params(8), name="pick",
    )(back.reshape(2 * CHIPS, LANES), code).reshape(ROWS)
    return best, fits


def on_device(embeddings, cluster_ids, tries=TRIES):
    if not tries:
        return gather_groups(embeddings, cluster_ids)
    best, fits = route(*tries[0], embeddings, cluster_ids)
    return lax.cond(
        fits,
        lambda best, embeddings, cluster_ids: best,
        lambda best, embeddings, cluster_ids: on_device(embeddings, cluster_ids, tries[1:]),
        best, embeddings, cluster_ids,
    )


def solution(mesh):
    axes = ("x", "z", "y", "c")
    grid = Mesh(mesh.devices.reshape(4, 4, 4, 2), axes)
    return jax.shard_map(
        on_device, mesh=grid, in_specs=(P(axes, None), P(axes)), out_specs=P(axes), check_vma=False
    )
```

```python
import functools

import jax
import jax.numpy as jnp
from jax import lax
from jax.experimental import pallas as pl
from jax.experimental.pallas import tpu as pltpu
from jax.sharding import Mesh, PartitionSpec as P

ROWS = 128
HALF_WIDTH = 2048
WIDTH = 512
LABEL_ROWS = 16
BINS = 16
CHIPS = 64
TRIES = ((24, 11), (32, 16))
GROUP = 32
GUESTS = 64
GUEST = 4096
LANES = 128
CAPS = (704, 512, 320, 192)
STARTS = (0, 704, 1216, 1536)
UNIT = 32
SHARES = (
    ((0, 0), (0, 256), (2, 0), (2, 128), (2, 256), (3, 0)),
    ((0, 128), (0, 384), (0, 512), (0, 640), (1, 0), (1, 128), (1, 256), (1, 384), (3, 128)),
)
BASES = ({0: 0, 2: 704, 3: 1024}, {0: -128, 1: 576, 3: 960})
SHARE_ROWS = 1216
SEGMENTS = (
    (0, 128, 0, None), (128, 576, 128, 0), (704, 256, None, 576), (960, 256, None, 832),
    (1216, 320, 704, None), (1536, 128, 1024, None), (1664, 64, 1152, 1088),
)
f32, bf16, i32 = jnp.float32, jnp.bfloat16, jnp.int32
WHOLE = pl.BlockSpec(memory_space=pltpu.VMEM)


def params(mib):
    return pltpu.CompilerParams(vmem_limit_bytes=mib * 1024 * 1024)


def index_on(axis):
    return lax.axis_index(axis)


def iota(shape, dim):
    return lax.broadcasted_iota(i32, shape, dim)


def dot_last(a, b):
    return lax.dot_general(a, b, (((1,), (1,)), ((), ())), preferred_element_type=f32)


def dot(a, b):
    return lax.dot_general(a, b, (((1,), (0,)), ((), ())), preferred_element_type=f32)


def as_bf16(mask):
    return jnp.where(mask, 1.0, 0.0).astype(bf16)


def bin_of(labels):
    rank, residue = labels >> 2, labels & 3
    row, col = rank >> 2, rank & 3
    col = jnp.where((row & 1) == 1, 3 - col, col)
    return 4 * col + ((row - residue) & 3)


def label_rows(ids_ref):
    ids = jnp.concatenate([ids_ref[...].astype(f32), jnp.zeros((1, HALF_WIDTH - ROWS), f32)], axis=1)
    return jnp.broadcast_to(ids, (LABEL_ROWS, HALF_WIDTH)).astype(bf16)


def half_of(core):
    return pl.ds(pl.multiple_of(core * HALF_WIDTH, HALF_WIDTH), HALF_WIDTH)


def unit_send_kernel(x_ref, ids_ref, out_ref, scale_ref):
    x = x_ref[...]
    scale = lax.rsqrt(jnp.sum(x * x, axis=1, keepdims=True) + 1e-06)
    scale_ref[...] = jnp.broadcast_to(scale, scale_ref.shape)
    out_ref[:ROWS, :] = (x_ref[:, half_of(1 - index_on("c"))] * scale).astype(bf16)
    out_ref[ROWS:, :] = label_rows(ids_ref)


def unit_keep_kernel(x_ref, ids_ref, scale_ref, out_ref, half_ref, sem):
    copy = pltpu.make_async_copy(x_ref.at[:, half_of(index_on("c"))], half_ref, sem)
    copy.start()
    out_ref[ROWS:, :] = label_rows(ids_ref)
    copy.wait()
    out_ref[:ROWS, :] = (half_ref[...] * scale_ref[:, :1]).astype(bf16)


def passed_on(over, before):
    once = before(over, 1)
    twice = before(over, 2)
    return jnp.maximum(jnp.maximum(over, 0), jnp.maximum(over + once, over + once + twice))


def pack_kernel(block, keep_ref, got_ref, out_ref, code_ref):
    first = index_on("c") == 0
    kept = jnp.max(keep_ref[ROWS:, :ROWS].astype(f32), axis=0, keepdims=True)
    got = jnp.max(got_ref[ROWS:, :ROWS].astype(f32), axis=0, keepdims=True)
    labels = jnp.concatenate([jnp.where(first, kept, got), jnp.where(first, got, kept)], axis=0).astype(i32)
    bins = bin_of(labels)
    upper = as_bf16(iota((ROWS, ROWS), 0) < iota((ROWS, ROWS), 1))

    def ranks_within(masks):
        member = jnp.concatenate([jnp.where(mask, 1.0, 0.0) for mask in masks], axis=0)
        row, col = iota((member.shape[0],) * 2, 0), iota((member.shape[0],) * 2, 1)
        earlier = dot(as_bf16(((row >> 1) == (col >> 1)) & (col < row)), member.astype(bf16))
        ranks = member * (dot(member.astype(bf16), upper) + jnp.sum(earlier, axis=1, keepdims=True))
        rank = sum(ranks[2 * b:2 * b + 2] for b in range(len(masks)))
        return rank.astype(i32), jnp.sum(member, axis=1, keepdims=True)

    rank, sizes = ranks_within([bins == b for b in range(BINS)])
    quad, line = bins >> 2, bins & 3
    taken = []
    for at in range(4):
        size = jnp.zeros(labels.shape, f32)
        for b in range(at, BINS, 4):
            size = jnp.where(quad == b >> 2, sizes[2 * b:2 * b + 1] + sizes[2 * b + 1:2 * b + 2], size)
        taken.append(size.astype(i32) - (block - 1))
    stays = []
    for at in range(4):
        moved = passed_on(taken[at], lambda _, back: taken[(at - back) & 3])
        stays.append(taken[at] + (block - 1) - moved)

    def of_line(values, which):
        out = values[0]
        for at in range(1, 4):
            out = jnp.where(which == at, values[at], out)
        return out

    stay = of_line(stays, line)
    to_line = jnp.where(rank < stay, line, (line + 1) & 3)
    to_slot = jnp.where(rank < stay, rank, of_line(stays, to_line) + rank - stay)
    placed = to_slot < (block - 1)
    lane = jnp.where(placed, to_line * GROUP + to_slot, -1)
    place = jnp.where(placed, (quad * 4 + to_line) * block + to_slot, -1)
    code_ref[...] = jnp.concatenate([jnp.where(placed, bins * LANES + lane, -1)] * 4, axis=0)
    docs = 2 * ROWS
    flat = lambda v: jnp.concatenate([v[:1], v[1:]], axis=1)
    label_row = flat(labels)
    counts = dot_last(jnp.ones((8, docs), bf16), as_bf16(iota((LANES, docs), 0) == label_row))[:1]
    named = jnp.where(iota((8, docs), 0) == flat(quad), (label_row + 1).astype(f32), 0.0).astype(bf16)
    names = dot_last(named, as_bf16(iota((LANES, docs), 0) == flat(lane)))
    own = jnp.where(first, place[:1], place[1:])
    other = jnp.where(first, place[1:], place[:1])
    onehot = as_bf16(iota((BINS * block, docs), 0) == jnp.concatenate([own, other], axis=1))
    is_last = iota((block, WIDTH), 0) == (block - 1)
    for y in range(4):
        columns = slice(y * WIDTH, (y + 1) * WIDTH)
        x = jnp.concatenate([keep_ref[:ROWS, columns], got_ref[:ROWS, columns]], axis=0)
        packed = dot(onehot, x)
        for b in range(BINS):
            extra = jnp.concatenate([names[b // 4:b // 4 + 1], counts, jnp.zeros((1, 2 * LANES), f32)], axis=1)
            out_ref[4 * b + y] = jnp.where(is_last, extra, packed[b * block:(b + 1) * block]).astype(bf16)


def labels_of(block, x_ref):
    tail = x_ref[:, block - 8:, :2 * LANES].astype(f32)
    tail = jnp.max(jnp.where(iota(tail.shape, 1) == 7, tail, 0.0), axis=1)
    return tail[:, :LANES].astype(i32) - 1, tail[:, LANES:].astype(bf16)


def counts_of(chip_counts):
    row, col = iota((LANES, LANES), 0), iota((LANES, LANES), 1)
    in_bin = (bin_of(row) == col) & (row < 4 * BINS)
    counts = [dot(chip_counts, as_bf16(in_bin & ((row & 3) == r))) for r in range(4)]
    return counts, [jnp.sum(v, axis=0, keepdims=True) for v in counts]


def in_order(sizes):
    a, b = jnp.maximum(sizes[0], sizes[1]), jnp.minimum(sizes[0], sizes[1])
    c, d = jnp.maximum(sizes[2], sizes[3]), jnp.minimum(sizes[2], sizes[3])
    first, e = jnp.maximum(a, c), jnp.minimum(a, c)
    g, fourth = jnp.maximum(b, d), jnp.minimum(b, d)
    return first, jnp.maximum(e, g), jnp.minimum(e, g), fourth


def names_kernel(block, x_ref, guest_ref, line_ref, key_ref, pos_ref, meta_ref):
    z = index_on("z")
    labels, _ = labels_of(block, x_ref)
    row, col = iota((LANES, LANES), 0), iota((LANES, LANES), 1)
    lane = iota(labels.shape, 1)
    group = lane >> 5
    valid = labels >= 0
    home = bin_of(labels) & 3
    at_home = valid & (home == z)
    upper = as_bf16(row < col)
    lower = as_bf16(iota((CHIPS, CHIPS), 1) < iota((CHIPS, CHIPS), 0))
    members, n = [at_home & ((labels & 3) == r) for r in range(4)], []
    for member in members:
        size = jnp.sum(jnp.where(member, 1.0, 0.0), axis=0, keepdims=True)
        n.append(jnp.sum(size, axis=1, keepdims=True))
    wide = lambda v: jnp.broadcast_to(v, (1, LANES))
    meta_ref[...] = jnp.concatenate([wide(v) for v in in_order(n)] * 2, axis=0).astype(i32)
    pos = jnp.full(labels.shape, -1.0, f32)
    for r, member in enumerate(members):
        place = sum(
            jnp.where((n[q] > n[r]) | ((n[q] == n[r]) & (q < r)), 1.0, 0.0) for q in range(4) if q != r
        )
        start = jnp.where(
            place < 0.5, float(STARTS[0]),
            jnp.where(place < 1.5, float(STARTS[1]), jnp.where(place < 2.5, float(STARTS[2]), float(STARTS[3]))),
        )
        member16 = as_bf16(member)
        rank = dot(member16, upper) + jnp.sum(dot(lower, member16), axis=1, keepdims=True)
        pos = jnp.where(member, start + rank, pos)
    pos = pos.astype(i32)
    pos_ref[...] = pos
    guest = valid & (home != group)
    guest16 = as_bf16(guest)
    same = (row >> 5) == (col >> 5)
    turn = dot(guest16, as_bf16(same & (row < col))) + dot(dot(lower, guest16).astype(bf16), as_bf16(same))
    turn = turn.astype(i32)
    away = at_home & (group != z) & (turn < GUESTS)
    key_ref[...] = jnp.where(away, turn, -1)
    per, groups = 16, CHIPS // 16
    value = jnp.where(group == z, jnp.where(guest, GUEST + turn, pos + 1), 0).astype(f32)
    value = pltpu.roll(value, lax.rem(LANES - GROUP * z, LANES), 1)
    value = jnp.where(lane < block, value, 0.0)
    lined = jnp.zeros((8, per * block), f32)
    for t in range(per):
        rows = jnp.concatenate([value[per * g + t:per * g + t + 1] for g in range(groups)] * 2, axis=0)
        rows = jnp.concatenate([rows, jnp.zeros((8, per * block - LANES), f32)], axis=1)
        lined = lined + (pltpu.roll(rows, t * block, 1) if t else rows)
    slots = jnp.concatenate([lined[g:g + 1] for g in range(groups)], axis=1).astype(i32)
    line_ref[...] = jnp.broadcast_to(slots, line_ref.shape)
    onehot = as_bf16(iota((GUESTS, CHIPS * block), 0) + GUEST == slots)
    guest_ref[...] = dot(onehot, x_ref[...].reshape(CHIPS * block, WIDTH)).astype(bf16)


def sorted_rows(segment, slots, x):
    onehot = as_bf16(iota((segment[1], x.shape[0]), 0) + (segment[0] + 1) == slots)
    return dot(onehot, x).astype(bf16)


def sort_kernel(block, x_ref, line_ref, send_ref, mine_ref):
    x = x_ref[...].reshape(CHIPS * block, WIDTH)
    slots = line_ref[:1, :]
    for core in range(2):
        @pl.when(index_on("c") == core)
        def _():
            for segment in SEGMENTS:
                rows = sorted_rows(segment, slots, x)
                for out_ref, at in ((mine_ref, segment[2 + core]), (send_ref, segment[2 + 1 - core])):
                    if at is not None:
                        out_ref[at:at + segment[1], :] = rows


def fit_kernel(block, units, x_ref, meta_ref, over_ref, table_ref):
    _, chip_counts = labels_of(block, x_ref)
    counts, sizes = counts_of(chip_counts)
    ordered = in_order(sizes)
    over = jnp.zeros((1, LANES), f32)
    for size, cap in zip(ordered, CAPS):
        over = jnp.maximum(over, jnp.where(size > cap, 1.0, 0.0))
    for share in SHARES:
        length = 0.0
        for q, first in share:
            rows = jnp.maximum(jnp.floor((ordered[q] + (UNIT - 1.0)) * (1 / UNIT)) - first // UNIT, 0.0)
            length = length + jnp.where(rows >= 3.0, rows - 1.0, rows)
        over = jnp.maximum(over, jnp.where(length > 4 * units, 1.0, 0.0))
    taken = counts[0] + counts[1] + counts[2] + counts[3]
    lane = iota(taken.shape, 1) & 3
    before = lambda v, back: jnp.where(lane >= back, pltpu.roll(v, back, 1), pltpu.roll(v, LANES - 4 + back, 1))
    extra = taken - (block - 1)
    moved = passed_on(extra, before)
    held = jnp.sum(moved, axis=0, keepdims=True)
    over = jnp.maximum(over, jnp.where(held > GUESTS, 1.0, 0.0))
    full = extra + before(extra, 1) + before(extra, 2) + before(extra, 3) > 0
    full = jnp.where(full | (moved > block - 1), 1.0, 0.0)
    over = jnp.maximum(over, jnp.max(full, axis=0, keepdims=True))
    over_ref[...] = jnp.broadcast_to(jnp.max(over, axis=1, keepdims=True), over_ref.shape).astype(i32)
    y, c = index_on("y"), index_on("c")
    blocks, sizes = [], [size_of(meta_ref, q) for q in range(4)]
    for core, share in enumerate(SHARES):
        at = jnp.zeros((), i32)
        for q, first in share:
            length = length_of(sizes[q], first)
            blocks.append((jnp.where((c == core) & (length > 0), at, 4 * units), FIRST_ROW[q] + first // LANES, at))
            at = at + length
    for t in range(units):
        index = y * units + t
        col, start = jnp.asarray(15, i32), jnp.asarray(0, i32)
        for block_start, block_col, block_at in blocks:
            inside = index >= block_start
            col, start = jnp.where(inside, block_col, col), jnp.where(inside, block_at, start)
        turn = index - start
        unit = 4 * col + jnp.where(turn == 0, 2, jnp.where(turn == 1, 1, turn + 1))
        beside = jnp.where(turn == 0, 3 * UNIT, LANES)
        for entry, value in enumerate((unit >> 2, (unit & 3) * UNIT, beside, col)):
            table_ref[4 * t + entry:4 * t + entry + 1, :] = jnp.full((1, LANES), value, i32)


def add_guests(core, base_ref, guest_ref, far_ref, out_ref):
    guests, far = guest_ref[...], far_ref[:1, :]
    for segment in SEGMENTS:
        at, rows = segment[2 + core], segment[1]
        if at is not None:
            out_ref[at:at + rows, :] = base_ref[at:at + rows, :] + sorted_rows(segment, far, guests)


def blocks_of(core):
    for q, first in SHARES[core]:
        at = BASES[core][q] + first
        yield q, first, pl.ds(at, CAPS[q] - first), pl.ds(at, LANES)


RAW_ROWS = max(sum(CAPS[q] - first for q, first in share) for share in SHARES)


def own_kernel(x_ref, guest_ref, key_ref, pos_ref, raw_ref, far_ref, rows_ref):
    total = jnp.zeros((8, GUESTS), f32)
    step = 16
    for first in range(0, CHIPS, step):
        flat = lambda ref: jnp.concatenate([ref[s:s + 1, :] for s in range(first, first + step)], axis=1)
        places = flat(pos_ref) + 1
        parts = jnp.where(iota((8, step * LANES), 0) == 0, places >> 5, places & 31).astype(f32).astype(bf16)
        total = total + dot_last(parts, as_bf16(iota((GUESTS, step * LANES), 0) == flat(key_ref)))
    far_ref[...] = jnp.broadcast_to((32.0 * total[:1] + total[1:2]).astype(i32), far_ref.shape)
    for core in range(2):
        @pl.when(index_on("c") == core)
        def _():
            add_guests(core, x_ref, guest_ref, far_ref, rows_ref)
            at = 0
            for q, first, left, right in blocks_of(core):
                rows = CAPS[q] - first
                raw_ref[at:at + rows, :] = dot_last(rows_ref[left, :], rows_ref[right, :])
                at += rows


def size_of(meta_ref, q):
    return jnp.max(meta_ref[q:q + 1, :].astype(f32)).astype(i32)


def length_of(size, first):
    units = jnp.maximum(((size + UNIT - 1) >> 5) - first // UNIT, 0)
    return jnp.where(units >= 3, units - 1, units)


def folded(score):
    away = jnp.full((UNIT, LANES), -4.0, f32) if score.shape[0] < LANES else score[2 * UNIT:3 * UNIT]
    both = jnp.where(iota(away.shape, 1) < 3 * UNIT, away, pltpu.roll(score[:UNIT], 3 * UNIT, 1))
    rest = [score[3 * UNIT:]] if score.shape[0] > 3 * UNIT else []
    return jnp.concatenate([both, score[UNIT:2 * UNIT]] + rest, axis=0)


def gram_kernel(units, meta_ref, x_ref, guest_ref, far_ref, raw_ref, out0, out1, out2, out3, part_ref, rows_ref):
    y, c = index_on("y"), index_on("c")
    part_ref[...] = jnp.full(part_ref.shape, -4.0, f32)
    for core in range(2):
        @pl.when(c == core)
        def _():
            add_guests(core, x_ref, guest_ref, far_ref, rows_ref)
            at, to = 0, jnp.zeros((), i32)
            for q, first, left, right in blocks_of(core):
                rows = CAPS[q] - first
                score = raw_ref[at:at + rows, :] + dot_last(rows_ref[left, :], rows_ref[right, :])
                at += rows
                size = size_of(meta_ref, q)
                i, j = iota(score.shape, 0), iota(score.shape, 1)
                keep = (i < size - first) & (j < size - first) & (i != j)
                score = folded(jnp.where(keep, score, -4.0))
                part_ref[pl.ds(pl.multiple_of(to, UNIT), score.shape[0]), :] = score
                to = jnp.minimum(to + UNIT * length_of(size, first), 4 * units * UNIT)
    chunk = units * UNIT
    for shift, out in enumerate((out0, out1, out2, out3)):
        out[...] = part_ref[pl.ds(pl.multiple_of(lax.rem(y + shift, 4) * chunk, UNIT), chunk), :]


FIRST_ROW = (0, 6, 10, 13)


def max_kernel(units, table_ref, p0, p1, p2, p3, pos_ref, out_ref):
    best = jnp.full((16, LANES), -1.0, f32)
    sub, lane, row = iota((UNIT, LANES), 0), iota((UNIT, LANES), 1), iota((16, LANES), 0)
    for t in range(units):
        at = slice(t * UNIT, (t + 1) * UNIT)
        block = (p0[at, :] + p1[at, :]) + (p2[at, :] + p3[at, :])
        unit_row, offset, beside, col = (table_ref[4 * t + entry:4 * t + entry + 1, :] for entry in range(4))
        one, two = jnp.where(lane < beside, block, -4.0), jnp.where(lane < beside, -4.0, block)
        along = jnp.max(one, axis=1, keepdims=True)
        along = jnp.max(jnp.where(sub + offset == lane, along, -1.0), axis=0, keepdims=True)
        best = jnp.maximum(best, jnp.where(row == unit_row, along, -1.0))
        along = jnp.max(two, axis=1, keepdims=True)
        two = jnp.maximum(jnp.where(sub == lane, along, -1.0), pltpu.roll(two, UNIT, 1))
        down = jnp.max(jnp.maximum(one, two), axis=0, keepdims=True)
        best = jnp.maximum(best, jnp.where(row == col, down, -1.0))
    pos = pos_ref[...]
    pos = jnp.where(pos >= STARTS[1], pos + 64, pos)
    pos = jnp.where(pos >= STARTS[3] + 64, pos + 64, pos)
    row, lane = pos >> 7, pos & (LANES - 1)
    out = jnp.full(pos.shape, -1.0, f32)
    for r in range(15):
        value = jnp.broadcast_to(best[r:r + 1, :], pos.shape)
        value = jnp.take_along_axis(value, lane, axis=1, mode="promise_in_bounds")
        out = jnp.where(row == r, value, out)
    out_ref[:CHIPS, :] = out
    out_ref[CHIPS:, :] = out


def pick_kernel(v_ref, code_ref, out_ref):
    c = index_on("c")
    values = jnp.maximum(v_ref[:CHIPS, :], v_ref[CHIPS:, :])
    values = jnp.max(values.reshape(BINS, 4, LANES), axis=1)
    eye = iota((LANES, LANES), 0) == iota((LANES, LANES), 1)
    code = jnp.max(jnp.where(iota((8, ROWS), 0) == c, code_ref[...], -1), axis=0, keepdims=True)
    code = jnp.max(jnp.where(eye, code.astype(f32), -1.0), axis=1, keepdims=True).astype(i32)
    slot = iota((ROWS, LANES), 1)
    best = jnp.full((ROWS, LANES), -1.0, f32)
    for b in range(BINS):
        best = jnp.where(slot + b * LANES == code, values[b:b + 1], best)
    best = jnp.max(best, axis=1, keepdims=True)
    out_ref[...] = jnp.max(jnp.where(eye, best, -1.0), axis=0, keepdims=True)


def gather_groups(embeddings, cluster_ids):
    split = ("z", "y", "c")
    rows = embeddings.shape[0]
    groups = lax.axis_size("x")
    cap = 2 * rows // groups
    slots = groups * cap
    owner_of = cluster_ids % groups
    onehot = (owner_of[:, None] == jnp.arange(groups, dtype=i32)[None, :]).astype(i32)
    before = jnp.cumsum(onehot, axis=0) - onehot
    rank = jnp.sum(before * onehot, axis=1)
    place = owner_of * cap + rank
    picked = place[None, :] == jnp.arange(slots, dtype=i32)[:, None]
    filled = jnp.any(picked, axis=1)
    source = jnp.sum(jnp.where(picked, jnp.arange(rows, dtype=i32)[None, :], 0), axis=1)
    out_labels = jnp.where(filled, cluster_ids[source], -1)
    squares = jnp.sum(embeddings * embeddings, axis=1, keepdims=True)
    local_unit = (embeddings * lax.rsqrt(squares + 1e-06)).astype(bf16)
    outgoing_unit = jnp.where(filled[:, None], local_unit[source], jnp.zeros((), bf16))
    unit = lax.all_to_all(outgoing_unit, "x", split_axis=0, concat_axis=0, tiled=True)
    labels = lax.all_to_all(out_labels, "x", split_axis=0, concat_axis=0, tiled=True)
    members = lax.axis_size(split)

    def everywhere(v):
        copies = jnp.broadcast_to(v[None], (members,) + v.shape).reshape((members * slots,) + v.shape[1:])
        return lax.all_to_all(copies, split, split_axis=0, concat_axis=0, tiled=True)

    def add_slice(i, scores):
        part = lax.dynamic_slice_in_dim(unit, i * WIDTH, WIDTH, 1)
        return scores + dot_last(part, everywhere(part))

    scores = lax.fori_loop(0, embeddings.shape[1] // WIDTH, add_slice, jnp.zeros((slots, members * slots), f32))
    all_labels = everywhere(labels)
    own = lax.axis_index(split) * slots + jnp.arange(slots, dtype=i32)
    mask = (
        (labels[:, None] == all_labels[None, :])
        & (labels[:, None] >= 0)
        & (own[:, None] != jnp.arange(members * slots, dtype=i32)[None, :])
    )
    scores = jnp.where(mask, scores, -1.0)
    best = jnp.maximum(-1.0, jnp.max(scores, axis=1))
    returned = lax.all_to_all(best, "x", split_axis=0, concat_axis=0, tiled=True)
    return returned[place]


def route(block, units, embeddings, cluster_ids):
    shape = jax.ShapeDtypeStruct
    half = shape((ROWS + LABEL_ROWS, HALF_WIDTH), bf16)
    ids = cluster_ids.reshape(1, ROWS)
    send, scale = pl.pallas_call(
        unit_send_kernel, out_shape=(half, shape((ROWS, LANES), f32)),
        in_specs=[WHOLE, WHOLE], out_specs=(WHOLE, WHOLE), compiler_params=params(12), name="unit_send",
    )(embeddings, ids)
    got = lax.ppermute(send, "c", [(0, 1), (1, 0)])
    keep = pl.pallas_call(
        unit_keep_kernel, out_shape=half,
        in_specs=[pl.BlockSpec(memory_space=pl.ANY), WHOLE, WHOLE], out_specs=WHOLE,
        scratch_shapes=[pltpu.VMEM((ROWS, HALF_WIDTH), f32), pltpu.SemaphoreType.DMA],
        compiler_params=params(8), name="unit_keep",
    )(embeddings, ids, scale)
    packed, code = pl.pallas_call(
        functools.partial(pack_kernel, block),
        out_shape=(shape((CHIPS, block, WIDTH), bf16), shape((8, ROWS), i32)),
        in_specs=[WHOLE, WHOLE], out_specs=(WHOLE, WHOLE), compiler_params=params(20), name="pack",
    )(keep, got)
    packed = lax.all_to_all(packed, ("x", "z", "y"), 0, 0, tiled=True)
    table = shape((CHIPS, LANES), i32)
    guests, line, key, pos, meta = pl.pallas_call(
        functools.partial(names_kernel, block),
        out_shape=(shape((GUESTS, WIDTH), bf16), shape((8, CHIPS * block), i32), table, table, shape((8, LANES), i32)),
        in_specs=[WHOLE], out_specs=(WHOLE,) * 5, compiler_params=params(12), name="names",
    )(packed)
    brought = lax.ppermute(guests, "z", [(i, (i + 3) % 4) for i in range(4)])
    share = shape((SHARE_ROWS, WIDTH), bf16)
    send, mine = pl.pallas_call(
        functools.partial(sort_kernel, block), out_shape=(share, share),
        in_specs=[WHOLE] * 2, out_specs=(WHOLE,) * 2, compiler_params=params(24), name="sort",
    )(packed, line)
    brought, mine, send = lax.optimization_barrier((brought, mine, send))
    other = lax.ppermute(send, "c", [(0, 1), (1, 0)])
    swapped = lax.ppermute(brought, "c", [(0, 1), (1, 0)])
    raw, far = pl.pallas_call(
        own_kernel, out_shape=(shape((RAW_ROWS, LANES), f32), shape((8, GUESTS), i32)),
        in_specs=[WHOLE] * 4, out_specs=(WHOLE,) * 2,
        scratch_shapes=[pltpu.VMEM((SHARE_ROWS, WIDTH), bf16)],
        compiler_params=params(16), name="own",
        cost_estimate=pl.CostEstimate(flops=2 * RAW_ROWS * LANES * WIDTH, bytes_accessed=4 << 20, transcendentals=0),
    )(mine, brought, key, pos)
    partial = pl.pallas_call(
        functools.partial(gram_kernel, units),
        out_shape=[shape((units * UNIT, LANES), f32)] * 4,
        in_specs=[WHOLE] * 5, out_specs=[WHOLE] * 4,
        scratch_shapes=[pltpu.VMEM((4 * units * UNIT + CAPS[0], LANES), f32), pltpu.VMEM((SHARE_ROWS, WIDTH), bf16)],
        compiler_params=params(16), name="gram",
    )(meta, other, swapped, far, raw)
    arrived = [partial[0]] + [
        lax.ppermute(partial[s], "y", [(i, (i + s) % 4) for i in range(4)]) for s in (2, 3, 1)
    ]
    over, table = pl.pallas_call(
        functools.partial(fit_kernel, block, units),
        out_shape=(shape((8, LANES), i32), shape((4 * units, LANES), i32)),
        in_specs=[WHOLE, WHOLE], out_specs=(WHOLE, WHOLE), compiler_params=params(8), name="fit",
    )(packed, meta)
    arrived, fits, table = lax.optimization_barrier((arrived, over[0, 0] == 0, table))
    best = pl.pallas_call(
        functools.partial(max_kernel, units),
        out_shape=shape((2 * CHIPS, LANES), f32),
        in_specs=[WHOLE] * 6, out_specs=WHOLE, compiler_params=params(8), name="maxima",
    )(table, *arrived, pos)
    back = lax.all_to_all(best.reshape(2 * CHIPS, 1, LANES), ("c", "x", "z", "y"), 0, 0, tiled=True)
    back, fits = lax.optimization_barrier((back, fits))
    best = pl.pallas_call(
        pick_kernel,
        out_shape=shape((1, ROWS), f32),
        in_specs=[WHOLE, WHOLE], out_specs=WHOLE, compiler_params=params(8), name="pick",
    )(back.reshape(2 * CHIPS, LANES), code).reshape(ROWS)
    return best, fits


def on_device(embeddings, cluster_ids, tries=TRIES):
    if not tries:
        return gather_groups(embeddings, cluster_ids)
    best, fits = route(*tries[0], embeddings, cluster_ids)
    return lax.cond(
        fits,
        lambda best, embeddings, cluster_ids: best,
        lambda best, embeddings, cluster_ids: on_device(embeddings, cluster_ids, tries[1:]),
        best, embeddings, cluster_ids,
    )


def solution(mesh):
    axes = ("x", "z", "y", "c")
    grid = Mesh(mesh.devices.reshape(4, 4, 4, 2), axes)
    return jax.shard_map(
        on_device, mesh=grid, in_specs=(P(axes, None), P(axes)), out_specs=P(axes), check_vma=False
    )
```

```python
import functools

import jax
import jax.numpy as jnp
from jax import lax
from jax.experimental import pallas as pl
from jax.experimental.pallas import tpu as pltpu
from jax.sharding import Mesh, PartitionSpec as P

ROWS = 128
HALF_WIDTH = 2048
WIDTH = 512
LABEL_ROWS = 16
BINS = 16
CHIPS = 64
TRIES = ((24, 11), (32, 16))
GROUP = 32
GUESTS = 64
GUEST = 4096
LANES = 128
CAPS = (704, 512, 320, 192)
STARTS = (0, 704, 1216, 1536)
UNIT = 32
SHARES = (
    ((0, 0), (0, 256), (2, 0), (2, 128), (2, 256), (3, 0)),
    ((0, 128), (0, 384), (0, 512), (0, 640), (1, 0), (1, 128), (1, 256), (1, 384), (3, 128)),
)
BASES = ({0: 0, 2: 704, 3: 1024}, {0: -128, 1: 576, 3: 960})
SHARE_ROWS = 1216
SEGMENTS = (
    (0, 128, 0, None), (128, 576, 128, 0), (704, 256, None, 576), (960, 256, None, 832),
    (1216, 320, 704, None), (1536, 128, 1024, None), (1664, 64, 1152, 1088),
)
f32, bf16, i32 = jnp.float32, jnp.bfloat16, jnp.int32
WHOLE = pl.BlockSpec(memory_space=pltpu.VMEM)


def params(mib):
    return pltpu.CompilerParams(vmem_limit_bytes=mib * 1024 * 1024)


def index_on(axis):
    return lax.axis_index(axis)


def iota(shape, dim):
    return lax.broadcasted_iota(i32, shape, dim)


def dot_last(a, b):
    return lax.dot_general(a, b, (((1,), (1,)), ((), ())), preferred_element_type=f32)


def dot(a, b):
    return lax.dot_general(a, b, (((1,), (0,)), ((), ())), preferred_element_type=f32)


def as_bf16(mask):
    return jnp.where(mask, 1.0, 0.0).astype(bf16)


def bin_of(labels):
    rank, residue = labels >> 2, labels & 3
    row, col = rank >> 2, rank & 3
    col = jnp.where((row & 1) == 1, 3 - col, col)
    return 4 * col + ((row - residue) & 3)


def label_rows(ids_ref):
    ids = jnp.concatenate([ids_ref[...].astype(f32), jnp.zeros((1, HALF_WIDTH - ROWS), f32)], axis=1)
    return jnp.broadcast_to(ids, (LABEL_ROWS, HALF_WIDTH)).astype(bf16)


def half_of(core):
    return pl.ds(pl.multiple_of(core * HALF_WIDTH, HALF_WIDTH), HALF_WIDTH)


def unit_send_kernel(x_ref, ids_ref, out_ref, scale_ref):
    x = x_ref[...]
    scale = lax.rsqrt(jnp.sum(x * x, axis=1, keepdims=True) + 1e-06)
    scale_ref[...] = jnp.broadcast_to(scale, scale_ref.shape)
    out_ref[:ROWS, :] = (x_ref[:, half_of(1 - index_on("c"))] * scale).astype(bf16)
    out_ref[ROWS:, :] = label_rows(ids_ref)


def unit_keep_kernel(x_ref, ids_ref, scale_ref, out_ref, half_ref, sem):
    copy = pltpu.make_async_copy(x_ref.at[:, half_of(index_on("c"))], half_ref, sem)
    copy.start()
    out_ref[ROWS:, :] = label_rows(ids_ref)
    copy.wait()
    out_ref[:ROWS, :] = (half_ref[...] * scale_ref[:, :1]).astype(bf16)


def passed_on(over, before):
    once = before(over, 1)
    twice = before(over, 2)
    return jnp.maximum(jnp.maximum(over, 0), jnp.maximum(over + once, over + once + twice))


def pack_kernel(block, keep_ref, got_ref, out_ref, code_ref):
    first = index_on("c") == 0
    kept = jnp.max(keep_ref[ROWS:, :ROWS].astype(f32), axis=0, keepdims=True)
    got = jnp.max(got_ref[ROWS:, :ROWS].astype(f32), axis=0, keepdims=True)
    labels = jnp.concatenate([jnp.where(first, kept, got), jnp.where(first, got, kept)], axis=0).astype(i32)
    bins = bin_of(labels)
    upper = as_bf16(iota((ROWS, ROWS), 0) < iota((ROWS, ROWS), 1))

    def ranks_within(masks):
        member = jnp.concatenate([jnp.where(mask, 1.0, 0.0) for mask in masks], axis=0)
        row, col = iota((member.shape[0],) * 2, 0), iota((member.shape[0],) * 2, 1)
        earlier = dot(as_bf16(((row >> 1) == (col >> 1)) & (col < row)), member.astype(bf16))
        ranks = member * (dot(member.astype(bf16), upper) + jnp.sum(earlier, axis=1, keepdims=True))
        rank = sum(ranks[2 * b:2 * b + 2] for b in range(len(masks)))
        return rank.astype(i32), jnp.sum(member, axis=1, keepdims=True)

    rank, sizes = ranks_within([bins == b for b in range(BINS)])
    quad, line = bins >> 2, bins & 3
    taken = []
    for at in range(4):
        size = jnp.zeros(labels.shape, f32)
        for b in range(at, BINS, 4):
            size = jnp.where(quad == b >> 2, sizes[2 * b:2 * b + 1] + sizes[2 * b + 1:2 * b + 2], size)
        taken.append(size.astype(i32) - (block - 1))
    stays = []
    for at in range(4):
        moved = passed_on(taken[at], lambda _, back: taken[(at - back) & 3])
        stays.append(taken[at] + (block - 1) - moved)

    def of_line(values, which):
        out = values[0]
        for at in range(1, 4):
            out = jnp.where(which == at, values[at], out)
        return out

    stay = of_line(stays, line)
    to_line = jnp.where(rank < stay, line, (line + 1) & 3)
    to_slot = jnp.where(rank < stay, rank, of_line(stays, to_line) + rank - stay)
    placed = to_slot < (block - 1)
    lane = jnp.where(placed, to_line * GROUP + to_slot, -1)
    place = jnp.where(placed, (quad * 4 + to_line) * block + to_slot, -1)
    code_ref[...] = jnp.concatenate([jnp.where(placed, bins * LANES + lane, -1)] * 4, axis=0)
    docs = 2 * ROWS
    flat = lambda v: jnp.concatenate([v[:1], v[1:]], axis=1)
    label_row = flat(labels)
    counts = dot_last(jnp.ones((8, docs), bf16), as_bf16(iota((LANES, docs), 0) == label_row))[:1]
    named = jnp.where(iota((8, docs), 0) == flat(quad), (label_row + 1).astype(f32), 0.0).astype(bf16)
    names = dot_last(named, as_bf16(iota((LANES, docs), 0) == flat(lane)))
    own = jnp.where(first, place[:1], place[1:])
    other = jnp.where(first, place[1:], place[:1])
    onehot = as_bf16(iota((BINS * block, docs), 0) == jnp.concatenate([own, other], axis=1))
    is_last = iota((block, WIDTH), 0) == (block - 1)
    for y in range(4):
        columns = slice(y * WIDTH, (y + 1) * WIDTH)
        x = jnp.concatenate([keep_ref[:ROWS, columns], got_ref[:ROWS, columns]], axis=0)
        packed = dot(onehot, x)
        for b in range(BINS):
            extra = jnp.concatenate([names[b // 4:b // 4 + 1], counts, jnp.zeros((1, 2 * LANES), f32)], axis=1)
            out_ref[4 * b + y] = jnp.where(is_last, extra, packed[b * block:(b + 1) * block]).astype(bf16)


def labels_of(block, x_ref):
    tail = x_ref[:, block - 8:, :2 * LANES].astype(f32)
    tail = jnp.max(jnp.where(iota(tail.shape, 1) == 7, tail, 0.0), axis=1)
    return tail[:, :LANES].astype(i32) - 1, tail[:, LANES:].astype(bf16)


def counts_of(chip_counts):
    row, col = iota((LANES, LANES), 0), iota((LANES, LANES), 1)
    in_bin = (bin_of(row) == col) & (row < 4 * BINS)
    counts = [dot(chip_counts, as_bf16(in_bin & ((row & 3) == r))) for r in range(4)]
    return counts, [jnp.sum(v, axis=0, keepdims=True) for v in counts]


def in_order(sizes):
    a, b = jnp.maximum(sizes[0], sizes[1]), jnp.minimum(sizes[0], sizes[1])
    c, d = jnp.maximum(sizes[2], sizes[3]), jnp.minimum(sizes[2], sizes[3])
    first, e = jnp.maximum(a, c), jnp.minimum(a, c)
    g, fourth = jnp.maximum(b, d), jnp.minimum(b, d)
    return first, jnp.maximum(e, g), jnp.minimum(e, g), fourth


def names_kernel(block, x_ref, guest_ref, line_ref, key_ref, pos_ref, meta_ref):
    z = index_on("z")
    labels, _ = labels_of(block, x_ref)
    row, col = iota((LANES, LANES), 0), iota((LANES, LANES), 1)
    lane = iota(labels.shape, 1)
    group = lane >> 5
    valid = labels >= 0
    home = bin_of(labels) & 3
    at_home = valid & (home == z)
    upper = as_bf16(row < col)
    lower = as_bf16(iota((CHIPS, CHIPS), 1) < iota((CHIPS, CHIPS), 0))
    members, n = [at_home & ((labels & 3) == r) for r in range(4)], []
    for member in members:
        size = jnp.sum(jnp.where(member, 1.0, 0.0), axis=0, keepdims=True)
        n.append(jnp.sum(size, axis=1, keepdims=True))
    wide = lambda v: jnp.broadcast_to(v, (1, LANES))
    meta_ref[...] = jnp.concatenate([wide(v) for v in in_order(n)] * 2, axis=0).astype(i32)
    pos = jnp.full(labels.shape, -1.0, f32)
    for r, member in enumerate(members):
        place = sum(
            jnp.where((n[q] > n[r]) | ((n[q] == n[r]) & (q < r)), 1.0, 0.0) for q in range(4) if q != r
        )
        start = jnp.where(
            place < 0.5, float(STARTS[0]),
            jnp.where(place < 1.5, float(STARTS[1]), jnp.where(place < 2.5, float(STARTS[2]), float(STARTS[3]))),
        )
        member16 = as_bf16(member)
        rank = dot(member16, upper) + jnp.sum(dot(lower, member16), axis=1, keepdims=True)
        pos = jnp.where(member, start + rank, pos)
    pos = pos.astype(i32)
    pos_ref[...] = pos
    guest = valid & (home != group)
    guest16 = as_bf16(guest)
    same = (row >> 5) == (col >> 5)
    turn = dot(guest16, as_bf16(same & (row < col))) + dot(dot(lower, guest16).astype(bf16), as_bf16(same))
    turn = turn.astype(i32)
    away = at_home & (group != z) & (turn < GUESTS)
    key_ref[...] = jnp.where(away, turn, -1)
    per, groups = 16, CHIPS // 16
    value = jnp.where(group == z, jnp.where(guest, GUEST + turn, pos + 1), 0).astype(f32)
    value = pltpu.roll(value, lax.rem(LANES - GROUP * z, LANES), 1)
    value = jnp.where(lane < block, value, 0.0)
    lined = jnp.zeros((8, per * block), f32)
    for t in range(per):
        rows = jnp.concatenate([value[per * g + t:per * g + t + 1] for g in range(groups)] * 2, axis=0)
        rows = jnp.concatenate([rows, jnp.zeros((8, per * block - LANES), f32)], axis=1)
        lined = lined + (pltpu.roll(rows, t * block, 1) if t else rows)
    slots = jnp.concatenate([lined[g:g + 1] for g in range(groups)], axis=1).astype(i32)
    line_ref[...] = jnp.broadcast_to(slots, line_ref.shape)
    onehot = as_bf16(iota((GUESTS, CHIPS * block), 0) + GUEST == slots)
    guest_ref[...] = dot(onehot, x_ref[...].reshape(CHIPS * block, WIDTH)).astype(bf16)


def sorted_rows(segment, slots, x):
    onehot = as_bf16(iota((segment[1], x.shape[0]), 0) + (segment[0] + 1) == slots)
    return dot(onehot, x).astype(bf16)


def sort_kernel(block, x_ref, line_ref, send_ref, mine_ref):
    x = x_ref[...].reshape(CHIPS * block, WIDTH)
    slots = line_ref[:1, :]
    for core in range(2):
        @pl.when(index_on("c") == core)
        def _():
            for segment in SEGMENTS:
                rows = sorted_rows(segment, slots, x)
                for out_ref, at in ((mine_ref, segment[2 + core]), (send_ref, segment[2 + 1 - core])):
                    if at is not None:
                        out_ref[at:at + segment[1], :] = rows


def fit_kernel(block, units, x_ref, meta_ref, over_ref, table_ref):
    _, chip_counts = labels_of(block, x_ref)
    counts, sizes = counts_of(chip_counts)
    ordered = in_order(sizes)
    over = jnp.zeros((1, LANES), f32)
    for size, cap in zip(ordered, CAPS):
        over = jnp.maximum(over, jnp.where(size > cap, 1.0, 0.0))
    for share in SHARES:
        length = 0.0
        for q, first in share:
            rows = jnp.maximum(jnp.floor((ordered[q] + (UNIT - 1.0)) * (1 / UNIT)) - first // UNIT, 0.0)
            length = length + jnp.where(rows >= 3.0, rows - 1.0, rows)
        over = jnp.maximum(over, jnp.where(length > 4 * units, 1.0, 0.0))
    taken = counts[0] + counts[1] + counts[2] + counts[3]
    lane = iota(taken.shape, 1) & 3
    before = lambda v, back: jnp.where(lane >= back, pltpu.roll(v, back, 1), pltpu.roll(v, LANES - 4 + back, 1))
    extra = taken - (block - 1)
    moved = passed_on(extra, before)
    held = jnp.sum(moved, axis=0, keepdims=True)
    over = jnp.maximum(over, jnp.where(held > GUESTS, 1.0, 0.0))
    full = extra + before(extra, 1) + before(extra, 2) + before(extra, 3) > 0
    full = jnp.where(full | (moved > block - 1), 1.0, 0.0)
    over = jnp.maximum(over, jnp.max(full, axis=0, keepdims=True))
    over_ref[...] = jnp.broadcast_to(jnp.max(over, axis=1, keepdims=True), over_ref.shape).astype(i32)
    y, c = index_on("y"), index_on("c")
    blocks, sizes = [], [size_of(meta_ref, q) for q in range(4)]
    for core, share in enumerate(SHARES):
        at = jnp.zeros((), i32)
        for q, first in share:
            length = length_of(sizes[q], first)
            blocks.append((jnp.where((c == core) & (length > 0), at, 4 * units), FIRST_ROW[q] + first // LANES, at))
            at = at + length
    for t in range(units):
        index = y * units + t
        col, start = jnp.asarray(15, i32), jnp.asarray(0, i32)
        for block_start, block_col, block_at in blocks:
            inside = index >= block_start
            col, start = jnp.where(inside, block_col, col), jnp.where(inside, block_at, start)
        turn = index - start
        unit = 4 * col + jnp.where(turn == 0, 2, jnp.where(turn == 1, 1, turn + 1))
        beside = jnp.where(turn == 0, 3 * UNIT, LANES)
        for entry, value in enumerate((unit >> 2, (unit & 3) * UNIT, beside, col)):
            table_ref[4 * t + entry:4 * t + entry + 1, :] = jnp.full((1, LANES), value, i32)


def add_guests(core, base_ref, guest_ref, far_ref, out_ref):
    guests, far = guest_ref[...], far_ref[:1, :]
    for segment in SEGMENTS:
        at, rows = segment[2 + core], segment[1]
        if at is not None:
            out_ref[at:at + rows, :] = base_ref[at:at + rows, :] + sorted_rows(segment, far, guests)


def blocks_of(core):
    for q, first in SHARES[core]:
        at = BASES[core][q] + first
        yield q, first, pl.ds(at, CAPS[q] - first), pl.ds(at, LANES)


RAW_ROWS = max(sum(CAPS[q] - first for q, first in share) for share in SHARES)


def own_kernel(x_ref, guest_ref, key_ref, pos_ref, raw_ref, far_ref, rows_ref):
    total = jnp.zeros((8, GUESTS), f32)
    step = 16
    for first in range(0, CHIPS, step):
        flat = lambda ref: jnp.concatenate([ref[s:s + 1, :] for s in range(first, first + step)], axis=1)
        places = flat(pos_ref) + 1
        parts = jnp.where(iota((8, step * LANES), 0) == 0, places >> 5, places & 31).astype(f32).astype(bf16)
        total = total + dot_last(parts, as_bf16(iota((GUESTS, step * LANES), 0) == flat(key_ref)))
    far_ref[...] = jnp.broadcast_to((32.0 * total[:1] + total[1:2]).astype(i32), far_ref.shape)
    for core in range(2):
        @pl.when(index_on("c") == core)
        def _():
            add_guests(core, x_ref, guest_ref, far_ref, rows_ref)
            at = 0
            for q, first, left, right in blocks_of(core):
                rows = CAPS[q] - first
                raw_ref[at:at + rows, :] = dot_last(rows_ref[left, :], rows_ref[right, :])
                at += rows


def size_of(meta_ref, q):
    return jnp.max(meta_ref[q:q + 1, :].astype(f32)).astype(i32)


def length_of(size, first):
    units = jnp.maximum(((size + UNIT - 1) >> 5) - first // UNIT, 0)
    return jnp.where(units >= 3, units - 1, units)


def folded(score):
    away = jnp.full((UNIT, LANES), -4.0, f32) if score.shape[0] < LANES else score[2 * UNIT:3 * UNIT]
    both = jnp.where(iota(away.shape, 1) < 3 * UNIT, away, pltpu.roll(score[:UNIT], 3 * UNIT, 1))
    rest = [score[3 * UNIT:]] if score.shape[0] > 3 * UNIT else []
    return jnp.concatenate([both, score[UNIT:2 * UNIT]] + rest, axis=0)


def gram_kernel(units, meta_ref, x_ref, guest_ref, far_ref, raw_ref, out0, out1, out2, out3, part_ref, rows_ref):
    y, c = index_on("y"), index_on("c")
    part_ref[...] = jnp.full(part_ref.shape, -4.0, f32)
    for core in range(2):
        @pl.when(c == core)
        def _():
            add_guests(core, x_ref, guest_ref, far_ref, rows_ref)
            at, to = 0, jnp.zeros((), i32)
            for q, first, left, right in blocks_of(core):
                rows = CAPS[q] - first
                score = raw_ref[at:at + rows, :] + dot_last(rows_ref[left, :], rows_ref[right, :])
                at += rows
                size = size_of(meta_ref, q)
                i, j = iota(score.shape, 0), iota(score.shape, 1)
                keep = (i < size - first) & (j < size - first) & (i != j)
                score = folded(jnp.where(keep, score, -4.0))
                part_ref[pl.ds(pl.multiple_of(to, UNIT), score.shape[0]), :] = score
                to = jnp.minimum(to + UNIT * length_of(size, first), 4 * units * UNIT)
    chunk = units * UNIT
    for shift, out in enumerate((out0, out1, out2, out3)):
        out[...] = part_ref[pl.ds(pl.multiple_of(lax.rem(y + shift, 4) * chunk, UNIT), chunk), :]


FIRST_ROW = (0, 6, 10, 13)


def max_kernel(units, table_ref, p0, p1, p2, p3, pos_ref, out_ref):
    best = jnp.full((16, LANES), -1.0, f32)
    sub, lane, row = iota((UNIT, LANES), 0), iota((UNIT, LANES), 1), iota((16, LANES), 0)
    for t in range(units):
        at = slice(t * UNIT, (t + 1) * UNIT)
        block = (p0[at, :] + p1[at, :]) + (p2[at, :] + p3[at, :])
        unit_row, offset, beside, col = (table_ref[4 * t + entry:4 * t + entry + 1, :] for entry in range(4))
        one, two = jnp.where(lane < beside, block, -4.0), jnp.where(lane < beside, -4.0, block)
        along = jnp.max(one, axis=1, keepdims=True)
        along = jnp.max(jnp.where(sub + offset == lane, along, -1.0), axis=0, keepdims=True)
        best = jnp.maximum(best, jnp.where(row == unit_row, along, -1.0))
        along = jnp.max(two, axis=1, keepdims=True)
        two = jnp.maximum(jnp.where(sub == lane, along, -1.0), pltpu.roll(two, UNIT, 1))
        down = jnp.max(jnp.maximum(one, two), axis=0, keepdims=True)
        best = jnp.maximum(best, jnp.where(row == col, down, -1.0))
    pos = pos_ref[...]
    pos = jnp.where(pos >= STARTS[1], pos + 64, pos)
    pos = jnp.where(pos >= STARTS[3] + 64, pos + 64, pos)
    row, lane = pos >> 7, pos & (LANES - 1)
    out = jnp.full(pos.shape, -1.0, f32)
    for r in range(15):
        value = jnp.broadcast_to(best[r:r + 1, :], pos.shape)
        value = jnp.take_along_axis(value, lane, axis=1, mode="promise_in_bounds")
        out = jnp.where(row == r, value, out)
    out_ref[:CHIPS, :] = out
    out_ref[CHIPS:, :] = out


def pick_kernel(v_ref, code_ref, out_ref):
    values = jnp.maximum(v_ref[:CHIPS, :], v_ref[CHIPS:, :])
    values = jnp.max(values.reshape(BINS, 4, LANES), axis=1)
    code = jnp.max(jnp.where(iota((8, ROWS), 0) == index_on("c"), code_ref[...], -1), axis=0, keepdims=True)
    code = jnp.broadcast_to(code, (8, ROWS))
    row, lane = code >> 7, code & (LANES - 1)
    best = jnp.full((8, ROWS), -1.0, f32)
    for b in range(BINS):
        value = jnp.broadcast_to(values[b:b + 1], (8, ROWS))
        best = jnp.where(row == b, jnp.take_along_axis(value, lane, axis=1, mode="promise_in_bounds"), best)
    out_ref[...] = best[:1]


def gather_groups(embeddings, cluster_ids):
    split = ("z", "y", "c")
    rows = embeddings.shape[0]
    groups = lax.axis_size("x")
    cap = 2 * rows // groups
    slots = groups * cap
    owner_of = cluster_ids % groups
    onehot = (owner_of[:, None] == jnp.arange(groups, dtype=i32)[None, :]).astype(i32)
    before = jnp.cumsum(onehot, axis=0) - onehot
    rank = jnp.sum(before * onehot, axis=1)
    place = owner_of * cap + rank
    picked = place[None, :] == jnp.arange(slots, dtype=i32)[:, None]
    filled = jnp.any(picked, axis=1)
    source = jnp.sum(jnp.where(picked, jnp.arange(rows, dtype=i32)[None, :], 0), axis=1)
    out_labels = jnp.where(filled, cluster_ids[source], -1)
    squares = jnp.sum(embeddings * embeddings, axis=1, keepdims=True)
    local_unit = (embeddings * lax.rsqrt(squares + 1e-06)).astype(bf16)
    outgoing_unit = jnp.where(filled[:, None], local_unit[source], jnp.zeros((), bf16))
    unit = lax.all_to_all(outgoing_unit, "x", split_axis=0, concat_axis=0, tiled=True)
    labels = lax.all_to_all(out_labels, "x", split_axis=0, concat_axis=0, tiled=True)
    members = lax.axis_size(split)

    def everywhere(v):
        copies = jnp.broadcast_to(v[None], (members,) + v.shape).reshape((members * slots,) + v.shape[1:])
        return lax.all_to_all(copies, split, split_axis=0, concat_axis=0, tiled=True)

    def add_slice(i, scores):
        part = lax.dynamic_slice_in_dim(unit, i * WIDTH, WIDTH, 1)
        return scores + dot_last(part, everywhere(part))

    scores = lax.fori_loop(0, embeddings.shape[1] // WIDTH, add_slice, jnp.zeros((slots, members * slots), f32))
    all_labels = everywhere(labels)
    own = lax.axis_index(split) * slots + jnp.arange(slots, dtype=i32)
    mask = (
        (labels[:, None] == all_labels[None, :])
        & (labels[:, None] >= 0)
        & (own[:, None] != jnp.arange(members * slots, dtype=i32)[None, :])
    )
    scores = jnp.where(mask, scores, -1.0)
    best = jnp.maximum(-1.0, jnp.max(scores, axis=1))
    returned = lax.all_to_all(best, "x", split_axis=0, concat_axis=0, tiled=True)
    return returned[place]


def route(block, units, embeddings, cluster_ids):
    shape = jax.ShapeDtypeStruct
    half = shape((ROWS + LABEL_ROWS, HALF_WIDTH), bf16)
    ids = cluster_ids.reshape(1, ROWS)
    send, scale = pl.pallas_call(
        unit_send_kernel, out_shape=(half, shape((ROWS, LANES), f32)),
        in_specs=[WHOLE, WHOLE], out_specs=(WHOLE, WHOLE), compiler_params=params(12), name="unit_send",
    )(embeddings, ids)
    got = lax.ppermute(send, "c", [(0, 1), (1, 0)])
    keep = pl.pallas_call(
        unit_keep_kernel, out_shape=half,
        in_specs=[pl.BlockSpec(memory_space=pl.ANY), WHOLE, WHOLE], out_specs=WHOLE,
        scratch_shapes=[pltpu.VMEM((ROWS, HALF_WIDTH), f32), pltpu.SemaphoreType.DMA],
        compiler_params=params(8), name="unit_keep",
    )(embeddings, ids, scale)
    packed, code = pl.pallas_call(
        functools.partial(pack_kernel, block),
        out_shape=(shape((CHIPS, block, WIDTH), bf16), shape((8, ROWS), i32)),
        in_specs=[WHOLE, WHOLE], out_specs=(WHOLE, WHOLE), compiler_params=params(20), name="pack",
    )(keep, got)
    packed = lax.all_to_all(packed, ("x", "z", "y"), 0, 0, tiled=True)
    table = shape((CHIPS, LANES), i32)
    guests, line, key, pos, meta = pl.pallas_call(
        functools.partial(names_kernel, block),
        out_shape=(shape((GUESTS, WIDTH), bf16), shape((8, CHIPS * block), i32), table, table, shape((8, LANES), i32)),
        in_specs=[WHOLE], out_specs=(WHOLE,) * 5, compiler_params=params(12), name="names",
    )(packed)
    brought = lax.ppermute(guests, "z", [(i, (i + 3) % 4) for i in range(4)])
    share = shape((SHARE_ROWS, WIDTH), bf16)
    send, mine = pl.pallas_call(
        functools.partial(sort_kernel, block), out_shape=(share, share),
        in_specs=[WHOLE] * 2, out_specs=(WHOLE,) * 2, compiler_params=params(24), name="sort",
    )(packed, line)
    brought, mine, send = lax.optimization_barrier((brought, mine, send))
    other = lax.ppermute(send, "c", [(0, 1), (1, 0)])
    swapped = lax.ppermute(brought, "c", [(0, 1), (1, 0)])
    raw, far = pl.pallas_call(
        own_kernel, out_shape=(shape((RAW_ROWS, LANES), f32), shape((8, GUESTS), i32)),
        in_specs=[WHOLE] * 4, out_specs=(WHOLE,) * 2,
        scratch_shapes=[pltpu.VMEM((SHARE_ROWS, WIDTH), bf16)],
        compiler_params=params(16), name="own",
        cost_estimate=pl.CostEstimate(flops=2 * RAW_ROWS * LANES * WIDTH, bytes_accessed=4 << 20, transcendentals=0),
    )(mine, brought, key, pos)
    partial = pl.pallas_call(
        functools.partial(gram_kernel, units),
        out_shape=[shape((units * UNIT, LANES), f32)] * 4,
        in_specs=[WHOLE] * 5, out_specs=[WHOLE] * 4,
        scratch_shapes=[pltpu.VMEM((4 * units * UNIT + CAPS[0], LANES), f32), pltpu.VMEM((SHARE_ROWS, WIDTH), bf16)],
        compiler_params=params(16), name="gram",
    )(meta, other, swapped, far, raw)
    arrived = [partial[0]] + [
        lax.ppermute(partial[s], "y", [(i, (i + s) % 4) for i in range(4)]) for s in (2, 3, 1)
    ]
    over, table = pl.pallas_call(
        functools.partial(fit_kernel, block, units),
        out_shape=(shape((8, LANES), i32), shape((4 * units, LANES), i32)),
        in_specs=[WHOLE, WHOLE], out_specs=(WHOLE, WHOLE), compiler_params=params(8), name="fit",
    )(packed, meta)
    arrived, fits, table = lax.optimization_barrier((arrived, over[0, 0] == 0, table))
    best = pl.pallas_call(
        functools.partial(max_kernel, units),
        out_shape=shape((2 * CHIPS, LANES), f32),
        in_specs=[WHOLE] * 6, out_specs=WHOLE, compiler_params=params(8), name="maxima",
    )(table, *arrived, pos)
    back = lax.all_to_all(best.reshape(2 * CHIPS, 1, LANES), ("c", "x", "z", "y"), 0, 0, tiled=True)
    back, fits = lax.optimization_barrier((back, fits))
    best = pl.pallas_call(
        pick_kernel,
        out_shape=shape((1, ROWS), f32),
        in_specs=[WHOLE, WHOLE], out_specs=WHOLE, compiler_params=params(8), name="pick",
    )(back.reshape(2 * CHIPS, LANES), code).reshape(ROWS)
    return best, fits


def on_device(embeddings, cluster_ids, tries=TRIES):
    if not tries:
        return gather_groups(embeddings, cluster_ids)
    best, fits = route(*tries[0], embeddings, cluster_ids)
    return lax.cond(
        fits,
        lambda best, embeddings, cluster_ids: best,
        lambda best, embeddings, cluster_ids: on_device(embeddings, cluster_ids, tries[1:]),
        best, embeddings, cluster_ids,
    )


def solution(mesh):
    axes = ("x", "z", "y", "c")
    grid = Mesh(mesh.devices.reshape(4, 4, 4, 2), axes)
    return jax.shard_map(
        on_device, mesh=grid, in_specs=(P(axes, None), P(axes)), out_specs=P(axes), check_vma=False
    )
```

```python
import functools

import jax
import jax.numpy as jnp
from jax import lax
from jax.experimental import pallas as pl
from jax.experimental.pallas import tpu as pltpu
from jax.sharding import Mesh, PartitionSpec as P

ROWS = 128
HALF_WIDTH = 2048
WIDTH = 512
LABEL_ROWS = 16
BINS = 16
CHIPS = 64
TRIES = ((24, 11), (32, 16))
GROUP = 32
GUESTS = 64
GUEST = 4096
LANES = 128
CAPS = (704, 512, 320, 192)
STARTS = (0, 704, 1216, 1536)
UNIT = 32
SHARES = (
    ((0, 0), (0, 256), (2, 0), (2, 128), (2, 256), (3, 0)),
    ((0, 128), (0, 384), (0, 512), (0, 640), (1, 0), (1, 128), (1, 256), (1, 384), (3, 128)),
)
BASES = ({0: 0, 2: 704, 3: 1024}, {0: -128, 1: 576, 3: 960})
SHARE_ROWS = 1216
SEGMENTS = (
    (0, 128, 0, None), (128, 576, 128, 0), (704, 256, None, 576), (960, 256, None, 832),
    (1216, 320, 704, None), (1536, 128, 1024, None), (1664, 64, 1152, 1088),
)
f32, bf16, i32 = jnp.float32, jnp.bfloat16, jnp.int32
WHOLE = pl.BlockSpec(memory_space=pltpu.VMEM)


def params(mib):
    return pltpu.CompilerParams(vmem_limit_bytes=mib * 1024 * 1024)


def index_on(axis):
    return lax.axis_index(axis)


def iota(shape, dim):
    return lax.broadcasted_iota(i32, shape, dim)


def dot_last(a, b):
    return lax.dot_general(a, b, (((1,), (1,)), ((), ())), preferred_element_type=f32)


def dot(a, b):
    return lax.dot_general(a, b, (((1,), (0,)), ((), ())), preferred_element_type=f32)


def as_bf16(mask):
    return jnp.where(mask, 1.0, 0.0).astype(bf16)


def bin_of(labels):
    rank, residue = labels >> 2, labels & 3
    row, col = rank >> 2, rank & 3
    col = jnp.where((row & 1) == 1, 3 - col, col)
    return 4 * col + ((row - residue) & 3)


def label_rows(ids_ref):
    ids = jnp.concatenate([ids_ref[...].astype(f32), jnp.zeros((1, HALF_WIDTH - ROWS), f32)], axis=1)
    return jnp.broadcast_to(ids, (LABEL_ROWS, HALF_WIDTH)).astype(bf16)


def half_of(core):
    return pl.ds(pl.multiple_of(core * HALF_WIDTH, HALF_WIDTH), HALF_WIDTH)


def unit_send_kernel(x_ref, ids_ref, out_ref, scale_ref):
    x = x_ref[...]
    scale = lax.rsqrt(jnp.sum(x * x, axis=1, keepdims=True) + 1e-06)
    scale_ref[...] = jnp.broadcast_to(scale, scale_ref.shape)
    out_ref[:ROWS, :] = (x_ref[:, half_of(1 - index_on("c"))] * scale).astype(bf16)
    out_ref[ROWS:, :] = label_rows(ids_ref)


def unit_keep_kernel(x_ref, ids_ref, scale_ref, out_ref, half_ref, sem):
    copy = pltpu.make_async_copy(x_ref.at[:, half_of(index_on("c"))], half_ref, sem)
    copy.start()
    out_ref[ROWS:, :] = label_rows(ids_ref)
    copy.wait()
    out_ref[:ROWS, :] = (half_ref[...] * scale_ref[:, :1]).astype(bf16)


def passed_on(over, before):
    once = before(over, 1)
    twice = before(over, 2)
    return jnp.maximum(jnp.maximum(over, 0), jnp.maximum(over + once, over + once + twice))


def pack_kernel(block, keep_ref, got_ref, out_ref, code_ref):
    first = index_on("c") == 0
    kept = jnp.max(keep_ref[ROWS:, :ROWS].astype(f32), axis=0, keepdims=True)
    got = jnp.max(got_ref[ROWS:, :ROWS].astype(f32), axis=0, keepdims=True)
    labels = jnp.concatenate([jnp.where(first, kept, got), jnp.where(first, got, kept)], axis=0).astype(i32)
    bins = bin_of(labels)
    upper = as_bf16(iota((ROWS, ROWS), 0) < iota((ROWS, ROWS), 1))

    def ranks_within(masks):
        member = jnp.concatenate([jnp.where(mask, 1.0, 0.0) for mask in masks], axis=0)
        row, col = iota((member.shape[0],) * 2, 0), iota((member.shape[0],) * 2, 1)
        earlier = dot(as_bf16(((row >> 1) == (col >> 1)) & (col < row)), member.astype(bf16))
        ranks = member * (dot(member.astype(bf16), upper) + jnp.sum(earlier, axis=1, keepdims=True))
        rank = sum(ranks[2 * b:2 * b + 2] for b in range(len(masks)))
        return rank.astype(i32), jnp.sum(member, axis=1, keepdims=True)

    rank, sizes = ranks_within([bins == b for b in range(BINS)])
    quad, line = bins >> 2, bins & 3
    taken = []
    for at in range(4):
        size = jnp.zeros(labels.shape, f32)
        for b in range(at, BINS, 4):
            size = jnp.where(quad == b >> 2, sizes[2 * b:2 * b + 1] + sizes[2 * b + 1:2 * b + 2], size)
        taken.append(size.astype(i32) - (block - 1))
    stays = []
    for at in range(4):
        moved = passed_on(taken[at], lambda _, back: taken[(at - back) & 3])
        stays.append(taken[at] + (block - 1) - moved)

    def of_line(values, which):
        out = values[0]
        for at in range(1, 4):
            out = jnp.where(which == at, values[at], out)
        return out

    stay = of_line(stays, line)
    to_line = jnp.where(rank < stay, line, (line + 1) & 3)
    to_slot = jnp.where(rank < stay, rank, of_line(stays, to_line) + rank - stay)
    placed = to_slot < (block - 1)
    lane = jnp.where(placed, to_line * GROUP + to_slot, -1)
    place = jnp.where(placed, (quad * 4 + to_line) * block + to_slot, -1)
    code_ref[...] = jnp.concatenate([jnp.where(placed, bins * LANES + lane, -1)] * 4, axis=0)
    docs = 2 * ROWS
    flat = lambda v: jnp.concatenate([v[:1], v[1:]], axis=1)
    label_row = flat(labels)
    counts = dot_last(jnp.ones((8, docs), bf16), as_bf16(iota((LANES, docs), 0) == label_row))[:1]
    named = jnp.where(iota((8, docs), 0) == flat(quad), (label_row + 1).astype(f32), 0.0).astype(bf16)
    names = dot_last(named, as_bf16(iota((LANES, docs), 0) == flat(lane)))
    own = jnp.where(first, place[:1], place[1:])
    other = jnp.where(first, place[1:], place[:1])
    onehot = as_bf16(iota((BINS * block, docs), 0) == jnp.concatenate([own, other], axis=1))
    is_last = iota((block, WIDTH), 0) == (block - 1)
    for y in range(4):
        columns = slice(y * WIDTH, (y + 1) * WIDTH)
        x = jnp.concatenate([keep_ref[:ROWS, columns], got_ref[:ROWS, columns]], axis=0)
        packed = dot(onehot, x)
        for b in range(BINS):
            extra = jnp.concatenate([names[b // 4:b // 4 + 1], counts, jnp.zeros((1, 2 * LANES), f32)], axis=1)
            out_ref[4 * b + y] = jnp.where(is_last, extra, packed[b * block:(b + 1) * block]).astype(bf16)


def labels_of(block, x_ref):
    tail = x_ref[:, block - 8:, :2 * LANES].astype(f32)
    tail = jnp.max(jnp.where(iota(tail.shape, 1) == 7, tail, 0.0), axis=1)
    return tail[:, :LANES].astype(i32) - 1, tail[:, LANES:].astype(bf16)


def counts_of(chip_counts):
    row, col = iota((LANES, LANES), 0), iota((LANES, LANES), 1)
    in_bin = (bin_of(row) == col) & (row < 4 * BINS)
    counts = [dot(chip_counts, as_bf16(in_bin & ((row & 3) == r))) for r in range(4)]
    return counts, [jnp.sum(v, axis=0, keepdims=True) for v in counts]


def in_order(sizes):
    a, b = jnp.maximum(sizes[0], sizes[1]), jnp.minimum(sizes[0], sizes[1])
    c, d = jnp.maximum(sizes[2], sizes[3]), jnp.minimum(sizes[2], sizes[3])
    first, e = jnp.maximum(a, c), jnp.minimum(a, c)
    g, fourth = jnp.maximum(b, d), jnp.minimum(b, d)
    return first, jnp.maximum(e, g), jnp.minimum(e, g), fourth


def names_kernel(block, x_ref, guest_ref, line_ref, key_ref, pos_ref, meta_ref):
    z = index_on("z")
    labels, _ = labels_of(block, x_ref)
    row, col = iota((LANES, LANES), 0), iota((LANES, LANES), 1)
    lane = iota(labels.shape, 1)
    group = lane >> 5
    valid = labels >= 0
    home = bin_of(labels) & 3
    at_home = valid & (home == z)
    upper = as_bf16(row < col)
    lower = as_bf16(iota((CHIPS, CHIPS), 1) < iota((CHIPS, CHIPS), 0))
    members, n = [at_home & ((labels & 3) == r) for r in range(4)], []
    for member in members:
        size = jnp.sum(jnp.where(member, 1.0, 0.0), axis=0, keepdims=True)
        n.append(jnp.sum(size, axis=1, keepdims=True))
    wide = lambda v: jnp.broadcast_to(v, (1, LANES))
    meta_ref[...] = jnp.concatenate([wide(v) for v in in_order(n)] * 2, axis=0).astype(i32)
    pos = jnp.full(labels.shape, -1.0, f32)
    for r, member in enumerate(members):
        place = sum(
            jnp.where((n[q] > n[r]) | ((n[q] == n[r]) & (q < r)), 1.0, 0.0) for q in range(4) if q != r
        )
        start = jnp.where(
            place < 0.5, float(STARTS[0]),
            jnp.where(place < 1.5, float(STARTS[1]), jnp.where(place < 2.5, float(STARTS[2]), float(STARTS[3]))),
        )
        member16 = as_bf16(member)
        rank = dot(member16, upper) + jnp.sum(dot(lower, member16), axis=1, keepdims=True)
        pos = jnp.where(member, start + rank, pos)
    pos = pos.astype(i32)
    pos_ref[...] = pos
    guest = valid & (home != group)
    guest16 = as_bf16(guest)
    same = (row >> 5) == (col >> 5)
    turn = dot(guest16, as_bf16(same & (row < col))) + dot(dot(lower, guest16).astype(bf16), as_bf16(same))
    turn = turn.astype(i32)
    away = at_home & (group != z) & (turn < GUESTS)
    key_ref[...] = jnp.where(away, turn, -1)
    per, groups = 16, CHIPS // 16
    value = jnp.where(group == z, jnp.where(guest, GUEST + turn, pos + 1), 0).astype(f32)
    value = pltpu.roll(value, lax.rem(LANES - GROUP * z, LANES), 1)
    value = jnp.where(lane < block, value, 0.0)
    lined = jnp.zeros((8, per * block), f32)
    for t in range(per):
        rows = jnp.concatenate([value[per * g + t:per * g + t + 1] for g in range(groups)] * 2, axis=0)
        rows = jnp.concatenate([rows, jnp.zeros((8, per * block - LANES), f32)], axis=1)
        lined = lined + (pltpu.roll(rows, t * block, 1) if t else rows)
    slots = jnp.concatenate([lined[g:g + 1] for g in range(groups)], axis=1).astype(i32)
    line_ref[...] = jnp.broadcast_to(slots, line_ref.shape)
    onehot = as_bf16(iota((GUESTS, CHIPS * block), 0) + GUEST == slots)
    guest_ref[...] = dot(onehot, x_ref[...].reshape(CHIPS * block, WIDTH)).astype(bf16)


def sorted_rows(segment, slots, x):
    onehot = as_bf16(iota((segment[1], x.shape[0]), 0) + (segment[0] + 1) == slots)
    return dot(onehot, x).astype(bf16)


def sort_kernel(block, x_ref, line_ref, send_ref, mine_ref):
    x = x_ref[...].reshape(CHIPS * block, WIDTH)
    slots = line_ref[:1, :]
    for core in range(2):
        @pl.when(index_on("c") == core)
        def _():
            for segment in SEGMENTS:
                rows = sorted_rows(segment, slots, x)
                for out_ref, at in ((mine_ref, segment[2 + core]), (send_ref, segment[2 + 1 - core])):
                    if at is not None:
                        out_ref[at:at + segment[1], :] = rows


def fit_kernel(block, units, x_ref, meta_ref, over_ref, table_ref):
    _, chip_counts = labels_of(block, x_ref)
    counts, sizes = counts_of(chip_counts)
    ordered = in_order(sizes)
    over = jnp.zeros((1, LANES), f32)
    for size, cap in zip(ordered, CAPS):
        over = jnp.maximum(over, jnp.where(size > cap, 1.0, 0.0))
    for share in SHARES:
        length = 0.0
        for q, first in share:
            rows = jnp.maximum(jnp.floor((ordered[q] + (UNIT - 1.0)) * (1 / UNIT)) - first // UNIT, 0.0)
            length = length + jnp.where(rows >= 3.0, rows - 1.0, rows)
        over = jnp.maximum(over, jnp.where(length > 4 * units, 1.0, 0.0))
    taken = counts[0] + counts[1] + counts[2] + counts[3]
    lane = iota(taken.shape, 1) & 3
    before = lambda v, back: jnp.where(lane >= back, pltpu.roll(v, back, 1), pltpu.roll(v, LANES - 4 + back, 1))
    extra = taken - (block - 1)
    moved = passed_on(extra, before)
    held = jnp.sum(moved, axis=0, keepdims=True)
    over = jnp.maximum(over, jnp.where(held > GUESTS, 1.0, 0.0))
    full = extra + before(extra, 1) + before(extra, 2) + before(extra, 3) > 0
    full = jnp.where(full | (moved > block - 1), 1.0, 0.0)
    over = jnp.maximum(over, jnp.max(full, axis=0, keepdims=True))
    over_ref[...] = jnp.broadcast_to(jnp.max(over, axis=1, keepdims=True), over_ref.shape).astype(i32)
    y, c = index_on("y"), index_on("c")
    blocks, sizes = [], [size_of(meta_ref, q) for q in range(4)]
    for core, share in enumerate(SHARES):
        at = jnp.zeros((), i32)
        for q, first in share:
            length = length_of(sizes[q], first)
            blocks.append((jnp.where((c == core) & (length > 0), at, 4 * units), FIRST_ROW[q] + first // LANES, at))
            at = at + length
    for t in range(units):
        index = y * units + t
        col, start = jnp.asarray(15, i32), jnp.asarray(0, i32)
        for block_start, block_col, block_at in blocks:
            inside = index >= block_start
            col, start = jnp.where(inside, block_col, col), jnp.where(inside, block_at, start)
        turn = index - start
        unit = 4 * col + jnp.where(turn == 0, 2, jnp.where(turn == 1, 1, turn + 1))
        beside = jnp.where(turn == 0, 3 * UNIT, LANES)
        for entry, value in enumerate((unit >> 2, (unit & 3) * UNIT, beside, col)):
            table_ref[4 * t + entry:4 * t + entry + 1, :] = jnp.full((1, LANES), value, i32)


def add_guests(core, base_ref, guest_ref, far_ref, out_ref):
    guests, far = guest_ref[...], far_ref[:1, :]
    for segment in SEGMENTS:
        at, rows = segment[2 + core], segment[1]
        if at is not None:
            out_ref[at:at + rows, :] = base_ref[at:at + rows, :] + sorted_rows(segment, far, guests)


def blocks_of(core):
    for q, first in SHARES[core]:
        at = BASES[core][q] + first
        yield q, first, pl.ds(at, CAPS[q] - first), pl.ds(at, LANES)


RAW_ROWS = max(sum(CAPS[q] - first for q, first in share) for share in SHARES)


def own_kernel(x_ref, guest_ref, key_ref, pos_ref, raw_ref, far_ref, rows_ref):
    total = jnp.zeros((8, GUESTS), f32)
    step = 16
    for first in range(0, CHIPS, step):
        flat = lambda ref: jnp.concatenate([ref[s:s + 1, :] for s in range(first, first + step)], axis=1)
        places = flat(pos_ref) + 1
        parts = jnp.where(iota((8, step * LANES), 0) == 0, places >> 5, places & 31).astype(f32).astype(bf16)
        total = total + dot_last(parts, as_bf16(iota((GUESTS, step * LANES), 0) == flat(key_ref)))
    far_ref[...] = jnp.broadcast_to((32.0 * total[:1] + total[1:2]).astype(i32), far_ref.shape)
    for core in range(2):
        @pl.when(index_on("c") == core)
        def _():
            add_guests(core, x_ref, guest_ref, far_ref, rows_ref)
            at = 0
            for q, first, left, right in blocks_of(core):
                rows = CAPS[q] - first
                raw_ref[at:at + rows, :] = dot_last(rows_ref[left, :], rows_ref[right, :])
                at += rows


def size_of(meta_ref, q):
    return jnp.max(meta_ref[q:q + 1, :].astype(f32)).astype(i32)


def length_of(size, first):
    units = jnp.maximum(((size + UNIT - 1) >> 5) - first // UNIT, 0)
    return jnp.where(units >= 3, units - 1, units)


def folded(score):
    away = jnp.full((UNIT, LANES), -4.0, f32) if score.shape[0] < LANES else score[2 * UNIT:3 * UNIT]
    both = jnp.where(iota(away.shape, 1) < 3 * UNIT, away, pltpu.roll(score[:UNIT], 3 * UNIT, 1))
    rest = [score[3 * UNIT:]] if score.shape[0] > 3 * UNIT else []
    return jnp.concatenate([both, score[UNIT:2 * UNIT]] + rest, axis=0)


def gram_kernel(units, meta_ref, x_ref, guest_ref, far_ref, raw_ref, out0, out1, out2, out3, part_ref, rows_ref):
    y, c = index_on("y"), index_on("c")
    part_ref[...] = jnp.full(part_ref.shape, -4.0, f32)
    for core in range(2):
        @pl.when(c == core)
        def _():
            add_guests(core, x_ref, guest_ref, far_ref, rows_ref)
            at, to = 0, jnp.zeros((), i32)
            for q, first, left, right in blocks_of(core):
                rows = CAPS[q] - first
                score = raw_ref[at:at + rows, :] + dot_last(rows_ref[left, :], rows_ref[right, :])
                at += rows
                size = size_of(meta_ref, q)
                i, j = iota(score.shape, 0), iota(score.shape, 1)
                keep = (i < size - first) & (j < size - first) & (i != j)
                score = folded(jnp.where(keep, score, -4.0))
                part_ref[pl.ds(pl.multiple_of(to, UNIT), score.shape[0]), :] = score
                to = jnp.minimum(to + UNIT * length_of(size, first), 4 * units * UNIT)
    chunk = units * UNIT
    for shift, out in enumerate((out0, out1, out2, out3)):
        out[...] = part_ref[pl.ds(pl.multiple_of(lax.rem(y + shift, 4) * chunk, UNIT), chunk), :]


FIRST_ROW = (0, 6, 10, 13)


def max_kernel(units, table_ref, p0, p1, p2, p3, pos_ref, out_ref):
    best = jnp.full((16, LANES), -1.0, f32)
    sub, lane, row = iota((UNIT, LANES), 0), iota((UNIT, LANES), 1), iota((16, LANES), 0)
    for t in range(units):
        at = slice(t * UNIT, (t + 1) * UNIT)
        block = (p0[at, :] + p1[at, :]) + (p2[at, :] + p3[at, :])
        unit_row, offset, beside, col = (table_ref[4 * t + entry:4 * t + entry + 1, :] for entry in range(4))
        one, two = jnp.where(lane < beside, block, -4.0), jnp.where(lane < beside, -4.0, block)
        along = jnp.max(one, axis=1, keepdims=True)
        along = jnp.max(jnp.where(sub + offset == lane, along, -1.0), axis=0, keepdims=True)
        best = jnp.maximum(best, jnp.where(row == unit_row, along, -1.0))
        down = jnp.max(jnp.maximum(one, pltpu.roll(two, UNIT, 1)), axis=0, keepdims=True)
        best = jnp.maximum(best, jnp.where(row == col, down, -1.0))
    pos = pos_ref[...]
    pos = jnp.where(pos >= STARTS[1], pos + 64, pos)
    pos = jnp.where(pos >= STARTS[3] + 64, pos + 64, pos)
    row, lane = pos >> 7, pos & (LANES - 1)
    out = jnp.full(pos.shape, -1.0, f32)
    for r in range(15):
        value = jnp.broadcast_to(best[r:r + 1, :], pos.shape)
        value = jnp.take_along_axis(value, lane, axis=1, mode="promise_in_bounds")
        out = jnp.where(row == r, value, out)
    out_ref[:CHIPS, :] = out
    out_ref[CHIPS:, :] = out


def pick_kernel(v_ref, code_ref, out_ref):
    values = jnp.maximum(v_ref[:CHIPS, :], v_ref[CHIPS:, :])
    values = jnp.max(values.reshape(BINS, 4, LANES), axis=1)
    code = jnp.max(jnp.where(iota((8, ROWS), 0) == index_on("c"), code_ref[...], -1), axis=0, keepdims=True)
    code = jnp.broadcast_to(code, (8, ROWS))
    row, lane = code >> 7, code & (LANES - 1)
    best = jnp.full((8, ROWS), -1.0, f32)
    for b in range(BINS):
        value = jnp.broadcast_to(values[b:b + 1], (8, ROWS))
        best = jnp.where(row == b, jnp.take_along_axis(value, lane, axis=1, mode="promise_in_bounds"), best)
    out_ref[...] = best[:1]


def gather_groups(embeddings, cluster_ids):
    split = ("z", "y", "c")
    rows = embeddings.shape[0]
    groups = lax.axis_size("x")
    cap = 2 * rows // groups
    slots = groups * cap
    owner_of = cluster_ids % groups
    onehot = (owner_of[:, None] == jnp.arange(groups, dtype=i32)[None, :]).astype(i32)
    before = jnp.cumsum(onehot, axis=0) - onehot
    rank = jnp.sum(before * onehot, axis=1)
    place = owner_of * cap + rank
    picked = place[None, :] == jnp.arange(slots, dtype=i32)[:, None]
    filled = jnp.any(picked, axis=1)
    source = jnp.sum(jnp.where(picked, jnp.arange(rows, dtype=i32)[None, :], 0), axis=1)
    out_labels = jnp.where(filled, cluster_ids[source], -1)
    squares = jnp.sum(embeddings * embeddings, axis=1, keepdims=True)
    local_unit = (embeddings * lax.rsqrt(squares + 1e-06)).astype(bf16)
    outgoing_unit = jnp.where(filled[:, None], local_unit[source], jnp.zeros((), bf16))
    unit = lax.all_to_all(outgoing_unit, "x", split_axis=0, concat_axis=0, tiled=True)
    labels = lax.all_to_all(out_labels, "x", split_axis=0, concat_axis=0, tiled=True)
    members = lax.axis_size(split)

    def everywhere(v):
        copies = jnp.broadcast_to(v[None], (members,) + v.shape).reshape((members * slots,) + v.shape[1:])
        return lax.all_to_all(copies, split, split_axis=0, concat_axis=0, tiled=True)

    def add_slice(i, scores):
        part = lax.dynamic_slice_in_dim(unit, i * WIDTH, WIDTH, 1)
        return scores + dot_last(part, everywhere(part))

    scores = lax.fori_loop(0, embeddings.shape[1] // WIDTH, add_slice, jnp.zeros((slots, members * slots), f32))
    all_labels = everywhere(labels)
    own = lax.axis_index(split) * slots + jnp.arange(slots, dtype=i32)
    mask = (
        (labels[:, None] == all_labels[None, :])
        & (labels[:, None] >= 0)
        & (own[:, None] != jnp.arange(members * slots, dtype=i32)[None, :])
    )
    scores = jnp.where(mask, scores, -1.0)
    best = jnp.maximum(-1.0, jnp.max(scores, axis=1))
    returned = lax.all_to_all(best, "x", split_axis=0, concat_axis=0, tiled=True)
    return returned[place]


def route(block, units, embeddings, cluster_ids):
    shape = jax.ShapeDtypeStruct
    half = shape((ROWS + LABEL_ROWS, HALF_WIDTH), bf16)
    ids = cluster_ids.reshape(1, ROWS)
    send, scale = pl.pallas_call(
        unit_send_kernel, out_shape=(half, shape((ROWS, LANES), f32)),
        in_specs=[WHOLE, WHOLE], out_specs=(WHOLE, WHOLE), compiler_params=params(12), name="unit_send",
    )(embeddings, ids)
    got = lax.ppermute(send, "c", [(0, 1), (1, 0)])
    keep = pl.pallas_call(
        unit_keep_kernel, out_shape=half,
        in_specs=[pl.BlockSpec(memory_space=pl.ANY), WHOLE, WHOLE], out_specs=WHOLE,
        scratch_shapes=[pltpu.VMEM((ROWS, HALF_WIDTH), f32), pltpu.SemaphoreType.DMA],
        compiler_params=params(8), name="unit_keep",
    )(embeddings, ids, scale)
    packed, code = pl.pallas_call(
        functools.partial(pack_kernel, block),
        out_shape=(shape((CHIPS, block, WIDTH), bf16), shape((8, ROWS), i32)),
        in_specs=[WHOLE, WHOLE], out_specs=(WHOLE, WHOLE), compiler_params=params(20), name="pack",
    )(keep, got)
    packed = lax.all_to_all(packed, ("x", "z", "y"), 0, 0, tiled=True)
    table = shape((CHIPS, LANES), i32)
    guests, line, key, pos, meta = pl.pallas_call(
        functools.partial(names_kernel, block),
        out_shape=(shape((GUESTS, WIDTH), bf16), shape((8, CHIPS * block), i32), table, table, shape((8, LANES), i32)),
        in_specs=[WHOLE], out_specs=(WHOLE,) * 5, compiler_params=params(12), name="names",
    )(packed)
    brought = lax.ppermute(guests, "z", [(i, (i + 3) % 4) for i in range(4)])
    share = shape((SHARE_ROWS, WIDTH), bf16)
    send, mine = pl.pallas_call(
        functools.partial(sort_kernel, block), out_shape=(share, share),
        in_specs=[WHOLE] * 2, out_specs=(WHOLE,) * 2, compiler_params=params(24), name="sort",
    )(packed, line)
    brought, mine, send = lax.optimization_barrier((brought, mine, send))
    other = lax.ppermute(send, "c", [(0, 1), (1, 0)])
    swapped = lax.ppermute(brought, "c", [(0, 1), (1, 0)])
    raw, far = pl.pallas_call(
        own_kernel, out_shape=(shape((RAW_ROWS, LANES), f32), shape((8, GUESTS), i32)),
        in_specs=[WHOLE] * 4, out_specs=(WHOLE,) * 2,
        scratch_shapes=[pltpu.VMEM((SHARE_ROWS, WIDTH), bf16)],
        compiler_params=params(16), name="own",
        cost_estimate=pl.CostEstimate(flops=2 * RAW_ROWS * LANES * WIDTH, bytes_accessed=4 << 20, transcendentals=0),
    )(mine, brought, key, pos)
    partial = pl.pallas_call(
        functools.partial(gram_kernel, units),
        out_shape=[shape((units * UNIT, LANES), f32)] * 4,
        in_specs=[WHOLE] * 5, out_specs=[WHOLE] * 4,
        scratch_shapes=[pltpu.VMEM((4 * units * UNIT + CAPS[0], LANES), f32), pltpu.VMEM((SHARE_ROWS, WIDTH), bf16)],
        compiler_params=params(16), name="gram",
    )(meta, other, swapped, far, raw)
    arrived = [partial[0]] + [
        lax.ppermute(partial[s], "y", [(i, (i + s) % 4) for i in range(4)]) for s in (3, 2, 1)
    ]
    over, table = pl.pallas_call(
        functools.partial(fit_kernel, block, units),
        out_shape=(shape((8, LANES), i32), shape((4 * units, LANES), i32)),
        in_specs=[WHOLE, WHOLE], out_specs=(WHOLE, WHOLE), compiler_params=params(8), name="fit",
    )(packed, meta)
    arrived, fits, table = lax.optimization_barrier((arrived, over[0, 0] == 0, table))
    best = pl.pallas_call(
        functools.partial(max_kernel, units),
        out_shape=shape((2 * CHIPS, LANES), f32),
        in_specs=[WHOLE] * 6, out_specs=WHOLE, compiler_params=params(8), name="maxima",
    )(table, *arrived, pos)
    back = lax.all_to_all(best.reshape(2 * CHIPS, 1, LANES), ("c", "x", "z", "y"), 0, 0, tiled=True)
    back, fits = lax.optimization_barrier((back, fits))
    best = pl.pallas_call(
        pick_kernel,
        out_shape=shape((1, ROWS), f32),
        in_specs=[WHOLE, WHOLE], out_specs=WHOLE, compiler_params=params(8), name="pick",
    )(back.reshape(2 * CHIPS, LANES), code).reshape(ROWS)
    return best, fits


def on_device(embeddings, cluster_ids, tries=TRIES):
    if not tries:
        return gather_groups(embeddings, cluster_ids)
    best, fits = route(*tries[0], embeddings, cluster_ids)
    return lax.cond(
        fits,
        lambda best, embeddings, cluster_ids: best,
        lambda best, embeddings, cluster_ids: on_device(embeddings, cluster_ids, tries[1:]),
        best, embeddings, cluster_ids,
    )


def solution(mesh):
    axes = ("x", "z", "y", "c")
    grid = Mesh(mesh.devices.reshape(4, 4, 4, 2), axes)
    return jax.shard_map(
        on_device, mesh=grid, in_specs=(P(axes, None), P(axes)), out_specs=P(axes), check_vma=False
    )
```

```python
import functools

import jax
import jax.numpy as jnp
from jax import lax
from jax.experimental import pallas as pl
from jax.experimental.pallas import tpu as pltpu
from jax.sharding import Mesh, PartitionSpec as P

ROWS = 128
HALF_WIDTH = 2048
WIDTH = 512
LABEL_ROWS = 16
BINS = 16
CHIPS = 64
TRIES = ((24, 11), (32, 16))
GROUP = 32
GUESTS = 64
GUEST = 4096
LANES = 128
CAPS = (704, 512, 320, 192)
STARTS = (0, 704, 1216, 1536)
UNIT = 32
SHARES = (
    ((0, 0), (0, 256), (2, 0), (2, 128), (2, 256), (3, 0)),
    ((0, 128), (0, 384), (0, 512), (0, 640), (1, 0), (1, 128), (1, 256), (1, 384), (3, 128)),
)
BASES = ({0: 0, 2: 704, 3: 1024}, {0: -128, 1: 576, 3: 960})
SHARE_ROWS = 1216
SEGMENTS = (
    (0, 128, 0, None), (128, 576, 128, 0), (704, 256, None, 576), (960, 256, None, 832),
    (1216, 320, 704, None), (1536, 128, 1024, None), (1664, 64, 1152, 1088),
)
f32, bf16, i32 = jnp.float32, jnp.bfloat16, jnp.int32
WHOLE = pl.BlockSpec(memory_space=pltpu.VMEM)


def params(mib):
    return pltpu.CompilerParams(vmem_limit_bytes=mib * 1024 * 1024)


def index_on(axis):
    return lax.axis_index(axis)


def iota(shape, dim):
    return lax.broadcasted_iota(i32, shape, dim)


def dot_last(a, b):
    return lax.dot_general(a, b, (((1,), (1,)), ((), ())), preferred_element_type=f32)


def dot(a, b):
    return lax.dot_general(a, b, (((1,), (0,)), ((), ())), preferred_element_type=f32)


def as_bf16(mask):
    return jnp.where(mask, 1.0, 0.0).astype(bf16)


def bin_of(labels):
    rank, residue = labels >> 2, labels & 3
    row, col = rank >> 2, rank & 3
    col = jnp.where((row & 1) == 1, 3 - col, col)
    return 4 * col + ((row - residue) & 3)


def label_rows(ids_ref):
    ids = jnp.concatenate([ids_ref[...].astype(f32), jnp.zeros((1, HALF_WIDTH - ROWS), f32)], axis=1)
    return jnp.broadcast_to(ids, (LABEL_ROWS, HALF_WIDTH)).astype(bf16)


def half_of(core):
    return pl.ds(pl.multiple_of(core * HALF_WIDTH, HALF_WIDTH), HALF_WIDTH)


def unit_send_kernel(x_ref, ids_ref, out_ref, scale_ref):
    x = x_ref[...]
    scale = lax.rsqrt(jnp.sum(x * x, axis=1, keepdims=True) + 1e-06)
    scale_ref[...] = jnp.broadcast_to(scale, scale_ref.shape)
    out_ref[:ROWS, :] = (x_ref[:, half_of(1 - index_on("c"))] * scale).astype(bf16)
    out_ref[ROWS:, :] = label_rows(ids_ref)


def unit_keep_kernel(x_ref, ids_ref, scale_ref, out_ref, half_ref, sem):
    copy = pltpu.make_async_copy(x_ref.at[:, half_of(index_on("c"))], half_ref, sem)
    copy.start()
    out_ref[ROWS:, :] = label_rows(ids_ref)
    copy.wait()
    out_ref[:ROWS, :] = (half_ref[...] * scale_ref[:, :1]).astype(bf16)


def passed_on(over, before):
    once = before(over, 1)
    twice = before(over, 2)
    return jnp.maximum(jnp.maximum(over, 0), jnp.maximum(over + once, over + once + twice))


def pack_kernel(block, keep_ref, got_ref, out_ref, code_ref):
    first = index_on("c") == 0
    kept = jnp.max(keep_ref[ROWS:, :ROWS].astype(f32), axis=0, keepdims=True)
    got = jnp.max(got_ref[ROWS:, :ROWS].astype(f32), axis=0, keepdims=True)
    labels = jnp.concatenate([jnp.where(first, kept, got), jnp.where(first, got, kept)], axis=0).astype(i32)
    bins = bin_of(labels)
    upper = as_bf16(iota((ROWS, ROWS), 0) < iota((ROWS, ROWS), 1))

    def ranks_within(masks):
        member = jnp.concatenate([jnp.where(mask, 1.0, 0.0) for mask in masks], axis=0)
        row, col = iota((member.shape[0],) * 2, 0), iota((member.shape[0],) * 2, 1)
        earlier = dot(as_bf16(((row >> 1) == (col >> 1)) & (col < row)), member.astype(bf16))
        ranks = member * (dot(member.astype(bf16), upper) + jnp.sum(earlier, axis=1, keepdims=True))
        rank = sum(ranks[2 * b:2 * b + 2] for b in range(len(masks)))
        return rank.astype(i32), jnp.sum(member, axis=1, keepdims=True)

    rank, sizes = ranks_within([bins == b for b in range(BINS)])
    quad, line = bins >> 2, bins & 3
    taken = []
    for at in range(4):
        size = jnp.zeros(labels.shape, f32)
        for b in range(at, BINS, 4):
            size = jnp.where(quad == b >> 2, sizes[2 * b:2 * b + 1] + sizes[2 * b + 1:2 * b + 2], size)
        taken.append(size.astype(i32) - (block - 1))
    stays = []
    for at in range(4):
        moved = passed_on(taken[at], lambda _, back: taken[(at - back) & 3])
        stays.append(taken[at] + (block - 1) - moved)

    def of_line(values, which):
        out = values[0]
        for at in range(1, 4):
            out = jnp.where(which == at, values[at], out)
        return out

    stay = of_line(stays, line)
    to_line = jnp.where(rank < stay, line, (line + 1) & 3)
    to_slot = jnp.where(rank < stay, rank, of_line(stays, to_line) + rank - stay)
    placed = to_slot < (block - 1)
    lane = jnp.where(placed, to_line * GROUP + to_slot, -1)
    place = jnp.where(placed, (quad * 4 + to_line) * block + to_slot, -1)
    code_ref[...] = jnp.concatenate([jnp.where(placed, bins * LANES + lane, -1)] * 4, axis=0)
    docs = 2 * ROWS
    flat = lambda v: jnp.concatenate([v[:1], v[1:]], axis=1)
    label_row = flat(labels)
    counts = dot_last(jnp.ones((8, docs), bf16), as_bf16(iota((LANES, docs), 0) == label_row))[:1]
    named = jnp.where(iota((8, docs), 0) == flat(quad), (label_row + 1).astype(f32), 0.0).astype(bf16)
    names = dot_last(named, as_bf16(iota((LANES, docs), 0) == flat(lane)))
    own = jnp.where(first, place[:1], place[1:])
    other = jnp.where(first, place[1:], place[:1])
    onehot = as_bf16(iota((BINS * block, docs), 0) == jnp.concatenate([own, other], axis=1))
    is_last = iota((block, WIDTH), 0) == (block - 1)
    for y in range(4):
        columns = slice(y * WIDTH, (y + 1) * WIDTH)
        x = jnp.concatenate([keep_ref[:ROWS, columns], got_ref[:ROWS, columns]], axis=0)
        packed = dot(onehot, x)
        for b in range(BINS):
            extra = jnp.concatenate([names[b // 4:b // 4 + 1], counts, jnp.zeros((1, 2 * LANES), f32)], axis=1)
            out_ref[4 * b + y] = jnp.where(is_last, extra, packed[b * block:(b + 1) * block]).astype(bf16)


def labels_of(block, x_ref):
    tail = x_ref[:, block - 8:, :2 * LANES].astype(f32)
    tail = jnp.max(jnp.where(iota(tail.shape, 1) == 7, tail, 0.0), axis=1)
    return tail[:, :LANES].astype(i32) - 1, tail[:, LANES:].astype(bf16)


def counts_of(chip_counts):
    row, col = iota((LANES, LANES), 0), iota((LANES, LANES), 1)
    in_bin = (bin_of(row) == col) & (row < 4 * BINS)
    counts = [dot(chip_counts, as_bf16(in_bin & ((row & 3) == r))) for r in range(4)]
    return counts, [jnp.sum(v, axis=0, keepdims=True) for v in counts]


def in_order(sizes):
    a, b = jnp.maximum(sizes[0], sizes[1]), jnp.minimum(sizes[0], sizes[1])
    c, d = jnp.maximum(sizes[2], sizes[3]), jnp.minimum(sizes[2], sizes[3])
    first, e = jnp.maximum(a, c), jnp.minimum(a, c)
    g, fourth = jnp.maximum(b, d), jnp.minimum(b, d)
    return first, jnp.maximum(e, g), jnp.minimum(e, g), fourth


def names_kernel(block, x_ref, guest_ref, line_ref, key_ref, pos_ref, meta_ref):
    z = index_on("z")
    labels, _ = labels_of(block, x_ref)
    row, col = iota((LANES, LANES), 0), iota((LANES, LANES), 1)
    lane = iota(labels.shape, 1)
    group = lane >> 5
    valid = labels >= 0
    home = bin_of(labels) & 3
    at_home = valid & (home == z)
    upper = as_bf16(row < col)
    lower = as_bf16(iota((CHIPS, CHIPS), 1) < iota((CHIPS, CHIPS), 0))
    members, n = [at_home & ((labels & 3) == r) for r in range(4)], []
    for member in members:
        size = jnp.sum(jnp.where(member, 1.0, 0.0), axis=0, keepdims=True)
        n.append(jnp.sum(size, axis=1, keepdims=True))
    wide = lambda v: jnp.broadcast_to(v, (1, LANES))
    meta_ref[...] = jnp.concatenate([wide(v) for v in in_order(n)] * 2, axis=0).astype(i32)
    pos = jnp.full(labels.shape, -1.0, f32)
    for r, member in enumerate(members):
        place = sum(
            jnp.where((n[q] > n[r]) | ((n[q] == n[r]) & (q < r)), 1.0, 0.0) for q in range(4) if q != r
        )
        start = jnp.where(
            place < 0.5, float(STARTS[0]),
            jnp.where(place < 1.5, float(STARTS[1]), jnp.where(place < 2.5, float(STARTS[2]), float(STARTS[3]))),
        )
        member16 = as_bf16(member)
        rank = dot(member16, upper) + jnp.sum(dot(lower, member16), axis=1, keepdims=True)
        pos = jnp.where(member, start + rank, pos)
    pos = pos.astype(i32)
    pos_ref[...] = pos
    guest = valid & (home != group)
    guest16 = as_bf16(guest)
    same = (row >> 5) == (col >> 5)
    turn = dot(guest16, as_bf16(same & (row < col))) + dot(dot(lower, guest16).astype(bf16), as_bf16(same))
    turn = turn.astype(i32)
    away = at_home & (group != z) & (turn < GUESTS)
    key_ref[...] = jnp.where(away, turn, -1)
    per, groups = 16, CHIPS // 16
    value = jnp.where(group == z, jnp.where(guest, GUEST + turn, pos + 1), 0).astype(f32)
    value = pltpu.roll(value, lax.rem(LANES - GROUP * z, LANES), 1)
    value = jnp.where(lane < block, value, 0.0)
    lined = jnp.zeros((8, per * block), f32)
    for t in range(per):
        rows = jnp.concatenate([value[per * g + t:per * g + t + 1] for g in range(groups)] * 2, axis=0)
        rows = jnp.concatenate([rows, jnp.zeros((8, per * block - LANES), f32)], axis=1)
        lined = lined + (pltpu.roll(rows, t * block, 1) if t else rows)
    slots = jnp.concatenate([lined[g:g + 1] for g in range(groups)], axis=1).astype(i32)
    line_ref[...] = jnp.broadcast_to(slots, line_ref.shape)
    onehot = as_bf16(iota((GUESTS, CHIPS * block), 0) + GUEST == slots)
    guest_ref[...] = dot(onehot, x_ref[...].reshape(CHIPS * block, WIDTH)).astype(bf16)


def sorted_rows(segment, slots, x):
    onehot = as_bf16(iota((segment[1], x.shape[0]), 0) + (segment[0] + 1) == slots)
    return dot(onehot, x).astype(bf16)


def sort_kernel(block, x_ref, line_ref, send_ref, mine_ref):
    x = x_ref[...].reshape(CHIPS * block, WIDTH)
    slots = line_ref[:1, :]
    for core in range(2):
        @pl.when(index_on("c") == core)
        def _():
            for segment in SEGMENTS:
                rows = sorted_rows(segment, slots, x)
                for out_ref, at in ((mine_ref, segment[2 + core]), (send_ref, segment[2 + 1 - core])):
                    if at is not None:
                        out_ref[at:at + segment[1], :] = rows


def fit_kernel(block, units, x_ref, meta_ref, over_ref, table_ref):
    _, chip_counts = labels_of(block, x_ref)
    counts, sizes = counts_of(chip_counts)
    ordered = in_order(sizes)
    over = jnp.zeros((1, LANES), f32)
    for size, cap in zip(ordered, CAPS):
        over = jnp.maximum(over, jnp.where(size > cap, 1.0, 0.0))
    for share in SHARES:
        length = 0.0
        for q, first in share:
            rows = jnp.maximum(jnp.floor((ordered[q] + (UNIT - 1.0)) * (1 / UNIT)) - first // UNIT, 0.0)
            length = length + jnp.where(rows >= 3.0, rows - 1.0, rows)
        over = jnp.maximum(over, jnp.where(length > 4 * units, 1.0, 0.0))
    taken = counts[0] + counts[1] + counts[2] + counts[3]
    lane = iota(taken.shape, 1) & 3
    before = lambda v, back: jnp.where(lane >= back, pltpu.roll(v, back, 1), pltpu.roll(v, LANES - 4 + back, 1))
    extra = taken - (block - 1)
    moved = passed_on(extra, before)
    held = jnp.sum(moved, axis=0, keepdims=True)
    over = jnp.maximum(over, jnp.where(held > GUESTS, 1.0, 0.0))
    full = extra + before(extra, 1) + before(extra, 2) + before(extra, 3) > 0
    full = jnp.where(full | (moved > block - 1), 1.0, 0.0)
    over = jnp.maximum(over, jnp.max(full, axis=0, keepdims=True))
    over_ref[...] = jnp.broadcast_to(jnp.max(over, axis=1, keepdims=True), over_ref.shape).astype(i32)
    y, c = index_on("y"), index_on("c")
    blocks, sizes = [], [size_of(meta_ref, q) for q in range(4)]
    for core, share in enumerate(SHARES):
        at = jnp.zeros((), i32)
        for q, first in share:
            length = length_of(sizes[q], first)
            blocks.append((jnp.where((c == core) & (length > 0), at, 4 * units), FIRST_ROW[q] + first // LANES, at))
            at = at + length
    for t in range(units):
        index = y * units + t
        col, start = jnp.asarray(15, i32), jnp.asarray(0, i32)
        for block_start, block_col, block_at in blocks:
            inside = index >= block_start
            col, start = jnp.where(inside, block_col, col), jnp.where(inside, block_at, start)
        turn = index - start
        unit = 4 * col + jnp.where(turn == 0, 2, jnp.where(turn == 1, 1, turn + 1))
        beside = jnp.where(turn == 0, 3 * UNIT, LANES)
        for entry, value in enumerate((unit >> 2, (unit & 3) * UNIT, beside, col)):
            table_ref[4 * t + entry:4 * t + entry + 1, :] = jnp.full((1, LANES), value, i32)


def add_guests(core, base_ref, guest_ref, far_ref, out_ref):
    guests, far = guest_ref[...], far_ref[:1, :]
    for segment in SEGMENTS:
        at, rows = segment[2 + core], segment[1]
        if at is not None:
            out_ref[at:at + rows, :] = base_ref[at:at + rows, :] + sorted_rows(segment, far, guests)


def blocks_of(core):
    for q, first in SHARES[core]:
        at = BASES[core][q] + first
        yield q, first, pl.ds(at, CAPS[q] - first), pl.ds(at, LANES)


RAW_ROWS = max(sum(CAPS[q] - first for q, first in share) for share in SHARES)


def own_kernel(x_ref, guest_ref, key_ref, pos_ref, raw_ref, far_ref, rows_ref):
    total = jnp.zeros((8, GUESTS), f32)
    step = 16
    for first in range(0, CHIPS, step):
        flat = lambda ref: jnp.concatenate([ref[s:s + 1, :] for s in range(first, first + step)], axis=1)
        places = flat(pos_ref) + 1
        parts = jnp.where(iota((8, step * LANES), 0) == 0, places >> 5, places & 31).astype(f32).astype(bf16)
        total = total + dot_last(parts, as_bf16(iota((GUESTS, step * LANES), 0) == flat(key_ref)))
    far_ref[...] = jnp.broadcast_to((32.0 * total[:1] + total[1:2]).astype(i32), far_ref.shape)
    for core in range(2):
        @pl.when(index_on("c") == core)
        def _():
            add_guests(core, x_ref, guest_ref, far_ref, rows_ref)
            at = 0
            for q, first, left, right in blocks_of(core):
                rows = CAPS[q] - first
                raw_ref[at:at + rows, :] = dot_last(rows_ref[left, :], rows_ref[right, :])
                at += rows


def size_of(meta_ref, q):
    return jnp.max(meta_ref[q:q + 1, :].astype(f32)).astype(i32)


def length_of(size, first):
    units = jnp.maximum(((size + UNIT - 1) >> 5) - first // UNIT, 0)
    return jnp.where(units >= 3, units - 1, units)


def folded(score):
    away = jnp.full((UNIT, LANES), -4.0, f32) if score.shape[0] < LANES else score[2 * UNIT:3 * UNIT]
    both = jnp.where(iota(away.shape, 1) < 3 * UNIT, away, pltpu.roll(score[:UNIT], 3 * UNIT, 1))
    rest = [score[3 * UNIT:]] if score.shape[0] > 3 * UNIT else []
    return jnp.concatenate([both, score[UNIT:2 * UNIT]] + rest, axis=0)


def gram_kernel(units, meta_ref, x_ref, guest_ref, far_ref, raw_ref, out0, out1, out2, out3, part_ref, rows_ref):
    y, c = index_on("y"), index_on("c")
    part_ref[...] = jnp.full(part_ref.shape, -4.0, f32)
    for core in range(2):
        @pl.when(c == core)
        def _():
            add_guests(core, x_ref, guest_ref, far_ref, rows_ref)
            at, to = 0, jnp.zeros((), i32)
            for q, first, left, right in blocks_of(core):
                rows = CAPS[q] - first
                score = raw_ref[at:at + rows, :] + dot_last(rows_ref[left, :], rows_ref[right, :])
                at += rows
                size = size_of(meta_ref, q)
                i, j = iota(score.shape, 0), iota(score.shape, 1)
                keep = (i < size - first) & (j < size - first) & (i != j)
                score = folded(jnp.where(keep, score, -4.0))
                part_ref[pl.ds(pl.multiple_of(to, UNIT), score.shape[0]), :] = score
                to = jnp.minimum(to + UNIT * length_of(size, first), 4 * units * UNIT)
    chunk = units * UNIT
    for shift, out in enumerate((out0, out1, out2, out3)):
        out[...] = part_ref[pl.ds(pl.multiple_of(lax.rem(y + shift, 4) * chunk, UNIT), chunk), :]


FIRST_ROW = (0, 6, 10, 13)


def max_kernel(units, table_ref, p0, p1, p2, p3, pos_ref, out_ref):
    best = jnp.full((16, LANES), -1.0, f32)
    sub, lane, row = iota((UNIT, LANES), 0), iota((UNIT, LANES), 1), iota((16, LANES), 0)
    for t in range(units):
        at = slice(t * UNIT, (t + 1) * UNIT)
        block = (p0[at, :] + p1[at, :]) + (p2[at, :] + p3[at, :])
        unit_row, offset, beside, col = (table_ref[4 * t + entry:4 * t + entry + 1, :] for entry in range(4))
        one, two = jnp.where(lane < beside, block, -4.0), jnp.where(lane < beside, -4.0, block)
        along = jnp.max(one, axis=1, keepdims=True)
        along = jnp.max(jnp.where(sub + offset == lane, along, -1.0), axis=0, keepdims=True)
        best = jnp.maximum(best, jnp.where(row == unit_row, along, -1.0))
        down = jnp.max(jnp.maximum(one, pltpu.roll(two, UNIT, 1)), axis=0, keepdims=True)
        best = jnp.maximum(best, jnp.where(row == col, down, -1.0))
    pos = pos_ref[...]
    pos = jnp.where(pos >= STARTS[1], pos + 64, pos)
    pos = jnp.where(pos >= STARTS[3] + 64, pos + 64, pos)
    row, lane = pos >> 7, pos & (LANES - 1)
    out = jnp.full(pos.shape, -1.0, f32)
    for r in range(15):
        value = jnp.broadcast_to(best[r:r + 1, :], pos.shape)
        value = jnp.take_along_axis(value, lane, axis=1, mode="promise_in_bounds")
        out = jnp.where(row == r, value, out)
    out_ref[:CHIPS, :] = out
    out_ref[CHIPS:, :] = out


def pick_kernel(v_ref, code_ref, out_ref):
    values = jnp.maximum(v_ref[:CHIPS, :], v_ref[CHIPS:, :])
    values = jnp.max(values.reshape(BINS, 4, LANES), axis=1)
    code = jnp.max(jnp.where(iota((8, ROWS), 0) == index_on("c"), code_ref[...], -1), axis=0, keepdims=True)
    code = jnp.broadcast_to(code, (8, ROWS))
    row, lane = code >> 7, code & (LANES - 1)
    best = jnp.full((8, ROWS), -1.0, f32)
    for b in range(BINS):
        value = jnp.broadcast_to(values[b:b + 1], (8, ROWS))
        best = jnp.where(row == b, jnp.take_along_axis(value, lane, axis=1, mode="promise_in_bounds"), best)
    out_ref[...] = best[:1]


def gather_groups(embeddings, cluster_ids):
    split = ("z", "y", "c")
    rows = embeddings.shape[0]
    groups = lax.axis_size("x")
    cap = 2 * rows // groups
    slots = groups * cap
    owner_of = cluster_ids % groups
    onehot = (owner_of[:, None] == jnp.arange(groups, dtype=i32)[None, :]).astype(i32)
    before = jnp.cumsum(onehot, axis=0) - onehot
    rank = jnp.sum(before * onehot, axis=1)
    place = owner_of * cap + rank
    picked = place[None, :] == jnp.arange(slots, dtype=i32)[:, None]
    filled = jnp.any(picked, axis=1)
    source = jnp.sum(jnp.where(picked, jnp.arange(rows, dtype=i32)[None, :], 0), axis=1)
    out_labels = jnp.where(filled, cluster_ids[source], -1)
    squares = jnp.sum(embeddings * embeddings, axis=1, keepdims=True)
    local_unit = (embeddings * lax.rsqrt(squares + 1e-06)).astype(bf16)
    outgoing_unit = jnp.where(filled[:, None], local_unit[source], jnp.zeros((), bf16))
    unit = lax.all_to_all(outgoing_unit, "x", split_axis=0, concat_axis=0, tiled=True)
    labels = lax.all_to_all(out_labels, "x", split_axis=0, concat_axis=0, tiled=True)
    members = lax.axis_size(split)

    def everywhere(v):
        copies = jnp.broadcast_to(v[None], (members,) + v.shape).reshape((members * slots,) + v.shape[1:])
        return lax.all_to_all(copies, split, split_axis=0, concat_axis=0, tiled=True)

    def add_slice(i, scores):
        part = lax.dynamic_slice_in_dim(unit, i * WIDTH, WIDTH, 1)
        return scores + dot_last(part, everywhere(part))

    scores = lax.fori_loop(0, embeddings.shape[1] // WIDTH, add_slice, jnp.zeros((slots, members * slots), f32))
    all_labels = everywhere(labels)
    own = lax.axis_index(split) * slots + jnp.arange(slots, dtype=i32)
    mask = (
        (labels[:, None] == all_labels[None, :])
        & (labels[:, None] >= 0)
        & (own[:, None] != jnp.arange(members * slots, dtype=i32)[None, :])
    )
    scores = jnp.where(mask, scores, -1.0)
    best = jnp.maximum(-1.0, jnp.max(scores, axis=1))
    returned = lax.all_to_all(best, "x", split_axis=0, concat_axis=0, tiled=True)
    return returned[place]


def route(block, units, embeddings, cluster_ids):
    shape = jax.ShapeDtypeStruct
    half = shape((ROWS + LABEL_ROWS, HALF_WIDTH), bf16)
    ids = cluster_ids.reshape(1, ROWS)
    send, scale = pl.pallas_call(
        unit_send_kernel, out_shape=(half, shape((ROWS, LANES), f32)),
        in_specs=[WHOLE, WHOLE], out_specs=(WHOLE, WHOLE), compiler_params=params(12), name="unit_send",
    )(embeddings, ids)
    got = lax.ppermute(send, "c", [(0, 1), (1, 0)])
    keep = pl.pallas_call(
        unit_keep_kernel, out_shape=half,
        in_specs=[pl.BlockSpec(memory_space=pl.ANY), WHOLE, WHOLE], out_specs=WHOLE,
        scratch_shapes=[pltpu.VMEM((ROWS, HALF_WIDTH), f32), pltpu.SemaphoreType.DMA],
        compiler_params=params(8), name="unit_keep",
    )(embeddings, ids, scale)
    packed, code = pl.pallas_call(
        functools.partial(pack_kernel, block),
        out_shape=(shape((CHIPS, block, WIDTH), bf16), shape((8, ROWS), i32)),
        in_specs=[WHOLE, WHOLE], out_specs=(WHOLE, WHOLE), compiler_params=params(20), name="pack",
    )(keep, got)
    packed = lax.all_to_all(packed, ("x", "z", "y"), 0, 0, tiled=True)
    table = shape((CHIPS, LANES), i32)
    guests, line, key, pos, meta = pl.pallas_call(
        functools.partial(names_kernel, block),
        out_shape=(shape((GUESTS, WIDTH), bf16), shape((8, CHIPS * block), i32), table, table, shape((8, LANES), i32)),
        in_specs=[WHOLE], out_specs=(WHOLE,) * 5, compiler_params=params(12), name="names",
    )(packed)
    brought = lax.ppermute(guests, "z", [(i, (i + 3) % 4) for i in range(4)])
    share = shape((SHARE_ROWS, WIDTH), bf16)
    send, mine = pl.pallas_call(
        functools.partial(sort_kernel, block), out_shape=(share, share),
        in_specs=[WHOLE] * 2, out_specs=(WHOLE,) * 2, compiler_params=params(24), name="sort",
    )(packed, line)
    brought, mine, send = lax.optimization_barrier((brought, mine, send))
    other = lax.ppermute(send, "c", [(0, 1), (1, 0)])
    swapped = lax.ppermute(brought, "c", [(0, 1), (1, 0)])
    raw, far = pl.pallas_call(
        own_kernel, out_shape=(shape((RAW_ROWS, LANES), f32), shape((8, GUESTS), i32)),
        in_specs=[WHOLE] * 4, out_specs=(WHOLE,) * 2,
        scratch_shapes=[pltpu.VMEM((SHARE_ROWS, WIDTH), bf16)],
        compiler_params=params(16), name="own",
        cost_estimate=pl.CostEstimate(flops=2 * RAW_ROWS * LANES * WIDTH, bytes_accessed=4 << 20, transcendentals=0),
    )(mine, brought, key, pos)
    partial = pl.pallas_call(
        functools.partial(gram_kernel, units),
        out_shape=[shape((units * UNIT, LANES), f32)] * 4,
        in_specs=[WHOLE] * 5, out_specs=[WHOLE] * 4,
        scratch_shapes=[pltpu.VMEM((4 * units * UNIT + CAPS[0], LANES), f32), pltpu.VMEM((SHARE_ROWS, WIDTH), bf16)],
        compiler_params=params(16), name="gram",
    )(meta, other, swapped, far, raw)
    arrived = [partial[0]] + [
        lax.ppermute(partial[s], "y", [(i, (i + s) % 4) for i in range(4)]) for s in (2, 1, 3)
    ]
    over, table = pl.pallas_call(
        functools.partial(fit_kernel, block, units),
        out_shape=(shape((8, LANES), i32), shape((4 * units, LANES), i32)),
        in_specs=[WHOLE, WHOLE], out_specs=(WHOLE, WHOLE), compiler_params=params(8), name="fit",
    )(packed, meta)
    arrived, fits, table = lax.optimization_barrier((arrived, over[0, 0] == 0, table))
    best = pl.pallas_call(
        functools.partial(max_kernel, units),
        out_shape=shape((2 * CHIPS, LANES), f32),
        in_specs=[WHOLE] * 6, out_specs=WHOLE, compiler_params=params(8), name="maxima",
    )(table, *arrived, pos)
    back = lax.all_to_all(best.reshape(2 * CHIPS, 1, LANES), ("c", "x", "z", "y"), 0, 0, tiled=True)
    back, fits = lax.optimization_barrier((back, fits))
    best = pl.pallas_call(
        pick_kernel,
        out_shape=shape((1, ROWS), f32),
        in_specs=[WHOLE, WHOLE], out_specs=WHOLE, compiler_params=params(8), name="pick",
    )(back.reshape(2 * CHIPS, LANES), code).reshape(ROWS)
    return best, fits


def on_device(embeddings, cluster_ids, tries=TRIES):
    if not tries:
        return gather_groups(embeddings, cluster_ids)
    best, fits = route(*tries[0], embeddings, cluster_ids)
    return lax.cond(
        fits,
        lambda best, embeddings, cluster_ids: best,
        lambda best, embeddings, cluster_ids: on_device(embeddings, cluster_ids, tries[1:]),
        best, embeddings, cluster_ids,
    )


def solution(mesh):
    axes = ("x", "z", "y", "c")
    grid = Mesh(mesh.devices.reshape(4, 4, 4, 2), axes)
    return jax.shard_map(
        on_device, mesh=grid, in_specs=(P(axes, None), P(axes)), out_specs=P(axes), check_vma=False
    )
```

```python
import functools

import jax
import jax.numpy as jnp
from jax import lax
from jax.experimental import pallas as pl
from jax.experimental.pallas import tpu as pltpu
from jax.sharding import Mesh, PartitionSpec as P

ROWS = 128
HALF_WIDTH = 2048
WIDTH = 512
LABEL_ROWS = 16
BINS = 16
CHIPS = 64
TRIES = ((24, 11), (32, 16))
GROUP = 32
GUESTS = 64
GUEST = 4096
LANES = 128
CAPS = (704, 512, 320, 192)
STARTS = (0, 704, 1216, 1536)
UNIT = 32
SHARES = (
    ((0, 0), (0, 256), (2, 0), (2, 128), (2, 256), (3, 0)),
    ((0, 128), (0, 384), (0, 512), (0, 640), (1, 0), (1, 128), (1, 256), (1, 384), (3, 128)),
)
BASES = ({0: 0, 2: 704, 3: 1024}, {0: -128, 1: 576, 3: 960})
SHARE_ROWS = 1216
SEGMENTS = (
    (0, 128, 0, None), (128, 576, 128, 0), (704, 256, None, 576), (960, 256, None, 832),
    (1216, 320, 704, None), (1536, 128, 1024, None), (1664, 64, 1152, 1088),
)
f32, bf16, i32 = jnp.float32, jnp.bfloat16, jnp.int32
WHOLE = pl.BlockSpec(memory_space=pltpu.VMEM)


def params(mib):
    return pltpu.CompilerParams(vmem_limit_bytes=mib * 1024 * 1024)


def index_on(axis):
    return lax.axis_index(axis)


def iota(shape, dim):
    return lax.broadcasted_iota(i32, shape, dim)


def dot_last(a, b):
    return lax.dot_general(a, b, (((1,), (1,)), ((), ())), preferred_element_type=f32)


def dot(a, b):
    return lax.dot_general(a, b, (((1,), (0,)), ((), ())), preferred_element_type=f32)


def as_bf16(mask):
    return jnp.where(mask, 1.0, 0.0).astype(bf16)


def bin_of(labels):
    rank, residue = labels >> 2, labels & 3
    row, col = rank >> 2, rank & 3
    col = jnp.where((row & 1) == 1, 3 - col, col)
    return 4 * col + ((row - residue) & 3)


def label_rows(ids_ref):
    ids = jnp.concatenate([ids_ref[...].astype(f32), jnp.zeros((1, HALF_WIDTH - ROWS), f32)], axis=1)
    return jnp.broadcast_to(ids, (LABEL_ROWS, HALF_WIDTH)).astype(bf16)


def half_of(core):
    return pl.ds(pl.multiple_of(core * HALF_WIDTH, HALF_WIDTH), HALF_WIDTH)


def unit_send_kernel(x_ref, ids_ref, out_ref, scale_ref):
    x = x_ref[...]
    scale = lax.rsqrt(jnp.sum(x * x, axis=1, keepdims=True) + 1e-06)
    scale_ref[...] = jnp.broadcast_to(scale, scale_ref.shape)
    out_ref[:ROWS, :] = (x_ref[:, half_of(1 - index_on("c"))] * scale).astype(bf16)
    out_ref[ROWS:, :] = label_rows(ids_ref)


def unit_keep_kernel(x_ref, ids_ref, scale_ref, out_ref, half_ref, sem):
    copy = pltpu.make_async_copy(x_ref.at[:, half_of(index_on("c"))], half_ref, sem)
    copy.start()
    out_ref[ROWS:, :] = label_rows(ids_ref)
    copy.wait()
    out_ref[:ROWS, :] = (half_ref[...] * scale_ref[:, :1]).astype(bf16)


def passed_on(over, before):
    once = before(over, 1)
    twice = before(over, 2)
    return jnp.maximum(jnp.maximum(over, 0), jnp.maximum(over + once, over + once + twice))


def pack_kernel(block, keep_ref, got_ref, out_ref, code_ref):
    first = index_on("c") == 0
    kept = jnp.max(keep_ref[ROWS:, :ROWS].astype(f32), axis=0, keepdims=True)
    got = jnp.max(got_ref[ROWS:, :ROWS].astype(f32), axis=0, keepdims=True)
    labels = jnp.concatenate([jnp.where(first, kept, got), jnp.where(first, got, kept)], axis=0).astype(i32)
    bins = bin_of(labels)
    upper = as_bf16(iota((ROWS, ROWS), 0) < iota((ROWS, ROWS), 1))

    def ranks_within(masks):
        member = jnp.concatenate([jnp.where(mask, 1.0, 0.0) for mask in masks], axis=0)
        row, col = iota((member.shape[0],) * 2, 0), iota((member.shape[0],) * 2, 1)
        earlier = dot(as_bf16(((row >> 1) == (col >> 1)) & (col < row)), member.astype(bf16))
        ranks = member * (dot(member.astype(bf16), upper) + jnp.sum(earlier, axis=1, keepdims=True))
        rank = sum(ranks[2 * b:2 * b + 2] for b in range(len(masks)))
        return rank.astype(i32), jnp.sum(member, axis=1, keepdims=True)

    rank, sizes = ranks_within([bins == b for b in range(BINS)])
    quad, line = bins >> 2, bins & 3
    taken = []
    for at in range(4):
        size = jnp.zeros(labels.shape, f32)
        for b in range(at, BINS, 4):
            size = jnp.where(quad == b >> 2, sizes[2 * b:2 * b + 1] + sizes[2 * b + 1:2 * b + 2], size)
        taken.append(size.astype(i32) - (block - 1))
    stays = []
    for at in range(4):
        moved = passed_on(taken[at], lambda _, back: taken[(at - back) & 3])
        stays.append(taken[at] + (block - 1) - moved)

    def of_line(values, which):
        out = values[0]
        for at in range(1, 4):
            out = jnp.where(which == at, values[at], out)
        return out

    stay = of_line(stays, line)
    to_line = jnp.where(rank < stay, line, (line + 1) & 3)
    to_slot = jnp.where(rank < stay, rank, of_line(stays, to_line) + rank - stay)
    placed = to_slot < (block - 1)
    lane = jnp.where(placed, to_line * GROUP + to_slot, -1)
    place = jnp.where(placed, (quad * 4 + to_line) * block + to_slot, -1)
    code_ref[...] = jnp.concatenate([jnp.where(placed, bins * LANES + lane, -1)] * 4, axis=0)
    docs = 2 * ROWS
    flat = lambda v: jnp.concatenate([v[:1], v[1:]], axis=1)
    label_row = flat(labels)
    counts = dot_last(jnp.ones((8, docs), bf16), as_bf16(iota((LANES, docs), 0) == label_row))[:1]
    named = jnp.where(iota((8, docs), 0) == flat(quad), (label_row + 1).astype(f32), 0.0).astype(bf16)
    names = dot_last(named, as_bf16(iota((LANES, docs), 0) == flat(lane)))
    own = jnp.where(first, place[:1], place[1:])
    other = jnp.where(first, place[1:], place[:1])
    onehot = as_bf16(iota((BINS * block, docs), 0) == jnp.concatenate([own, other], axis=1))
    is_last = iota((block, WIDTH), 0) == (block - 1)
    for y in range(4):
        columns = slice(y * WIDTH, (y + 1) * WIDTH)
        x = jnp.concatenate([keep_ref[:ROWS, columns], got_ref[:ROWS, columns]], axis=0)
        packed = dot(onehot, x)
        for b in range(BINS):
            extra = jnp.concatenate([names[b // 4:b // 4 + 1], counts, jnp.zeros((1, 2 * LANES), f32)], axis=1)
            out_ref[4 * b + y] = jnp.where(is_last, extra, packed[b * block:(b + 1) * block]).astype(bf16)


def labels_of(block, x_ref):
    tail = x_ref[:, block - 8:, :2 * LANES].astype(f32)
    tail = jnp.max(jnp.where(iota(tail.shape, 1) == 7, tail, 0.0), axis=1)
    return tail[:, :LANES].astype(i32) - 1, tail[:, LANES:].astype(bf16)


def counts_of(chip_counts):
    row, col = iota((LANES, LANES), 0), iota((LANES, LANES), 1)
    in_bin = (bin_of(row) == col) & (row < 4 * BINS)
    counts = [dot(chip_counts, as_bf16(in_bin & ((row & 3) == r))) for r in range(4)]
    return counts, [jnp.sum(v, axis=0, keepdims=True) for v in counts]


def in_order(sizes):
    a, b = jnp.maximum(sizes[0], sizes[1]), jnp.minimum(sizes[0], sizes[1])
    c, d = jnp.maximum(sizes[2], sizes[3]), jnp.minimum(sizes[2], sizes[3])
    first, e = jnp.maximum(a, c), jnp.minimum(a, c)
    g, fourth = jnp.maximum(b, d), jnp.minimum(b, d)
    return first, jnp.maximum(e, g), jnp.minimum(e, g), fourth


def names_kernel(block, x_ref, guest_ref, line_ref, key_ref, pos_ref, meta_ref):
    z = index_on("z")
    labels, _ = labels_of(block, x_ref)
    row, col = iota((LANES, LANES), 0), iota((LANES, LANES), 1)
    lane = iota(labels.shape, 1)
    group = lane >> 5
    valid = labels >= 0
    home = bin_of(labels) & 3
    at_home = valid & (home == z)
    upper = as_bf16(row < col)
    lower = as_bf16(iota((CHIPS, CHIPS), 1) < iota((CHIPS, CHIPS), 0))
    members, n = [at_home & ((labels & 3) == r) for r in range(4)], []
    for member in members:
        size = jnp.sum(jnp.where(member, 1.0, 0.0), axis=0, keepdims=True)
        n.append(jnp.sum(size, axis=1, keepdims=True))
    wide = lambda v: jnp.broadcast_to(v, (1, LANES))
    meta_ref[...] = jnp.concatenate([wide(v) for v in in_order(n)] * 2, axis=0).astype(i32)
    pos = jnp.full(labels.shape, -1.0, f32)
    for r, member in enumerate(members):
        place = sum(
            jnp.where((n[q] > n[r]) | ((n[q] == n[r]) & (q < r)), 1.0, 0.0) for q in range(4) if q != r
        )
        start = jnp.where(
            place < 0.5, float(STARTS[0]),
            jnp.where(place < 1.5, float(STARTS[1]), jnp.where(place < 2.5, float(STARTS[2]), float(STARTS[3]))),
        )
        member16 = as_bf16(member)
        rank = dot(member16, upper) + jnp.sum(dot(lower, member16), axis=1, keepdims=True)
        pos = jnp.where(member, start + rank, pos)
    pos = pos.astype(i32)
    pos_ref[...] = pos
    guest = valid & (home != group)
    guest16 = as_bf16(guest)
    same = (row >> 5) == (col >> 5)
    turn = dot(guest16, as_bf16(same & (row < col))) + dot(dot(lower, guest16).astype(bf16), as_bf16(same))
    turn = turn.astype(i32)
    away = at_home & (group != z) & (turn < GUESTS)
    key_ref[...] = jnp.where(away, turn, -1)
    per, groups = 16, CHIPS // 16
    value = jnp.where(group == z, jnp.where(guest, GUEST + turn, pos + 1), 0).astype(f32)
    value = pltpu.roll(value, lax.rem(LANES - GROUP * z, LANES), 1)
    value = jnp.where(lane < block, value, 0.0)
    lined = jnp.zeros((8, per * block), f32)
    for t in range(per):
        rows = jnp.concatenate([value[per * g + t:per * g + t + 1] for g in range(groups)] * 2, axis=0)
        rows = jnp.concatenate([rows, jnp.zeros((8, per * block - LANES), f32)], axis=1)
        lined = lined + (pltpu.roll(rows, t * block, 1) if t else rows)
    slots = jnp.concatenate([lined[g:g + 1] for g in range(groups)], axis=1).astype(i32)
    line_ref[...] = jnp.broadcast_to(slots, line_ref.shape)
    onehot = as_bf16(iota((GUESTS, CHIPS * block), 0) + GUEST == slots)
    guest_ref[...] = dot(onehot, x_ref[...].reshape(CHIPS * block, WIDTH)).astype(bf16)


def sorted_rows(segment, slots, x):
    onehot = as_bf16(iota((segment[1], x.shape[0]), 0) + (segment[0] + 1) == slots)
    return dot(onehot, x).astype(bf16)


def sort_kernel(block, x_ref, line_ref, send_ref, mine_ref):
    x = x_ref[...].reshape(CHIPS * block, WIDTH)
    slots = line_ref[:1, :]
    for core in range(2):
        @pl.when(index_on("c") == core)
        def _():
            for segment in SEGMENTS:
                rows = sorted_rows(segment, slots, x)
                for out_ref, at in ((mine_ref, segment[2 + core]), (send_ref, segment[2 + 1 - core])):
                    if at is not None:
                        out_ref[at:at + segment[1], :] = rows


def fit_kernel(block, units, x_ref, meta_ref, over_ref, table_ref):
    _, chip_counts = labels_of(block, x_ref)
    counts, sizes = counts_of(chip_counts)
    ordered = in_order(sizes)
    over = jnp.zeros((1, LANES), f32)
    for size, cap in zip(ordered, CAPS):
        over = jnp.maximum(over, jnp.where(size > cap, 1.0, 0.0))
    for share in SHARES:
        length = 0.0
        for q, first in share:
            rows = jnp.maximum(jnp.floor((ordered[q] + (UNIT - 1.0)) * (1 / UNIT)) - first // UNIT, 0.0)
            length = length + jnp.where(rows >= 3.0, rows - 1.0, rows)
        over = jnp.maximum(over, jnp.where(length > 4 * units, 1.0, 0.0))
    taken = counts[0] + counts[1] + counts[2] + counts[3]
    lane = iota(taken.shape, 1) & 3
    before = lambda v, back: jnp.where(lane >= back, pltpu.roll(v, back, 1), pltpu.roll(v, LANES - 4 + back, 1))
    extra = taken - (block - 1)
    moved = passed_on(extra, before)
    held = jnp.sum(moved, axis=0, keepdims=True)
    over = jnp.maximum(over, jnp.where(held > GUESTS, 1.0, 0.0))
    full = extra + before(extra, 1) + before(extra, 2) + before(extra, 3) > 0
    full = jnp.where(full | (moved > block - 1), 1.0, 0.0)
    over = jnp.maximum(over, jnp.max(full, axis=0, keepdims=True))
    over_ref[...] = jnp.broadcast_to(jnp.max(over, axis=1, keepdims=True), over_ref.shape).astype(i32)
    y, c = index_on("y"), index_on("c")
    blocks, sizes = [], [size_of(meta_ref, q) for q in range(4)]
    for core, share in enumerate(SHARES):
        at = jnp.zeros((), i32)
        for q, first in share:
            length = length_of(sizes[q], first)
            blocks.append((jnp.where((c == core) & (length > 0), at, 4 * units), FIRST_ROW[q] + first // LANES, at))
            at = at + length
    for t in range(units):
        index = y * units + t
        col, start = jnp.asarray(15, i32), jnp.asarray(0, i32)
        for block_start, block_col, block_at in blocks:
            inside = index >= block_start
            col, start = jnp.where(inside, block_col, col), jnp.where(inside, block_at, start)
        turn = index - start
        unit = 4 * col + jnp.where(turn == 0, 2, jnp.where(turn == 1, 1, turn + 1))
        beside = jnp.where(turn == 0, 3 * UNIT, LANES)
        for entry, value in enumerate((unit >> 2, (unit & 3) * UNIT, beside, col)):
            table_ref[4 * t + entry:4 * t + entry + 1, :] = jnp.full((1, LANES), value, i32)


def add_guests(core, base_ref, guest_ref, far_ref, out_ref):
    guests, far = guest_ref[...], far_ref[:1, :]
    filled = max(segment[2 + core] + segment[1] for segment in SEGMENTS if segment[2 + core] is not None)
    if filled < SHARE_ROWS:
        out_ref[filled:, :] = jnp.zeros((SHARE_ROWS - filled, WIDTH), bf16)
    for segment in SEGMENTS:
        at, rows = segment[2 + core], segment[1]
        if at is not None:
            out_ref[at:at + rows, :] = base_ref[at:at + rows, :] + sorted_rows(segment, far, guests)


def blocks_of(core):
    for q, first in SHARES[core]:
        at = BASES[core][q] + first
        yield q, first, pl.ds(at, CAPS[q] - first), pl.ds(at, LANES)


RAW_ROWS = max(sum(CAPS[q] - first for q, first in share) for share in SHARES)


def own_kernel(meta_ref, x_ref, guest_ref, key_ref, pos_ref, raw_ref, far_ref, rows_ref):
    total = jnp.zeros((8, GUESTS), f32)
    step = 16
    for first in range(0, CHIPS, step):
        flat = lambda ref: jnp.concatenate([ref[s:s + 1, :] for s in range(first, first + step)], axis=1)
        places = flat(pos_ref) + 1
        parts = jnp.where(iota((8, step * LANES), 0) == 0, places >> 5, places & 31).astype(f32).astype(bf16)
        total = total + dot_last(parts, as_bf16(iota((GUESTS, step * LANES), 0) == flat(key_ref)))
    far_ref[...] = jnp.broadcast_to((32.0 * total[:1] + total[1:2]).astype(i32), far_ref.shape)
    for core in range(2):
        @pl.when(index_on("c") == core)
        def _():
            add_guests(core, x_ref, guest_ref, far_ref, rows_ref)
            at = 0
            for q, first, left, right in blocks_of(core):
                rows = CAPS[q] - first
                score = dot_last(rows_ref[left, :], rows_ref[right, :])
                size = size_of(meta_ref, q) - first
                i, j = iota(score.shape, 0), iota(score.shape, 1)
                raw_ref[at:at + rows, :] = jnp.where((i < size) & (j < size) & (i != j), score, -4.0)
                at += rows


def size_of(meta_ref, q):
    return jnp.max(meta_ref[q:q + 1, :].astype(f32)).astype(i32)


def length_of(size, first):
    units = jnp.maximum(((size + UNIT - 1) >> 5) - first // UNIT, 0)
    return jnp.where(units >= 3, units - 1, units)


def folded(score):
    away = jnp.full((UNIT, LANES), -4.0, f32) if score.shape[0] < LANES else score[2 * UNIT:3 * UNIT]
    both = jnp.where(iota(away.shape, 1) < 3 * UNIT, away, pltpu.roll(score[:UNIT], 3 * UNIT, 1))
    rest = [score[3 * UNIT:]] if score.shape[0] > 3 * UNIT else []
    return jnp.concatenate([both, score[UNIT:2 * UNIT]] + rest, axis=0)


def gram_kernel(units, meta_ref, x_ref, guest_ref, far_ref, raw_ref, out0, out1, out2, out3, part_ref, rows_ref):
    y, c = index_on("y"), index_on("c")
    part_ref[...] = jnp.full(part_ref.shape, -4.0, f32)
    for core in range(2):
        @pl.when(c == core)
        def _():
            add_guests(core, x_ref, guest_ref, far_ref, rows_ref)
            at, to = 0, jnp.zeros((), i32)
            for q, first, left, right in blocks_of(core):
                rows = CAPS[q] - first
                score = raw_ref[at:at + rows, :] + dot_last(rows_ref[left, :], rows_ref[right, :])
                at += rows
                score = folded(score)
                part_ref[pl.ds(pl.multiple_of(to, UNIT), score.shape[0]), :] = score
                to = jnp.minimum(to + UNIT * length_of(size_of(meta_ref, q), first), 4 * units * UNIT)
    chunk = units * UNIT
    for shift, out in enumerate((out0, out1, out2, out3)):
        out[...] = part_ref[pl.ds(pl.multiple_of(lax.rem(y + shift, 4) * chunk, UNIT), chunk), :]


FIRST_ROW = (0, 6, 10, 13)


def max_kernel(units, table_ref, p0, p1, p2, p3, pos_ref, out_ref):
    best = jnp.full((16, LANES), -1.0, f32)
    sub, lane, row = iota((UNIT, LANES), 0), iota((UNIT, LANES), 1), iota((16, LANES), 0)
    for t in range(units):
        at = slice(t * UNIT, (t + 1) * UNIT)
        block = (p0[at, :] + p1[at, :]) + (p2[at, :] + p3[at, :])
        unit_row, offset, beside, col = (table_ref[4 * t + entry:4 * t + entry + 1, :] for entry in range(4))
        one, two = jnp.where(lane < beside, block, -4.0), jnp.where(lane < beside, -4.0, block)
        along = jnp.max(one, axis=1, keepdims=True)
        along = jnp.max(jnp.where(sub + offset == lane, along, -1.0), axis=0, keepdims=True)
        best = jnp.maximum(best, jnp.where(row == unit_row, along, -1.0))
        down = jnp.max(jnp.maximum(one, pltpu.roll(two, UNIT, 1)), axis=0, keepdims=True)
        best = jnp.maximum(best, jnp.where(row == col, down, -1.0))
    pos = pos_ref[...]
    pos = jnp.where(pos >= STARTS[1], pos + 64, pos)
    pos = jnp.where(pos >= STARTS[3] + 64, pos + 64, pos)
    row, lane = pos >> 7, pos & (LANES - 1)
    out = jnp.full(pos.shape, -1.0, f32)
    for r in range(15):
        value = jnp.broadcast_to(best[r:r + 1, :], pos.shape)
        value = jnp.take_along_axis(value, lane, axis=1, mode="promise_in_bounds")
        out = jnp.where(row == r, value, out)
    out_ref[:CHIPS, :] = out
    out_ref[CHIPS:, :] = out


def pick_kernel(v_ref, code_ref, out_ref):
    values = jnp.maximum(v_ref[:CHIPS, :], v_ref[CHIPS:, :])
    values = jnp.max(values.reshape(BINS, 4, LANES), axis=1)
    code = jnp.max(jnp.where(iota((8, ROWS), 0) == index_on("c"), code_ref[...], -1), axis=0, keepdims=True)
    code = jnp.broadcast_to(code, (8, ROWS))
    row, lane = code >> 7, code & (LANES - 1)
    best = jnp.full((8, ROWS), -1.0, f32)
    for b in range(BINS):
        value = jnp.broadcast_to(values[b:b + 1], (8, ROWS))
        best = jnp.where(row == b, jnp.take_along_axis(value, lane, axis=1, mode="promise_in_bounds"), best)
    out_ref[...] = best[:1]


def gather_groups(embeddings, cluster_ids):
    split = ("z", "y", "c")
    rows = embeddings.shape[0]
    groups = lax.axis_size("x")
    cap = 2 * rows // groups
    slots = groups * cap
    owner_of = cluster_ids % groups
    onehot = (owner_of[:, None] == jnp.arange(groups, dtype=i32)[None, :]).astype(i32)
    before = jnp.cumsum(onehot, axis=0) - onehot
    rank = jnp.sum(before * onehot, axis=1)
    place = owner_of * cap + rank
    picked = place[None, :] == jnp.arange(slots, dtype=i32)[:, None]
    filled = jnp.any(picked, axis=1)
    source = jnp.sum(jnp.where(picked, jnp.arange(rows, dtype=i32)[None, :], 0), axis=1)
    out_labels = jnp.where(filled, cluster_ids[source], -1)
    squares = jnp.sum(embeddings * embeddings, axis=1, keepdims=True)
    local_unit = (embeddings * lax.rsqrt(squares + 1e-06)).astype(bf16)
    outgoing_unit = jnp.where(filled[:, None], local_unit[source], jnp.zeros((), bf16))
    unit = lax.all_to_all(outgoing_unit, "x", split_axis=0, concat_axis=0, tiled=True)
    labels = lax.all_to_all(out_labels, "x", split_axis=0, concat_axis=0, tiled=True)
    members = lax.axis_size(split)

    def everywhere(v):
        copies = jnp.broadcast_to(v[None], (members,) + v.shape).reshape((members * slots,) + v.shape[1:])
        return lax.all_to_all(copies, split, split_axis=0, concat_axis=0, tiled=True)

    def add_slice(i, scores):
        part = lax.dynamic_slice_in_dim(unit, i * WIDTH, WIDTH, 1)
        return scores + dot_last(part, everywhere(part))

    scores = lax.fori_loop(0, embeddings.shape[1] // WIDTH, add_slice, jnp.zeros((slots, members * slots), f32))
    all_labels = everywhere(labels)
    own = lax.axis_index(split) * slots + jnp.arange(slots, dtype=i32)
    mask = (
        (labels[:, None] == all_labels[None, :])
        & (labels[:, None] >= 0)
        & (own[:, None] != jnp.arange(members * slots, dtype=i32)[None, :])
    )
    scores = jnp.where(mask, scores, -1.0)
    best = jnp.maximum(-1.0, jnp.max(scores, axis=1))
    returned = lax.all_to_all(best, "x", split_axis=0, concat_axis=0, tiled=True)
    return returned[place]


def route(block, units, embeddings, cluster_ids):
    shape = jax.ShapeDtypeStruct
    half = shape((ROWS + LABEL_ROWS, HALF_WIDTH), bf16)
    ids = cluster_ids.reshape(1, ROWS)
    send, scale = pl.pallas_call(
        unit_send_kernel, out_shape=(half, shape((ROWS, LANES), f32)),
        in_specs=[WHOLE, WHOLE], out_specs=(WHOLE, WHOLE), compiler_params=params(12), name="unit_send",
    )(embeddings, ids)
    got = lax.ppermute(send, "c", [(0, 1), (1, 0)])
    keep = pl.pallas_call(
        unit_keep_kernel, out_shape=half,
        in_specs=[pl.BlockSpec(memory_space=pl.ANY), WHOLE, WHOLE], out_specs=WHOLE,
        scratch_shapes=[pltpu.VMEM((ROWS, HALF_WIDTH), f32), pltpu.SemaphoreType.DMA],
        compiler_params=params(8), name="unit_keep",
    )(embeddings, ids, scale)
    packed, code = pl.pallas_call(
        functools.partial(pack_kernel, block),
        out_shape=(shape((CHIPS, block, WIDTH), bf16), shape((8, ROWS), i32)),
        in_specs=[WHOLE, WHOLE], out_specs=(WHOLE, WHOLE), compiler_params=params(20), name="pack",
    )(keep, got)
    packed = lax.all_to_all(packed, ("x", "z", "y"), 0, 0, tiled=True)
    table = shape((CHIPS, LANES), i32)
    guests, line, key, pos, meta = pl.pallas_call(
        functools.partial(names_kernel, block),
        out_shape=(shape((GUESTS, WIDTH), bf16), shape((8, CHIPS * block), i32), table, table, shape((8, LANES), i32)),
        in_specs=[WHOLE], out_specs=(WHOLE,) * 5, compiler_params=params(12), name="names",
    )(packed)
    brought = lax.ppermute(guests, "z", [(i, (i + 3) % 4) for i in range(4)])
    share = shape((SHARE_ROWS, WIDTH), bf16)
    send, mine = pl.pallas_call(
        functools.partial(sort_kernel, block), out_shape=(share, share),
        in_specs=[WHOLE] * 2, out_specs=(WHOLE,) * 2, compiler_params=params(24), name="sort",
    )(packed, line)
    brought, mine, send = lax.optimization_barrier((brought, mine, send))
    other = lax.ppermute(send, "c", [(0, 1), (1, 0)])
    swapped = lax.ppermute(brought, "c", [(0, 1), (1, 0)])
    raw, far = pl.pallas_call(
        own_kernel, out_shape=(shape((RAW_ROWS, LANES), f32), shape((8, GUESTS), i32)),
        in_specs=[WHOLE] * 5, out_specs=(WHOLE,) * 2,
        scratch_shapes=[pltpu.VMEM((SHARE_ROWS, WIDTH), bf16)],
        compiler_params=params(16), name="own",
        cost_estimate=pl.CostEstimate(flops=2 * RAW_ROWS * LANES * WIDTH, bytes_accessed=4 << 20, transcendentals=0),
    )(meta, mine, brought, key, pos)
    partial = pl.pallas_call(
        functools.partial(gram_kernel, units),
        out_shape=[shape((units * UNIT, LANES), f32)] * 4,
        in_specs=[WHOLE] * 5, out_specs=[WHOLE] * 4,
        scratch_shapes=[pltpu.VMEM((4 * units * UNIT + CAPS[0], LANES), f32), pltpu.VMEM((SHARE_ROWS, WIDTH), bf16)],
        compiler_params=params(16), name="gram",
    )(meta, other, swapped, far, raw)
    arrived = [partial[0]] + [
        lax.ppermute(partial[s], "y", [(i, (i + s) % 4) for i in range(4)]) for s in (2, 1, 3)
    ]
    over, table = pl.pallas_call(
        functools.partial(fit_kernel, block, units),
        out_shape=(shape((8, LANES), i32), shape((4 * units, LANES), i32)),
        in_specs=[WHOLE, WHOLE], out_specs=(WHOLE, WHOLE), compiler_params=params(8), name="fit",
    )(packed, meta)
    arrived, fits, table = lax.optimization_barrier((arrived, over[0, 0] == 0, table))
    best = pl.pallas_call(
        functools.partial(max_kernel, units),
        out_shape=shape((2 * CHIPS, LANES), f32),
        in_specs=[WHOLE] * 6, out_specs=WHOLE, compiler_params=params(8), name="maxima",
    )(table, *arrived, pos)
    back = lax.all_to_all(best.reshape(2 * CHIPS, 1, LANES), ("c", "x", "z", "y"), 0, 0, tiled=True)
    back, fits = lax.optimization_barrier((back, fits))
    best = pl.pallas_call(
        pick_kernel,
        out_shape=shape((1, ROWS), f32),
        in_specs=[WHOLE, WHOLE], out_specs=WHOLE, compiler_params=params(8), name="pick",
    )(back.reshape(2 * CHIPS, LANES), code).reshape(ROWS)
    return best, fits


def on_device(embeddings, cluster_ids, tries=TRIES):
    if not tries:
        return gather_groups(embeddings, cluster_ids)
    best, fits = route(*tries[0], embeddings, cluster_ids)
    return lax.cond(
        fits,
        lambda best, embeddings, cluster_ids: best,
        lambda best, embeddings, cluster_ids: on_device(embeddings, cluster_ids, tries[1:]),
        best, embeddings, cluster_ids,
    )


def solution(mesh):
    axes = ("x", "z", "y", "c")
    grid = Mesh(mesh.devices.reshape(4, 4, 4, 2), axes)
    return jax.shard_map(
        on_device, mesh=grid, in_specs=(P(axes, None), P(axes)), out_specs=P(axes), check_vma=False
    )
```

```python
import functools

import jax
import jax.numpy as jnp
from jax import lax
from jax.experimental import pallas as pl
from jax.experimental.pallas import tpu as pltpu
from jax.sharding import Mesh, PartitionSpec as P

ROWS = 128
HALF_WIDTH = 2048
WIDTH = 512
LABEL_ROWS = 16
BINS = 16
CHIPS = 64
TRIES = ((24, 11), (32, 16))
GROUP = 32
GUESTS = 64
GUEST = 4096
LANES = 128
CAPS = (704, 512, 320, 192)
STARTS = (0, 704, 1216, 1536)
UNIT = 32
SHARES = (
    ((0, 0), (0, 256), (2, 0), (2, 128), (2, 256), (3, 0)),
    ((0, 128), (0, 384), (0, 512), (0, 640), (1, 0), (1, 128), (1, 256), (1, 384), (3, 128)),
)
BASES = ({0: 0, 2: 704, 3: 1024}, {0: -128, 1: 576, 3: 960})
SHARE_ROWS = 1216
SEGMENTS = (
    (0, 128, 0, None), (128, 576, 128, 0), (704, 256, None, 576), (960, 256, None, 832),
    (1216, 320, 704, None), (1536, 128, 1024, None), (1664, 64, 1152, 1088),
)
f32, bf16, i32 = jnp.float32, jnp.bfloat16, jnp.int32
WHOLE = pl.BlockSpec(memory_space=pltpu.VMEM)


def params(mib):
    return pltpu.CompilerParams(vmem_limit_bytes=mib * 1024 * 1024)


def index_on(axis):
    return lax.axis_index(axis)


def iota(shape, dim):
    return lax.broadcasted_iota(i32, shape, dim)


def dot_last(a, b):
    return lax.dot_general(a, b, (((1,), (1,)), ((), ())), preferred_element_type=f32)


def dot(a, b):
    return lax.dot_general(a, b, (((1,), (0,)), ((), ())), preferred_element_type=f32)


def as_bf16(mask):
    return jnp.where(mask, 1.0, 0.0).astype(bf16)


def bin_of(labels):
    rank, residue = labels >> 2, labels & 3
    row, col = rank >> 2, rank & 3
    col = jnp.where((row & 1) == 1, 3 - col, col)
    return 4 * col + ((row - residue) & 3)


def label_rows(ids_ref):
    ids = jnp.concatenate([ids_ref[...].astype(f32), jnp.zeros((1, HALF_WIDTH - ROWS), f32)], axis=1)
    return jnp.broadcast_to(ids, (LABEL_ROWS, HALF_WIDTH)).astype(bf16)


def half_of(core):
    return pl.ds(pl.multiple_of(core * HALF_WIDTH, HALF_WIDTH), HALF_WIDTH)


def unit_send_kernel(x_ref, ids_ref, out_ref, scale_ref):
    x = x_ref[...]
    scale = lax.rsqrt(jnp.sum(x * x, axis=1, keepdims=True) + 1e-06)
    scale_ref[...] = jnp.broadcast_to(scale, scale_ref.shape)
    out_ref[:ROWS, :] = (x_ref[:, half_of(1 - index_on("c"))] * scale).astype(bf16)
    out_ref[ROWS:, :] = label_rows(ids_ref)


def unit_keep_kernel(x_ref, ids_ref, scale_ref, out_ref, half_ref, sem):
    copy = pltpu.make_async_copy(x_ref.at[:, half_of(index_on("c"))], half_ref, sem)
    copy.start()
    out_ref[ROWS:, :] = label_rows(ids_ref)
    copy.wait()
    out_ref[:ROWS, :] = (half_ref[...] * scale_ref[:, :1]).astype(bf16)


def passed_on(over, before):
    once = before(over, 1)
    twice = before(over, 2)
    return jnp.maximum(jnp.maximum(over, 0), jnp.maximum(over + once, over + once + twice))


def pack_kernel(block, keep_ref, got_ref, out_ref, code_ref):
    first = index_on("c") == 0
    kept = jnp.max(keep_ref[ROWS:, :ROWS].astype(f32), axis=0, keepdims=True)
    got = jnp.max(got_ref[ROWS:, :ROWS].astype(f32), axis=0, keepdims=True)
    labels = jnp.concatenate([jnp.where(first, kept, got), jnp.where(first, got, kept)], axis=0).astype(i32)
    bins = bin_of(labels)
    upper = as_bf16(iota((ROWS, ROWS), 0) < iota((ROWS, ROWS), 1))

    def ranks_within(masks):
        member = jnp.concatenate([jnp.where(mask, 1.0, 0.0) for mask in masks], axis=0)
        row, col = iota((member.shape[0],) * 2, 0), iota((member.shape[0],) * 2, 1)
        earlier = dot(as_bf16(((row >> 1) == (col >> 1)) & (col < row)), member.astype(bf16))
        ranks = member * (dot(member.astype(bf16), upper) + jnp.sum(earlier, axis=1, keepdims=True))
        rank = sum(ranks[2 * b:2 * b + 2] for b in range(len(masks)))
        return rank.astype(i32), jnp.sum(member, axis=1, keepdims=True)

    rank, sizes = ranks_within([bins == b for b in range(BINS)])
    quad, line = bins >> 2, bins & 3
    taken = []
    for at in range(4):
        size = jnp.zeros(labels.shape, f32)
        for b in range(at, BINS, 4):
            size = jnp.where(quad == b >> 2, sizes[2 * b:2 * b + 1] + sizes[2 * b + 1:2 * b + 2], size)
        taken.append(size.astype(i32) - (block - 1))
    stays = []
    for at in range(4):
        moved = passed_on(taken[at], lambda _, back: taken[(at - back) & 3])
        stays.append(taken[at] + (block - 1) - moved)

    def of_line(values, which):
        out = values[0]
        for at in range(1, 4):
            out = jnp.where(which == at, values[at], out)
        return out

    stay = of_line(stays, line)
    to_line = jnp.where(rank < stay, line, (line + 1) & 3)
    to_slot = jnp.where(rank < stay, rank, of_line(stays, to_line) + rank - stay)
    placed = to_slot < (block - 1)
    lane = jnp.where(placed, to_line * GROUP + to_slot, -1)
    place = jnp.where(placed, (quad * 4 + to_line) * block + to_slot, -1)
    code_ref[...] = jnp.concatenate([jnp.where(placed, bins * LANES + lane, -1)] * 4, axis=0)
    docs = 2 * ROWS
    flat = lambda v: jnp.concatenate([v[:1], v[1:]], axis=1)
    label_row = flat(labels)
    counts = dot_last(jnp.ones((8, docs), bf16), as_bf16(iota((LANES, docs), 0) == label_row))[:1]
    named = jnp.where(iota((8, docs), 0) == flat(quad), (label_row + 1).astype(f32), 0.0).astype(bf16)
    names = dot_last(named, as_bf16(iota((LANES, docs), 0) == flat(lane)))
    own = jnp.where(first, place[:1], place[1:])
    other = jnp.where(first, place[1:], place[:1])
    onehot = as_bf16(iota((BINS * block, docs), 0) == jnp.concatenate([own, other], axis=1))
    is_last = iota((block, WIDTH), 0) == (block - 1)
    for y in range(4):
        columns = slice(y * WIDTH, (y + 1) * WIDTH)
        x = jnp.concatenate([keep_ref[:ROWS, columns], got_ref[:ROWS, columns]], axis=0)
        packed = dot(onehot, x)
        for b in range(BINS):
            extra = jnp.concatenate([names[b // 4:b // 4 + 1], counts, jnp.zeros((1, 2 * LANES), f32)], axis=1)
            out_ref[4 * b + y] = jnp.where(is_last, extra, packed[b * block:(b + 1) * block]).astype(bf16)


def labels_of(block, x_ref):
    tail = x_ref[:, block - 8:, :2 * LANES].astype(f32)
    tail = jnp.max(jnp.where(iota(tail.shape, 1) == 7, tail, 0.0), axis=1)
    return tail[:, :LANES].astype(i32) - 1, tail[:, LANES:].astype(bf16)


def counts_of(chip_counts):
    row, col = iota((LANES, LANES), 0), iota((LANES, LANES), 1)
    in_bin = (bin_of(row) == col) & (row < 4 * BINS)
    counts = [dot(chip_counts, as_bf16(in_bin & ((row & 3) == r))) for r in range(4)]
    return counts, [jnp.sum(v, axis=0, keepdims=True) for v in counts]


def in_order(sizes):
    a, b = jnp.maximum(sizes[0], sizes[1]), jnp.minimum(sizes[0], sizes[1])
    c, d = jnp.maximum(sizes[2], sizes[3]), jnp.minimum(sizes[2], sizes[3])
    first, e = jnp.maximum(a, c), jnp.minimum(a, c)
    g, fourth = jnp.maximum(b, d), jnp.minimum(b, d)
    return first, jnp.maximum(e, g), jnp.minimum(e, g), fourth


def names_kernel(block, x_ref, guest_ref, line_ref, key_ref, pos_ref, meta_ref):
    z = index_on("z")
    labels, _ = labels_of(block, x_ref)
    row, col = iota((LANES, LANES), 0), iota((LANES, LANES), 1)
    lane = iota(labels.shape, 1)
    group = lane >> 5
    valid = labels >= 0
    home = bin_of(labels) & 3
    at_home = valid & (home == z)
    upper = as_bf16(row < col)
    lower = as_bf16(iota((CHIPS, CHIPS), 1) < iota((CHIPS, CHIPS), 0))
    members, n = [at_home & ((labels & 3) == r) for r in range(4)], []
    for member in members:
        size = jnp.sum(jnp.where(member, 1.0, 0.0), axis=0, keepdims=True)
        n.append(jnp.sum(size, axis=1, keepdims=True))
    wide = lambda v: jnp.broadcast_to(v, (1, LANES))
    meta_ref[...] = jnp.concatenate([wide(v) for v in in_order(n)] * 2, axis=0).astype(i32)
    guest = valid & (home != group)
    guest16, members16 = as_bf16(guest), [as_bf16(member) for member in members]
    along = dot(jnp.concatenate(members16, axis=0), upper)
    earlier = dot(lower, jnp.concatenate(members16 + [guest16], axis=1))
    pos = jnp.full(labels.shape, -1.0, f32)
    for r, member in enumerate(members):
        place = sum(
            jnp.where((n[q] > n[r]) | ((n[q] == n[r]) & (q < r)), 1.0, 0.0) for q in range(4) if q != r
        )
        start = jnp.where(
            place < 0.5, float(STARTS[0]),
            jnp.where(place < 1.5, float(STARTS[1]), jnp.where(place < 2.5, float(STARTS[2]), float(STARTS[3]))),
        )
        rank = along[CHIPS * r:CHIPS * (r + 1)] + jnp.sum(
            earlier[:, LANES * r:LANES * (r + 1)], axis=1, keepdims=True)
        pos = jnp.where(member, start + rank, pos)
    pos = pos.astype(i32)
    pos_ref[...] = pos
    same = (row >> 5) == (col >> 5)
    turn = dot(guest16, as_bf16(same & (row < col))) + dot(earlier[:, 4 * LANES:].astype(bf16), as_bf16(same))
    turn = turn.astype(i32)
    away = at_home & (group != z) & (turn < GUESTS)
    key_ref[...] = jnp.where(away, turn, -1)
    per, groups = 16, CHIPS // 16
    value = jnp.where(group == z, jnp.where(guest, GUEST + turn, pos + 1), 0).astype(f32)
    value = pltpu.roll(value, lax.rem(LANES - GROUP * z, LANES), 1)
    value = jnp.where(lane < block, value, 0.0)
    lined = jnp.zeros((8, per * block), f32)
    for t in range(per):
        rows = jnp.concatenate([value[per * g + t:per * g + t + 1] for g in range(groups)] * 2, axis=0)
        rows = jnp.concatenate([rows, jnp.zeros((8, per * block - LANES), f32)], axis=1)
        lined = lined + (pltpu.roll(rows, t * block, 1) if t else rows)
    slots = jnp.concatenate([lined[g:g + 1] for g in range(groups)], axis=1).astype(i32)
    line_ref[...] = jnp.broadcast_to(slots, line_ref.shape)
    onehot = as_bf16(iota((GUESTS, CHIPS * block), 0) + GUEST == slots)
    guest_ref[...] = dot(onehot, x_ref[...].reshape(CHIPS * block, WIDTH)).astype(bf16)


def sorted_rows(segment, slots, x):
    onehot = as_bf16(iota((segment[1], x.shape[0]), 0) + (segment[0] + 1) == slots)
    return dot(onehot, x).astype(bf16)


def sort_kernel(block, x_ref, line_ref, send_ref, mine_ref):
    x = x_ref[...].reshape(CHIPS * block, WIDTH)
    slots = line_ref[:1, :]
    for core in range(2):
        @pl.when(index_on("c") == core)
        def _():
            for segment in SEGMENTS:
                rows = sorted_rows(segment, slots, x)
                for out_ref, at in ((mine_ref, segment[2 + core]), (send_ref, segment[2 + 1 - core])):
                    if at is not None:
                        out_ref[at:at + segment[1], :] = rows


def fit_kernel(block, units, x_ref, meta_ref, over_ref, table_ref):
    _, chip_counts = labels_of(block, x_ref)
    counts, sizes = counts_of(chip_counts)
    ordered = in_order(sizes)
    over = jnp.zeros((1, LANES), f32)
    for size, cap in zip(ordered, CAPS):
        over = jnp.maximum(over, jnp.where(size > cap, 1.0, 0.0))
    for share in SHARES:
        length = 0.0
        for q, first in share:
            rows = jnp.maximum(jnp.floor((ordered[q] + (UNIT - 1.0)) * (1 / UNIT)) - first // UNIT, 0.0)
            length = length + jnp.where(rows >= 3.0, rows - 1.0, rows)
        over = jnp.maximum(over, jnp.where(length > 4 * units, 1.0, 0.0))
    taken = counts[0] + counts[1] + counts[2] + counts[3]
    lane = iota(taken.shape, 1) & 3
    before = lambda v, back: jnp.where(lane >= back, pltpu.roll(v, back, 1), pltpu.roll(v, LANES - 4 + back, 1))
    extra = taken - (block - 1)
    moved = passed_on(extra, before)
    held = jnp.sum(moved, axis=0, keepdims=True)
    over = jnp.maximum(over, jnp.where(held > GUESTS, 1.0, 0.0))
    full = extra + before(extra, 1) + before(extra, 2) + before(extra, 3) > 0
    full = jnp.where(full | (moved > block - 1), 1.0, 0.0)
    over = jnp.maximum(over, jnp.max(full, axis=0, keepdims=True))
    over_ref[...] = jnp.broadcast_to(jnp.max(over, axis=1, keepdims=True), over_ref.shape).astype(i32)
    y, c = index_on("y"), index_on("c")
    blocks, sizes = [], [size_of(meta_ref, q) for q in range(4)]
    for core, share in enumerate(SHARES):
        at = jnp.zeros((), i32)
        for q, first in share:
            length = length_of(sizes[q], first)
            blocks.append((jnp.where((c == core) & (length > 0), at, 4 * units), FIRST_ROW[q] + first // LANES, at))
            at = at + length
    for t in range(units):
        index = y * units + t
        col, start = jnp.asarray(15, i32), jnp.asarray(0, i32)
        for block_start, block_col, block_at in blocks:
            inside = index >= block_start
            col, start = jnp.where(inside, block_col, col), jnp.where(inside, block_at, start)
        turn = index - start
        unit = 4 * col + jnp.where(turn == 0, 2, jnp.where(turn == 1, 1, turn + 1))
        beside = jnp.where(turn == 0, 3 * UNIT, LANES)
        for entry, value in enumerate((unit >> 2, (unit & 3) * UNIT, beside, col)):
            table_ref[4 * t + entry:4 * t + entry + 1, :] = jnp.full((1, LANES), value, i32)


def add_guests(core, base_ref, guest_ref, far_ref, out_ref):
    guests, far = guest_ref[...], far_ref[:1, :]
    for segment in SEGMENTS:
        at, rows = segment[2 + core], segment[1]
        if at is not None:
            out_ref[at:at + rows, :] = base_ref[at:at + rows, :] + sorted_rows(segment, far, guests)


def blocks_of(core):
    for q, first in SHARES[core]:
        at = BASES[core][q] + first
        yield q, first, pl.ds(at, CAPS[q] - first), pl.ds(at, LANES)


RAW_ROWS = max(sum(CAPS[q] - first for q, first in share) for share in SHARES)


def own_kernel(x_ref, guest_ref, key_ref, pos_ref, raw_ref, far_ref, rows_ref):
    total = jnp.zeros((8, GUESTS), f32)
    step = 16
    for first in range(0, CHIPS, step):
        flat = lambda ref: jnp.concatenate([ref[s:s + 1, :] for s in range(first, first + step)], axis=1)
        places = flat(pos_ref) + 1
        parts = jnp.where(iota((8, step * LANES), 0) == 0, places >> 5, places & 31).astype(f32).astype(bf16)
        total = total + dot_last(parts, as_bf16(iota((GUESTS, step * LANES), 0) == flat(key_ref)))
    far_ref[...] = jnp.broadcast_to((32.0 * total[:1] + total[1:2]).astype(i32), far_ref.shape)
    for core in range(2):
        @pl.when(index_on("c") == core)
        def _():
            add_guests(core, x_ref, guest_ref, far_ref, rows_ref)
            at = 0
            for q, first, left, right in blocks_of(core):
                rows = CAPS[q] - first
                raw_ref[at:at + rows, :] = dot_last(rows_ref[left, :], rows_ref[right, :])
                at += rows


def size_of(meta_ref, q):
    return jnp.max(meta_ref[q:q + 1, :].astype(f32)).astype(i32)


def length_of(size, first):
    units = jnp.maximum(((size + UNIT - 1) >> 5) - first // UNIT, 0)
    return jnp.where(units >= 3, units - 1, units)


def folded(score):
    away = jnp.full((UNIT, LANES), -4.0, f32) if score.shape[0] < LANES else score[2 * UNIT:3 * UNIT]
    both = jnp.where(iota(away.shape, 1) < 3 * UNIT, away, pltpu.roll(score[:UNIT], 3 * UNIT, 1))
    rest = [score[3 * UNIT:]] if score.shape[0] > 3 * UNIT else []
    return jnp.concatenate([both, score[UNIT:2 * UNIT]] + rest, axis=0)


def gram_kernel(units, meta_ref, x_ref, guest_ref, far_ref, raw_ref, out0, out1, out2, out3, part_ref, rows_ref):
    y, c = index_on("y"), index_on("c")
    part_ref[...] = jnp.full(part_ref.shape, -4.0, f32)
    for core in range(2):
        @pl.when(c == core)
        def _():
            add_guests(core, x_ref, guest_ref, far_ref, rows_ref)
            at, to = 0, jnp.zeros((), i32)
            for q, first, left, right in blocks_of(core):
                rows = CAPS[q] - first
                score = raw_ref[at:at + rows, :] + dot_last(rows_ref[left, :], rows_ref[right, :])
                at += rows
                size = size_of(meta_ref, q)
                i, j = iota(score.shape, 0), iota(score.shape, 1)
                keep = (i < size - first) & (j < size - first) & (i != j)
                score = folded(jnp.where(keep, score, -4.0))
                part_ref[pl.ds(pl.multiple_of(to, UNIT), score.shape[0]), :] = score
                to = jnp.minimum(to + UNIT * length_of(size, first), 4 * units * UNIT)
    chunk = units * UNIT
    for shift, out in enumerate((out0, out1, out2, out3)):
        out[...] = part_ref[pl.ds(pl.multiple_of(lax.rem(y + shift, 4) * chunk, UNIT), chunk), :]


FIRST_ROW = (0, 6, 10, 13)


def max_kernel(units, table_ref, p0, p1, p2, p3, pos_ref, out_ref):
    best = jnp.full((16, LANES), -1.0, f32)
    sub, lane, row = iota((UNIT, LANES), 0), iota((UNIT, LANES), 1), iota((16, LANES), 0)
    for t in range(units):
        at = slice(t * UNIT, (t + 1) * UNIT)
        block = (p0[at, :] + p1[at, :]) + (p2[at, :] + p3[at, :])
        unit_row, offset, beside, col = (table_ref[4 * t + entry:4 * t + entry + 1, :] for entry in range(4))
        one, two = jnp.where(lane < beside, block, -4.0), jnp.where(lane < beside, -4.0, block)
        along = jnp.max(one, axis=1, keepdims=True)
        along = jnp.max(jnp.where(sub + offset == lane, along, -1.0), axis=0, keepdims=True)
        best = jnp.maximum(best, jnp.where(row == unit_row, along, -1.0))
        down = jnp.max(jnp.maximum(one, pltpu.roll(two, UNIT, 1)), axis=0, keepdims=True)
        best = jnp.maximum(best, jnp.where(row == col, down, -1.0))
    pos = pos_ref[...]
    pos = jnp.where(pos >= STARTS[1], pos + 64, pos)
    pos = jnp.where(pos >= STARTS[3] + 64, pos + 64, pos)
    row, lane = pos >> 7, pos & (LANES - 1)
    out = jnp.full(pos.shape, -1.0, f32)
    for r in range(15):
        value = jnp.broadcast_to(best[r:r + 1, :], pos.shape)
        value = jnp.take_along_axis(value, lane, axis=1, mode="promise_in_bounds")
        out = jnp.where(row == r, value, out)
    out_ref[:CHIPS, :] = out
    out_ref[CHIPS:, :] = out


def pick_kernel(v_ref, code_ref, out_ref):
    values = jnp.maximum(v_ref[:CHIPS, :], v_ref[CHIPS:, :])
    values = jnp.max(values.reshape(BINS, 4, LANES), axis=1)
    code = jnp.max(jnp.where(iota((8, ROWS), 0) == index_on("c"), code_ref[...], -1), axis=0, keepdims=True)
    code = jnp.broadcast_to(code, (8, ROWS))
    row, lane = code >> 7, code & (LANES - 1)
    best = jnp.full((8, ROWS), -1.0, f32)
    for b in range(BINS):
        value = jnp.broadcast_to(values[b:b + 1], (8, ROWS))
        best = jnp.where(row == b, jnp.take_along_axis(value, lane, axis=1, mode="promise_in_bounds"), best)
    out_ref[...] = best[:1]


def gather_groups(embeddings, cluster_ids):
    split = ("z", "y", "c")
    rows = embeddings.shape[0]
    groups = lax.axis_size("x")
    cap = 2 * rows // groups
    slots = groups * cap
    owner_of = cluster_ids % groups
    onehot = (owner_of[:, None] == jnp.arange(groups, dtype=i32)[None, :]).astype(i32)
    before = jnp.cumsum(onehot, axis=0) - onehot
    rank = jnp.sum(before * onehot, axis=1)
    place = owner_of * cap + rank
    picked = place[None, :] == jnp.arange(slots, dtype=i32)[:, None]
    filled = jnp.any(picked, axis=1)
    source = jnp.sum(jnp.where(picked, jnp.arange(rows, dtype=i32)[None, :], 0), axis=1)
    out_labels = jnp.where(filled, cluster_ids[source], -1)
    squares = jnp.sum(embeddings * embeddings, axis=1, keepdims=True)
    local_unit = (embeddings * lax.rsqrt(squares + 1e-06)).astype(bf16)
    outgoing_unit = jnp.where(filled[:, None], local_unit[source], jnp.zeros((), bf16))
    unit = lax.all_to_all(outgoing_unit, "x", split_axis=0, concat_axis=0, tiled=True)
    labels = lax.all_to_all(out_labels, "x", split_axis=0, concat_axis=0, tiled=True)
    members = lax.axis_size(split)

    def everywhere(v):
        copies = jnp.broadcast_to(v[None], (members,) + v.shape).reshape((members * slots,) + v.shape[1:])
        return lax.all_to_all(copies, split, split_axis=0, concat_axis=0, tiled=True)

    def add_slice(i, scores):
        part = lax.dynamic_slice_in_dim(unit, i * WIDTH, WIDTH, 1)
        return scores + dot_last(part, everywhere(part))

    scores = lax.fori_loop(0, embeddings.shape[1] // WIDTH, add_slice, jnp.zeros((slots, members * slots), f32))
    all_labels = everywhere(labels)
    own = lax.axis_index(split) * slots + jnp.arange(slots, dtype=i32)
    mask = (
        (labels[:, None] == all_labels[None, :])
        & (labels[:, None] >= 0)
        & (own[:, None] != jnp.arange(members * slots, dtype=i32)[None, :])
    )
    scores = jnp.where(mask, scores, -1.0)
    best = jnp.maximum(-1.0, jnp.max(scores, axis=1))
    returned = lax.all_to_all(best, "x", split_axis=0, concat_axis=0, tiled=True)
    return returned[place]


def route(block, units, embeddings, cluster_ids):
    shape = jax.ShapeDtypeStruct
    half = shape((ROWS + LABEL_ROWS, HALF_WIDTH), bf16)
    ids = cluster_ids.reshape(1, ROWS)
    send, scale = pl.pallas_call(
        unit_send_kernel, out_shape=(half, shape((ROWS, LANES), f32)),
        in_specs=[WHOLE, WHOLE], out_specs=(WHOLE, WHOLE), compiler_params=params(12), name="unit_send",
    )(embeddings, ids)
    got = lax.ppermute(send, "c", [(0, 1), (1, 0)])
    keep = pl.pallas_call(
        unit_keep_kernel, out_shape=half,
        in_specs=[pl.BlockSpec(memory_space=pl.ANY), WHOLE, WHOLE], out_specs=WHOLE,
        scratch_shapes=[pltpu.VMEM((ROWS, HALF_WIDTH), f32), pltpu.SemaphoreType.DMA],
        compiler_params=params(8), name="unit_keep",
    )(embeddings, ids, scale)
    packed, code = pl.pallas_call(
        functools.partial(pack_kernel, block),
        out_shape=(shape((CHIPS, block, WIDTH), bf16), shape((8, ROWS), i32)),
        in_specs=[WHOLE, WHOLE], out_specs=(WHOLE, WHOLE), compiler_params=params(20), name="pack",
    )(keep, got)
    packed = lax.all_to_all(packed, ("x", "z", "y"), 0, 0, tiled=True)
    table = shape((CHIPS, LANES), i32)
    guests, line, key, pos, meta = pl.pallas_call(
        functools.partial(names_kernel, block),
        out_shape=(shape((GUESTS, WIDTH), bf16), shape((8, CHIPS * block), i32), table, table, shape((8, LANES), i32)),
        in_specs=[WHOLE], out_specs=(WHOLE,) * 5, compiler_params=params(12), name="names",
    )(packed)
    brought = lax.ppermute(guests, "z", [(i, (i + 3) % 4) for i in range(4)])
    share = shape((SHARE_ROWS, WIDTH), bf16)
    send, mine = pl.pallas_call(
        functools.partial(sort_kernel, block), out_shape=(share, share),
        in_specs=[WHOLE] * 2, out_specs=(WHOLE,) * 2, compiler_params=params(24), name="sort",
    )(packed, line)
    brought, mine, send = lax.optimization_barrier((brought, mine, send))
    other = lax.ppermute(send, "c", [(0, 1), (1, 0)])
    swapped = lax.ppermute(brought, "c", [(0, 1), (1, 0)])
    raw, far = pl.pallas_call(
        own_kernel, out_shape=(shape((RAW_ROWS, LANES), f32), shape((8, GUESTS), i32)),
        in_specs=[WHOLE] * 4, out_specs=(WHOLE,) * 2,
        scratch_shapes=[pltpu.VMEM((SHARE_ROWS, WIDTH), bf16)],
        compiler_params=params(16), name="own",
        cost_estimate=pl.CostEstimate(flops=2 * RAW_ROWS * LANES * WIDTH, bytes_accessed=4 << 20, transcendentals=0),
    )(mine, brought, key, pos)
    partial = pl.pallas_call(
        functools.partial(gram_kernel, units),
        out_shape=[shape((units * UNIT, LANES), f32)] * 4,
        in_specs=[WHOLE] * 5, out_specs=[WHOLE] * 4,
        scratch_shapes=[pltpu.VMEM((4 * units * UNIT + CAPS[0], LANES), f32), pltpu.VMEM((SHARE_ROWS, WIDTH), bf16)],
        compiler_params=params(16), name="gram",
    )(meta, other, swapped, far, raw)
    arrived = [partial[0]] + [
        lax.ppermute(partial[s], "y", [(i, (i + s) % 4) for i in range(4)]) for s in (2, 1, 3)
    ]
    over, table = pl.pallas_call(
        functools.partial(fit_kernel, block, units),
        out_shape=(shape((8, LANES), i32), shape((4 * units, LANES), i32)),
        in_specs=[WHOLE, WHOLE], out_specs=(WHOLE, WHOLE), compiler_params=params(8), name="fit",
    )(packed, meta)
    arrived, fits, table = lax.optimization_barrier((arrived, over[0, 0] == 0, table))
    best = pl.pallas_call(
        functools.partial(max_kernel, units),
        out_shape=shape((2 * CHIPS, LANES), f32),
        in_specs=[WHOLE] * 6, out_specs=WHOLE, compiler_params=params(8), name="maxima",
    )(table, *arrived, pos)
    back = lax.all_to_all(best.reshape(2 * CHIPS, 1, LANES), ("c", "x", "z", "y"), 0, 0, tiled=True)
    back, fits = lax.optimization_barrier((back, fits))
    best = pl.pallas_call(
        pick_kernel,
        out_shape=shape((1, ROWS), f32),
        in_specs=[WHOLE, WHOLE], out_specs=WHOLE, compiler_params=params(8), name="pick",
    )(back.reshape(2 * CHIPS, LANES), code).reshape(ROWS)
    return best, fits


def on_device(embeddings, cluster_ids, tries=TRIES):
    if not tries:
        return gather_groups(embeddings, cluster_ids)
    best, fits = route(*tries[0], embeddings, cluster_ids)
    return lax.cond(
        fits,
        lambda best, embeddings, cluster_ids: best,
        lambda best, embeddings, cluster_ids: on_device(embeddings, cluster_ids, tries[1:]),
        best, embeddings, cluster_ids,
    )


def solution(mesh):
    axes = ("x", "z", "y", "c")
    grid = Mesh(mesh.devices.reshape(4, 4, 4, 2), axes)
    return jax.shard_map(
        on_device, mesh=grid, in_specs=(P(axes, None), P(axes)), out_specs=P(axes), check_vma=False
    )
```

```python
import functools

import jax
import jax.numpy as jnp
from jax import lax
from jax.experimental import pallas as pl
from jax.experimental.pallas import tpu as pltpu
from jax.sharding import Mesh, PartitionSpec as P

ROWS = 128
HALF_WIDTH = 2048
WIDTH = 512
LABEL_ROWS = 16
BINS = 16
CHIPS = 64
TRIES = ((24, 11), (32, 16))
GROUP = 32
GUESTS = 64
GUEST = 4096
LANES = 128
CAPS = (704, 512, 320, 192)
STARTS = (0, 704, 1216, 1536)
UNIT = 32
SHARES = (
    ((0, 0), (0, 256), (2, 0), (2, 128), (2, 256), (3, 0)),
    ((0, 128), (0, 384), (0, 512), (0, 640), (1, 0), (1, 128), (1, 256), (1, 384), (3, 128)),
)
BASES = ({0: 0, 2: 704, 3: 1024}, {0: -128, 1: 576, 3: 960})
SHARE_ROWS = 1216
SEGMENTS = (
    (0, 128, 0, None), (128, 576, 128, 0), (704, 256, None, 576), (960, 256, None, 832),
    (1216, 320, 704, None), (1536, 128, 1024, None), (1664, 64, 1152, 1088),
)
f32, bf16, i32 = jnp.float32, jnp.bfloat16, jnp.int32
WHOLE = pl.BlockSpec(memory_space=pltpu.VMEM)


def params(mib):
    return pltpu.CompilerParams(vmem_limit_bytes=mib * 1024 * 1024)


def index_on(axis):
    return lax.axis_index(axis)


def iota(shape, dim):
    return lax.broadcasted_iota(i32, shape, dim)


def dot_last(a, b):
    return lax.dot_general(a, b, (((1,), (1,)), ((), ())), preferred_element_type=f32)


def dot(a, b):
    return lax.dot_general(a, b, (((1,), (0,)), ((), ())), preferred_element_type=f32)


def as_bf16(mask):
    return jnp.where(mask, 1.0, 0.0).astype(bf16)


def bin_of(labels):
    rank, residue = labels >> 2, labels & 3
    row, col = rank >> 2, rank & 3
    col = jnp.where((row & 1) == 1, 3 - col, col)
    return 4 * col + ((row - residue) & 3)


def label_rows(ids_ref):
    ids = jnp.concatenate([ids_ref[...].astype(f32), jnp.zeros((1, HALF_WIDTH - ROWS), f32)], axis=1)
    return jnp.broadcast_to(ids, (LABEL_ROWS, HALF_WIDTH)).astype(bf16)


def half_of(core):
    return pl.ds(pl.multiple_of(core * HALF_WIDTH, HALF_WIDTH), HALF_WIDTH)


def unit_send_kernel(x_ref, ids_ref, out_ref, scale_ref):
    x = x_ref[...]
    scale = lax.rsqrt(jnp.sum(x * x, axis=1, keepdims=True) + 1e-06)
    scale_ref[...] = jnp.broadcast_to(scale, scale_ref.shape)
    out_ref[:ROWS, :] = (x_ref[:, half_of(1 - index_on("c"))] * scale).astype(bf16)
    out_ref[ROWS:, :] = label_rows(ids_ref)


def unit_keep_kernel(x_ref, ids_ref, scale_ref, out_ref, half_ref, sem):
    copy = pltpu.make_async_copy(x_ref.at[:, half_of(index_on("c"))], half_ref, sem)
    copy.start()
    out_ref[ROWS:, :] = label_rows(ids_ref)
    copy.wait()
    out_ref[:ROWS, :] = (half_ref[...] * scale_ref[:, :1]).astype(bf16)


def passed_on(over, before):
    once = before(over, 1)
    twice = before(over, 2)
    return jnp.maximum(jnp.maximum(over, 0), jnp.maximum(over + once, over + once + twice))


def pack_kernel(block, keep_ref, got_ref, out_ref, code_ref):
    first = index_on("c") == 0
    kept = jnp.max(keep_ref[ROWS:, :ROWS].astype(f32), axis=0, keepdims=True)
    got = jnp.max(got_ref[ROWS:, :ROWS].astype(f32), axis=0, keepdims=True)
    labels = jnp.concatenate([jnp.where(first, kept, got), jnp.where(first, got, kept)], axis=0).astype(i32)
    bins = bin_of(labels)
    upper = as_bf16(iota((ROWS, ROWS), 0) < iota((ROWS, ROWS), 1))

    def ranks_within(masks):
        member = jnp.concatenate([jnp.where(mask, 1.0, 0.0) for mask in masks], axis=0)
        row, col = iota((member.shape[0],) * 2, 0), iota((member.shape[0],) * 2, 1)
        earlier = dot(as_bf16(((row >> 1) == (col >> 1)) & (col < row)), member.astype(bf16))
        ranks = member * (dot(member.astype(bf16), upper) + jnp.sum(earlier, axis=1, keepdims=True))
        rank = sum(ranks[2 * b:2 * b + 2] for b in range(len(masks)))
        return rank.astype(i32), jnp.sum(member, axis=1, keepdims=True)

    rank, sizes = ranks_within([bins == b for b in range(BINS)])
    quad, line = bins >> 2, bins & 3
    taken = []
    for at in range(4):
        size = jnp.zeros(labels.shape, f32)
        for b in range(at, BINS, 4):
            size = jnp.where(quad == b >> 2, sizes[2 * b:2 * b + 1] + sizes[2 * b + 1:2 * b + 2], size)
        taken.append(size.astype(i32) - (block - 1))
    stays = []
    for at in range(4):
        moved = passed_on(taken[at], lambda _, back: taken[(at - back) & 3])
        stays.append(taken[at] + (block - 1) - moved)

    def of_line(values, which):
        out = values[0]
        for at in range(1, 4):
            out = jnp.where(which == at, values[at], out)
        return out

    stay = of_line(stays, line)
    to_line = jnp.where(rank < stay, line, (line + 1) & 3)
    to_slot = jnp.where(rank < stay, rank, of_line(stays, to_line) + rank - stay)
    placed = to_slot < (block - 1)
    lane = jnp.where(placed, to_line * GROUP + to_slot, -1)
    place = jnp.where(placed, (quad * 4 + to_line) * block + to_slot, -1)
    code_ref[...] = jnp.concatenate([jnp.where(placed, bins * LANES + lane, -1)] * 4, axis=0)
    docs = 2 * ROWS
    flat = lambda v: jnp.concatenate([v[:1], v[1:]], axis=1)
    label_row = flat(labels)
    counts = dot_last(jnp.ones((8, docs), bf16), as_bf16(iota((LANES, docs), 0) == label_row))[:1]
    named = jnp.where(iota((8, docs), 0) == flat(quad), (label_row + 1).astype(f32), 0.0).astype(bf16)
    names = dot_last(named, as_bf16(iota((LANES, docs), 0) == flat(lane)))
    own = jnp.where(first, place[:1], place[1:])
    other = jnp.where(first, place[1:], place[:1])
    onehot = as_bf16(iota((BINS * block, docs), 0) == jnp.concatenate([own, other], axis=1))
    is_last = iota((block, WIDTH), 0) == (block - 1)
    for y in range(4):
        columns = slice(y * WIDTH, (y + 1) * WIDTH)
        x = jnp.concatenate([keep_ref[:ROWS, columns], got_ref[:ROWS, columns]], axis=0)
        packed = dot(onehot, x)
        for b in range(BINS):
            extra = jnp.concatenate([names[b // 4:b // 4 + 1], counts, jnp.zeros((1, 2 * LANES), f32)], axis=1)
            out_ref[4 * b + y] = jnp.where(is_last, extra, packed[b * block:(b + 1) * block]).astype(bf16)


def labels_of(block, x_ref):
    tail = x_ref[:, block - 8:, :2 * LANES].astype(f32)
    tail = jnp.max(jnp.where(iota(tail.shape, 1) == 7, tail, 0.0), axis=1)
    return tail[:, :LANES].astype(i32) - 1, tail[:, LANES:].astype(bf16)


def counts_of(chip_counts):
    row, col = iota((LANES, LANES), 0), iota((LANES, LANES), 1)
    in_bin = (bin_of(row) == col) & (row < 4 * BINS)
    counts = [dot(chip_counts, as_bf16(in_bin & ((row & 3) == r))) for r in range(4)]
    return counts, [jnp.sum(v, axis=0, keepdims=True) for v in counts]


def in_order(sizes):
    a, b = jnp.maximum(sizes[0], sizes[1]), jnp.minimum(sizes[0], sizes[1])
    c, d = jnp.maximum(sizes[2], sizes[3]), jnp.minimum(sizes[2], sizes[3])
    first, e = jnp.maximum(a, c), jnp.minimum(a, c)
    g, fourth = jnp.maximum(b, d), jnp.minimum(b, d)
    return first, jnp.maximum(e, g), jnp.minimum(e, g), fourth


def names_kernel(block, x_ref, guest_ref, line_ref, key_ref, pos_ref, meta_ref):
    z = index_on("z")
    labels, _ = labels_of(block, x_ref)
    row, col = iota((LANES, LANES), 0), iota((LANES, LANES), 1)
    lane = iota(labels.shape, 1)
    group = lane >> 5
    valid = labels >= 0
    home = bin_of(labels) & 3
    at_home = valid & (home == z)
    upper = as_bf16(row < col)
    lower = as_bf16(iota((CHIPS, CHIPS), 1) < iota((CHIPS, CHIPS), 0))
    members, n = [at_home & ((labels & 3) == r) for r in range(4)], []
    for member in members:
        size = jnp.sum(jnp.where(member, 1.0, 0.0), axis=0, keepdims=True)
        n.append(jnp.sum(size, axis=1, keepdims=True))
    wide = lambda v: jnp.broadcast_to(v, (1, LANES))
    meta_ref[...] = jnp.concatenate([wide(v) for v in in_order(n)] * 2, axis=0).astype(i32)
    pos = jnp.full(labels.shape, -1.0, f32)
    for r, member in enumerate(members):
        place = sum(
            jnp.where((n[q] > n[r]) | ((n[q] == n[r]) & (q < r)), 1.0, 0.0) for q in range(4) if q != r
        )
        start = jnp.where(
            place < 0.5, float(STARTS[0]),
            jnp.where(place < 1.5, float(STARTS[1]), jnp.where(place < 2.5, float(STARTS[2]), float(STARTS[3]))),
        )
        member16 = as_bf16(member)
        rank = dot(member16, upper) + jnp.sum(dot(lower, member16), axis=1, keepdims=True)
        pos = jnp.where(member, start + rank, pos)
    pos = pos.astype(i32)
    pos_ref[...] = pos
    guest = valid & (home != group)
    guest16 = as_bf16(guest)
    same = (row >> 5) == (col >> 5)
    turn = dot(guest16, as_bf16(same & (row < col))) + dot(dot(lower, guest16).astype(bf16), as_bf16(same))
    turn = turn.astype(i32)
    away = at_home & (group != z) & (turn < GUESTS)
    key_ref[...] = jnp.where(away, turn, -1)
    per, groups = 16, CHIPS // 16
    value = jnp.where(group == z, jnp.where(guest, GUEST + turn, pos + 1), 0).astype(f32)
    value = pltpu.roll(value, lax.rem(LANES - GROUP * z, LANES), 1)
    value = jnp.where(lane < block, value, 0.0)
    lined = jnp.zeros((8, per * block), f32)
    for t in range(per):
        rows = jnp.concatenate([value[per * g + t:per * g + t + 1] for g in range(groups)] * 2, axis=0)
        rows = jnp.concatenate([rows, jnp.zeros((8, per * block - LANES), f32)], axis=1)
        lined = lined + (pltpu.roll(rows, t * block, 1) if t else rows)
    slots = jnp.concatenate([lined[g:g + 1] for g in range(groups)], axis=1).astype(i32)
    line_ref[...] = jnp.broadcast_to(slots, line_ref.shape)
    onehot = as_bf16(iota((GUESTS, CHIPS * block), 0) + GUEST == slots)
    guest_ref[...] = dot(onehot, x_ref[...].reshape(CHIPS * block, WIDTH)).astype(bf16)


def sorted_rows(segment, slots, x):
    onehot = as_bf16(iota((segment[1], x.shape[0]), 0) + (segment[0] + 1) == slots)
    return dot(onehot, x).astype(bf16)


def sort_kernel(block, x_ref, line_ref, send_ref, mine_ref):
    x = x_ref[...].reshape(CHIPS * block, WIDTH)
    slots = line_ref[:1, :]
    for core in range(2):
        @pl.when(index_on("c") == core)
        def _():
            for segment in SEGMENTS:
                rows = sorted_rows(segment, slots, x)
                for out_ref, at in ((mine_ref, segment[2 + core]), (send_ref, segment[2 + 1 - core])):
                    if at is not None:
                        out_ref[at:at + segment[1], :] = rows


def fit_kernel(block, units, x_ref, meta_ref, over_ref, table_ref):
    _, chip_counts = labels_of(block, x_ref)
    counts, sizes = counts_of(chip_counts)
    ordered = in_order(sizes)
    over = jnp.zeros((1, LANES), f32)
    for size, cap in zip(ordered, CAPS):
        over = jnp.maximum(over, jnp.where(size > cap, 1.0, 0.0))
    for share in SHARES:
        length = 0.0
        for q, first in share:
            rows = jnp.maximum(jnp.floor((ordered[q] + (UNIT - 1.0)) * (1 / UNIT)) - first // UNIT, 0.0)
            length = length + jnp.where(rows >= 3.0, rows - 1.0, rows)
        over = jnp.maximum(over, jnp.where(length > 4 * units, 1.0, 0.0))
    taken = counts[0] + counts[1] + counts[2] + counts[3]
    lane = iota(taken.shape, 1) & 3
    before = lambda v, back: jnp.where(lane >= back, pltpu.roll(v, back, 1), pltpu.roll(v, LANES - 4 + back, 1))
    extra = taken - (block - 1)
    moved = passed_on(extra, before)
    held = jnp.sum(moved, axis=0, keepdims=True)
    over = jnp.maximum(over, jnp.where(held > GUESTS, 1.0, 0.0))
    full = extra + before(extra, 1) + before(extra, 2) + before(extra, 3) > 0
    full = jnp.where(full | (moved > block - 1), 1.0, 0.0)
    over = jnp.maximum(over, jnp.max(full, axis=0, keepdims=True))
    over_ref[...] = jnp.broadcast_to(jnp.max(over, axis=1, keepdims=True), over_ref.shape).astype(i32)
    y, c = index_on("y"), index_on("c")
    blocks, sizes = [], [size_of(meta_ref, q) for q in range(4)]
    for core, share in enumerate(SHARES):
        at = jnp.zeros((), i32)
        for q, first in share:
            length = length_of(sizes[q], first)
            blocks.append((jnp.where((c == core) & (length > 0), at, 4 * units), FIRST_ROW[q] + first // LANES, at))
            at = at + length
    for t in range(units):
        index = y * units + t
        col, start = jnp.asarray(15, i32), jnp.asarray(0, i32)
        for block_start, block_col, block_at in blocks:
            inside = index >= block_start
            col, start = jnp.where(inside, block_col, col), jnp.where(inside, block_at, start)
        turn = index - start
        unit = 4 * col + jnp.where(turn == 0, 2, jnp.where(turn == 1, 1, turn + 1))
        beside = jnp.where(turn == 0, 3 * UNIT, LANES)
        for entry, value in enumerate((unit >> 2, (unit & 3) * UNIT, beside, col)):
            table_ref[4 * t + entry:4 * t + entry + 1, :] = jnp.full((1, LANES), value, i32)


def add_guests(core, base_ref, guest_ref, far_ref, out_ref):
    guests, far = guest_ref[...], far_ref[:1, :]
    for segment in SEGMENTS:
        at, rows = segment[2 + core], segment[1]
        if at is not None:
            out_ref[at:at + rows, :] = base_ref[at:at + rows, :] + sorted_rows(segment, far, guests)


def blocks_of(core):
    for q, first in SHARES[core]:
        at = BASES[core][q] + first
        yield q, first, pl.ds(at, CAPS[q] - first), pl.ds(at, LANES)


RAW_ROWS = max(sum(CAPS[q] - first for q, first in share) for share in SHARES)


def own_kernel(x_ref, guest_ref, key_ref, pos_ref, raw_ref, far_ref, rows_ref):
    total = jnp.zeros((8, GUESTS), f32)
    step = 16
    for first in range(0, CHIPS, step):
        flat = lambda ref: jnp.concatenate([ref[s:s + 1, :] for s in range(first, first + step)], axis=1)
        places = flat(pos_ref) + 1
        parts = jnp.where(iota((8, step * LANES), 0) == 0, places >> 5, places & 31).astype(f32).astype(bf16)
        total = total + dot_last(parts, as_bf16(iota((GUESTS, step * LANES), 0) == flat(key_ref)))
    far_ref[...] = jnp.broadcast_to((32.0 * total[:1] + total[1:2]).astype(i32), far_ref.shape)
    for core in range(2):
        @pl.when(index_on("c") == core)
        def _():
            add_guests(core, x_ref, guest_ref, far_ref, rows_ref)
            at = 0
            for q, first, left, right in blocks_of(core):
                rows = CAPS[q] - first
                raw_ref[at:at + rows, :] = dot_last(rows_ref[left, :], rows_ref[right, :])
                at += rows


def size_of(meta_ref, q):
    return jnp.max(meta_ref[q:q + 1, :].astype(f32)).astype(i32)


def length_of(size, first):
    units = jnp.maximum(((size + UNIT - 1) >> 5) - first // UNIT, 0)
    return jnp.where(units >= 3, units - 1, units)


def folded(score):
    away = jnp.full((UNIT, LANES), -4.0, f32) if score.shape[0] < LANES else score[2 * UNIT:3 * UNIT]
    both = jnp.where(iota(away.shape, 1) < 3 * UNIT, away, pltpu.roll(score[:UNIT], 3 * UNIT, 1))
    rest = [score[3 * UNIT:]] if score.shape[0] > 3 * UNIT else []
    return jnp.concatenate([both, score[UNIT:2 * UNIT]] + rest, axis=0)


def gram_kernel(units, meta_ref, x_ref, guest_ref, far_ref, raw_ref, out0, out1, out2, out3, part_ref, rows_ref):
    y, c = index_on("y"), index_on("c")
    part_ref[:4 * units * UNIT, :] = jnp.full((4 * units * UNIT, LANES), -4.0, f32)
    for core in range(2):
        @pl.when(c == core)
        def _():
            add_guests(core, x_ref, guest_ref, far_ref, rows_ref)
            at, to = 0, jnp.zeros((), i32)
            for q, first, left, right in blocks_of(core):
                rows = CAPS[q] - first
                score = raw_ref[at:at + rows, :] + dot_last(rows_ref[left, :], rows_ref[right, :])
                at += rows
                size = size_of(meta_ref, q)
                i, j = iota(score.shape, 0), iota(score.shape, 1)
                keep = (i < size - first) & (j < size - first) & (i != j)
                score = folded(jnp.where(keep, score, -4.0))
                part_ref[pl.ds(pl.multiple_of(to, UNIT), score.shape[0]), :] = score
                to = jnp.minimum(to + UNIT * length_of(size, first), 4 * units * UNIT)
    chunk = units * UNIT
    for shift, out in enumerate((out0, out1, out2, out3)):
        out[...] = part_ref[pl.ds(pl.multiple_of(lax.rem(y + shift, 4) * chunk, UNIT), chunk), :]


FIRST_ROW = (0, 6, 10, 13)


def max_kernel(units, table_ref, p0, p1, p2, p3, pos_ref, out_ref):
    best = jnp.full((16, LANES), -1.0, f32)
    sub, lane, row = iota((UNIT, LANES), 0), iota((UNIT, LANES), 1), iota((16, LANES), 0)
    for t in range(units):
        at = slice(t * UNIT, (t + 1) * UNIT)
        block = (p0[at, :] + p1[at, :]) + (p2[at, :] + p3[at, :])
        unit_row, offset, beside, col = (table_ref[4 * t + entry:4 * t + entry + 1, :] for entry in range(4))
        one, two = jnp.where(lane < beside, block, -4.0), jnp.where(lane < beside, -4.0, block)
        along = jnp.max(one, axis=1, keepdims=True)
        along = jnp.max(jnp.where(sub + offset == lane, along, -1.0), axis=0, keepdims=True)
        best = jnp.maximum(best, jnp.where(row == unit_row, along, -1.0))
        down = jnp.max(jnp.maximum(one, pltpu.roll(two, UNIT, 1)), axis=0, keepdims=True)
        best = jnp.maximum(best, jnp.where(row == col, down, -1.0))
    pos = pos_ref[...]
    pos = jnp.where(pos >= STARTS[1], pos + 64, pos)
    pos = jnp.where(pos >= STARTS[3] + 64, pos + 64, pos)
    row, lane = pos >> 7, pos & (LANES - 1)
    out = jnp.full(pos.shape, -1.0, f32)
    for r in range(15):
        value = jnp.broadcast_to(best[r:r + 1, :], pos.shape)
        value = jnp.take_along_axis(value, lane, axis=1, mode="promise_in_bounds")
        out = jnp.where(row == r, value, out)
    out_ref[:CHIPS, :] = out
    out_ref[CHIPS:, :] = out


def pick_kernel(v_ref, code_ref, out_ref):
    values = jnp.maximum(v_ref[:CHIPS, :], v_ref[CHIPS:, :])
    values = jnp.max(values.reshape(BINS, 4, LANES), axis=1)
    code = jnp.max(jnp.where(iota((8, ROWS), 0) == index_on("c"), code_ref[...], -1), axis=0, keepdims=True)
    code = jnp.broadcast_to(code, (8, ROWS))
    row, lane = code >> 7, code & (LANES - 1)
    best = jnp.full((8, ROWS), -1.0, f32)
    for b in range(BINS):
        value = jnp.broadcast_to(values[b:b + 1], (8, ROWS))
        best = jnp.where(row == b, jnp.take_along_axis(value, lane, axis=1, mode="promise_in_bounds"), best)
    out_ref[...] = best[:1]


def gather_groups(embeddings, cluster_ids):
    split = ("z", "y", "c")
    rows = embeddings.shape[0]
    groups = lax.axis_size("x")
    cap = 2 * rows // groups
    slots = groups * cap
    owner_of = cluster_ids % groups
    onehot = (owner_of[:, None] == jnp.arange(groups, dtype=i32)[None, :]).astype(i32)
    before = jnp.cumsum(onehot, axis=0) - onehot
    rank = jnp.sum(before * onehot, axis=1)
    place = owner_of * cap + rank
    picked = place[None, :] == jnp.arange(slots, dtype=i32)[:, None]
    filled = jnp.any(picked, axis=1)
    source = jnp.sum(jnp.where(picked, jnp.arange(rows, dtype=i32)[None, :], 0), axis=1)
    out_labels = jnp.where(filled, cluster_ids[source], -1)
    squares = jnp.sum(embeddings * embeddings, axis=1, keepdims=True)
    local_unit = (embeddings * lax.rsqrt(squares + 1e-06)).astype(bf16)
    outgoing_unit = jnp.where(filled[:, None], local_unit[source], jnp.zeros((), bf16))
    unit = lax.all_to_all(outgoing_unit, "x", split_axis=0, concat_axis=0, tiled=True)
    labels = lax.all_to_all(out_labels, "x", split_axis=0, concat_axis=0, tiled=True)
    members = lax.axis_size(split)

    def everywhere(v):
        copies = jnp.broadcast_to(v[None], (members,) + v.shape).reshape((members * slots,) + v.shape[1:])
        return lax.all_to_all(copies, split, split_axis=0, concat_axis=0, tiled=True)

    def add_slice(i, scores):
        part = lax.dynamic_slice_in_dim(unit, i * WIDTH, WIDTH, 1)
        return scores + dot_last(part, everywhere(part))

    scores = lax.fori_loop(0, embeddings.shape[1] // WIDTH, add_slice, jnp.zeros((slots, members * slots), f32))
    all_labels = everywhere(labels)
    own = lax.axis_index(split) * slots + jnp.arange(slots, dtype=i32)
    mask = (
        (labels[:, None] == all_labels[None, :])
        & (labels[:, None] >= 0)
        & (own[:, None] != jnp.arange(members * slots, dtype=i32)[None, :])
    )
    scores = jnp.where(mask, scores, -1.0)
    best = jnp.maximum(-1.0, jnp.max(scores, axis=1))
    returned = lax.all_to_all(best, "x", split_axis=0, concat_axis=0, tiled=True)
    return returned[place]


def route(block, units, embeddings, cluster_ids):
    shape = jax.ShapeDtypeStruct
    half = shape((ROWS + LABEL_ROWS, HALF_WIDTH), bf16)
    ids = cluster_ids.reshape(1, ROWS)
    send, scale = pl.pallas_call(
        unit_send_kernel, out_shape=(half, shape((ROWS, LANES), f32)),
        in_specs=[WHOLE, WHOLE], out_specs=(WHOLE, WHOLE), compiler_params=params(12), name="unit_send",
    )(embeddings, ids)
    got = lax.ppermute(send, "c", [(0, 1), (1, 0)])
    keep = pl.pallas_call(
        unit_keep_kernel, out_shape=half,
        in_specs=[pl.BlockSpec(memory_space=pl.ANY), WHOLE, WHOLE], out_specs=WHOLE,
        scratch_shapes=[pltpu.VMEM((ROWS, HALF_WIDTH), f32), pltpu.SemaphoreType.DMA],
        compiler_params=params(8), name="unit_keep",
    )(embeddings, ids, scale)
    packed, code = pl.pallas_call(
        functools.partial(pack_kernel, block),
        out_shape=(shape((CHIPS, block, WIDTH), bf16), shape((8, ROWS), i32)),
        in_specs=[WHOLE, WHOLE], out_specs=(WHOLE, WHOLE), compiler_params=params(20), name="pack",
    )(keep, got)
    packed = lax.all_to_all(packed, ("x", "z", "y"), 0, 0, tiled=True)
    table = shape((CHIPS, LANES), i32)
    guests, line, key, pos, meta = pl.pallas_call(
        functools.partial(names_kernel, block),
        out_shape=(shape((GUESTS, WIDTH), bf16), shape((8, CHIPS * block), i32), table, table, shape((8, LANES), i32)),
        in_specs=[WHOLE], out_specs=(WHOLE,) * 5, compiler_params=params(12), name="names",
    )(packed)
    brought = lax.ppermute(guests, "z", [(i, (i + 3) % 4) for i in range(4)])
    share = shape((SHARE_ROWS, WIDTH), bf16)
    send, mine = pl.pallas_call(
        functools.partial(sort_kernel, block), out_shape=(share, share),
        in_specs=[WHOLE] * 2, out_specs=(WHOLE,) * 2, compiler_params=params(24), name="sort",
    )(packed, line)
    brought, mine, send = lax.optimization_barrier((brought, mine, send))
    other = lax.ppermute(send, "c", [(0, 1), (1, 0)])
    swapped = lax.ppermute(brought, "c", [(0, 1), (1, 0)])
    raw, far = pl.pallas_call(
        own_kernel, out_shape=(shape((RAW_ROWS, LANES), f32), shape((8, GUESTS), i32)),
        in_specs=[WHOLE] * 4, out_specs=(WHOLE,) * 2,
        scratch_shapes=[pltpu.VMEM((SHARE_ROWS, WIDTH), bf16)],
        compiler_params=params(16), name="own",
        cost_estimate=pl.CostEstimate(flops=2 * RAW_ROWS * LANES * WIDTH, bytes_accessed=4 << 20, transcendentals=0),
    )(mine, brought, key, pos)
    partial = pl.pallas_call(
        functools.partial(gram_kernel, units),
        out_shape=[shape((units * UNIT, LANES), f32)] * 4,
        in_specs=[WHOLE] * 5, out_specs=[WHOLE] * 4,
        scratch_shapes=[pltpu.VMEM((4 * units * UNIT + CAPS[0], LANES), f32), pltpu.VMEM((SHARE_ROWS, WIDTH), bf16)],
        compiler_params=params(16), name="gram",
    )(meta, other, swapped, far, raw)
    arrived = [partial[0]] + [
        lax.ppermute(partial[s], "y", [(i, (i + s) % 4) for i in range(4)]) for s in (2, 1, 3)
    ]
    over, table = pl.pallas_call(
        functools.partial(fit_kernel, block, units),
        out_shape=(shape((8, LANES), i32), shape((4 * units, LANES), i32)),
        in_specs=[WHOLE, WHOLE], out_specs=(WHOLE, WHOLE), compiler_params=params(8), name="fit",
    )(packed, meta)
    arrived, fits, table = lax.optimization_barrier((arrived, over[0, 0] == 0, table))
    best = pl.pallas_call(
        functools.partial(max_kernel, units),
        out_shape=shape((2 * CHIPS, LANES), f32),
        in_specs=[WHOLE] * 6, out_specs=WHOLE, compiler_params=params(8), name="maxima",
    )(table, *arrived, pos)
    back = lax.all_to_all(best.reshape(2 * CHIPS, 1, LANES), ("c", "x", "z", "y"), 0, 0, tiled=True)
    back, fits = lax.optimization_barrier((back, fits))
    best = pl.pallas_call(
        pick_kernel,
        out_shape=shape((1, ROWS), f32),
        in_specs=[WHOLE, WHOLE], out_specs=WHOLE, compiler_params=params(8), name="pick",
    )(back.reshape(2 * CHIPS, LANES), code).reshape(ROWS)
    return best, fits


def on_device(embeddings, cluster_ids, tries=TRIES):
    if not tries:
        return gather_groups(embeddings, cluster_ids)
    best, fits = route(*tries[0], embeddings, cluster_ids)
    return lax.cond(
        fits,
        lambda best, embeddings, cluster_ids: best,
        lambda best, embeddings, cluster_ids: on_device(embeddings, cluster_ids, tries[1:]),
        best, embeddings, cluster_ids,
    )


def solution(mesh):
    axes = ("x", "z", "y", "c")
    grid = Mesh(mesh.devices.reshape(4, 4, 4, 2), axes)
    return jax.shard_map(
        on_device, mesh=grid, in_specs=(P(axes, None), P(axes)), out_specs=P(axes), check_vma=False
    )
```
